32 devices in a mesh: groups: 2 (over y), px: 8 (over z, x), py: 2 (over core).
Axes of the slice: x: 2, y: 2, z: 4, core: 2. Of those that a mesh axis runs over, the one named last changes fastest.
Arguments:
- velocity: float32 [3, 16, 128, 128], P(None, ('groups', 'px'), 'py'), parts along dimension 1, may hold values from -6 to 6
- cotangent: float32 [3, 16, 128, 128], P(None, ('groups', 'px'), 'py'), parts along dimension 1, may hold values from -6 to 6
- first_kernel: float32 [16, 3, 3, 3, 3], replicated, may hold values from -0.625 to 0.625
- first_bias: float32 [16], replicated, may hold values from -3 to 3
- second_kernel: float32 [6, 16, 3, 3, 3], replicated, may hold values from -0.3125 to 0.3125
- second_bias: float32 [6], replicated, may hold values from -4 to 4
Outputs:
- grad_velocity: float32 [3, 16, 128, 128], P(None, ('groups', 'px'), 'py'), parts along dimension 1
- grad_first_kernel: float32 [32, 3, 3, 3, 3], P('groups'), parts along dimension 0
- grad_first_bias: float32 [32], P('groups'), parts along dimension 0
- grad_second_kernel: float32 [12, 16, 3, 3, 3], P('groups'), parts along dimension 0
- grad_second_bias: float32 [12], P('groups'), parts along dimension 0
The draws below stay inside these ranges and needn't reach their ends.
There are 2 independent parts, one for each index of `groups`. The reference program is written for one: setup_inputs(seed, part) draws one part's arguments, and reference() takes and returns one part's arrays. A program takes and returns all parts, laid end to end along the dimension named above; an argument that names none is the same for every part. Nothing has to cross between parts.
All inputs are finite; a program needn't handle non-finite values.
Results may differ from the reference program's by a relative error of at most 0.0003.
Values sent between devices are 32-bit elements; how exact they have to be, the bound alone decides.
No kernel may reach another device: no remote copies, remote signals or barrier semaphores. Data moves between devices by JAX's collectives and lax.ppermute only.
A program may use at most 128 MiB of HBM per device.

```python
import jax
import jax.numpy as jnp
from jax import lax

NZ = 128
CHANNELS = 16
COEFFS = 6
ITERS = 2
NX = 8
NY = 128


def block_scale(rng, extent, split, low, high):
    def one(dim, blocks):
        heights = jax.random.uniform(jax.random.fold_in(jax.random.fold_in(rng, 6), dim), (blocks,), jnp.float32, low / len(split), high / len(split))
        return jnp.repeat(jnp.exp(heights), extent[dim] // blocks).reshape((-1,) + (1,) * (len(extent) - dim - 1))

    loudness = one(*split[0])
    for cut in split[1:]:
        loudness = loudness * one(*cut)
    return loudness


def gaussian(rng, dims, scale, reach, shards=(), kind=jnp.bfloat16):
    factor_of = block_scale(rng, dims, shards, -0.22, 0.18) if shards else 1.0
    values = jax.random.normal(rng, dims, jnp.float32) * scale * factor_of
    return jnp.minimum(jnp.maximum(values, -reach), reach).astype(kind)


def setup_inputs(seed: int = 0, part: int = 0) -> dict:
    keys = jax.random.split(jax.random.key(seed), 7)
    part_keys = jax.random.split(jax.random.fold_in(keys[6], part), 7)
    velocity = gaussian(part_keys[0], (3, NX, NY, NZ), 1.0, 6.0, ((1, 8), (2, 2)), jnp.float32)
    cotangent = gaussian(part_keys[1], (3, NX, NY, NZ), 1.0, 6.0, ((1, 8), (2, 2)), jnp.float32)
    first_kernel = gaussian(keys[2], (CHANNELS, 3, 3, 3, 3), (3 * 27) ** -0.5, 0.625, (), jnp.float32)
    first_bias = gaussian(keys[3], (CHANNELS,), 0.5, 3.0, (), jnp.float32)
    second_kernel = gaussian(keys[4], (COEFFS, CHANNELS, 3, 3, 3), (CHANNELS * 27) ** -0.5, 0.3125, (), jnp.float32)
    second_bias = gaussian(keys[5], (COEFFS,), 1.0, 4.0, (), jnp.float32)
    return dict(velocity=velocity, cotangent=cotangent, first_kernel=first_kernel, first_bias=first_bias, second_kernel=second_kernel, second_bias=second_bias)


KAPPA = 0.25

def pad_all(field):
    return jnp.pad(field, ((0, 0), (1, 1), (1, 1), (1, 1)), mode='wrap')

def convolve(padded, kernel, offset):
    result = lax.conv_general_dilated(padded[None], kernel, (1, 1, 1), 'VALID', dimension_numbers=('NCDHW', 'OIDHW', 'NCDHW'), precision=lax.Precision.HIGHEST)
    return result[0] + offset[:, None, None, None]

def moved(padded, axis_dim, offset_cells):
    index = [slice(None), slice(1, -1), slice(1, -1), slice(1, -1)]
    index[axis_dim] = slice(1 + offset_cells, padded.shape[axis_dim] - 1 + offset_cells)
    return padded[tuple(index)]

def advect(padded, weights):
    center = moved(padded, 1, 0)
    total = jnp.zeros_like(center)
    for direction in range(3):
        ahead = moved(padded, direction + 1, 1)
        behind = moved(padded, direction + 1, -1)
        vplus = 0.5 * (center[direction] + ahead[direction])
        vminus = 0.5 * (behind[direction] + center[direction])
        upper = center + weights[2 * direction] * (ahead - center)
        lower = center + weights[2 * direction + 1] * (behind - center)
        total = total + vplus * upper - vminus * lower
    return total

def wavenumbers(count):
    index = jnp.arange(count)
    return jnp.where(index < count // 2, index, index - count).astype(jnp.float32)

def project(field):
    spectrum = jnp.fft.fftn(field, axes=(1, 2, 3))
    wave_x = wavenumbers(field.shape[1])[:, None, None]
    wave_y = wavenumbers(field.shape[2])[None, :, None]
    wave_z = wavenumbers(field.shape[3])[None, None, :]
    vectors = jnp.stack(jnp.broadcast_arrays(wave_x, wave_y, wave_z))
    size = jnp.maximum(wave_x * wave_x + wave_y * wave_y + wave_z * wave_z, 1.0)
    inner = wave_x * spectrum[0] + wave_y * spectrum[1] + wave_z * spectrum[2]
    spectrum = spectrum - vectors * (inner / size)
    return jnp.real(jnp.fft.ifftn(spectrum, axes=(1, 2, 3)))

def advance(field, first_kernel, first_bias, second_kernel, second_bias):
    padded = pad_all(field)
    hidden = jnp.tanh(convolve(padded, first_kernel, first_bias))
    weights = jax.nn.sigmoid(convolve(pad_all(hidden), second_kernel, second_bias))
    return project(field - KAPPA * advect(padded, weights))

def reference(velocity, cotangent, first_kernel, first_bias, second_kernel, second_bias):

    def run(field, kernel_one, bias_one, kernel_two, bias_two):
        for section in range(ITERS):
            field = advance(field, kernel_one, bias_one, kernel_two, bias_two)
        return field
    final, pullback = jax.vjp(run, velocity, first_kernel, first_bias, second_kernel, second_bias)
    grads = pullback(cotangent)
    return (grads[0], grads[1], grads[2], grads[3], grads[4])
```

```python
import functools
import math

import jax
import jax.numpy as jnp
import numpy as np
from jax import lax
from jax.experimental import pallas as pl
from jax.experimental.pallas import tpu as pltpu
from jax.sharding import PartitionSpec as P

ITERS = 2


KAPPA = 0.25


def padded_2(value, sides, width):
    for axis, dim in sides:
        size, length = (lax.axis_size(axis), value.shape[dim])
        up = [(i, (i + 1) % size) for i in range(size)]
        down = [(j, i) for i, j in up]
        last = lax.slice_in_dim(value, length - width, length, axis=dim)
        initial = lax.slice_in_dim(value, 0, width, axis=dim)
        before = lax.ppermute(last, axis, up)
        after = lax.ppermute(initial, axis, down)
        value = jnp.concatenate([before, value, after], axis=dim)
    return value


def extend(field):
    rimmed = padded_2(field, (("px", 1), ("py", 2)), 1)
    return jnp.concatenate([rimmed[..., -1:], rimmed, rimmed[..., :1]], axis=3)


def across_columns(spectrum):
    return lax.all_to_all(spectrum, "px", split_axis=2, concat_axis=4, tiled=True)


def across_pairs(spectrum):
    return lax.all_to_all(spectrum, "py", split_axis=3, concat_axis=4, tiled=True)


def summed(grads):
    return lax.psum((grads[0], grads[1], grads[2], grads[3]), ("px", "py"))


def all_taps():
    return [
        (shift_x, shift_y, shift_z)
        for shift_x in range(3)
        for shift_y in range(3)
        for shift_z in range(3)
    ]


def gather_conv(padded, kernel):
    size_x = padded.shape[1] - 2
    size_y = padded.shape[2] - 2
    size_z = padded.shape[3] - 2
    stacked = jnp.concatenate(
        [
            padded[:, sx_one : sx_one + size_x, sy_one : sy_one + size_y, sz_one : sz_one + size_z]
            for sx_one, sy_one, sz_one in all_taps()
        ],
        axis=0,
    )
    matrix = jnp.transpose(kernel, (0, 2, 3, 4, 1)).reshape(kernel.shape[0], -1)
    result = jnp.einsum("ok,kxyz->oxyz", matrix, stacked, precision=lax.Precision.HIGHEST)
    return (result, stacked)


def scatter_conv(padded, kernel):
    outputs = kernel.shape[0]
    inputs = kernel.shape[1]
    size_x = padded.shape[1] - 2
    size_y = padded.shape[2] - 2
    size_z = padded.shape[3] - 2
    total = jnp.zeros((outputs, size_x, size_y, size_z), jnp.float32)
    for shift_x in range(3):
        matrix = jnp.transpose(kernel[:, :, shift_x], (0, 2, 3, 1)).reshape(outputs * 9, inputs)
        layer = jnp.einsum(
            "km,mxyz->kxyz",
            matrix,
            padded[:, shift_x : shift_x + size_x],
            precision=lax.Precision.HIGHEST,
        )
        layer = layer.reshape(outputs, 3, 3, size_x, size_y + 2, size_z + 2)
        for shift_y in range(3):
            for shift_z in range(3):
                total = (
                    total
                    + layer[
                        :,
                        shift_y,
                        shift_z,
                        :,
                        shift_y : shift_y + size_y,
                        shift_z : shift_z + size_z,
                    ]
                )
    return total


def flipped(kernel):
    return jnp.transpose(kernel[:, :, ::-1, ::-1, ::-1], (1, 0, 2, 3, 4))


def moved(padded, axis_dim, offset_cells):
    index = [slice(None), slice(1, -1), slice(1, -1), slice(1, -1)]
    index[axis_dim] = slice(1 + offset_cells, padded.shape[axis_dim] - 1 + offset_cells)
    return padded[tuple(index)]


def advect(padded, weights):
    center = moved(padded, 1, 0)
    total = jnp.zeros_like(center)
    for direction in range(3):
        ahead = moved(padded, direction + 1, 1)
        behind = moved(padded, direction + 1, -1)
        vplus = 0.5 * (center[direction] + ahead[direction])
        vminus = 0.5 * (behind[direction] + center[direction])
        upper = center + weights[2 * direction] * (ahead - center)
        lower = center + weights[2 * direction + 1] * (behind - center)
        total = total + vplus * upper - vminus * lower
    return total


def advect_back(padded, weights_pad, source_pad):
    center = moved(padded, 1, 0)
    source = moved(source_pad, 1, 0)
    weights = moved(weights_pad, 1, 0)
    grad_field = jnp.zeros_like(center)
    fluxes = []
    parts = []
    for direction in range(3):
        ahead = moved(padded, direction + 1, 1)
        behind = moved(padded, direction + 1, -1)
        vplus = 0.5 * (center[direction] + ahead[direction])
        vminus = 0.5 * (behind[direction] + center[direction])
        rate_up = weights[2 * direction]
        rate_low = weights[2 * direction + 1]
        rate_before = moved(weights_pad[2 * direction : 2 * direction + 1], direction + 1, -1)[0]
        rate_after = moved(weights_pad[2 * direction + 1 : 2 * direction + 2], direction + 1, 1)[0]
        source_before = moved(source_pad, direction + 1, -1)
        source_after = moved(source_pad, direction + 1, 1)
        upper = center + rate_up * (ahead - center)
        lower = center + rate_low * (behind - center)
        upper_before = behind + rate_before * (center - behind)
        lower_after = ahead + rate_after * (center - ahead)
        grad_field = grad_field + source * (vplus * (1.0 - rate_up) - vminus * (1.0 - rate_low))
        grad_field = (
            grad_field + vminus * rate_before * source_before - vplus * rate_after * source_after
        )
        fluxes.append(
            0.5
            * (
                jnp.sum(source * upper, 0)
                - jnp.sum(source * lower, 0)
                + jnp.sum(source_before * upper_before, 0)
                - jnp.sum(source_after * lower_after, 0)
            )
        )
        parts.append(jnp.sum(source * vplus * (ahead - center), 0))
        parts.append(-jnp.sum(source * vminus * (behind - center), 0))
    return (grad_field + jnp.stack(fluxes), jnp.stack(parts))


def tables(count):
    index = jnp.arange(count, dtype=jnp.int32)
    phase = index[:, None] * index[None, :] % count
    angle = phase.astype(jnp.float32) * (2.0 * math.pi / count)
    return (jnp.cos(angle), jnp.sin(angle))


def mix(form, data, table):
    return jnp.einsum(form, data, table, precision=lax.Precision.HIGHEST)


def waves(start, count, total):
    index = start + jnp.arange(count, dtype=jnp.int32)
    return jnp.where(index < total // 2, index, index - total).astype(jnp.float32)


def project(field):
    depth = field.shape[3]
    cos_z, sin_z = tables(depth)
    real_z = mix("cxyz,zk->cxky", field, cos_z)
    imag_z = -mix("cxyz,zk->cxky", field, sin_z)
    spectrum = across_pairs(jnp.stack([real_z, imag_z]))
    span_y = spectrum.shape[4]
    cos_y, sin_y = tables(span_y)
    real_y = mix("cxky,yq->cqkx", spectrum[0], cos_y) + mix("cxky,yq->cqkx", spectrum[1], sin_y)
    imag_y = mix("cxky,yq->cqkx", spectrum[1], cos_y) - mix("cxky,yq->cqkx", spectrum[0], sin_y)
    spectrum = across_columns(jnp.stack([real_y, imag_y]))
    span_x = spectrum.shape[4]
    cos_x, sin_x = tables(span_x)
    real_x = mix("cqkx,xp->cqkp", spectrum[0], cos_x) + mix("cqkx,xp->cqkp", spectrum[1], sin_x)
    imag_x = mix("cqkx,xp->cqkp", spectrum[1], cos_x) - mix("cqkx,xp->cqkp", spectrum[0], sin_x)
    rows_y = spectrum.shape[2]
    rows_z = spectrum.shape[3]
    wave_y = waves(lax.axis_index("px") * rows_y, rows_y, span_y)[:, None, None]
    wave_z = waves(lax.axis_index("py") * rows_z, rows_z, depth)[None, :, None]
    wave_x = waves(0, span_x, span_x)[None, None, :]
    size = jnp.maximum(wave_x * wave_x + wave_y * wave_y + wave_z * wave_z, 1.0)
    vectors = jnp.stack(jnp.broadcast_arrays(wave_x, wave_y, wave_z))
    real_x = real_x - vectors * (
        (wave_x * real_x[0] + wave_y * real_x[1] + wave_z * real_x[2]) / size
    )
    imag_x = imag_x - vectors * (
        (wave_x * imag_x[0] + wave_y * imag_x[1] + wave_z * imag_x[2]) / size
    )
    back_real = (mix("cqkp,px->cxkq", real_x, cos_x) - mix("cqkp,px->cxkq", imag_x, sin_x)) / span_x
    back_imag = (mix("cqkp,px->cxkq", imag_x, cos_x) + mix("cqkp,px->cxkq", real_x, sin_x)) / span_x
    spectrum = across_columns(jnp.stack([back_real, back_imag]))
    rows_real = (
        mix("cxkq,qy->cxyk", spectrum[0], cos_y) - mix("cxkq,qy->cxyk", spectrum[1], sin_y)
    ) / span_y
    rows_imag = (
        mix("cxkq,qy->cxyk", spectrum[1], cos_y) + mix("cxkq,qy->cxyk", spectrum[0], sin_y)
    ) / span_y
    spectrum = across_pairs(jnp.stack([rows_real, rows_imag]))
    return (
        mix("cxyk,kz->cxyz", spectrum[0], cos_z) - mix("cxyk,kz->cxyz", spectrum[1], sin_z)
    ) / depth


def forward_state(field, first_kernel, first_bias, second_kernel, second_bias):
    padded = extend(field)
    first_out, field_taps = gather_conv(padded, first_kernel)
    hidden = jnp.tanh(first_out + first_bias[:, None, None, None])
    weights = jax.nn.sigmoid(
        scatter_conv(extend(hidden), second_kernel) + second_bias[:, None, None, None]
    )
    return (padded, hidden, weights, field_taps)


def backward_step(state, upstream, first_kernel, second_kernel):
    padded, hidden, weights, field_taps = state
    moved_grad = project(upstream)
    source = -KAPPA * moved_grad
    stacked = extend(jnp.concatenate([source, weights], axis=0))
    grad_field, grad_weights = advect_back(padded, stacked[3:], stacked[:3])
    grad_field = grad_field + moved_grad
    grad_logits = grad_weights * weights * (1.0 - weights)
    logits_pad = extend(grad_logits)
    grad_hidden, logit_taps = gather_conv(logits_pad, flipped(second_kernel))
    product = jnp.einsum("kxyz,mxyz->km", logit_taps, hidden, precision=lax.Precision.HIGHEST)
    product = product.reshape(3, 3, 3, second_kernel.shape[0], second_kernel.shape[1])
    grad_second = jnp.transpose(product[::-1, ::-1, ::-1], (3, 4, 0, 1, 2))
    grad_second_bias = jnp.sum(grad_logits, axis=(1, 2, 3))
    grad_pre = grad_hidden * (1.0 - hidden * hidden)
    pre_pad = extend(grad_pre)
    grad_field = grad_field + scatter_conv(pre_pad, flipped(first_kernel))
    first_product = jnp.einsum(
        "oxyz,kxyz->ok", grad_pre, field_taps, precision=lax.Precision.HIGHEST
    )
    first_product = first_product.reshape(first_kernel.shape[0], 3, 3, 3, first_kernel.shape[1])
    grad_first = jnp.transpose(first_product, (0, 4, 1, 2, 3))
    grad_first_bias = jnp.sum(grad_pre, axis=(1, 2, 3))
    return (grad_field, (grad_first, grad_first_bias, grad_second, grad_second_bias))


def on_device(velocity, cotangent, first_kernel, first_bias, second_kernel, second_bias):
    field = velocity
    fields = [velocity]
    saved = []
    for section in range(ITERS):
        state = forward_state(field, first_kernel, first_bias, second_kernel, second_bias)
        saved.append(state)
        field = project(field - KAPPA * advect(state[0], state[2]))
        fields.append(field)
    upstream = cotangent
    totals = None
    for section in reversed(range(ITERS)):
        state = saved[section]
        upstream, grads = backward_step(state, upstream, first_kernel, second_kernel)
        grads = summed(grads)
        if totals is None:
            totals = grads
        else:
            totals = tuple((older + newer for older, newer in zip(totals, grads)))
    return (upstream, totals[0], totals[1], totals[2], totals[3])


SLAB = 8
RIM = 2
REACH = SLAB + 2 * RIM
WIDE = SLAB + 2
PLANES = 8
DEPTH = 128
ROWS = 128
CHANNELS = 16
COEFFS = 6
BAND = 32
HID = CHANNELS * WIDE
LOG = COEFFS * SLAB
STACK = 9 * 48
FLAT = PLANES * DEPTH
NN = ((1,), (0,))
NT = ((1,), (1,))


def real_basis(count):
    half = count // 2
    angle = 2.0 * np.pi * np.arange(count) / count
    rows = [np.full(count, 1.0 / np.sqrt(count))]
    rows += [np.sqrt(2.0 / count) * np.cos(k * angle) for k in range(1, half)]
    rows += [np.cos(half * angle) / np.sqrt(count)]
    rows += [np.sqrt(2.0 / count) * np.sin(k * angle) for k in range(1, half)]
    return np.stack(rows)


def halves(table):
    high = table.astype(np.float32).astype(jnp.bfloat16)
    low = (table - high.astype(np.float64)).astype(np.float32).astype(jnp.bfloat16)
    return high, low


def slab_of(device):
    return (device % 2) * PLANES + device // 2


@functools.cache
def constants():
    basis_x = real_basis(PLANES)
    mode_x = np.stack([basis_x[(k // 2) + (PLANES // 2) * (k % 2)] for k in range(PLANES)])
    basis_z = real_basis(DEPTH)
    order = []
    for group in range(4):
        order += [16 * group + i for i in range(16)] + [64 + 16 * group + i for i in range(16)]
    mode_z = basis_z[order]
    basis_y = real_basis(ROWS)

    def columns(device, offset, count):
        return basis_y[:, (SLAB * slab_of(device) + offset + np.arange(count)) % ROWS]

    def table(block, offset, count):
        out = np.zeros((3, ROWS, 16, block))
        for device in range(16):
            for m in range(3):
                out[m, :, device, m * count : (m + 1) * count] = columns(device, offset, count)
        return out.reshape(3 * ROWS, 16 * block)

    both_in = table(24, 0, 8)
    both_out = table(40, -RIM, REACH).T
    one_in = np.concatenate([table(24, -RIM, 6), table(24, -RIM + 6, 6)])
    one_out = np.concatenate([table(16, 0, 4).T, table(16, 4, 4).T])

    spread = np.zeros((2 * STACK, 96))
    mask = np.zeros((3, 2 * STACK, HID))
    for tap in range(9):
        for o in range(COEFFS):
            for q in range(SLAB):
                row = tap * 48 + o * SLAB + q
                spread[row, tap * COEFFS + o] = 1.0
                for b in range(3):
                    mask[b, row, np.arange(CHANNELS) * WIDE + q + b] = 1.0
        for m in range(3):
            for r in range(REACH):
                row = STACK + tap * 48 + m * REACH + r
                spread[row, 54 + tap * 3 + m] = 1.0
                for b in range(3):
                    if 0 <= r - b < WIDE:
                        mask[b, row, np.arange(CHANNELS) * WIDE + r - b] = 1.0
    lift = np.zeros((HID, 128))
    lift[np.arange(HID), np.arange(HID) // WIDE] = 1.0
    count = np.zeros((LOG, 128))
    count[np.arange(LOG), 16 + np.arange(LOG) // SLAB] = 1.0
    half = jnp.bfloat16
    return dict(
        mode_x=mode_x,
        to_z=halves(mode_z.T),
        from_z=halves(mode_z),
        both_in=halves(both_in),
        both_out=halves(both_out),
        one_in=halves(one_in),
        one_out=halves(one_out),
        spread=spread.astype(half),
        spread_t=np.ascontiguousarray(spread.T).astype(half),
        mask=mask.astype(half),
        mask_t=np.ascontiguousarray(mask.transpose(0, 2, 1)).astype(half),
        lift=lift.astype(half),
        lift_t=np.ascontiguousarray(lift[:, :CHANNELS].T).astype(half),
        count=count.astype(half),
    )


def dot(left, right, dims=NN):
    return lax.dot_general(left, right, (dims, ((), ())), preferred_element_type=jnp.float32)


def split(value):
    high = value.astype(jnp.bfloat16)
    return high, (value - high.astype(jnp.float32)).astype(jnp.bfloat16)


def dot3(left, right, dims=NN):
    return dot(left[0], right[0], dims) + (dot(left[0], right[1], dims) + dot(left[1], right[0], dims))


def turn(value, shift):
    shift = shift % value.shape[-1]
    return value if shift == 0 else pltpu.roll(value, shift, value.ndim - 1)


def plane(x):
    x = x % PLANES
    return slice(x * DEPTH, (x + 1) * DEPTH)


def call(kernel, outs, args, scratch=()):
    single = not isinstance(outs, (list, tuple))
    shapes = [outs] if single else outs
    return pl.pallas_call(
        kernel,
        out_shape=outs,
        in_specs=[pl.BlockSpec(memory_space=pltpu.VMEM)] * len(args),
        out_specs=(
            pl.BlockSpec(memory_space=pltpu.VMEM)
            if single
            else [pl.BlockSpec(memory_space=pltpu.VMEM)] * len(shapes)
        ),
        scratch_shapes=list(scratch),
        compiler_params=pltpu.CompilerParams(vmem_limit_bytes=56 * 2**20),
    )(*args)


def shape(*dims, kind=jnp.float32):
    return jax.ShapeDtypeStruct(dims, kind)


def weights_kernel(taps, spread, spread_t, mask, mask_t, lift, lift_t, fwd2, fwd1, back2, back1):
    parts = split(taps[...])
    for half in range(2):
        tall = jnp.zeros((2 * STACK, HID), jnp.float32)
        wide = jnp.zeros((HID, 2 * STACK), jnp.float32)
        for b in range(3):
            block = parts[half][:, b * 16 : (b + 1) * 16]
            rows = dot(spread[...], block).astype(jnp.bfloat16)
            tall = tall + mask[b].astype(jnp.float32) * dot(rows, lift_t[...])
            cols = dot(lift[:, :CHANNELS], block, NT).astype(jnp.bfloat16)
            wide = wide + mask_t[b].astype(jnp.float32) * dot(cols, spread_t[...])
        fwd2[half] = tall[:STACK].astype(jnp.bfloat16)
        back1[half] = tall[STACK:].astype(jnp.bfloat16)
        back2[half] = wide[:, :STACK].astype(jnp.bfloat16)
        fwd1[half] = wide[:, STACK:].astype(jnp.bfloat16)


def pack_kernel(field, cot, edges, out, ext):
    for m in range(3):
        ext[m, 6:8, :] = edges[m, 2:4, :]
        ext[m, 8:72, :] = field[m, 0]
        ext[m, 72:74, :] = edges[m, 0:2, :]
    for q in range(PLANES):
        for m in range(3):
            out[q, m * REACH : (m + 1) * REACH, :] = ext[m, 8 * q + 6 : 8 * q + 18, :]
            out[q, 36 + 8 * m : 44 + 8 * m, :] = cot[m, 0, 8 * q : 8 * q + 8, :]
        out[q, 60:64, :] = jnp.zeros((4, DEPTH), jnp.float32)


def stack_field(field, high, low):
    for x in range(PLANES):
        whole = field[x, 0:48, :]
        for e in range(3):
            parts = split(turn(whole, 1 - e))
            for a in range(3):
                rows = slice((a * 3 + e) * 48, (a * 3 + e) * 48 + 48)
                high[rows, plane(x - a + 1)] = parts[0]
                low[rows, plane(x - a + 1)] = parts[1]


def network(field, fwd1, fwd2, bias1, bias2, hidden, weights, u_hi, u_lo, h_hi, h_lo, work):
    stack_field(field, u_hi, u_lo)
    for pair in range(4):
        cut = slice(pair * 256, pair * 256 + 256)
        out = dot3((fwd1[0], fwd1[1]), (u_hi[:, cut], u_lo[:, cut]))
        value = jnp.tanh(out + bias1[...])
        hidden[:, cut] = value
        parts = split(value)
        h_hi[:, cut] = parts[0]
        h_lo[:, cut] = parts[1]
        work[:, cut] = dot3((fwd2[0], fwd2[1]), parts)
    for x in range(PLANES):
        total = bias2[:, :DEPTH]
        for a in range(3):
            for e in range(3):
                tap = a * 3 + e
                total = total + turn(work[tap * 48 : tap * 48 + 48, plane(x + a - 1)], 1 - e)
        weights[:, plane(x)] = jax.nn.sigmoid(total)


def around(field, x, direction, sign):
    if direction == 0:
        return [field[(x + sign) % PLANES, m * REACH + RIM : m * REACH + RIM + SLAB, :] for m in range(3)]
    if direction == 1:
        first = RIM + sign
        return [field[x, m * REACH + first : m * REACH + first + SLAB, :] for m in range(3)]
    return [turn(field[x, m * REACH + RIM : m * REACH + RIM + SLAB, :], -sign) for m in range(3)]


def advected(field, weights, x):
    center = around(field, x, 0, 0)
    total = [jnp.zeros((SLAB, DEPTH), jnp.float32)] * 3
    for d in range(3):
        ahead = around(field, x, d, 1)
        behind = around(field, x, d, -1)
        plus = 0.5 * (center[d] + ahead[d])
        minus = 0.5 * (behind[d] + center[d])
        rate_up = weights[2 * d * SLAB : (2 * d + 1) * SLAB, plane(x)]
        rate_low = weights[(2 * d + 1) * SLAB : (2 * d + 2) * SLAB, plane(x)]
        for m in range(3):
            upper = center[m] + rate_up * (ahead[m] - center[m])
            lower = center[m] + rate_low * (behind[m] - center[m])
            total[m] = total[m] + plus * upper - minus * lower
    return [center[m] - KAPPA * total[m] for m in range(3)]


def mixed(values, table):
    outs = []
    for row in table:
        total = None
        for weight, value in zip(row, values):
            term = value * float(weight)
            total = term if total is None else total + term
        outs.append(total)
    return outs


def lane_groups(size):
    return lax.broadcasted_iota(jnp.int32, (size, DEPTH), 1) // BAND


def scatter_modes(source, rows, out):
    groups = lane_groups(rows)
    for p in range(4):
        for g in range(4):
            total = None
            for f in range(2):
                for t in range(2):
                    slot = 2 * f + t
                    value = turn(source(f, 2 * p + t), BAND * (slot - g))
                    total = value if total is None else jnp.where(groups == slot, value, total)
            out[p * 4 + g] = total


def gather_modes(recv, f, k, rows):
    groups = lane_groups(rows)
    slot = 2 * f + k % 2
    total = None
    for g in range(4):
        value = turn(recv[(k // 2) * 4 + g, 0:rows, :], BAND * (g - slot))
        total = value if total is None else jnp.where(groups == g, value, total)
    return total


def first_kernel_body(mode_x, recv, fwd1, fwd2, bias1, bias2, z_hi, z_lo, out, hidden, weights, u_hi, u_lo, h_hi, h_lo, work, modes):
    network(recv, fwd1, fwd2, bias1, bias2, hidden, weights, u_hi, u_lo, h_hi, h_lo, work)
    table = (z_hi[...], z_lo[...])
    moved_field = [jnp.concatenate(advected(recv, weights, x), axis=0) for x in range(PLANES)]
    for f in range(2):
        planes = moved_field if f == 0 else [recv[x, 36:60, :] for x in range(PLANES)]
        for k, value in enumerate(mixed(planes, mode_x)):
            modes[f, k] = value
    for f in range(2):
        flat = modes[f].reshape(PLANES * 24, DEPTH)
        modes[f] = dot3(split(flat), table).reshape(PLANES, 24, DEPTH)
    scatter_modes(lambda f, k: modes[f, k], 24, out)


def leray(parts):
    device = lax.axis_index("px") * 2 + lax.axis_index("py")
    pair = device // 4
    group = device % 4
    lane = lax.broadcasted_iota(jnp.int32, (ROWS, DEPTH), 1)
    row = lax.broadcasted_iota(jnp.int32, (ROWS, DEPTH), 0)
    odd_x = (lane // BAND) % 2
    odd_z = (lane // 16) % 2
    number_z = 16 * group + lane % 16
    top_x = (odd_x == 1) & (pair == 0)
    top_y = row == ROWS // 2
    top_z = (odd_z == 1) & (number_z == 0)
    number_y = row % (ROWS // 2)
    real = lambda value: value.astype(jnp.float32)
    rate_x = real(jnp.where(odd_x == 1, -pair, pair))
    rate_y = real(jnp.where(row < ROWS // 2, number_y, -number_y))
    rate_z = real(jnp.where(odd_z == 1, -number_z, number_z))
    high_x = real(jnp.where(top_x, PLANES // 2, 0))
    high_y = real(jnp.where(top_y, ROWS // 2, 0))
    high_z = real(jnp.where(top_z, DEPTH // 2, 0))
    size = rate_x * rate_x + rate_y * rate_y + rate_z * rate_z
    size = size + high_x * high_x + high_y * high_y + high_z * high_z
    inverse = 1.0 / jnp.maximum(size, 1.0)

    def slope_x(value):
        return rate_x * jnp.where(odd_x == 1, turn(value, BAND), turn(value, -BAND))

    def slope_y(value):
        return rate_y * jnp.concatenate([value[ROWS // 2 :], value[: ROWS // 2]], axis=0)

    def slope_z(value):
        return rate_z * jnp.where(odd_z == 1, turn(value, 16), turn(value, -16))

    spread = (slope_x(parts[0]) + slope_y(parts[1]) + slope_z(parts[2])) * inverse
    high = (high_x * parts[0] + high_y * parts[1] + high_z * parts[2]) * inverse
    return (
        parts[0] + slope_x(spread) - high_x * high,
        parts[1] + slope_y(spread) - high_y * high,
        parts[2] + slope_z(spread) - high_z * high,
    )


def both_kernel(recv, in_hi, in_lo, out_hi, out_lo, out):
    data = split(recv[...].reshape(16 * 24, DEPTH))
    modes = dot3((in_hi[...], in_lo[...]), data)
    fixed = leray([modes[m * ROWS : (m + 1) * ROWS] for m in range(3)])
    back = dot3((out_hi[...], out_lo[...]), split(jnp.concatenate(fixed, axis=0)))
    out[...] = back.reshape(16, 40, DEPTH)


def one_kernel(recv, in_hi, in_lo, out_hi, out_lo, out):
    data = split(recv[...].reshape(16 * 24, DEPTH))
    modes = dot3((in_hi[...], in_lo[...]), data)
    modes = modes[: 3 * ROWS] + turn(modes[3 * ROWS :], DEPTH // 2)
    fixed = leray([modes[m * ROWS : (m + 1) * ROWS] for m in range(3)])
    back = dot3((out_hi[...], out_lo[...]), split(jnp.concatenate(fixed, axis=0)))
    lane = lax.broadcasted_iota(jnp.int32, (256, DEPTH), 1)
    whole = jnp.where(lane < DEPTH // 2, back[:256], turn(back[256:], DEPTH // 2))
    out[...] = whole.reshape(16, 16, DEPTH)


def pullback(field, grad, hidden, weights, back2, back1, u_hi, u_lo, h_hi, h_lo, l_hi, l_lo, p_hi, p_lo, work, slope, sums, ends, earlier):
    slope[...] = jnp.zeros_like(slope)
    for x in range(PLANES):
        center = around(field, x, 0, 0)
        source = [-KAPPA * grad[x, m * SLAB : (m + 1) * SLAB, :] for m in range(3)]
        own = [grad[x, m * SLAB : (m + 1) * SLAB, :] for m in range(3)]
        logits = []
        for d in range(3):
            ahead = around(field, x, d, 1)
            behind = around(field, x, d, -1)
            plus = 0.5 * (center[d] + ahead[d])
            minus = 0.5 * (behind[d] + center[d])
            rate_up = weights[2 * d * SLAB : (2 * d + 1) * SLAB, plane(x)]
            rate_low = weights[(2 * d + 1) * SLAB : (2 * d + 2) * SLAB, plane(x)]
            grad_up = grad_low = grad_plus = grad_minus = None
            to_ahead, to_behind = [], []
            add = lambda total, term: term if total is None else total + term
            for m in range(3):
                gap_up = ahead[m] - center[m]
                gap_low = behind[m] - center[m]
                grad_plus = add(grad_plus, source[m] * (center[m] + rate_up * gap_up))
                grad_minus = add(grad_minus, -source[m] * (center[m] + rate_low * gap_low))
                grad_up = add(grad_up, source[m] * gap_up)
                grad_low = add(grad_low, -source[m] * gap_low)
                push_up = source[m] * plus
                push_low = -source[m] * minus
                to_ahead.append(push_up * rate_up)
                to_behind.append(push_low * rate_low)
                own[m] = own[m] + (push_up - to_ahead[m]) + (push_low - to_behind[m])
            own[d] = own[d] + 0.5 * (grad_plus + grad_minus)
            to_ahead[d] = to_ahead[d] + 0.5 * grad_plus
            to_behind[d] = to_behind[d] + 0.5 * grad_minus
            logits.append(grad_up * plus * rate_up * (1.0 - rate_up))
            logits.append(grad_low * minus * rate_low * (1.0 - rate_low))
            for m in range(3):
                first = m * REACH + RIM
                if d == 0:
                    slope[(x + 1) % PLANES, first : first + SLAB, :] += to_ahead[m]
                    slope[(x - 1) % PLANES, first : first + SLAB, :] += to_behind[m]
                elif d == 1:
                    slope[x, first + 1 : first + 1 + SLAB, :] += to_ahead[m]
                    slope[x, first - 1 : first - 1 + SLAB, :] += to_behind[m]
                else:
                    own[m] = own[m] + turn(to_ahead[m], 1) + turn(to_behind[m], -1)
        for m in range(3):
            slope[x, m * REACH + RIM : m * REACH + RIM + SLAB, :] += own[m]
        whole = jnp.concatenate(logits, axis=0)
        for e in range(3):
            parts = split(turn(whole, e - 1))
            for a in range(3):
                rows = slice((a * 3 + e) * 48, (a * 3 + e) * 48 + 48)
                l_hi[rows, plane(x + a - 1)] = parts[0]
                l_lo[rows, plane(x + a - 1)] = parts[1]
    for pair in range(4):
        cut = slice(pair * 256, pair * 256 + 256)
        value = dot3((back2[0], back2[1]), (l_hi[:, cut], l_lo[:, cut]))
        parts = split(value * (1.0 - hidden[:, cut] * hidden[:, cut]))
        p_hi[:, cut] = parts[0]
        p_lo[:, cut] = parts[1]
        work[:, cut] = dot3((back1[0], back1[1]), parts)
    for x in range(PLANES):
        total = slope[x, 0:40, :]
        for a in range(3):
            for e in range(3):
                tap = a * 3 + e
                total = total + turn(work[tap * 48 : tap * 48 + 40, plane(x - a + 1)], e - 1)
        slope[x, 0:40, :] = total
    second = dot3((l_hi[...], l_lo[...]), (h_hi[...], h_lo[...]), NT)
    first = dot3((u_hi[...], u_lo[...]), (p_hi[...], p_lo[...]), NT)
    ones = jnp.ones((16, FLAT), jnp.bfloat16)
    end1 = dot(ones, p_hi[...], NT) + dot(ones, p_lo[...], NT)
    end2 = dot(ones, l_hi[4 * 48 : 5 * 48, :], NT) + dot(ones, l_lo[4 * 48 : 5 * 48, :], NT)
    if earlier is None:
        sums[0:STACK, :] = second
        sums[STACK:, :] = first
        ends[0:16, :] = end1
        ends[16:32, 0:LOG] = end2
    else:
        old_sums, old_ends = earlier
        sums[0:STACK, :] = old_sums[0:STACK, :] + second
        sums[STACK:, :] = old_sums[STACK:, :] + first
        ends[0:16, :] = old_ends[0:16, :] + end1
        ends[16:32, 0:LOG] = old_ends[16:32, 0:LOG] + end2


def second_kernel_body(
    mode_x, recv, fwd1, fwd2, back2, back1, bias1, bias2, to_hi, to_lo, from_hi, from_lo,
    out, sums, ends,
    field, grad, modes, rows6, hidden, weights, u_hi, u_lo, h_hi, h_lo, l_hi, l_lo, p_hi, p_lo, work, slope,
):
    back_z = (from_hi[...], from_lo[...])
    for f in range(2):
        for k in range(PLANES):
            modes[k] = gather_modes(recv, f, k, 40)
        flat = dot3(split(modes[...].reshape(PLANES * 40, DEPTH)), back_z)
        modes[...] = flat.reshape(PLANES, 40, DEPTH)
        for x, value in enumerate(mixed([modes[k] for k in range(PLANES)], mode_x.T)):
            field[x, 0:40, :] = value
            field[x, 40:48, :] = jnp.zeros((8, DEPTH), jnp.float32)
        if f == 0:
            network(field, fwd1, fwd2, bias1, bias2, hidden, weights, u_hi, u_lo, h_hi, h_lo, work)
            for x in range(PLANES):
                slope[x] = field[x]
        else:
            for x in range(PLANES):
                for m in range(3):
                    first = m * REACH + RIM
                    grad[x, m * SLAB : (m + 1) * SLAB, :] = field[x, first : first + SLAB, :]
    for x in range(PLANES):
        field[x] = slope[x]
    pullback(
        field, grad, hidden, weights, back2, back1, u_hi, u_lo, h_hi, h_lo, l_hi, l_lo, p_hi, p_lo,
        work, slope, sums, ends, None,
    )
    for k, value in enumerate(mixed([slope[x, 0:40, :] for x in range(PLANES)], mode_x)):
        modes[k] = value
    flat = dot3(split(modes[...].reshape(PLANES * 40, DEPTH)), (to_hi[...], to_lo[...]))
    modes[...] = flat.reshape(PLANES, 40, DEPTH)
    for h in range(2):
        for k in range(PLANES):
            for m in range(3):
                rows6[h, k, m * 6 : m * 6 + 6, :] = modes[k, m * REACH + 6 * h : m * REACH + 6 * h + 6, :]
            rows6[h, k, 18:24, :] = jnp.zeros((6, DEPTH), jnp.float32)
    scatter_modes(lambda h, k: rows6[h, k], 24, out)


def third_kernel_body(
    mode_x, recv, field, hidden, weights, back2, back1, from_hi, from_lo, old_sums, old_ends,
    spread_t, mask, lift, count,
    out,
    grad, modes, u_hi, u_lo, h_hi, h_lo, l_hi, l_lo, p_hi, p_lo, work, slope, sums, ends, pieces,
):
    back_z = (from_hi[...], from_lo[...])
    for h in range(2):
        for k in range(PLANES):
            modes[k] = gather_modes(recv, h, k, 16)
        flat = dot3(split(modes[...].reshape(PLANES * 16, DEPTH)), back_z)
        modes[...] = flat.reshape(PLANES, 16, DEPTH)
        for x, value in enumerate(mixed([modes[k] for k in range(PLANES)], mode_x.T)):
            for m in range(3):
                grad[x, m * SLAB + 4 * h : m * SLAB + 4 * h + 4, :] = value[m * 4 : m * 4 + 4, :]
    stack_field(field, u_hi, u_lo)
    parts = split(hidden[...])
    h_hi[...] = parts[0]
    h_lo[...] = parts[1]
    pullback(
        field, grad, hidden, weights, back2, back1, u_hi, u_lo, h_hi, h_lo, l_hi, l_lo, p_hi, p_lo,
        work, slope, sums, ends, (old_sums, old_ends),
    )
    for x in range(PLANES):
        out[x, 0:40, :] = slope[x, 0:40, :]
        out[x, 36:40, :] = jnp.zeros((4, DEPTH), jnp.float32)
    pack_grads(sums, ends, spread_t, mask, lift, count, pieces)
    for x in range(PLANES):
        out[x, 40:80, :] = pieces[96:136, :]


def pack_grads(sums, ends, spread_t, mask, lift, count, pieces):
    pieces[...] = jnp.zeros_like(pieces)
    for b in range(3):
        parts = split(sums[...] * mask[b].astype(jnp.float32))
        rows = dot(spread_t[...], parts[0]) + dot(spread_t[...], parts[1])
        parts = split(rows)
        pieces[0:96, :] = dot(parts[0], lift[...]) + dot(parts[1], lift[...])
        for c in range(3):
            slot = b * 3 + c
            if slot < 8:
                pieces[96:123, :] += turn(pieces[c * 27 : c * 27 + 27, :], 16 * slot)
            else:
                for third in range(3):
                    first = c * 27 + third * 9
                    pieces[123:132, :] += turn(pieces[first : first + 9, :], 16 * third)
    parts = split(ends[0:16, :])
    total = dot(parts[0], lift[...]) + dot(parts[1], lift[...])
    parts = split(ends[16:32, 0:LOG])
    total = total + dot(parts[0], count[...]) + dot(parts[1], count[...])
    pieces[135:136, :] = total[0:1, :]


def fold_kernel(recv, main, edge, ext):
    ext[...] = jnp.zeros_like(ext)
    total = None
    for q in range(PLANES):
        for m in range(3):
            ext[m, 8 * q + 6 : 8 * q + 18, :] += recv[q, m * REACH : (m + 1) * REACH, :]
        block = recv[q, 40:80, :]
        total = block if total is None else total + block
    for m in range(3):
        main[m, 0] = ext[m, 8:72, :]
        edge[m * 8 : m * 8 + 2, :] = ext[m, 72:74, :]
        edge[m * 8 + 2 : m * 8 + 4, :] = ext[m, 6:8, :]
        edge[m * 8 + 4 : m * 8 + 8, :] = jnp.zeros((4, DEPTH), jnp.float32)
    edge[24:64, :] = total


def last_kernel(main, edge, other, out, grads):
    for m in range(3):
        out[m, 0] = main[m, 0]
        out[m, 0, 0:2, :] += other[m * 8 : m * 8 + 2, :]
        out[m, 0, 62:64, :] += other[m * 8 + 2 : m * 8 + 4, :]
    grads[...] = edge[24:64, :] + other[24:64, :]


def slab_device(velocity, cotangent, first_kernel, first_bias, second_kernel, second_bias):
    c = constants()
    mode_x = c["mode_x"]
    half = jnp.bfloat16
    f32 = lambda *dims: pltpu.VMEM(dims, jnp.float32)
    b16 = lambda *dims: pltpu.VMEM(dims, half)
    swap = [(0, 1), (1, 0)]

    edges = jnp.concatenate([velocity[:, 0, :RIM], velocity[:, 0, -RIM:]], axis=1)
    edges = lax.ppermute(edges, "py", swap)
    packed = call(pack_kernel, shape(PLANES, 64, DEPTH), (velocity, cotangent, edges), [f32(3, 80, DEPTH)])
    recv = lax.all_to_all(packed, "px", 0, 0)

    taps = jnp.concatenate(
        [
            jnp.transpose(second_kernel, (2, 4, 0, 3, 1)).reshape(54, 48),
            jnp.transpose(first_kernel, (2, 4, 1, 3, 0)).reshape(27, 48),
            jnp.zeros((15, 48), jnp.float32),
        ]
    )
    fwd2, fwd1, back2, back1 = call(
        weights_kernel,
        [
            shape(2, STACK, HID, kind=half),
            shape(2, HID, STACK, kind=half),
            shape(2, HID, STACK, kind=half),
            shape(2, STACK, HID, kind=half),
        ],
        (taps, c["spread"], c["spread_t"], c["mask"], c["mask_t"], c["lift"], c["lift_t"]),
    )
    bias1 = jnp.broadcast_to(jnp.repeat(first_bias, WIDE)[:, None], (HID, 256))
    bias2 = jnp.broadcast_to(jnp.repeat(second_bias, SLAB)[:, None], (LOG, 256))

    stacks = lambda rows: [b16(rows, FLAT), b16(rows, FLAT)]
    sent, hidden, weights = call(
        functools.partial(first_kernel_body, mode_x),
        [shape(16, 24, DEPTH), shape(HID, FLAT), shape(LOG, FLAT)],
        (recv, fwd1, fwd2, bias1, bias2, *c["to_z"]),
        stacks(STACK) + stacks(HID) + [f32(STACK, FLAT), f32(2, PLANES, 24, DEPTH)],
    )
    both = ("px", "py")
    moved_modes = lax.all_to_all(sent, both, 0, 0)
    moved_modes = call(both_kernel, shape(16, 40, DEPTH), (moved_modes, *c["both_in"], *c["both_out"]))
    moved_modes = lax.all_to_all(moved_modes, both, 0, 0)

    sent, sums, ends = call(
        functools.partial(second_kernel_body, mode_x),
        [shape(16, 24, DEPTH), shape(2 * STACK, HID), shape(32, HID)],
        (moved_modes, fwd1, fwd2, back2, back1, bias1, bias2, *c["to_z"], *c["from_z"]),
        [f32(PLANES, 48, DEPTH), f32(PLANES, 24, DEPTH), f32(PLANES, 40, DEPTH), f32(2, PLANES, 24, DEPTH)]
        + [f32(HID, FLAT), f32(LOG, FLAT)]
        + stacks(STACK) + stacks(HID) + stacks(STACK) + stacks(HID)
        + [f32(STACK, FLAT), f32(PLANES, 48, DEPTH)],
    )
    moved_modes = lax.all_to_all(sent, both, 0, 0)
    moved_modes = call(one_kernel, shape(16, 16, DEPTH), (moved_modes, *c["one_in"], *c["one_out"]))
    moved_modes = lax.all_to_all(moved_modes, both, 0, 0)

    sent = call(
        functools.partial(third_kernel_body, mode_x),
        shape(PLANES, 80, DEPTH),
        (
            moved_modes, recv, hidden, weights, back2, back1, *c["from_z"], sums, ends,
            c["spread_t"], c["mask"], c["lift"], c["count"],
        ),
        [f32(PLANES, 24, DEPTH), f32(PLANES, 16, DEPTH)]
        + stacks(STACK) + stacks(HID) + stacks(STACK) + stacks(HID)
        + [f32(STACK, FLAT), f32(PLANES, 48, DEPTH), f32(2 * STACK, HID), f32(32, HID), f32(136, DEPTH)],
    )
    recv = lax.all_to_all(sent, "px", 0, 0)
    main, edge = call(
        fold_kernel, [shape(3, 1, 64, DEPTH), shape(64, DEPTH)], (recv,), [f32(3, 80, DEPTH)]
    )
    other = lax.ppermute(edge, "py", swap)
    grad_velocity, grads = call(
        last_kernel, [shape(3, 1, 64, DEPTH), shape(40, DEPTH)], (main, edge, other)
    )

    def piece(b, kind):
        slot = b * 3 + kind
        if slot < 8:
            return grads[0:27, 16 * slot : 16 * slot + 16]
        return jnp.concatenate([grads[27:36, 16 * i : 16 * i + 16] for i in range(3)])

    first = jnp.stack([piece(b, 2) for b in range(3)]).reshape(3, 3, 3, 3, CHANNELS)
    second = jnp.stack([jnp.concatenate([piece(b, 0), piece(b, 1)]) for b in range(3)])
    second = second.reshape(3, 3, 3, COEFFS, CHANNELS)
    return (
        grad_velocity,
        jnp.transpose(first, (4, 3, 1, 0, 2)),
        grads[39, 0:16],
        jnp.transpose(second, (3, 4, 1, 0, 2)),
        grads[39, 16:22],
    )


def fits_slabs(mesh):
    return mesh.shape["px"] == PLANES and mesh.shape["py"] == 2


def solution(mesh):
    return jax.shard_map(
        slab_device if fits_slabs(mesh) else on_device,
        mesh=mesh,
        in_specs=(
            P(None, ("groups", "px"), "py", None),
            P(None, ("groups", "px"), "py", None),
            P(),
            P(),
            P(),
            P(),
        ),
        out_specs=(
            P(None, ("groups", "px"), "py", None),
            P("groups", None, None, None, None),
            P("groups"),
            P("groups", None, None, None, None),
            P("groups"),
        ),
        check_vma=False,
    )
```

```python
import functools
import math

import jax
import jax.numpy as jnp
import numpy as np
from jax import lax
from jax.experimental import pallas as pl
from jax.experimental.pallas import tpu as pltpu
from jax.sharding import PartitionSpec as P

ITERS = 2


KAPPA = 0.25


def padded_2(value, sides, width):
    for axis, dim in sides:
        size, length = (lax.axis_size(axis), value.shape[dim])
        up = [(i, (i + 1) % size) for i in range(size)]
        down = [(j, i) for i, j in up]
        last = lax.slice_in_dim(value, length - width, length, axis=dim)
        initial = lax.slice_in_dim(value, 0, width, axis=dim)
        before = lax.ppermute(last, axis, up)
        after = lax.ppermute(initial, axis, down)
        value = jnp.concatenate([before, value, after], axis=dim)
    return value


def extend(field):
    rimmed = padded_2(field, (("px", 1), ("py", 2)), 1)
    return jnp.concatenate([rimmed[..., -1:], rimmed, rimmed[..., :1]], axis=3)


def across_columns(spectrum):
    return lax.all_to_all(spectrum, "px", split_axis=2, concat_axis=4, tiled=True)


def across_pairs(spectrum):
    return lax.all_to_all(spectrum, "py", split_axis=3, concat_axis=4, tiled=True)


def summed(grads):
    return lax.psum((grads[0], grads[1], grads[2], grads[3]), ("px", "py"))


def all_taps():
    return [
        (shift_x, shift_y, shift_z)
        for shift_x in range(3)
        for shift_y in range(3)
        for shift_z in range(3)
    ]


def gather_conv(padded, kernel):
    size_x = padded.shape[1] - 2
    size_y = padded.shape[2] - 2
    size_z = padded.shape[3] - 2
    stacked = jnp.concatenate(
        [
            padded[:, sx_one : sx_one + size_x, sy_one : sy_one + size_y, sz_one : sz_one + size_z]
            for sx_one, sy_one, sz_one in all_taps()
        ],
        axis=0,
    )
    matrix = jnp.transpose(kernel, (0, 2, 3, 4, 1)).reshape(kernel.shape[0], -1)
    result = jnp.einsum("ok,kxyz->oxyz", matrix, stacked, precision=lax.Precision.HIGHEST)
    return (result, stacked)


def scatter_conv(padded, kernel):
    outputs = kernel.shape[0]
    inputs = kernel.shape[1]
    size_x = padded.shape[1] - 2
    size_y = padded.shape[2] - 2
    size_z = padded.shape[3] - 2
    total = jnp.zeros((outputs, size_x, size_y, size_z), jnp.float32)
    for shift_x in range(3):
        matrix = jnp.transpose(kernel[:, :, shift_x], (0, 2, 3, 1)).reshape(outputs * 9, inputs)
        layer = jnp.einsum(
            "km,mxyz->kxyz",
            matrix,
            padded[:, shift_x : shift_x + size_x],
            precision=lax.Precision.HIGHEST,
        )
        layer = layer.reshape(outputs, 3, 3, size_x, size_y + 2, size_z + 2)
        for shift_y in range(3):
            for shift_z in range(3):
                total = (
                    total
                    + layer[
                        :,
                        shift_y,
                        shift_z,
                        :,
                        shift_y : shift_y + size_y,
                        shift_z : shift_z + size_z,
                    ]
                )
    return total


def flipped(kernel):
    return jnp.transpose(kernel[:, :, ::-1, ::-1, ::-1], (1, 0, 2, 3, 4))


def moved(padded, axis_dim, offset_cells):
    index = [slice(None), slice(1, -1), slice(1, -1), slice(1, -1)]
    index[axis_dim] = slice(1 + offset_cells, padded.shape[axis_dim] - 1 + offset_cells)
    return padded[tuple(index)]


def advect(padded, weights):
    center = moved(padded, 1, 0)
    total = jnp.zeros_like(center)
    for direction in range(3):
        ahead = moved(padded, direction + 1, 1)
        behind = moved(padded, direction + 1, -1)
        vplus = 0.5 * (center[direction] + ahead[direction])
        vminus = 0.5 * (behind[direction] + center[direction])
        upper = center + weights[2 * direction] * (ahead - center)
        lower = center + weights[2 * direction + 1] * (behind - center)
        total = total + vplus * upper - vminus * lower
    return total


def advect_back(padded, weights_pad, source_pad):
    center = moved(padded, 1, 0)
    source = moved(source_pad, 1, 0)
    weights = moved(weights_pad, 1, 0)
    grad_field = jnp.zeros_like(center)
    fluxes = []
    parts = []
    for direction in range(3):
        ahead = moved(padded, direction + 1, 1)
        behind = moved(padded, direction + 1, -1)
        vplus = 0.5 * (center[direction] + ahead[direction])
        vminus = 0.5 * (behind[direction] + center[direction])
        rate_up = weights[2 * direction]
        rate_low = weights[2 * direction + 1]
        rate_before = moved(weights_pad[2 * direction : 2 * direction + 1], direction + 1, -1)[0]
        rate_after = moved(weights_pad[2 * direction + 1 : 2 * direction + 2], direction + 1, 1)[0]
        source_before = moved(source_pad, direction + 1, -1)
        source_after = moved(source_pad, direction + 1, 1)
        upper = center + rate_up * (ahead - center)
        lower = center + rate_low * (behind - center)
        upper_before = behind + rate_before * (center - behind)
        lower_after = ahead + rate_after * (center - ahead)
        grad_field = grad_field + source * (vplus * (1.0 - rate_up) - vminus * (1.0 - rate_low))
        grad_field = (
            grad_field + vminus * rate_before * source_before - vplus * rate_after * source_after
        )
        fluxes.append(
            0.5
            * (
                jnp.sum(source * upper, 0)
                - jnp.sum(source * lower, 0)
                + jnp.sum(source_before * upper_before, 0)
                - jnp.sum(source_after * lower_after, 0)
            )
        )
        parts.append(jnp.sum(source * vplus * (ahead - center), 0))
        parts.append(-jnp.sum(source * vminus * (behind - center), 0))
    return (grad_field + jnp.stack(fluxes), jnp.stack(parts))


def tables(count):
    index = jnp.arange(count, dtype=jnp.int32)
    phase = index[:, None] * index[None, :] % count
    angle = phase.astype(jnp.float32) * (2.0 * math.pi / count)
    return (jnp.cos(angle), jnp.sin(angle))


def mix(form, data, table):
    return jnp.einsum(form, data, table, precision=lax.Precision.HIGHEST)


def waves(start, count, total):
    index = start + jnp.arange(count, dtype=jnp.int32)
    return jnp.where(index < total // 2, index, index - total).astype(jnp.float32)


def project(field):
    depth = field.shape[3]
    cos_z, sin_z = tables(depth)
    real_z = mix("cxyz,zk->cxky", field, cos_z)
    imag_z = -mix("cxyz,zk->cxky", field, sin_z)
    spectrum = across_pairs(jnp.stack([real_z, imag_z]))
    span_y = spectrum.shape[4]
    cos_y, sin_y = tables(span_y)
    real_y = mix("cxky,yq->cqkx", spectrum[0], cos_y) + mix("cxky,yq->cqkx", spectrum[1], sin_y)
    imag_y = mix("cxky,yq->cqkx", spectrum[1], cos_y) - mix("cxky,yq->cqkx", spectrum[0], sin_y)
    spectrum = across_columns(jnp.stack([real_y, imag_y]))
    span_x = spectrum.shape[4]
    cos_x, sin_x = tables(span_x)
    real_x = mix("cqkx,xp->cqkp", spectrum[0], cos_x) + mix("cqkx,xp->cqkp", spectrum[1], sin_x)
    imag_x = mix("cqkx,xp->cqkp", spectrum[1], cos_x) - mix("cqkx,xp->cqkp", spectrum[0], sin_x)
    rows_y = spectrum.shape[2]
    rows_z = spectrum.shape[3]
    wave_y = waves(lax.axis_index("px") * rows_y, rows_y, span_y)[:, None, None]
    wave_z = waves(lax.axis_index("py") * rows_z, rows_z, depth)[None, :, None]
    wave_x = waves(0, span_x, span_x)[None, None, :]
    size = jnp.maximum(wave_x * wave_x + wave_y * wave_y + wave_z * wave_z, 1.0)
    vectors = jnp.stack(jnp.broadcast_arrays(wave_x, wave_y, wave_z))
    real_x = real_x - vectors * (
        (wave_x * real_x[0] + wave_y * real_x[1] + wave_z * real_x[2]) / size
    )
    imag_x = imag_x - vectors * (
        (wave_x * imag_x[0] + wave_y * imag_x[1] + wave_z * imag_x[2]) / size
    )
    back_real = (mix("cqkp,px->cxkq", real_x, cos_x) - mix("cqkp,px->cxkq", imag_x, sin_x)) / span_x
    back_imag = (mix("cqkp,px->cxkq", imag_x, cos_x) + mix("cqkp,px->cxkq", real_x, sin_x)) / span_x
    spectrum = across_columns(jnp.stack([back_real, back_imag]))
    rows_real = (
        mix("cxkq,qy->cxyk", spectrum[0], cos_y) - mix("cxkq,qy->cxyk", spectrum[1], sin_y)
    ) / span_y
    rows_imag = (
        mix("cxkq,qy->cxyk", spectrum[1], cos_y) + mix("cxkq,qy->cxyk", spectrum[0], sin_y)
    ) / span_y
    spectrum = across_pairs(jnp.stack([rows_real, rows_imag]))
    return (
        mix("cxyk,kz->cxyz", spectrum[0], cos_z) - mix("cxyk,kz->cxyz", spectrum[1], sin_z)
    ) / depth


def forward_state(field, first_kernel, first_bias, second_kernel, second_bias):
    padded = extend(field)
    first_out, field_taps = gather_conv(padded, first_kernel)
    hidden = jnp.tanh(first_out + first_bias[:, None, None, None])
    weights = jax.nn.sigmoid(
        scatter_conv(extend(hidden), second_kernel) + second_bias[:, None, None, None]
    )
    return (padded, hidden, weights, field_taps)


def backward_step(state, upstream, first_kernel, second_kernel):
    padded, hidden, weights, field_taps = state
    moved_grad = project(upstream)
    source = -KAPPA * moved_grad
    stacked = extend(jnp.concatenate([source, weights], axis=0))
    grad_field, grad_weights = advect_back(padded, stacked[3:], stacked[:3])
    grad_field = grad_field + moved_grad
    grad_logits = grad_weights * weights * (1.0 - weights)
    logits_pad = extend(grad_logits)
    grad_hidden, logit_taps = gather_conv(logits_pad, flipped(second_kernel))
    product = jnp.einsum("kxyz,mxyz->km", logit_taps, hidden, precision=lax.Precision.HIGHEST)
    product = product.reshape(3, 3, 3, second_kernel.shape[0], second_kernel.shape[1])
    grad_second = jnp.transpose(product[::-1, ::-1, ::-1], (3, 4, 0, 1, 2))
    grad_second_bias = jnp.sum(grad_logits, axis=(1, 2, 3))
    grad_pre = grad_hidden * (1.0 - hidden * hidden)
    pre_pad = extend(grad_pre)
    grad_field = grad_field + scatter_conv(pre_pad, flipped(first_kernel))
    first_product = jnp.einsum(
        "oxyz,kxyz->ok", grad_pre, field_taps, precision=lax.Precision.HIGHEST
    )
    first_product = first_product.reshape(first_kernel.shape[0], 3, 3, 3, first_kernel.shape[1])
    grad_first = jnp.transpose(first_product, (0, 4, 1, 2, 3))
    grad_first_bias = jnp.sum(grad_pre, axis=(1, 2, 3))
    return (grad_field, (grad_first, grad_first_bias, grad_second, grad_second_bias))


def on_device(velocity, cotangent, first_kernel, first_bias, second_kernel, second_bias):
    field = velocity
    fields = [velocity]
    saved = []
    for section in range(ITERS):
        state = forward_state(field, first_kernel, first_bias, second_kernel, second_bias)
        saved.append(state)
        field = project(field - KAPPA * advect(state[0], state[2]))
        fields.append(field)
    upstream = cotangent
    totals = None
    for section in reversed(range(ITERS)):
        state = saved[section]
        upstream, grads = backward_step(state, upstream, first_kernel, second_kernel)
        grads = summed(grads)
        if totals is None:
            totals = grads
        else:
            totals = tuple((older + newer for older, newer in zip(totals, grads)))
    return (upstream, totals[0], totals[1], totals[2], totals[3])


SLAB = 8
RIM = 2
REACH = SLAB + 2 * RIM
WIDE = SLAB + 2
PLANES = 8
DEPTH = 128
ROWS = 128
CHANNELS = 16
COEFFS = 6
BAND = 32
HID = CHANNELS * WIDE
LOG = COEFFS * SLAB
STACK = 9 * 48
FLAT = PLANES * DEPTH
NN = ((1,), (0,))
NT = ((1,), (1,))


def real_basis(count):
    half = count // 2
    angle = 2.0 * np.pi * np.arange(count) / count
    rows = [np.full(count, 1.0 / np.sqrt(count))]
    rows += [np.sqrt(2.0 / count) * np.cos(k * angle) for k in range(1, half)]
    rows += [np.cos(half * angle) / np.sqrt(count)]
    rows += [np.sqrt(2.0 / count) * np.sin(k * angle) for k in range(1, half)]
    return np.stack(rows)


def halves(table):
    high = table.astype(np.float32).astype(jnp.bfloat16)
    low = (table - high.astype(np.float64)).astype(np.float32).astype(jnp.bfloat16)
    return high, low


def slab_of(device):
    return (device % 2) * PLANES + device // 2


@functools.cache
def constants():
    basis_x = real_basis(PLANES)
    mode_x = np.stack([basis_x[(k // 2) + (PLANES // 2) * (k % 2)] for k in range(PLANES)])
    basis_z = real_basis(DEPTH)
    order = []
    for group in range(4):
        order += [16 * group + i for i in range(16)] + [64 + 16 * group + i for i in range(16)]
    mode_z = basis_z[order]
    basis_y = real_basis(ROWS)

    def columns(device, offset, count):
        return basis_y[:, (SLAB * slab_of(device) + offset + np.arange(count)) % ROWS]

    def table(block, offset, count):
        out = np.zeros((3, ROWS, 16, block))
        for device in range(16):
            for m in range(3):
                out[m, :, device, m * count : (m + 1) * count] = columns(device, offset, count)
        return out.reshape(3 * ROWS, 16 * block)

    both_in = table(24, 0, 8)
    wide_out = table(40, -RIM, REACH).T.reshape(16, 40, 3 * ROWS)
    own_out = table(24, 0, 8).T.reshape(16, 24, 3 * ROWS)
    rest = np.concatenate([own_out, wide_out[:, 32:]], axis=1)
    both_out = np.stack([wide_out[:, :32], rest]).reshape(2 * 16 * 32, 3 * ROWS)
    one_in = np.concatenate([table(24, -RIM, 6), table(24, -RIM + 6, 6)])
    one_out = np.concatenate([table(16, 0, 4).T, table(16, 4, 4).T])

    spread = np.zeros((2 * STACK, 96))
    mask = np.zeros((3, 2 * STACK, HID))
    for tap in range(9):
        for o in range(COEFFS):
            for q in range(SLAB):
                row = tap * 48 + o * SLAB + q
                spread[row, tap * COEFFS + o] = 1.0
                for b in range(3):
                    mask[b, row, np.arange(CHANNELS) * WIDE + q + b] = 1.0
        for m in range(3):
            for r in range(REACH):
                row = STACK + tap * 48 + m * REACH + r
                spread[row, 54 + tap * 3 + m] = 1.0
                for b in range(3):
                    if 0 <= r - b < WIDE:
                        mask[b, row, np.arange(CHANNELS) * WIDE + r - b] = 1.0
    lift = np.zeros((HID, 128))
    lift[np.arange(HID), np.arange(HID) // WIDE] = 1.0
    count = np.zeros((LOG, 128))
    count[np.arange(LOG), 16 + np.arange(LOG) // SLAB] = 1.0
    half = jnp.bfloat16
    return dict(
        mode_x=mode_x,
        to_z=halves(mode_z.T),
        from_z=halves(mode_z),
        both_in=halves(both_in),
        both_out=halves(both_out),
        one_in=halves(one_in),
        one_out=halves(one_out),
        spread_t=np.ascontiguousarray(spread.T).astype(half),
        mask=mask.astype(half),
        lift=lift.astype(half),
        count=count.astype(half),
    )


def dot(left, right, dims=NN):
    return lax.dot_general(left, right, (dims, ((), ())), preferred_element_type=jnp.float32)


def split(value):
    high = value.astype(jnp.bfloat16)
    return high, (value - high.astype(jnp.float32)).astype(jnp.bfloat16)


def dot3(left, right, dims=NN):
    return dot(left[0], right[0], dims) + (dot(left[0], right[1], dims) + dot(left[1], right[0], dims))


def turn(value, shift):
    shift = shift % value.shape[-1]
    return value if shift == 0 else pltpu.roll(value, shift, value.ndim - 1)


def plane(x):
    x = x % PLANES
    return slice(x * DEPTH, (x + 1) * DEPTH)


def call(kernel, outs, args, scratch=(), room=16):
    single = not isinstance(outs, (list, tuple))
    shapes = [outs] if single else outs
    return pl.pallas_call(
        kernel,
        out_shape=outs,
        in_specs=[pl.BlockSpec(memory_space=pltpu.VMEM)] * len(args),
        out_specs=(
            pl.BlockSpec(memory_space=pltpu.VMEM)
            if single
            else [pl.BlockSpec(memory_space=pltpu.VMEM)] * len(shapes)
        ),
        scratch_shapes=list(scratch),
        compiler_params=pltpu.CompilerParams(vmem_limit_bytes=room * 2**20),
    )(*args)


def shape(*dims, kind=jnp.float32):
    return jax.ShapeDtypeStruct(dims, kind)


def counting(size, dim):
    return lax.broadcasted_iota(jnp.int32, size, dim).astype(jnp.float32)


def remainder(value, count):
    return value - count * jnp.floor((value + 0.5) / count)


def band_tables(tall):
    row, col = (0, 1) if tall else (1, 0)
    size = lambda rows, cols: (rows, cols) if tall else (cols, rows)
    where = counting(size(2 * STACK, 96), row)
    to = counting(size(2 * STACK, 96), col)
    first = where - 8.0 * to
    third = to - 54.0
    second = where - STACK - (16.0 * third - 4.0 * remainder(third, 3.0))
    picks = ((to < 54.0) & (first >= 0.0) & (first < 8.0)) | (
        (to >= 54.0) & (to < 81.0) & (second >= 0.0) & (second < 12.0)
    )
    where = counting(size(2 * STACK, HID), row)
    inner = remainder(counting(size(2 * STACK, HID), col), 10.0)
    outer = where - STACK
    offset = jnp.where(
        where < STACK,
        inner - remainder(where, 8.0),
        remainder(remainder(outer, 48.0), 12.0) - inner,
    )
    gap = counting(size(HID, CHANNELS), row) - 10.0 * counting(size(HID, CHANNELS), col)
    lift = (gap >= 0.0) & (gap < 10.0)
    half = jnp.bfloat16
    return picks.astype(jnp.float32).astype(half), offset, lift.astype(jnp.float32).astype(half)


def weights_kernel(taps1, taps2, bias1, bias2, fwd2, fwd1, back2, back1, wide1, wide2, blocks):
    blocks[...] = jnp.zeros_like(blocks)
    for b in range(3):
        for a in range(3):
            for e in range(3):
                tap = a * 3 + e
                for o in range(COEFFS):
                    blocks[b, tap * 6 + o, :] = taps2[o * 9 + a * 3 + b, e, :]
                for m in range(3):
                    blocks[b, 54 + tap * 3 + m, :] = taps1[m * 9 + a * 3 + b, e, :]
    spread, offset, lift = band_tables(True)
    spread_t, offset_t, lift_t = band_tables(False)
    tall = [jnp.zeros((2 * STACK, HID), jnp.float32)] * 2
    wide = [jnp.zeros((HID, 2 * STACK), jnp.float32)] * 2
    for b in range(3):
        for half, block in enumerate(split(blocks[b])):
            rows = dot(spread, block).astype(jnp.bfloat16)
            tall[half] = jnp.where(offset == float(b), dot(rows, lift_t), tall[half])
            cols = dot(lift, block, NT).astype(jnp.bfloat16)
            wide[half] = jnp.where(offset_t == float(b), dot(cols, spread_t), wide[half])
    for half in range(2):
        fwd2[half] = tall[half][:STACK].astype(jnp.bfloat16)
        back1[half] = tall[half][STACK:].astype(jnp.bfloat16)
        back2[half] = wide[half][:, :STACK].astype(jnp.bfloat16)
        fwd1[half] = wide[half][:, STACK:].astype(jnp.bfloat16)
    one = split(jnp.broadcast_to(bias1[...], (256, CHANNELS)))
    wide1[...] = dot(lift, one[0], NT) + dot(lift, one[1], NT)
    gap = counting((LOG, COEFFS), 0) - 8.0 * counting((LOG, COEFFS), 1)
    pick = ((gap >= 0.0) & (gap < 8.0)).astype(jnp.float32).astype(jnp.bfloat16)
    two = split(jnp.broadcast_to(bias2[...], (DEPTH, COEFFS)))
    wide2[...] = dot(pick, two[0], NT) + dot(pick, two[1], NT)


def pack_kernel(field, cot, other, out, ext):
    for m in range(3):
        ext[m, 6:8, :] = other[m, 0, 62:64, :]
        ext[m, 8:72, :] = field[m, 0]
        ext[m, 72:74, :] = other[m, 0, 0:2, :]
    for q in range(PLANES):
        for m in range(3):
            out[q, m * REACH : (m + 1) * REACH, :] = ext[m, 8 * q + 6 : 8 * q + 18, :]
            out[q, 36 + 8 * m : 44 + 8 * m, :] = cot[m, 0, 8 * q : 8 * q + 8, :]
        out[q, 60:64, :] = jnp.zeros((4, DEPTH), jnp.float32)


def stack_field(field, high, low):
    for x in range(PLANES):
        whole = field[x, 0:48, :]
        for e in range(3):
            parts = split(turn(whole, 1 - e))
            for a in range(3):
                rows = slice((a * 3 + e) * 48, (a * 3 + e) * 48 + 48)
                high[rows, plane(x - a + 1)] = parts[0]
                low[rows, plane(x - a + 1)] = parts[1]


def network(field, fwd1, fwd2, bias1, bias2, hidden, weights, u_hi, u_lo, h_hi, h_lo, work):
    stack_field(field, u_hi, u_lo)
    for pair in range(4):
        cut = slice(pair * 256, pair * 256 + 256)
        out = dot3((fwd1[0], fwd1[1]), (u_hi[:, cut], u_lo[:, cut]))
        value = jnp.tanh(out + bias1[...])
        hidden[:, cut] = value
        parts = split(value)
        h_hi[:, cut] = parts[0]
        h_lo[:, cut] = parts[1]
        work[:, cut] = dot3((fwd2[0], fwd2[1]), parts)
    for x in range(PLANES):
        total = bias2[...]
        for a in range(3):
            for e in range(3):
                tap = a * 3 + e
                total = total + turn(work[tap * 48 : tap * 48 + 48, plane(x + a - 1)], 1 - e)
        weights[:, plane(x)] = jax.nn.sigmoid(total)


def around(field, x, direction, sign):
    if direction == 0:
        return [field[(x + sign) % PLANES, m * REACH + RIM : m * REACH + RIM + SLAB, :] for m in range(3)]
    if direction == 1:
        first = RIM + sign
        return [field[x, m * REACH + first : m * REACH + first + SLAB, :] for m in range(3)]
    return [turn(field[x, m * REACH + RIM : m * REACH + RIM + SLAB, :], -sign) for m in range(3)]


def advected(field, weights, x):
    center = around(field, x, 0, 0)
    total = [jnp.zeros((SLAB, DEPTH), jnp.float32)] * 3
    for d in range(3):
        ahead = around(field, x, d, 1)
        behind = around(field, x, d, -1)
        plus = 0.5 * (center[d] + ahead[d])
        minus = 0.5 * (behind[d] + center[d])
        rate_up = weights[2 * d * SLAB : (2 * d + 1) * SLAB, plane(x)]
        rate_low = weights[(2 * d + 1) * SLAB : (2 * d + 2) * SLAB, plane(x)]
        for m in range(3):
            upper = center[m] + rate_up * (ahead[m] - center[m])
            lower = center[m] + rate_low * (behind[m] - center[m])
            total[m] = total[m] + plus * upper - minus * lower
    return [center[m] - KAPPA * total[m] for m in range(3)]


def mixed(values, table):
    outs = []
    for row in table:
        total = None
        for weight, value in zip(row, values):
            term = value * float(weight)
            total = term if total is None else total + term
        outs.append(total)
    return outs


def lane_groups(size):
    return lax.broadcasted_iota(jnp.int32, (size, DEPTH), 1) // BAND


def scatter_modes(source, rows, out):
    groups = lane_groups(rows)
    for p in range(4):
        for g in range(4):
            total = None
            for f in range(2):
                for t in range(2):
                    slot = 2 * f + t
                    value = turn(source(f, 2 * p + t), BAND * (slot - g))
                    total = value if total is None else jnp.where(groups == slot, value, total)
            out[p * 4 + g] = total


def gather_modes(recv, f, k, first, rows):
    groups = lane_groups(rows)
    slot = 2 * f + k % 2
    total = None
    for g in range(4):
        value = turn(recv[(k // 2) * 4 + g, first : first + rows, :], BAND * (g - slot))
        total = value if total is None else jnp.where(groups == g, value, total)
    return total


def first_kernel_body(mode_x, recv, fwd1, fwd2, bias1, bias2, z_hi, z_lo, out, hidden, weights, u_hi, u_lo, h_hi, h_lo, work, modes):
    network(recv, fwd1, fwd2, bias1, bias2, hidden, weights, u_hi, u_lo, h_hi, h_lo, work)
    table = (z_hi[...], z_lo[...])
    moved_field = [jnp.concatenate(advected(recv, weights, x), axis=0) for x in range(PLANES)]
    for f in range(2):
        planes = moved_field if f == 0 else [recv[x, 36:60, :] for x in range(PLANES)]
        for k, value in enumerate(mixed(planes, mode_x)):
            modes[f, k] = value
    for f in range(2):
        flat = modes[f].reshape(PLANES * 24, DEPTH)
        modes[f] = dot3(split(flat), table).reshape(PLANES, 24, DEPTH)
    scatter_modes(lambda f, k: modes[f, k], 24, out)


def leray(parts):
    device = lax.axis_index("px") * 2 + lax.axis_index("py")
    pair = device // 4
    group = device % 4
    lane = lax.broadcasted_iota(jnp.int32, (ROWS, DEPTH), 1)
    row = lax.broadcasted_iota(jnp.int32, (ROWS, DEPTH), 0)
    odd_x = (lane // BAND) % 2
    odd_z = (lane // 16) % 2
    number_z = 16 * group + lane % 16
    top_x = (odd_x == 1) & (pair == 0)
    top_y = row == ROWS // 2
    top_z = (odd_z == 1) & (number_z == 0)
    number_y = row % (ROWS // 2)
    real = lambda value: value.astype(jnp.float32)
    rate_x = real(jnp.where(odd_x == 1, -pair, pair))
    rate_y = real(jnp.where(row < ROWS // 2, number_y, -number_y))
    rate_z = real(jnp.where(odd_z == 1, -number_z, number_z))
    high_x = real(jnp.where(top_x, PLANES // 2, 0))
    high_y = real(jnp.where(top_y, ROWS // 2, 0))
    high_z = real(jnp.where(top_z, DEPTH // 2, 0))
    size = rate_x * rate_x + rate_y * rate_y + rate_z * rate_z
    size = size + high_x * high_x + high_y * high_y + high_z * high_z
    inverse = 1.0 / jnp.maximum(size, 1.0)

    def slope_x(value):
        return rate_x * jnp.where(odd_x == 1, turn(value, BAND), turn(value, -BAND))

    def slope_y(value):
        return rate_y * jnp.concatenate([value[ROWS // 2 :], value[: ROWS // 2]], axis=0)

    def slope_z(value):
        return rate_z * jnp.where(odd_z == 1, turn(value, 16), turn(value, -16))

    spread = (slope_x(parts[0]) + slope_y(parts[1]) + slope_z(parts[2])) * inverse
    high = (high_x * parts[0] + high_y * parts[1] + high_z * parts[2]) * inverse
    return (
        parts[0] + slope_x(spread) - high_x * high,
        parts[1] + slope_y(spread) - high_y * high,
        parts[2] + slope_z(spread) - high_z * high,
    )


def both_kernel(recv, in_hi, in_lo, out_hi, out_lo, out):
    data = split(recv[...].reshape(16 * 24, DEPTH))
    modes = dot3((in_hi[...], in_lo[...]), data)
    fixed = leray([modes[m * ROWS : (m + 1) * ROWS] for m in range(3)])
    back = dot3((out_hi[...], out_lo[...]), split(jnp.concatenate(fixed, axis=0)))
    wide, rest = back[:512].reshape(16, 32, DEPTH), back[512:].reshape(16, 32, DEPTH)
    low = lax.broadcasted_iota(jnp.int32, (16, 24, DEPTH), 2) < DEPTH // 2
    out[:, 0:24, :] = jnp.where(low, wide[:, :24], rest[:, :24])
    out[:, 24:32, :] = jnp.where(low[:, :8], wide[:, 24:], turn(rest[:, 24:], DEPTH // 2))


def one_kernel(recv, in_hi, in_lo, out_hi, out_lo, out):
    data = split(recv[...].reshape(16 * 24, DEPTH))
    modes = dot3((in_hi[...], in_lo[...]), data)
    modes = modes[: 3 * ROWS] + turn(modes[3 * ROWS :], DEPTH // 2)
    fixed = leray([modes[m * ROWS : (m + 1) * ROWS] for m in range(3)])
    back = dot3((out_hi[...], out_lo[...]), split(jnp.concatenate(fixed, axis=0)))
    lane = lax.broadcasted_iota(jnp.int32, (256, DEPTH), 1)
    whole = jnp.where(lane < DEPTH // 2, back[:256], turn(back[256:], DEPTH // 2))
    out[...] = whole.reshape(16, 16, DEPTH)


def pullback(field, grad, hidden, weights, back2, back1, u_hi, u_lo, h_hi, h_lo, l_hi, l_lo, p_hi, p_lo, work, slope, sums, ends, earlier):
    slope[...] = jnp.zeros_like(slope)
    for x in range(PLANES):
        center = around(field, x, 0, 0)
        source = [-KAPPA * grad[x, m * SLAB : (m + 1) * SLAB, :] for m in range(3)]
        own = [grad[x, m * SLAB : (m + 1) * SLAB, :] for m in range(3)]
        logits = []
        for d in range(3):
            ahead = around(field, x, d, 1)
            behind = around(field, x, d, -1)
            plus = 0.5 * (center[d] + ahead[d])
            minus = 0.5 * (behind[d] + center[d])
            rate_up = weights[2 * d * SLAB : (2 * d + 1) * SLAB, plane(x)]
            rate_low = weights[(2 * d + 1) * SLAB : (2 * d + 2) * SLAB, plane(x)]
            grad_up = grad_low = grad_plus = grad_minus = None
            to_ahead, to_behind = [], []
            add = lambda total, term: term if total is None else total + term
            for m in range(3):
                gap_up = ahead[m] - center[m]
                gap_low = behind[m] - center[m]
                grad_plus = add(grad_plus, source[m] * (center[m] + rate_up * gap_up))
                grad_minus = add(grad_minus, -source[m] * (center[m] + rate_low * gap_low))
                grad_up = add(grad_up, source[m] * gap_up)
                grad_low = add(grad_low, -source[m] * gap_low)
                push_up = source[m] * plus
                push_low = -source[m] * minus
                to_ahead.append(push_up * rate_up)
                to_behind.append(push_low * rate_low)
                own[m] = own[m] + (push_up - to_ahead[m]) + (push_low - to_behind[m])
            own[d] = own[d] + 0.5 * (grad_plus + grad_minus)
            to_ahead[d] = to_ahead[d] + 0.5 * grad_plus
            to_behind[d] = to_behind[d] + 0.5 * grad_minus
            logits.append(grad_up * plus * rate_up * (1.0 - rate_up))
            logits.append(grad_low * minus * rate_low * (1.0 - rate_low))
            for m in range(3):
                first = m * REACH + RIM
                if d == 0:
                    slope[(x + 1) % PLANES, first : first + SLAB, :] += to_ahead[m]
                    slope[(x - 1) % PLANES, first : first + SLAB, :] += to_behind[m]
                elif d == 1:
                    slope[x, first + 1 : first + 1 + SLAB, :] += to_ahead[m]
                    slope[x, first - 1 : first - 1 + SLAB, :] += to_behind[m]
                else:
                    own[m] = own[m] + turn(to_ahead[m], 1) + turn(to_behind[m], -1)
        for m in range(3):
            slope[x, m * REACH + RIM : m * REACH + RIM + SLAB, :] += own[m]
        whole = jnp.concatenate(logits, axis=0)
        for e in range(3):
            parts = split(turn(whole, e - 1))
            for a in range(3):
                rows = slice((a * 3 + e) * 48, (a * 3 + e) * 48 + 48)
                l_hi[rows, plane(x + a - 1)] = parts[0]
                l_lo[rows, plane(x + a - 1)] = parts[1]
    for pair in range(4):
        cut = slice(pair * 256, pair * 256 + 256)
        value = dot3((back2[0], back2[1]), (l_hi[:, cut], l_lo[:, cut]))
        parts = split(value * (1.0 - hidden[:, cut] * hidden[:, cut]))
        p_hi[:, cut] = parts[0]
        p_lo[:, cut] = parts[1]
        work[:, cut] = dot3((back1[0], back1[1]), parts)
    for x in range(PLANES):
        total = slope[x, 0:40, :]
        for a in range(3):
            for e in range(3):
                tap = a * 3 + e
                total = total + turn(work[tap * 48 : tap * 48 + 40, plane(x - a + 1)], e - 1)
        slope[x, 0:40, :] = total
    second = dot3((l_hi[...], l_lo[...]), (h_hi[...], h_lo[...]), NT)
    first = dot3((u_hi[...], u_lo[...]), (p_hi[...], p_lo[...]), NT)
    ones = jnp.ones((16, FLAT), jnp.bfloat16)
    end1 = dot(ones, p_hi[...], NT) + dot(ones, p_lo[...], NT)
    end2 = dot(ones, l_hi[4 * 48 : 5 * 48, :], NT) + dot(ones, l_lo[4 * 48 : 5 * 48, :], NT)
    if earlier is None:
        sums[0:STACK, :] = second
        sums[STACK:, :] = first
        ends[0:16, :] = end1
        ends[16:32, 0:LOG] = end2
    else:
        old_sums, old_ends = earlier
        sums[0:STACK, :] = old_sums[0:STACK, :] + second
        sums[STACK:, :] = old_sums[STACK:, :] + first
        ends[0:16, :] = old_ends[0:16, :] + end1
        ends[16:32, 0:LOG] = old_ends[16:32, 0:LOG] + end2


def second_kernel_body(
    mode_x, recv, fwd1, fwd2, back2, back1, bias1, bias2, to_hi, to_lo, from_hi, from_lo,
    out, sums, ends,
    field, grad, modes, rows6, hidden, weights, u_hi, u_lo, h_hi, h_lo, l_hi, l_lo, p_hi, p_lo, work, slope,
):
    back_z = (from_hi[...], from_lo[...])
    for k in range(PLANES):
        modes[k, 0:32, :] = gather_modes(recv, 0, k, 0, 32)
        modes[k, 32:40, :] = gather_modes(recv, 1, k, 24, 8)
    flat = dot3(split(modes[...].reshape(PLANES * 40, DEPTH)), back_z)
    modes[...] = flat.reshape(PLANES, 40, DEPTH)
    for x, value in enumerate(mixed([modes[k] for k in range(PLANES)], mode_x.T)):
        field[x, 0:40, :] = value
        field[x, 40:48, :] = jnp.zeros((8, DEPTH), jnp.float32)
    for k in range(PLANES):
        grad[k] = gather_modes(recv, 1, k, 0, 24)
    flat = dot3(split(grad[...].reshape(PLANES * 24, DEPTH)), back_z)
    flat = flat.reshape(PLANES, 24, DEPTH)
    for x, value in enumerate(mixed([flat[k] for k in range(PLANES)], mode_x.T)):
        grad[x] = value
    network(field, fwd1, fwd2, bias1, bias2, hidden, weights, u_hi, u_lo, h_hi, h_lo, work)
    pullback(
        field, grad, hidden, weights, back2, back1, u_hi, u_lo, h_hi, h_lo, l_hi, l_lo, p_hi, p_lo,
        work, slope, sums, ends, None,
    )
    for k, value in enumerate(mixed([slope[x, 0:40, :] for x in range(PLANES)], mode_x)):
        modes[k] = value
    flat = dot3(split(modes[...].reshape(PLANES * 40, DEPTH)), (to_hi[...], to_lo[...]))
    modes[...] = flat.reshape(PLANES, 40, DEPTH)
    for h in range(2):
        for k in range(PLANES):
            for m in range(3):
                rows6[h, k, m * 6 : m * 6 + 6, :] = modes[k, m * REACH + 6 * h : m * REACH + 6 * h + 6, :]
            rows6[h, k, 18:24, :] = jnp.zeros((6, DEPTH), jnp.float32)
    scatter_modes(lambda h, k: rows6[h, k], 24, out)


def third_kernel_body(
    mode_x, recv, field, hidden, weights, back2, back1, from_hi, from_lo, old_sums, old_ends,
    spread_t, mask, lift, count,
    out,
    grad, modes, u_hi, u_lo, h_hi, h_lo, l_hi, l_lo, p_hi, p_lo, work, slope, sums, ends, pieces,
):
    back_z = (from_hi[...], from_lo[...])
    for h in range(2):
        for k in range(PLANES):
            modes[k] = gather_modes(recv, h, k, 0, 16)
        flat = dot3(split(modes[...].reshape(PLANES * 16, DEPTH)), back_z)
        modes[...] = flat.reshape(PLANES, 16, DEPTH)
        for x, value in enumerate(mixed([modes[k] for k in range(PLANES)], mode_x.T)):
            for m in range(3):
                grad[x, m * SLAB + 4 * h : m * SLAB + 4 * h + 4, :] = value[m * 4 : m * 4 + 4, :]
    stack_field(field, u_hi, u_lo)
    parts = split(hidden[...])
    h_hi[...] = parts[0]
    h_lo[...] = parts[1]
    pullback(
        field, grad, hidden, weights, back2, back1, u_hi, u_lo, h_hi, h_lo, l_hi, l_lo, p_hi, p_lo,
        work, slope, sums, ends, (old_sums, old_ends),
    )
    for x in range(PLANES):
        out[x, 0:40, :] = slope[x, 0:40, :]
        out[x, 36:40, :] = jnp.zeros((4, DEPTH), jnp.float32)
    pack_grads(sums, ends, spread_t, mask, lift, count, pieces)
    for x in range(PLANES):
        out[x, 40:72, :] = pieces[96:128, :]


def pack_grads(sums, ends, spread_t, mask, lift, count, pieces):
    pieces[...] = jnp.zeros_like(pieces)
    for b in range(3):
        parts = split(sums[...] * mask[b].astype(jnp.float32))
        rows = dot(spread_t[...], parts[0]) + dot(spread_t[...], parts[1])
        parts = split(rows)
        pieces[0:96, :] = dot(parts[0], lift[...]) + dot(parts[1], lift[...])
        for c in range(3):
            slot = b * 3 + c
            if slot < 8:
                pieces[96:123, :] += turn(pieces[c * 27 : c * 27 + 27, :], 16 * slot)
            else:
                for part in range(7):
                    first = c * 27 + part * 4
                    count_rows = min(4, c * 27 + 27 - first)
                    pieces[123 : 123 + count_rows, :] += turn(
                        pieces[first : first + count_rows, :], 16 * part
                    )
    parts = split(ends[0:16, :])
    total = dot(parts[0], lift[...]) + dot(parts[1], lift[...])
    parts = split(ends[16:32, 0:LOG])
    total = total + dot(parts[0], count[...]) + dot(parts[1], count[...])
    pieces[127:128, :] = total[0:1, :]


def fold_kernel(recv, main, edge, ext):
    ext[...] = jnp.zeros_like(ext)
    total = None
    for q in range(PLANES):
        for m in range(3):
            ext[m, 8 * q + 6 : 8 * q + 18, :] += recv[q, m * REACH : (m + 1) * REACH, :]
        block = recv[q, 40:72, :]
        total = block if total is None else total + block
    for m in range(3):
        main[m, 0] = ext[m, 8:72, :]
        edge[m * 8 : m * 8 + 2, :] = ext[m, 72:74, :]
        edge[m * 8 + 2 : m * 8 + 4, :] = ext[m, 6:8, :]
        edge[m * 8 + 4 : m * 8 + 8, :] = jnp.zeros((4, DEPTH), jnp.float32)
    edge[24:56, :] = total


def last_kernel(main, edge, other, out, first, end1, second, end2, turned):
    for m in range(3):
        out[m, 0] = main[m, 0]
        out[m, 0, 0:2, :] += other[m * 8 : m * 8 + 2, :]
        out[m, 0, 62:64, :] += other[m * 8 + 2 : m * 8 + 4, :]
    grads = edge[24:56, :] + other[24:56, :]
    for slot in range(8):
        turned[slot] = turn(grads, -16 * slot)
    for b in range(3):
        for a in range(3):
            for e in range(3):
                for i in range(9):
                    row = (a * 3 + e) * 6 + i if i < 6 else 54 + (a * 3 + e) * 3 + i - 6
                    slot, inner = b * 3 + row // 27, row % 27
                    if slot == 8:
                        slot, inner = inner // 4, 27 + inner % 4
                    line = turned[slot, inner, 0:16]
                    if i < 6:
                        second[i * 9 + a * 3 + b, e, :] = line
                    else:
                        first[(i - 6) * 9 + a * 3 + b, e, :] = line
    end1[...] = turned[0, 31:32, 0:16]
    end2[...] = turned[1, 31:32, 0:6]


def slab_device(velocity, cotangent, first_kernel, first_bias, second_kernel, second_bias):
    c = constants()
    mode_x = c["mode_x"]
    half = jnp.bfloat16
    f32 = lambda *dims: pltpu.VMEM(dims, jnp.float32)
    b16 = lambda *dims: pltpu.VMEM(dims, half)
    swap = [(0, 1), (1, 0)]

    other = lax.ppermute(velocity, "py", swap)
    packed = call(
        pack_kernel, shape(PLANES, 64, DEPTH), (velocity, cotangent, other), [f32(3, 80, DEPTH)], 56
    )
    recv = lax.all_to_all(packed, "px", 0, 0)

    fwd2, fwd1, back2, back1, bias1, bias2 = call(
        weights_kernel,
        [
            shape(2, STACK, HID, kind=half),
            shape(2, HID, STACK, kind=half),
            shape(2, HID, STACK, kind=half),
            shape(2, STACK, HID, kind=half),
            shape(HID, 256),
            shape(LOG, DEPTH),
        ],
        (
            jnp.transpose(first_kernel, (1, 2, 3, 4, 0)).reshape(27, 3, CHANNELS),
            jnp.transpose(second_kernel, (0, 2, 3, 4, 1)).reshape(54, 3, CHANNELS),
            first_bias.reshape(1, CHANNELS),
            second_bias.reshape(1, COEFFS),
        ),
        [f32(3, 96, CHANNELS)],
    )

    stacks = lambda rows: [b16(rows, FLAT), b16(rows, FLAT)]
    sent, hidden, weights = call(
        functools.partial(first_kernel_body, mode_x),
        [shape(16, 24, DEPTH), shape(HID, FLAT), shape(LOG, FLAT)],
        (recv, fwd1, fwd2, bias1, bias2, *c["to_z"]),
        stacks(STACK) + stacks(HID) + [f32(STACK, FLAT), f32(2, PLANES, 24, DEPTH)],
    )
    both = ("px", "py")
    moved_modes = lax.all_to_all(sent, both, 0, 0)
    moved_modes = call(both_kernel, shape(16, 32, DEPTH), (moved_modes, *c["both_in"], *c["both_out"]))
    moved_modes = lax.all_to_all(moved_modes, both, 0, 0)

    sent, sums, ends = call(
        functools.partial(second_kernel_body, mode_x),
        [shape(16, 24, DEPTH), shape(2 * STACK, HID), shape(32, HID)],
        (moved_modes, fwd1, fwd2, back2, back1, bias1, bias2, *c["to_z"], *c["from_z"]),
        [f32(PLANES, 48, DEPTH), f32(PLANES, 24, DEPTH), f32(PLANES, 40, DEPTH), f32(2, PLANES, 24, DEPTH)]
        + [f32(HID, FLAT), f32(LOG, FLAT)]
        + stacks(STACK) + stacks(HID) + stacks(STACK) + stacks(HID)
        + [f32(STACK, FLAT), f32(PLANES, 48, DEPTH)],
    )
    moved_modes = lax.all_to_all(sent, both, 0, 0)
    moved_modes = call(one_kernel, shape(16, 16, DEPTH), (moved_modes, *c["one_in"], *c["one_out"]))
    moved_modes = lax.all_to_all(moved_modes, both, 0, 0)

    sent = call(
        functools.partial(third_kernel_body, mode_x),
        shape(PLANES, 72, DEPTH),
        (
            moved_modes, recv, hidden, weights, back2, back1, *c["from_z"], sums, ends,
            c["spread_t"], c["mask"], c["lift"], c["count"],
        ),
        [f32(PLANES, 24, DEPTH), f32(PLANES, 16, DEPTH)]
        + stacks(STACK) + stacks(HID) + stacks(STACK) + stacks(HID)
        + [f32(STACK, FLAT), f32(PLANES, 48, DEPTH), f32(2 * STACK, HID), f32(32, HID), f32(128, DEPTH)],
    )
    recv = lax.all_to_all(sent, "px", 0, 0)
    main, edge = call(
        fold_kernel, [shape(3, 1, 64, DEPTH), shape(56, DEPTH)], (recv,), [f32(3, 80, DEPTH)]
    )
    other = lax.ppermute(edge, "py", swap)
    grad_velocity, first, end1, second, end2 = call(
        last_kernel,
        [
            shape(3, 1, 64, DEPTH),
            shape(27, 3, CHANNELS),
            shape(1, CHANNELS),
            shape(54, 3, CHANNELS),
            shape(1, COEFFS),
        ],
        (main, edge, other),
        [f32(8, 32, DEPTH)],
    )
    return (
        grad_velocity,
        jnp.transpose(first.reshape(3, 3, 3, 3, CHANNELS), (4, 0, 1, 2, 3)),
        end1.reshape(CHANNELS),
        jnp.transpose(second.reshape(COEFFS, 3, 3, 3, CHANNELS), (0, 4, 1, 2, 3)),
        end2.reshape(COEFFS),
    )


def fits_slabs(mesh):
    return mesh.shape["px"] == PLANES and mesh.shape["py"] == 2


def solution(mesh):
    return jax.shard_map(
        slab_device if fits_slabs(mesh) else on_device,
        mesh=mesh,
        in_specs=(
            P(None, ("groups", "px"), "py", None),
            P(None, ("groups", "px"), "py", None),
            P(),
            P(),
            P(),
            P(),
        ),
        out_specs=(
            P(None, ("groups", "px"), "py", None),
            P("groups", None, None, None, None),
            P("groups"),
            P("groups", None, None, None, None),
            P("groups"),
        ),
        check_vma=False,
    )
```

```python
import functools
import math

import jax
import jax.numpy as jnp
import numpy as np
from jax import lax
from jax.experimental import pallas as pl
from jax.experimental.pallas import tpu as pltpu
from jax.sharding import PartitionSpec as P

ITERS = 2


KAPPA = 0.25


def padded_2(value, sides, width):
    for axis, dim in sides:
        size, length = (lax.axis_size(axis), value.shape[dim])
        up = [(i, (i + 1) % size) for i in range(size)]
        down = [(j, i) for i, j in up]
        last = lax.slice_in_dim(value, length - width, length, axis=dim)
        initial = lax.slice_in_dim(value, 0, width, axis=dim)
        before = lax.ppermute(last, axis, up)
        after = lax.ppermute(initial, axis, down)
        value = jnp.concatenate([before, value, after], axis=dim)
    return value


def extend(field):
    rimmed = padded_2(field, (("px", 1), ("py", 2)), 1)
    return jnp.concatenate([rimmed[..., -1:], rimmed, rimmed[..., :1]], axis=3)


def across_columns(spectrum):
    return lax.all_to_all(spectrum, "px", split_axis=2, concat_axis=4, tiled=True)


def across_pairs(spectrum):
    return lax.all_to_all(spectrum, "py", split_axis=3, concat_axis=4, tiled=True)


def summed(grads):
    return lax.psum((grads[0], grads[1], grads[2], grads[3]), ("px", "py"))


def all_taps():
    return [
        (shift_x, shift_y, shift_z)
        for shift_x in range(3)
        for shift_y in range(3)
        for shift_z in range(3)
    ]


def gather_conv(padded, kernel):
    size_x = padded.shape[1] - 2
    size_y = padded.shape[2] - 2
    size_z = padded.shape[3] - 2
    stacked = jnp.concatenate(
        [
            padded[:, sx_one : sx_one + size_x, sy_one : sy_one + size_y, sz_one : sz_one + size_z]
            for sx_one, sy_one, sz_one in all_taps()
        ],
        axis=0,
    )
    matrix = jnp.transpose(kernel, (0, 2, 3, 4, 1)).reshape(kernel.shape[0], -1)
    result = jnp.einsum("ok,kxyz->oxyz", matrix, stacked, precision=lax.Precision.HIGHEST)
    return (result, stacked)


def scatter_conv(padded, kernel):
    outputs = kernel.shape[0]
    inputs = kernel.shape[1]
    size_x = padded.shape[1] - 2
    size_y = padded.shape[2] - 2
    size_z = padded.shape[3] - 2
    total = jnp.zeros((outputs, size_x, size_y, size_z), jnp.float32)
    for shift_x in range(3):
        matrix = jnp.transpose(kernel[:, :, shift_x], (0, 2, 3, 1)).reshape(outputs * 9, inputs)
        layer = jnp.einsum(
            "km,mxyz->kxyz",
            matrix,
            padded[:, shift_x : shift_x + size_x],
            precision=lax.Precision.HIGHEST,
        )
        layer = layer.reshape(outputs, 3, 3, size_x, size_y + 2, size_z + 2)
        for shift_y in range(3):
            for shift_z in range(3):
                total = (
                    total
                    + layer[
                        :,
                        shift_y,
                        shift_z,
                        :,
                        shift_y : shift_y + size_y,
                        shift_z : shift_z + size_z,
                    ]
                )
    return total


def flipped(kernel):
    return jnp.transpose(kernel[:, :, ::-1, ::-1, ::-1], (1, 0, 2, 3, 4))


def moved(padded, axis_dim, offset_cells):
    index = [slice(None), slice(1, -1), slice(1, -1), slice(1, -1)]
    index[axis_dim] = slice(1 + offset_cells, padded.shape[axis_dim] - 1 + offset_cells)
    return padded[tuple(index)]


def advect(padded, weights):
    center = moved(padded, 1, 0)
    total = jnp.zeros_like(center)
    for direction in range(3):
        ahead = moved(padded, direction + 1, 1)
        behind = moved(padded, direction + 1, -1)
        vplus = 0.5 * (center[direction] + ahead[direction])
        vminus = 0.5 * (behind[direction] + center[direction])
        upper = center + weights[2 * direction] * (ahead - center)
        lower = center + weights[2 * direction + 1] * (behind - center)
        total = total + vplus * upper - vminus * lower
    return total


def advect_back(padded, weights_pad, source_pad):
    center = moved(padded, 1, 0)
    source = moved(source_pad, 1, 0)
    weights = moved(weights_pad, 1, 0)
    grad_field = jnp.zeros_like(center)
    fluxes = []
    parts = []
    for direction in range(3):
        ahead = moved(padded, direction + 1, 1)
        behind = moved(padded, direction + 1, -1)
        vplus = 0.5 * (center[direction] + ahead[direction])
        vminus = 0.5 * (behind[direction] + center[direction])
        rate_up = weights[2 * direction]
        rate_low = weights[2 * direction + 1]
        rate_before = moved(weights_pad[2 * direction : 2 * direction + 1], direction + 1, -1)[0]
        rate_after = moved(weights_pad[2 * direction + 1 : 2 * direction + 2], direction + 1, 1)[0]
        source_before = moved(source_pad, direction + 1, -1)
        source_after = moved(source_pad, direction + 1, 1)
        upper = center + rate_up * (ahead - center)
        lower = center + rate_low * (behind - center)
        upper_before = behind + rate_before * (center - behind)
        lower_after = ahead + rate_after * (center - ahead)
        grad_field = grad_field + source * (vplus * (1.0 - rate_up) - vminus * (1.0 - rate_low))
        grad_field = (
            grad_field + vminus * rate_before * source_before - vplus * rate_after * source_after
        )
        fluxes.append(
            0.5
            * (
                jnp.sum(source * upper, 0)
                - jnp.sum(source * lower, 0)
                + jnp.sum(source_before * upper_before, 0)
                - jnp.sum(source_after * lower_after, 0)
            )
        )
        parts.append(jnp.sum(source * vplus * (ahead - center), 0))
        parts.append(-jnp.sum(source * vminus * (behind - center), 0))
    return (grad_field + jnp.stack(fluxes), jnp.stack(parts))


def tables(count):
    index = jnp.arange(count, dtype=jnp.int32)
    phase = index[:, None] * index[None, :] % count
    angle = phase.astype(jnp.float32) * (2.0 * math.pi / count)
    return (jnp.cos(angle), jnp.sin(angle))


def mix(form, data, table):
    return jnp.einsum(form, data, table, precision=lax.Precision.HIGHEST)


def waves(start, count, total):
    index = start + jnp.arange(count, dtype=jnp.int32)
    return jnp.where(index < total // 2, index, index - total).astype(jnp.float32)


def project(field):
    depth = field.shape[3]
    cos_z, sin_z = tables(depth)
    real_z = mix("cxyz,zk->cxky", field, cos_z)
    imag_z = -mix("cxyz,zk->cxky", field, sin_z)
    spectrum = across_pairs(jnp.stack([real_z, imag_z]))
    span_y = spectrum.shape[4]
    cos_y, sin_y = tables(span_y)
    real_y = mix("cxky,yq->cqkx", spectrum[0], cos_y) + mix("cxky,yq->cqkx", spectrum[1], sin_y)
    imag_y = mix("cxky,yq->cqkx", spectrum[1], cos_y) - mix("cxky,yq->cqkx", spectrum[0], sin_y)
    spectrum = across_columns(jnp.stack([real_y, imag_y]))
    span_x = spectrum.shape[4]
    cos_x, sin_x = tables(span_x)
    real_x = mix("cqkx,xp->cqkp", spectrum[0], cos_x) + mix("cqkx,xp->cqkp", spectrum[1], sin_x)
    imag_x = mix("cqkx,xp->cqkp", spectrum[1], cos_x) - mix("cqkx,xp->cqkp", spectrum[0], sin_x)
    rows_y = spectrum.shape[2]
    rows_z = spectrum.shape[3]
    wave_y = waves(lax.axis_index("px") * rows_y, rows_y, span_y)[:, None, None]
    wave_z = waves(lax.axis_index("py") * rows_z, rows_z, depth)[None, :, None]
    wave_x = waves(0, span_x, span_x)[None, None, :]
    size = jnp.maximum(wave_x * wave_x + wave_y * wave_y + wave_z * wave_z, 1.0)
    vectors = jnp.stack(jnp.broadcast_arrays(wave_x, wave_y, wave_z))
    real_x = real_x - vectors * (
        (wave_x * real_x[0] + wave_y * real_x[1] + wave_z * real_x[2]) / size
    )
    imag_x = imag_x - vectors * (
        (wave_x * imag_x[0] + wave_y * imag_x[1] + wave_z * imag_x[2]) / size
    )
    back_real = (mix("cqkp,px->cxkq", real_x, cos_x) - mix("cqkp,px->cxkq", imag_x, sin_x)) / span_x
    back_imag = (mix("cqkp,px->cxkq", imag_x, cos_x) + mix("cqkp,px->cxkq", real_x, sin_x)) / span_x
    spectrum = across_columns(jnp.stack([back_real, back_imag]))
    rows_real = (
        mix("cxkq,qy->cxyk", spectrum[0], cos_y) - mix("cxkq,qy->cxyk", spectrum[1], sin_y)
    ) / span_y
    rows_imag = (
        mix("cxkq,qy->cxyk", spectrum[1], cos_y) + mix("cxkq,qy->cxyk", spectrum[0], sin_y)
    ) / span_y
    spectrum = across_pairs(jnp.stack([rows_real, rows_imag]))
    return (
        mix("cxyk,kz->cxyz", spectrum[0], cos_z) - mix("cxyk,kz->cxyz", spectrum[1], sin_z)
    ) / depth


def forward_state(field, first_kernel, first_bias, second_kernel, second_bias):
    padded = extend(field)
    first_out, field_taps = gather_conv(padded, first_kernel)
    hidden = jnp.tanh(first_out + first_bias[:, None, None, None])
    weights = jax.nn.sigmoid(
        scatter_conv(extend(hidden), second_kernel) + second_bias[:, None, None, None]
    )
    return (padded, hidden, weights, field_taps)


def backward_step(state, upstream, first_kernel, second_kernel):
    padded, hidden, weights, field_taps = state
    moved_grad = project(upstream)
    source = -KAPPA * moved_grad
    stacked = extend(jnp.concatenate([source, weights], axis=0))
    grad_field, grad_weights = advect_back(padded, stacked[3:], stacked[:3])
    grad_field = grad_field + moved_grad
    grad_logits = grad_weights * weights * (1.0 - weights)
    logits_pad = extend(grad_logits)
    grad_hidden, logit_taps = gather_conv(logits_pad, flipped(second_kernel))
    product = jnp.einsum("kxyz,mxyz->km", logit_taps, hidden, precision=lax.Precision.HIGHEST)
    product = product.reshape(3, 3, 3, second_kernel.shape[0], second_kernel.shape[1])
    grad_second = jnp.transpose(product[::-1, ::-1, ::-1], (3, 4, 0, 1, 2))
    grad_second_bias = jnp.sum(grad_logits, axis=(1, 2, 3))
    grad_pre = grad_hidden * (1.0 - hidden * hidden)
    pre_pad = extend(grad_pre)
    grad_field = grad_field + scatter_conv(pre_pad, flipped(first_kernel))
    first_product = jnp.einsum(
        "oxyz,kxyz->ok", grad_pre, field_taps, precision=lax.Precision.HIGHEST
    )
    first_product = first_product.reshape(first_kernel.shape[0], 3, 3, 3, first_kernel.shape[1])
    grad_first = jnp.transpose(first_product, (0, 4, 1, 2, 3))
    grad_first_bias = jnp.sum(grad_pre, axis=(1, 2, 3))
    return (grad_field, (grad_first, grad_first_bias, grad_second, grad_second_bias))


def on_device(velocity, cotangent, first_kernel, first_bias, second_kernel, second_bias):
    field = velocity
    fields = [velocity]
    saved = []
    for section in range(ITERS):
        state = forward_state(field, first_kernel, first_bias, second_kernel, second_bias)
        saved.append(state)
        field = project(field - KAPPA * advect(state[0], state[2]))
        fields.append(field)
    upstream = cotangent
    totals = None
    for section in reversed(range(ITERS)):
        state = saved[section]
        upstream, grads = backward_step(state, upstream, first_kernel, second_kernel)
        grads = summed(grads)
        if totals is None:
            totals = grads
        else:
            totals = tuple((older + newer for older, newer in zip(totals, grads)))
    return (upstream, totals[0], totals[1], totals[2], totals[3])


SLAB = 8
RIM = 2
REACH = SLAB + 2 * RIM
WIDE = SLAB + 2
PLANES = 8
DEPTH = 128
ROWS = 128
CHANNELS = 16
COEFFS = 6
BAND = 32
HID = CHANNELS * WIDE
LOG = COEFFS * SLAB
STACK = 9 * 48
TALL = STACK + 16
BROAD = HID + 16
DEEP = 3 * HID + 16
PLACE = (0, 2, 1)
FLAT = PLANES * DEPTH
NN = ((1,), (0,))
NT = ((1,), (1,))


def real_basis(count):
    half = count // 2
    angle = 2.0 * np.pi * np.arange(count) / count
    rows = [np.full(count, 1.0 / np.sqrt(count))]
    rows += [np.sqrt(2.0 / count) * np.cos(k * angle) for k in range(1, half)]
    rows += [np.cos(half * angle) / np.sqrt(count)]
    rows += [np.sqrt(2.0 / count) * np.sin(k * angle) for k in range(1, half)]
    return np.stack(rows)


def stacked_table(table):
    return np.concatenate(halves(table))


def halves(table):
    high = table.astype(np.float32).astype(jnp.bfloat16)
    low = (table - high.astype(np.float64)).astype(np.float32).astype(jnp.bfloat16)
    return high, low


def slab_of(device):
    return (device % 2) * PLANES + device // 2


@functools.cache
def constants():
    basis_x = real_basis(PLANES)
    mode_x = np.stack([basis_x[(k // 2) + (PLANES // 2) * (k % 2)] for k in range(PLANES)])
    basis_z = real_basis(DEPTH)
    order = []
    for group in range(4):
        order += [16 * group + i for i in range(16)] + [64 + 16 * group + i for i in range(16)]
    mode_z = basis_z[order]
    basis_y = real_basis(ROWS)

    def columns(device, offset, count):
        return basis_y[:, (SLAB * slab_of(device) + offset + np.arange(count)) % ROWS]

    def table(block, offset, count):
        out = np.zeros((3, ROWS, 16, block))
        for device in range(16):
            for m in range(3):
                out[m, :, device, m * count : (m + 1) * count] = columns(device, offset, count)
        return out.reshape(3 * ROWS, 16 * block)

    both_in = table(24, 0, 8)
    wide_out = table(40, -RIM, REACH).T.reshape(16, 40, 3 * ROWS)
    own_out = table(24, 0, 8).T.reshape(16, 24, 3 * ROWS)
    rest = np.concatenate([own_out, wide_out[:, 32:]], axis=1)
    both_out = np.stack([wide_out[:, :32], rest]).reshape(2 * 16 * 32, 3 * ROWS)
    one_in = np.concatenate([table(24, -RIM, 6), table(24, -RIM + 6, 6)])
    one_out = np.concatenate([table(16, 0, 4).T, table(16, 4, 4).T])

    spread = np.zeros((STACK + TALL, 96))
    mask = np.zeros((3, STACK + TALL, BROAD))
    for tap in range(9):
        for o in range(COEFFS):
            for q in range(SLAB):
                row = tap * 48 + o * SLAB + q
                spread[row, tap * COEFFS + o] = 1.0
                for b in range(3):
                    mask[b, row, np.arange(CHANNELS) * WIDE + q + b] = 1.0
        for m in range(3):
            for r in range(REACH):
                row = STACK + tap * 48 + m * REACH + r
                spread[row, 54 + tap * 3 + m] = 1.0
                for b in range(3):
                    if 0 <= r - b < WIDE:
                        mask[b, row, np.arange(CHANNELS) * WIDE + r - b] = 1.0
    lift = np.zeros((BROAD, 128))
    lift[np.arange(HID), np.arange(HID) // WIDE] = 1.0
    count = np.zeros((LOG, 128))
    count[np.arange(LOG), 16 + np.arange(LOG) // SLAB] = 1.0
    half = jnp.bfloat16
    return dict(
        mode_x=mode_x,
        to_z=np.stack(halves(mode_z.T)),
        from_z=np.stack(halves(mode_z)),
        both_in=stacked_table(both_in),
        both_out=stacked_table(both_out),
        one_in=stacked_table(one_in),
        one_out=stacked_table(one_out),
        spread_t=np.ascontiguousarray(spread.T).astype(half),
        mask=mask.astype(half),
        lift=lift.astype(half),
        count=count.astype(half),
    )


def dot(left, right, dims=NN):
    return lax.dot_general(left, right, (dims, ((), ())), preferred_element_type=jnp.float32)


def split(value):
    high = value.astype(jnp.bfloat16)
    return high, (value - high.astype(jnp.float32)).astype(jnp.bfloat16)


def dot_stacked(left, right, dims=NN):
    rows = left.shape[0] // 2
    main = dot(left[...], right[0], dims)
    return main[:rows] + (main[rows:] + dot(left[0:rows, :], right[1], dims))


def stacked(value):
    return jnp.concatenate(split(value), axis=0)


def turn(value, shift):
    shift = shift % value.shape[-1]
    return value if shift == 0 else pltpu.roll(value, shift, value.ndim - 1)


def plane(x):
    x = x % PLANES
    return slice(x * DEPTH, (x + 1) * DEPTH)


def call(kernel, outs, args, scratch=(), room=16, away=()):
    single = not isinstance(outs, (list, tuple))
    vmem = pl.BlockSpec(memory_space=pltpu.VMEM)
    cost = pl.CostEstimate(flops=1, bytes_accessed=1, transcendentals=0) if away else None
    return pl.pallas_call(
        kernel,
        out_shape=outs,
        in_specs=[
            pl.BlockSpec(memory_space=pltpu.HBM) if i in away else vmem for i in range(len(args))
        ],
        out_specs=vmem if single else [vmem] * len(outs),
        scratch_shapes=list(scratch),
        cost_estimate=cost,
        compiler_params=pltpu.CompilerParams(vmem_limit_bytes=room * 2**20),
    )(*args)


def fetch(pairs, sems):
    copies = [pltpu.make_async_copy(src, dst, sems.at[i]) for i, (src, dst) in enumerate(pairs)]
    for copy in copies:
        copy.start()
    return copies


def shape(*dims, kind=jnp.float32):
    return jax.ShapeDtypeStruct(dims, kind)


def counting(size, dim):
    return lax.broadcasted_iota(jnp.int32, size, dim).astype(jnp.float32)


def remainder(value, count):
    return value - count * jnp.floor((value + 0.5) / count)


def band_tables(tall):
    row, col = (0, 1) if tall else (1, 0)
    size = lambda rows, cols: (rows, cols) if tall else (cols, rows)
    where = counting(size(2 * STACK, 96), row)
    to = counting(size(2 * STACK, 96), col)
    first = where - 8.0 * to
    third = to - 54.0
    second = where - STACK - (16.0 * third - 4.0 * remainder(third, 3.0))
    picks = ((to < 54.0) & (first >= 0.0) & (first < 8.0)) | (
        (to >= 54.0) & (to < 81.0) & (second >= 0.0) & (second < 12.0)
    )
    where = counting(size(2 * STACK, HID), row)
    inner = remainder(counting(size(2 * STACK, HID), col), 10.0)
    outer = where - STACK
    offset = jnp.where(
        where < STACK,
        inner - remainder(where, 8.0),
        remainder(remainder(outer, 48.0), 12.0) - inner,
    )
    gap = counting(size(HID, CHANNELS), row) - 10.0 * counting(size(HID, CHANNELS), col)
    lift = (gap >= 0.0) & (gap < 10.0)
    half = jnp.bfloat16
    return picks.astype(jnp.float32).astype(half), offset, lift.astype(jnp.float32).astype(half)


def weights_kernel(
    far1, far2, far3, far4, z_in, fwd2, fwd1, back2, back1, z_out, blocks, taps1, taps2, bias1, bias2, sems
):
    copies = fetch([(far1, taps1), (far2, taps2), (far3, bias1), (far4, bias2)], sems)
    blocks[...] = jnp.zeros_like(blocks)
    z_out[...] = z_in[...]
    spread, offset, lift = band_tables(True)
    spread_t, offset_t, lift_t = band_tables(False)
    for copy in copies:
        copy.wait()
    for b in range(3):
        for a in range(3):
            for e in range(3):
                tap = a * 3 + e
                for o in range(COEFFS):
                    blocks[b, tap * 6 + o, :] = taps2[o * 9 + a * 3 + b, e, :]
                for m in range(3):
                    blocks[b, 54 + tap * 3 + m, :] = taps1[m * 9 + a * 3 + b, e, :]
    tall = [jnp.zeros((2 * STACK, HID), jnp.float32)] * 2
    flat = [jnp.zeros((HID, 2 * STACK), jnp.float32)] * 2
    for b in range(3):
        for half, block in enumerate(split(blocks[b])):
            rows = dot(spread, block).astype(jnp.bfloat16)
            tall[half] = jnp.where(offset == float(b), dot(rows, lift_t), tall[half])
            cols = dot(lift, block, NT).astype(jnp.bfloat16)
            flat[half] = jnp.where(offset_t == float(b), dot(cols, spread_t), flat[half])
    for half in range(2):
        rows, cols = slice(half * 144, half * 144 + 144), slice(half * HID, half * HID + HID)
        for a in range(3):
            first = PLACE[a] * HID
            part = tall[half][a * 144 : a * 144 + 144]
            fwd2[rows, first : first + HID] = part.astype(jnp.bfloat16)
            part = tall[half][STACK + a * 144 : STACK + a * 144 + 144]
            back1[rows, first : first + HID] = part.astype(jnp.bfloat16)
        back2[cols, :] = flat[half][:, :STACK].astype(jnp.bfloat16)
        fwd1[cols, 0:STACK] = flat[half][:, STACK:].astype(jnp.bfloat16)
    gap = counting((LOG, COEFFS), 0) - 8.0 * counting((LOG, COEFFS), 1)
    pick = ((gap >= 0.0) & (gap < 8.0)).astype(jnp.float32).astype(jnp.bfloat16)
    first = counting((HID, 16), 1) < 1.0
    second = counting((LOG, 16), 1) < 1.0
    one = split(jnp.broadcast_to(bias1[...], (16, CHANNELS)))
    two = split(jnp.broadcast_to(bias2[...], (16, COEFFS)))
    fwd2[:, 3 * HID :] = jnp.zeros((288, 16), jnp.bfloat16)
    back1[:, 3 * HID :] = jnp.zeros((288, 16), jnp.bfloat16)
    for half in range(2):
        value = jnp.where(first, dot(lift, one[half], NT), 0.0)
        fwd1[half * HID : half * HID + HID, STACK:] = value.astype(jnp.bfloat16)
        value = jnp.where(second, dot(pick, two[half], NT), 0.0)
        start = half * 144 + LOG
        fwd2[start : start + LOG, 3 * HID :] = value.astype(jnp.bfloat16)


def pack_kernel(field, cot, out, ext):
    ext[...] = jnp.zeros_like(ext)
    for m in range(3):
        ext[m, 8:72, :] = field[m, 0]
    for q in range(PLANES):
        for m in range(3):
            out[q, m * REACH : (m + 1) * REACH, :] = ext[m, 8 * q + 6 : 8 * q + 18, :]
            out[q, 36 + 8 * m : 44 + 8 * m, :] = cot[m, 0, 8 * q : 8 * q + 8, :]
        out[q, 60:64, :] = jnp.zeros((4, DEPTH), jnp.float32)


def rim_kernel(packed, other, out):
    out[...] = packed[...]
    for m in range(3):
        out[0, m * REACH : m * REACH + 2, :] = other[m, 0, 62:64, :]
        out[PLANES - 1, m * REACH + 10 : m * REACH + 12, :] = other[m, 0, 0:2, :]


def unit_row():
    row = lax.broadcasted_iota(jnp.int32, (16, FLAT), 0)
    return jnp.where(row == 0, 1.0, 0.0).astype(jnp.bfloat16)


def stack_planes(value, first, sign, high, low):
    parts = split(value)
    for i in range(value.shape[1] // DEPTH):
        for a in range(3):
            rows = slice(PLACE[a] * HID, PLACE[a] * HID + HID)
            to = plane(first + i + sign * (a - 1))
            high[rows, to] = parts[0][:, i * DEPTH : (i + 1) * DEPTH]
            low[rows, to] = parts[1][:, i * DEPTH : (i + 1) * DEPTH]


def finish_planes(high, low):
    high[3 * HID :, :] = unit_row()
    low[3 * HID :, :] = jnp.zeros((16, FLAT), jnp.bfloat16)


def stack_logits(whole, x, l_taps):
    for e in range(3):
        parts = split(turn(whole, e - 1))
        for a in range(3):
            for half in range(2):
                first = half * STACK + (a * 3 + e) * 48
                l_taps[first : first + 48, plane(x + a - 1)] = parts[half]


def stack_field(field, taps):
    for x in range(PLANES):
        whole = field[x, 0:48, :]
        for e in range(3):
            parts = split(turn(whole, 1 - e))
            for a in range(3):
                rows = slice((a * 3 + e) * 48, (a * 3 + e) * 48 + 48)
                taps[rows, plane(x - a + 1)] = parts[0]
                taps[TALL + rows.start : TALL + rows.stop, plane(x - a + 1)] = parts[1]
    taps[STACK:TALL, :] = unit_row()
    taps[TALL + STACK :, :] = jnp.zeros((16, FLAT), jnp.bfloat16)


def network(field, fwd1, fwd2, hidden, weights, u_taps, h_hi, h_lo, work):
    stack_field(field, u_taps)
    finish_planes(h_hi, h_lo)
    for pair in range(4):
        cut = slice(pair * 256, pair * 256 + 256)
        value = jnp.tanh(dot_stacked(fwd1, (u_taps[0:TALL, cut], u_taps[TALL:, cut])))
        hidden[:, cut] = value
        stack_planes(value, 2 * pair, -1, h_hi, h_lo)
    for pair in range(4):
        cut = slice(pair * 256, pair * 256 + 256)
        work[:, cut] = dot_stacked(fwd2, (h_hi[:, cut], h_lo[:, cut]))
    for x in range(PLANES):
        total = work[LOG : 2 * LOG, plane(x)]
        total = total + turn(work[0:LOG, plane(x)], 1) + turn(work[2 * LOG : 3 * LOG, plane(x)], -1)
        weights[:, plane(x)] = jax.nn.sigmoid(total)


def around(field, x, direction, sign):
    if direction == 0:
        return [field[(x + sign) % PLANES, m * REACH + RIM : m * REACH + RIM + SLAB, :] for m in range(3)]
    if direction == 1:
        first = RIM + sign
        return [field[x, m * REACH + first : m * REACH + first + SLAB, :] for m in range(3)]
    return [turn(field[x, m * REACH + RIM : m * REACH + RIM + SLAB, :], -sign) for m in range(3)]


def advected(field, weights, x):
    center = around(field, x, 0, 0)
    total = [jnp.zeros((SLAB, DEPTH), jnp.float32)] * 3
    for d in range(3):
        ahead = around(field, x, d, 1)
        behind = around(field, x, d, -1)
        plus = 0.5 * (center[d] + ahead[d])
        minus = 0.5 * (behind[d] + center[d])
        rate_up = weights[2 * d * SLAB : (2 * d + 1) * SLAB, plane(x)]
        rate_low = weights[(2 * d + 1) * SLAB : (2 * d + 2) * SLAB, plane(x)]
        for m in range(3):
            upper = center[m] + rate_up * (ahead[m] - center[m])
            lower = center[m] + rate_low * (behind[m] - center[m])
            total[m] = total[m] + plus * upper - minus * lower
    return [center[m] - KAPPA * total[m] for m in range(3)]


def mixed(values, table):
    outs = []
    for row in table:
        total = None
        for weight, value in zip(row, values):
            term = value * float(weight)
            total = term if total is None else total + term
        outs.append(total)
    return outs


def lane_groups(size):
    return lax.broadcasted_iota(jnp.int32, (size, DEPTH), 1) // BAND


def scatter_modes(source, rows, out):
    groups = lane_groups(rows)
    for p in range(4):
        for g in range(4):
            total = None
            for f in range(2):
                for t in range(2):
                    slot = 2 * f + t
                    value = turn(source(f, 2 * p + t), BAND * (slot - g))
                    total = value if total is None else jnp.where(groups == slot, value, total)
            out[p * 4 + g] = total


def gather_modes(recv, f, k, first, rows):
    groups = lane_groups(rows)
    slot = 2 * f + k % 2
    total = None
    for g in range(4):
        value = turn(recv[(k // 2) * 4 + g, first : first + rows, :], BAND * (g - slot))
        total = value if total is None else jnp.where(groups == g, value, total)
    return total


def first_kernel_body(
    mode_x, recv, fwd1, fwd2, to_z, out, hidden, weights, u_taps, h_hi, h_lo, work, modes
):
    network(recv, fwd1, fwd2, hidden, weights, u_taps, h_hi, h_lo, work)
    table = (to_z[0], to_z[1])
    moved_field = [jnp.concatenate(advected(recv, weights, x), axis=0) for x in range(PLANES)]
    for f in range(2):
        planes = moved_field if f == 0 else [recv[x, 36:60, :] for x in range(PLANES)]
        for k, value in enumerate(mixed(planes, mode_x)):
            modes[f, k] = value
    for f in range(2):
        flat = modes[f].reshape(PLANES * 24, DEPTH)
        modes[f] = dot_stacked(stacked(flat), table).reshape(PLANES, 24, DEPTH)
    scatter_modes(lambda f, k: modes[f, k], 24, out)


def leray(parts):
    device = lax.axis_index("px") * 2 + lax.axis_index("py")
    pair = device // 4
    group = device % 4
    lane = lax.broadcasted_iota(jnp.int32, (ROWS, DEPTH), 1)
    row = lax.broadcasted_iota(jnp.int32, (ROWS, DEPTH), 0)
    odd_x = (lane // BAND) % 2
    odd_z = (lane // 16) % 2
    number_z = 16 * group + lane % 16
    top_x = (odd_x == 1) & (pair == 0)
    top_y = row == ROWS // 2
    top_z = (odd_z == 1) & (number_z == 0)
    number_y = row % (ROWS // 2)
    real = lambda value: value.astype(jnp.float32)
    rate_x = real(jnp.where(odd_x == 1, -pair, pair))
    rate_y = real(jnp.where(row < ROWS // 2, number_y, -number_y))
    rate_z = real(jnp.where(odd_z == 1, -number_z, number_z))
    high_x = real(jnp.where(top_x, PLANES // 2, 0))
    high_y = real(jnp.where(top_y, ROWS // 2, 0))
    high_z = real(jnp.where(top_z, DEPTH // 2, 0))
    size = rate_x * rate_x + rate_y * rate_y + rate_z * rate_z
    size = size + high_x * high_x + high_y * high_y + high_z * high_z
    inverse = 1.0 / jnp.maximum(size, 1.0)

    def slope_x(value):
        return rate_x * jnp.where(odd_x == 1, turn(value, BAND), turn(value, -BAND))

    def slope_y(value):
        return rate_y * jnp.concatenate([value[ROWS // 2 :], value[: ROWS // 2]], axis=0)

    def slope_z(value):
        return rate_z * jnp.where(odd_z == 1, turn(value, 16), turn(value, -16))

    spread = (slope_x(parts[0]) + slope_y(parts[1]) + slope_z(parts[2])) * inverse
    high = (high_x * parts[0] + high_y * parts[1] + high_z * parts[2]) * inverse
    return (
        parts[0] + slope_x(spread) - high_x * high,
        parts[1] + slope_y(spread) - high_y * high,
        parts[2] + slope_z(spread) - high_z * high,
    )


def both_kernel(recv, table_in, table_out, out):
    data = split(recv[...].reshape(16 * 24, DEPTH))
    modes = dot_stacked(table_in, data)
    fixed = leray([modes[m * ROWS : (m + 1) * ROWS] for m in range(3)])
    back = dot_stacked(table_out, split(jnp.concatenate(fixed, axis=0)))
    wide, rest = back[:512].reshape(16, 32, DEPTH), back[512:].reshape(16, 32, DEPTH)
    low = lax.broadcasted_iota(jnp.int32, (16, 24, DEPTH), 2) < DEPTH // 2
    out[:, 0:24, :] = jnp.where(low, wide[:, :24], rest[:, :24])
    out[:, 24:32, :] = jnp.where(low[:, :8], wide[:, 24:], turn(rest[:, 24:], DEPTH // 2))


def one_kernel(recv, table_in, table_out, out):
    data = split(recv[...].reshape(16 * 24, DEPTH))
    modes = dot_stacked(table_in, data)
    modes = modes[: 3 * ROWS] + turn(modes[3 * ROWS :], DEPTH // 2)
    fixed = leray([modes[m * ROWS : (m + 1) * ROWS] for m in range(3)])
    back = dot_stacked(table_out, split(jnp.concatenate(fixed, axis=0)))
    lane = lax.broadcasted_iota(jnp.int32, (256, DEPTH), 1)
    whole = jnp.where(lane < DEPTH // 2, back[:256], turn(back[256:], DEPTH // 2))
    out[...] = whole.reshape(16, 16, DEPTH)


def pullback(field, grad, hidden, weights, back2, back1, l_taps, p_hi, p_lo, work, slope):
    slope[...] = jnp.zeros_like(slope)
    for x in range(PLANES):
        center = around(field, x, 0, 0)
        source = [-KAPPA * grad[x, m * SLAB : (m + 1) * SLAB, :] for m in range(3)]
        own = [grad[x, m * SLAB : (m + 1) * SLAB, :] for m in range(3)]
        logits = []
        for d in range(3):
            ahead = around(field, x, d, 1)
            behind = around(field, x, d, -1)
            plus = 0.5 * (center[d] + ahead[d])
            minus = 0.5 * (behind[d] + center[d])
            rate_up = weights[2 * d * SLAB : (2 * d + 1) * SLAB, plane(x)]
            rate_low = weights[(2 * d + 1) * SLAB : (2 * d + 2) * SLAB, plane(x)]
            grad_up = grad_low = grad_plus = grad_minus = None
            to_ahead, to_behind = [], []
            add = lambda total, term: term if total is None else total + term
            for m in range(3):
                gap_up = ahead[m] - center[m]
                gap_low = behind[m] - center[m]
                grad_plus = add(grad_plus, source[m] * (center[m] + rate_up * gap_up))
                grad_minus = add(grad_minus, -source[m] * (center[m] + rate_low * gap_low))
                grad_up = add(grad_up, source[m] * gap_up)
                grad_low = add(grad_low, -source[m] * gap_low)
                push_up = source[m] * plus
                push_low = -source[m] * minus
                to_ahead.append(push_up * rate_up)
                to_behind.append(push_low * rate_low)
                own[m] = own[m] + (push_up - to_ahead[m]) + (push_low - to_behind[m])
            own[d] = own[d] + 0.5 * (grad_plus + grad_minus)
            to_ahead[d] = to_ahead[d] + 0.5 * grad_plus
            to_behind[d] = to_behind[d] + 0.5 * grad_minus
            logits.append(grad_up * plus * rate_up * (1.0 - rate_up))
            logits.append(grad_low * minus * rate_low * (1.0 - rate_low))
            for m in range(3):
                first = m * REACH + RIM
                if d == 0:
                    slope[(x + 1) % PLANES, first : first + SLAB, :] += to_ahead[m]
                    slope[(x - 1) % PLANES, first : first + SLAB, :] += to_behind[m]
                elif d == 1:
                    slope[x, first + 1 : first + 1 + SLAB, :] += to_ahead[m]
                    slope[x, first - 1 : first - 1 + SLAB, :] += to_behind[m]
                else:
                    own[m] = own[m] + turn(to_ahead[m], 1) + turn(to_behind[m], -1)
        for m in range(3):
            slope[x, m * REACH + RIM : m * REACH + RIM + SLAB, :] += own[m]
        whole = jnp.concatenate(logits, axis=0)
        stack_logits(whole, x, l_taps)
    for pair in range(4):
        cut = slice(pair * 256, pair * 256 + 256)
        value = dot_stacked(back2, (l_taps[0:STACK, cut], l_taps[STACK:, cut]))
        value = value * (1.0 - hidden[:, cut] * hidden[:, cut])
        stack_planes(value, 2 * pair, 1, p_hi, p_lo)
    finish_planes(p_hi, p_lo)
    for pair in range(4):
        cut = slice(pair * 256, pair * 256 + 256)
        work[:, cut] = dot_stacked(back1, (p_hi[:, cut], p_lo[:, cut]))
    for x in range(PLANES):
        total = slope[x, 0:40, :] + work[48:88, plane(x)]
        slope[x, 0:40, :] = total + turn(work[0:40, plane(x)], -1) + turn(work[96:136, plane(x)], 1)


def kernel_sums(u_taps, h_hi, h_lo, l_taps, p_hi, p_lo, sums):
    here = slice(2 * HID, DEEP)
    sums[0:STACK, :] = dot_stacked(l_taps, (h_hi[here, :], h_lo[here, :]), NT)
    sums[STACK:, :] = dot_stacked(u_taps, (p_hi[here, :], p_lo[here, :]), NT)


def second_kernel_body(
    mode_x, recv, fwd1, fwd2, back2, back1, to_z, from_z,
    out, sums,
    field, hidden, grad, modes, rows6, weights, work, slope,
    u_taps, h_hi, h_lo, l_taps, p_hi, p_lo,
):
    back_z = (from_z[0], from_z[1])
    for k in range(PLANES):
        modes[k, 0:32, :] = gather_modes(recv, 0, k, 0, 32)
        modes[k, 32:40, :] = gather_modes(recv, 1, k, 24, 8)
    flat = dot_stacked(stacked(modes[...].reshape(PLANES * 40, DEPTH)), back_z)
    modes[...] = flat.reshape(PLANES, 40, DEPTH)
    for x, value in enumerate(mixed([modes[k] for k in range(PLANES)], mode_x.T)):
        field[x, 0:40, :] = value
        field[x, 40:48, :] = jnp.zeros((8, DEPTH), jnp.float32)
    for k in range(PLANES):
        grad[k] = gather_modes(recv, 1, k, 0, 24)
    flat = dot_stacked(stacked(grad[...].reshape(PLANES * 24, DEPTH)), back_z)
    flat = flat.reshape(PLANES, 24, DEPTH)
    for x, value in enumerate(mixed([flat[k] for k in range(PLANES)], mode_x.T)):
        grad[x] = value
    network(field, fwd1, fwd2, hidden, weights, u_taps, h_hi, h_lo, work)
    pullback(
        field, grad, hidden, weights, back2, back1, l_taps, p_hi, p_lo, work, slope
    )
    kernel_sums(u_taps, h_hi, h_lo, l_taps, p_hi, p_lo, sums)
    for k, value in enumerate(mixed([slope[x, 0:40, :] for x in range(PLANES)], mode_x)):
        modes[k] = value
    flat = dot_stacked(stacked(modes[...].reshape(PLANES * 40, DEPTH)), (to_z[0], to_z[1]))
    modes[...] = flat.reshape(PLANES, 40, DEPTH)
    for h in range(2):
        for k in range(PLANES):
            for m in range(3):
                rows6[h, k, m * 6 : m * 6 + 6, :] = modes[k, m * REACH + 6 * h : m * REACH + 6 * h + 6, :]
            rows6[h, k, 18:24, :] = jnp.zeros((6, DEPTH), jnp.float32)
    scatter_modes(lambda h, k: rows6[h, k], 24, out)


def third_kernel_body(
    mode_x, recv, field, hidden, weights, back2, back1, from_z, old_sums,
    spread_t, mask, lift, count,
    out,
    grad, modes, u_taps, h_hi, h_lo, l_taps, p_hi, p_lo, work, slope, sums, pieces,
):
    back_z = (from_z[0], from_z[1])
    for h in range(2):
        for k in range(PLANES):
            modes[k] = gather_modes(recv, h, k, 0, 16)
        flat = dot_stacked(stacked(modes[...].reshape(PLANES * 16, DEPTH)), back_z)
        modes[...] = flat.reshape(PLANES, 16, DEPTH)
        for x, value in enumerate(mixed([modes[k] for k in range(PLANES)], mode_x.T)):
            for m in range(3):
                grad[x, m * SLAB + 4 * h : m * SLAB + 4 * h + 4, :] = value[m * 4 : m * 4 + 4, :]
    stack_field(field, u_taps)
    stack_planes(hidden[...], 0, -1, h_hi, h_lo)
    finish_planes(h_hi, h_lo)
    pullback(field, grad, hidden, weights, back2, back1, l_taps, p_hi, p_lo, work, slope)
    kernel_sums(u_taps, h_hi, h_lo, l_taps, p_hi, p_lo, sums)
    sums[...] += old_sums[...]
    for x in range(PLANES):
        out[x, 0:40, :] = slope[x, 0:40, :]
        out[x, 36:40, :] = jnp.zeros((4, DEPTH), jnp.float32)
    pack_grads(sums, spread_t, mask, lift, count, pieces)
    for x in range(PLANES):
        out[x, 40:72, :] = pieces[96:128, :]


def pack_grads(sums, spread_t, mask, lift, count, pieces):
    pieces[...] = jnp.zeros_like(pieces)
    whole = split(sums[...])
    for b in range(3):
        rows = dot(spread_t[...], whole[0] * mask[b]) + dot(spread_t[...], whole[1] * mask[b])
        parts = split(rows)
        pieces[0:96, :] = dot(parts[0], lift[...]) + dot(parts[1], lift[...])
        for c in range(3):
            slot = b * 3 + c
            if slot < 8:
                pieces[96:123, :] += turn(pieces[c * 27 : c * 27 + 27, :], 16 * slot)
            else:
                for part in range(7):
                    first = c * 27 + part * 4
                    count_rows = min(4, c * 27 + 27 - first)
                    pieces[123 : 123 + count_rows, :] += turn(
                        pieces[first : first + count_rows, :], 16 * part
                    )
    parts = split(sums[2 * STACK :, :])
    total = dot(parts[0], lift[...]) + dot(parts[1], lift[...])
    parts = split(sums[4 * LOG : 5 * LOG, 128:BROAD])
    across = ((0,), (0,))
    other = dot(parts[0], count[...], across) + dot(parts[1], count[...], across)
    pieces[127:128, :] = total[0:1, :] + other[HID - 128 : HID - 127, :]


def fold_kernel(recv, main, edge, ext):
    ext[...] = jnp.zeros_like(ext)
    total = None
    for q in range(PLANES):
        for m in range(3):
            ext[m, 8 * q + 6 : 8 * q + 18, :] += recv[q, m * REACH : (m + 1) * REACH, :]
        block = recv[q, 40:72, :]
        total = block if total is None else total + block
    for m in range(3):
        main[m, 0] = ext[m, 8:72, :]
        edge[m * 8 : m * 8 + 2, :] = ext[m, 72:74, :]
        edge[m * 8 + 2 : m * 8 + 4, :] = ext[m, 6:8, :]
        edge[m * 8 + 4 : m * 8 + 8, :] = jnp.zeros((4, DEPTH), jnp.float32)
    edge[24:56, :] = total


def last_kernel(main, edge, other, out, first, end1, second, end2, turned):
    for m in range(3):
        out[m, 0] = main[m, 0]
        out[m, 0, 0:2, :] += other[m * 8 : m * 8 + 2, :]
        out[m, 0, 62:64, :] += other[m * 8 + 2 : m * 8 + 4, :]
    grads = edge[24:56, :] + other[24:56, :]
    for slot in range(8):
        turned[slot] = turn(grads, -16 * slot)
    for b in range(3):
        for a in range(3):
            for e in range(3):
                for i in range(9):
                    row = (a * 3 + e) * 6 + i if i < 6 else 54 + (a * 3 + e) * 3 + i - 6
                    slot, inner = b * 3 + row // 27, row % 27
                    if slot == 8:
                        slot, inner = inner // 4, 27 + inner % 4
                    line = turned[slot, inner, 0:16]
                    if i < 6:
                        second[i * 9 + a * 3 + b, e, :] = line
                    else:
                        first[(i - 6) * 9 + a * 3 + b, e, :] = line
    end1[...] = turned[0, 31:32, 0:16]
    end2[...] = turned[1, 31:32, 0:6]


def slab_device(velocity, cotangent, first_kernel, first_bias, second_kernel, second_bias):
    c = constants()
    mode_x = c["mode_x"]
    half = jnp.bfloat16
    f32 = lambda *dims: pltpu.VMEM(dims, jnp.float32)
    b16 = lambda *dims: pltpu.VMEM(dims, half)
    swap = [(0, 1), (1, 0)]

    other = lax.ppermute(velocity, "py", swap)
    packed = call(
        pack_kernel, shape(PLANES, 64, DEPTH), (velocity, cotangent), [f32(3, 80, DEPTH)], room=4
    )
    packed = call(rim_kernel, shape(PLANES, 64, DEPTH), (packed, other), room=4)
    recv = lax.all_to_all(packed, "px", 0, 0)

    fwd2, fwd1, back2, back1, to_z = call(
        weights_kernel,
        [
            shape(288, DEEP, kind=half),
            shape(2 * HID, TALL, kind=half),
            shape(2 * HID, STACK, kind=half),
            shape(288, DEEP, kind=half),
            shape(2, DEPTH, DEPTH, kind=half),
        ],
        (
            jnp.transpose(first_kernel, (1, 2, 3, 4, 0)).reshape(27, 3, CHANNELS),
            jnp.transpose(second_kernel, (0, 2, 3, 4, 1)).reshape(54, 3, CHANNELS),
            first_bias.reshape(1, CHANNELS),
            second_bias.reshape(1, COEFFS),
            c["to_z"],
        ),
        [
            f32(3, 96, CHANNELS),
            f32(27, 3, CHANNELS),
            f32(54, 3, CHANNELS),
            f32(1, CHANNELS),
            f32(1, COEFFS),
            pltpu.SemaphoreType.DMA((4,)),
        ],
        away=(0, 1, 2, 3),
    )

    near = lambda rows: [b16(rows, FLAT), b16(rows, FLAT)]
    stacks = near(2 * TALL)[:1] + near(DEEP) + near(2 * STACK)[:1] + near(DEEP)
    sent, hidden, weights = call(
        functools.partial(first_kernel_body, mode_x),
        [shape(16, 24, DEPTH), shape(HID, FLAT), shape(LOG, FLAT)],
        (recv, fwd1, fwd2, to_z),
        near(2 * TALL)[:1] + near(DEEP) + [f32(144, FLAT), f32(2, PLANES, 24, DEPTH)],
    )
    both = ("px", "py")
    moved_modes = lax.all_to_all(sent, both, 0, 0)
    moved_modes = call(both_kernel, shape(16, 32, DEPTH), (moved_modes, c["both_in"], c["both_out"]))
    moved_modes = lax.all_to_all(moved_modes, both, 0, 0)

    sent, sums = call(
        functools.partial(second_kernel_body, mode_x),
        [shape(16, 24, DEPTH), shape(STACK + TALL, BROAD)],
        (moved_modes, fwd1, fwd2, back2, back1, to_z, c["from_z"]),
        [
            f32(PLANES, 48, DEPTH),
            f32(HID, FLAT),
            f32(PLANES, 24, DEPTH),
            f32(PLANES, 40, DEPTH),
            f32(2, PLANES, 24, DEPTH),
            f32(LOG, FLAT),
            f32(144, FLAT),
            f32(PLANES, 48, DEPTH),
        ]
        + stacks,
    )
    moved_modes = lax.all_to_all(sent, both, 0, 0)
    moved_modes = call(one_kernel, shape(16, 16, DEPTH), (moved_modes, c["one_in"], c["one_out"]))
    moved_modes = lax.all_to_all(moved_modes, both, 0, 0)

    sent = call(
        functools.partial(third_kernel_body, mode_x),
        shape(PLANES, 72, DEPTH),
        (
            moved_modes, recv, hidden, weights, back2, back1, c["from_z"], sums,
            c["spread_t"], c["mask"], c["lift"], c["count"],
        ),
        [f32(PLANES, 24, DEPTH), f32(PLANES, 16, DEPTH)]
        + stacks
        + [
            f32(144, FLAT),
            f32(PLANES, 48, DEPTH),
            f32(STACK + TALL, BROAD),
            f32(128, DEPTH),
        ],
    )
    recv = lax.all_to_all(sent, "px", 0, 0)
    main, edge = call(
        fold_kernel, [shape(3, 1, 64, DEPTH), shape(56, DEPTH)], (recv,), [f32(3, 80, DEPTH)]
    )
    other = lax.ppermute(edge, "py", swap)
    grad_velocity, first, end1, second, end2 = call(
        last_kernel,
        [
            shape(3, 1, 64, DEPTH),
            shape(27, 3, CHANNELS),
            shape(1, CHANNELS),
            shape(54, 3, CHANNELS),
            shape(1, COEFFS),
        ],
        (main, edge, other),
        [f32(8, 32, DEPTH)],
    )
    return (
        grad_velocity,
        jnp.transpose(first.reshape(3, 3, 3, 3, CHANNELS), (4, 0, 1, 2, 3)),
        end1.reshape(CHANNELS),
        jnp.transpose(second.reshape(COEFFS, 3, 3, 3, CHANNELS), (0, 4, 1, 2, 3)),
        end2.reshape(COEFFS),
    )


def fits_slabs(mesh):
    return mesh.shape["px"] == PLANES and mesh.shape["py"] == 2


def solution(mesh):
    return jax.shard_map(
        slab_device if fits_slabs(mesh) else on_device,
        mesh=mesh,
        in_specs=(
            P(None, ("groups", "px"), "py", None),
            P(None, ("groups", "px"), "py", None),
            P(),
            P(),
            P(),
            P(),
        ),
        out_specs=(
            P(None, ("groups", "px"), "py", None),
            P("groups", None, None, None, None),
            P("groups"),
            P("groups", None, None, None, None),
            P("groups"),
        ),
        check_vma=False,
    )
```

```python
import functools
import math

import jax
import jax.numpy as jnp
import numpy as np
from jax import lax
from jax.experimental import pallas as pl
from jax.experimental.pallas import tpu as pltpu
from jax.sharding import PartitionSpec as P

ITERS = 2


KAPPA = 0.25


def padded_2(value, sides, width):
    for axis, dim in sides:
        size, length = (lax.axis_size(axis), value.shape[dim])
        up = [(i, (i + 1) % size) for i in range(size)]
        down = [(j, i) for i, j in up]
        last = lax.slice_in_dim(value, length - width, length, axis=dim)
        initial = lax.slice_in_dim(value, 0, width, axis=dim)
        before = lax.ppermute(last, axis, up)
        after = lax.ppermute(initial, axis, down)
        value = jnp.concatenate([before, value, after], axis=dim)
    return value


def extend(field):
    rimmed = padded_2(field, (("px", 1), ("py", 2)), 1)
    return jnp.concatenate([rimmed[..., -1:], rimmed, rimmed[..., :1]], axis=3)


def across_columns(spectrum):
    return lax.all_to_all(spectrum, "px", split_axis=2, concat_axis=4, tiled=True)


def across_pairs(spectrum):
    return lax.all_to_all(spectrum, "py", split_axis=3, concat_axis=4, tiled=True)


def summed(grads):
    return lax.psum((grads[0], grads[1], grads[2], grads[3]), ("px", "py"))


def all_taps():
    return [
        (shift_x, shift_y, shift_z)
        for shift_x in range(3)
        for shift_y in range(3)
        for shift_z in range(3)
    ]


def gather_conv(padded, kernel):
    size_x = padded.shape[1] - 2
    size_y = padded.shape[2] - 2
    size_z = padded.shape[3] - 2
    stacked = jnp.concatenate(
        [
            padded[:, sx_one : sx_one + size_x, sy_one : sy_one + size_y, sz_one : sz_one + size_z]
            for sx_one, sy_one, sz_one in all_taps()
        ],
        axis=0,
    )
    matrix = jnp.transpose(kernel, (0, 2, 3, 4, 1)).reshape(kernel.shape[0], -1)
    result = jnp.einsum("ok,kxyz->oxyz", matrix, stacked, precision=lax.Precision.HIGHEST)
    return (result, stacked)


def scatter_conv(padded, kernel):
    outputs = kernel.shape[0]
    inputs = kernel.shape[1]
    size_x = padded.shape[1] - 2
    size_y = padded.shape[2] - 2
    size_z = padded.shape[3] - 2
    total = jnp.zeros((outputs, size_x, size_y, size_z), jnp.float32)
    for shift_x in range(3):
        matrix = jnp.transpose(kernel[:, :, shift_x], (0, 2, 3, 1)).reshape(outputs * 9, inputs)
        layer = jnp.einsum(
            "km,mxyz->kxyz",
            matrix,
            padded[:, shift_x : shift_x + size_x],
            precision=lax.Precision.HIGHEST,
        )
        layer = layer.reshape(outputs, 3, 3, size_x, size_y + 2, size_z + 2)
        for shift_y in range(3):
            for shift_z in range(3):
                total = (
                    total
                    + layer[
                        :,
                        shift_y,
                        shift_z,
                        :,
                        shift_y : shift_y + size_y,
                        shift_z : shift_z + size_z,
                    ]
                )
    return total


def flipped(kernel):
    return jnp.transpose(kernel[:, :, ::-1, ::-1, ::-1], (1, 0, 2, 3, 4))


def moved(padded, axis_dim, offset_cells):
    index = [slice(None), slice(1, -1), slice(1, -1), slice(1, -1)]
    index[axis_dim] = slice(1 + offset_cells, padded.shape[axis_dim] - 1 + offset_cells)
    return padded[tuple(index)]


def advect(padded, weights):
    center = moved(padded, 1, 0)
    total = jnp.zeros_like(center)
    for direction in range(3):
        ahead = moved(padded, direction + 1, 1)
        behind = moved(padded, direction + 1, -1)
        vplus = 0.5 * (center[direction] + ahead[direction])
        vminus = 0.5 * (behind[direction] + center[direction])
        upper = center + weights[2 * direction] * (ahead - center)
        lower = center + weights[2 * direction + 1] * (behind - center)
        total = total + vplus * upper - vminus * lower
    return total


def advect_back(padded, weights_pad, source_pad):
    center = moved(padded, 1, 0)
    source = moved(source_pad, 1, 0)
    weights = moved(weights_pad, 1, 0)
    grad_field = jnp.zeros_like(center)
    fluxes = []
    parts = []
    for direction in range(3):
        ahead = moved(padded, direction + 1, 1)
        behind = moved(padded, direction + 1, -1)
        vplus = 0.5 * (center[direction] + ahead[direction])
        vminus = 0.5 * (behind[direction] + center[direction])
        rate_up = weights[2 * direction]
        rate_low = weights[2 * direction + 1]
        rate_before = moved(weights_pad[2 * direction : 2 * direction + 1], direction + 1, -1)[0]
        rate_after = moved(weights_pad[2 * direction + 1 : 2 * direction + 2], direction + 1, 1)[0]
        source_before = moved(source_pad, direction + 1, -1)
        source_after = moved(source_pad, direction + 1, 1)
        upper = center + rate_up * (ahead - center)
        lower = center + rate_low * (behind - center)
        upper_before = behind + rate_before * (center - behind)
        lower_after = ahead + rate_after * (center - ahead)
        grad_field = grad_field + source * (vplus * (1.0 - rate_up) - vminus * (1.0 - rate_low))
        grad_field = (
            grad_field + vminus * rate_before * source_before - vplus * rate_after * source_after
        )
        fluxes.append(
            0.5
            * (
                jnp.sum(source * upper, 0)
                - jnp.sum(source * lower, 0)
                + jnp.sum(source_before * upper_before, 0)
                - jnp.sum(source_after * lower_after, 0)
            )
        )
        parts.append(jnp.sum(source * vplus * (ahead - center), 0))
        parts.append(-jnp.sum(source * vminus * (behind - center), 0))
    return (grad_field + jnp.stack(fluxes), jnp.stack(parts))


def tables(count):
    index = jnp.arange(count, dtype=jnp.int32)
    phase = index[:, None] * index[None, :] % count
    angle = phase.astype(jnp.float32) * (2.0 * math.pi / count)
    return (jnp.cos(angle), jnp.sin(angle))


def mix(form, data, table):
    return jnp.einsum(form, data, table, precision=lax.Precision.HIGHEST)


def waves(start, count, total):
    index = start + jnp.arange(count, dtype=jnp.int32)
    return jnp.where(index < total // 2, index, index - total).astype(jnp.float32)


def project(field):
    depth = field.shape[3]
    cos_z, sin_z = tables(depth)
    real_z = mix("cxyz,zk->cxky", field, cos_z)
    imag_z = -mix("cxyz,zk->cxky", field, sin_z)
    spectrum = across_pairs(jnp.stack([real_z, imag_z]))
    span_y = spectrum.shape[4]
    cos_y, sin_y = tables(span_y)
    real_y = mix("cxky,yq->cqkx", spectrum[0], cos_y) + mix("cxky,yq->cqkx", spectrum[1], sin_y)
    imag_y = mix("cxky,yq->cqkx", spectrum[1], cos_y) - mix("cxky,yq->cqkx", spectrum[0], sin_y)
    spectrum = across_columns(jnp.stack([real_y, imag_y]))
    span_x = spectrum.shape[4]
    cos_x, sin_x = tables(span_x)
    real_x = mix("cqkx,xp->cqkp", spectrum[0], cos_x) + mix("cqkx,xp->cqkp", spectrum[1], sin_x)
    imag_x = mix("cqkx,xp->cqkp", spectrum[1], cos_x) - mix("cqkx,xp->cqkp", spectrum[0], sin_x)
    rows_y = spectrum.shape[2]
    rows_z = spectrum.shape[3]
    wave_y = waves(lax.axis_index("px") * rows_y, rows_y, span_y)[:, None, None]
    wave_z = waves(lax.axis_index("py") * rows_z, rows_z, depth)[None, :, None]
    wave_x = waves(0, span_x, span_x)[None, None, :]
    size = jnp.maximum(wave_x * wave_x + wave_y * wave_y + wave_z * wave_z, 1.0)
    vectors = jnp.stack(jnp.broadcast_arrays(wave_x, wave_y, wave_z))
    real_x = real_x - vectors * (
        (wave_x * real_x[0] + wave_y * real_x[1] + wave_z * real_x[2]) / size
    )
    imag_x = imag_x - vectors * (
        (wave_x * imag_x[0] + wave_y * imag_x[1] + wave_z * imag_x[2]) / size
    )
    back_real = (mix("cqkp,px->cxkq", real_x, cos_x) - mix("cqkp,px->cxkq", imag_x, sin_x)) / span_x
    back_imag = (mix("cqkp,px->cxkq", imag_x, cos_x) + mix("cqkp,px->cxkq", real_x, sin_x)) / span_x
    spectrum = across_columns(jnp.stack([back_real, back_imag]))
    rows_real = (
        mix("cxkq,qy->cxyk", spectrum[0], cos_y) - mix("cxkq,qy->cxyk", spectrum[1], sin_y)
    ) / span_y
    rows_imag = (
        mix("cxkq,qy->cxyk", spectrum[1], cos_y) + mix("cxkq,qy->cxyk", spectrum[0], sin_y)
    ) / span_y
    spectrum = across_pairs(jnp.stack([rows_real, rows_imag]))
    return (
        mix("cxyk,kz->cxyz", spectrum[0], cos_z) - mix("cxyk,kz->cxyz", spectrum[1], sin_z)
    ) / depth


def forward_state(field, first_kernel, first_bias, second_kernel, second_bias):
    padded = extend(field)
    first_out, field_taps = gather_conv(padded, first_kernel)
    hidden = jnp.tanh(first_out + first_bias[:, None, None, None])
    weights = jax.nn.sigmoid(
        scatter_conv(extend(hidden), second_kernel) + second_bias[:, None, None, None]
    )
    return (padded, hidden, weights, field_taps)


def backward_step(state, upstream, first_kernel, second_kernel):
    padded, hidden, weights, field_taps = state
    moved_grad = project(upstream)
    source = -KAPPA * moved_grad
    stacked = extend(jnp.concatenate([source, weights], axis=0))
    grad_field, grad_weights = advect_back(padded, stacked[3:], stacked[:3])
    grad_field = grad_field + moved_grad
    grad_logits = grad_weights * weights * (1.0 - weights)
    logits_pad = extend(grad_logits)
    grad_hidden, logit_taps = gather_conv(logits_pad, flipped(second_kernel))
    product = jnp.einsum("kxyz,mxyz->km", logit_taps, hidden, precision=lax.Precision.HIGHEST)
    product = product.reshape(3, 3, 3, second_kernel.shape[0], second_kernel.shape[1])
    grad_second = jnp.transpose(product[::-1, ::-1, ::-1], (3, 4, 0, 1, 2))
    grad_second_bias = jnp.sum(grad_logits, axis=(1, 2, 3))
    grad_pre = grad_hidden * (1.0 - hidden * hidden)
    pre_pad = extend(grad_pre)
    grad_field = grad_field + scatter_conv(pre_pad, flipped(first_kernel))
    first_product = jnp.einsum(
        "oxyz,kxyz->ok", grad_pre, field_taps, precision=lax.Precision.HIGHEST
    )
    first_product = first_product.reshape(first_kernel.shape[0], 3, 3, 3, first_kernel.shape[1])
    grad_first = jnp.transpose(first_product, (0, 4, 1, 2, 3))
    grad_first_bias = jnp.sum(grad_pre, axis=(1, 2, 3))
    return (grad_field, (grad_first, grad_first_bias, grad_second, grad_second_bias))


def on_device(velocity, cotangent, first_kernel, first_bias, second_kernel, second_bias):
    field = velocity
    fields = [velocity]
    saved = []
    for section in range(ITERS):
        state = forward_state(field, first_kernel, first_bias, second_kernel, second_bias)
        saved.append(state)
        field = project(field - KAPPA * advect(state[0], state[2]))
        fields.append(field)
    upstream = cotangent
    totals = None
    for section in reversed(range(ITERS)):
        state = saved[section]
        upstream, grads = backward_step(state, upstream, first_kernel, second_kernel)
        grads = summed(grads)
        if totals is None:
            totals = grads
        else:
            totals = tuple((older + newer for older, newer in zip(totals, grads)))
    return (upstream, totals[0], totals[1], totals[2], totals[3])


SLAB = 8
RIM = 2
REACH = SLAB + 2 * RIM
WIDE = SLAB + 2
PLANES = 8
DEPTH = 128
ROWS = 128
CHANNELS = 16
COEFFS = 6
BAND = 32
HID = CHANNELS * WIDE
LOG = COEFFS * SLAB
STACK = 9 * 48
UNIT = 36
DEEP = 3 * HID + 16
PLACE = (0, 2, 1)
FLAT = PLANES * DEPTH
NN = ((1,), (0,))
NT = ((1,), (1,))


def real_basis(count):
    half = count // 2
    angle = 2.0 * np.pi * np.arange(count) / count
    rows = [np.full(count, 1.0 / np.sqrt(count))]
    rows += [np.sqrt(2.0 / count) * np.cos(k * angle) for k in range(1, half)]
    rows += [np.cos(half * angle) / np.sqrt(count)]
    rows += [np.sqrt(2.0 / count) * np.sin(k * angle) for k in range(1, half)]
    return np.stack(rows)


def stacked_table(table):
    return np.concatenate(halves(table))


def halves(table):
    high = table.astype(np.float32).astype(jnp.bfloat16)
    low = (table - high.astype(np.float64)).astype(np.float32).astype(jnp.bfloat16)
    return high, low


def slab_of(device):
    return (device % 2) * PLANES + device // 2


@functools.cache
def constants():
    basis_x = real_basis(PLANES)
    mode_x = np.stack([basis_x[(k // 2) + (PLANES // 2) * (k % 2)] for k in range(PLANES)])
    basis_z = real_basis(DEPTH)
    order = []
    for group in range(4):
        order += [16 * group + i for i in range(16)] + [64 + 16 * group + i for i in range(16)]
    mode_z = basis_z[order]
    basis_y = real_basis(ROWS)

    def rows(offset, count):
        at = [SLAB * slab_of(j) + offset + i for j in range(16) for i in range(count)]
        return basis_y[:, np.array(at) % ROWS]

    own, half_one, half_two = rows(0, SLAB), rows(0, 4), rows(4, 4)
    before, after = rows(-RIM, RIM), rows(SLAB, RIM)
    both_in = own
    both_out = np.concatenate([own, before, after], axis=1).T
    one_in = np.concatenate(
        [np.concatenate([half_one, before], axis=1), np.concatenate([half_two, after], axis=1)]
    )
    one_out = np.concatenate([half_one, half_two], axis=1).T

    spread = np.zeros((288, 32))
    mask = np.zeros((3, 288, DEEP))
    lanes = np.arange(CHANNELS) * WIDE
    for e in range(3):
        for o in range(COEFFS):
            for q in range(SLAB):
                row = e * 48 + o * SLAB + q
                spread[row, e * COEFFS + o] = 1.0
                for b in range(3):
                    for a in range(3):
                        mask[b, row, a * HID + lanes + q + b] = 1.0
        for m in range(3):
            for r in range(REACH):
                row = 144 + e * 48 + m * REACH + r
                spread[row, 18 + e * 3 + m] = 1.0
                for b in range(3):
                    for a in range(3):
                        if 0 <= r - b < WIDE:
                            mask[b, row, a * HID + lanes + r - b] = 1.0
    spread[144 + 48 + UNIT, 27] = 1.0
    mask[0, 144 + 48 + UNIT, PLACE[1] * HID : (PLACE[1] + 1) * HID] = 1.0
    mask[0, 48:96, 3 * HID] = 1.0
    lift = np.zeros((3, 512, 256))
    for b in range(3):
        for a in range(3):
            lift[b, PLACE[a] * HID + np.arange(HID), 16 * (3 * b + a) + np.arange(HID) // WIDE] = 1.0
    lift[0, 3 * HID, 128 + 64] = 1.0
    lift = lift.reshape(3 * 512, 256)
    half = jnp.bfloat16
    return dict(
        mode_x=mode_x,
        to_z=np.stack(halves(mode_z.T)),
        from_z=np.stack(halves(mode_z)),
        both_in=stacked_table(both_in),
        both_out=stacked_table(both_out),
        one_in=stacked_table(one_in),
        one_out=stacked_table(one_out),
        spread_t=np.ascontiguousarray(spread.T).astype(half),
        mask=mask.astype(half),
        lift=lift.astype(half),
    )


def dot(left, right, dims=NN):
    return lax.dot_general(left, right, (dims, ((), ())), preferred_element_type=jnp.float32)


def split(value):
    high = value.astype(jnp.bfloat16)
    return high, (value - high.astype(jnp.float32)).astype(jnp.bfloat16)


def dot_stacked(left, right, dims=NN):
    rows = left.shape[0] // 2
    main = dot(left[...], right[0], dims)
    return main[:rows] + (main[rows:] + dot(left[0:rows, :], right[1], dims))


def stacked(value):
    return jnp.concatenate(split(value), axis=0)


def turn(value, shift):
    shift = shift % value.shape[-1]
    return value if shift == 0 else pltpu.roll(value, shift, value.ndim - 1)


def plane(x):
    x = x % PLANES
    return slice(x * DEPTH, (x + 1) * DEPTH)


def call(kernel, outs, args, scratch=(), room=16, away=()):
    single = not isinstance(outs, (list, tuple))
    vmem = pl.BlockSpec(memory_space=pltpu.VMEM)
    cost = pl.CostEstimate(flops=1, bytes_accessed=1, transcendentals=0) if away else None
    return pl.pallas_call(
        kernel,
        out_shape=outs,
        in_specs=[
            pl.BlockSpec(memory_space=pltpu.HBM) if i in away else vmem for i in range(len(args))
        ],
        out_specs=vmem if single else [vmem] * len(outs),
        scratch_shapes=list(scratch),
        cost_estimate=cost,
        compiler_params=pltpu.CompilerParams(vmem_limit_bytes=room * 2**20),
    )(*args)


def fetch(pairs, sems):
    copies = [pltpu.make_async_copy(src, dst, sems.at[i]) for i, (src, dst) in enumerate(pairs)]
    for copy in copies:
        copy.start()
    return copies


def shape(*dims, kind=jnp.float32):
    return jax.ShapeDtypeStruct(dims, kind)


def counting(size, dim):
    return lax.broadcasted_iota(jnp.int32, size, dim).astype(jnp.float32)


def remainder(value, count):
    return value - count * jnp.floor((value + 0.5) / count)


def band_tables(tall):
    row, col = (0, 1) if tall else (1, 0)
    size = lambda rows, cols: (rows, cols) if tall else (cols, rows)
    where = counting(size(2 * STACK, 96), row)
    to = counting(size(2 * STACK, 96), col)
    first = where - 8.0 * to
    third = to - 54.0
    second = where - STACK - (16.0 * third - 4.0 * remainder(third, 3.0))
    picks = ((to < 54.0) & (first >= 0.0) & (first < 8.0)) | (
        (to >= 54.0) & (to < 81.0) & (second >= 0.0) & (second < 12.0)
    )
    where = counting(size(2 * STACK, HID), row)
    inner = remainder(counting(size(2 * STACK, HID), col), 10.0)
    outer = where - STACK
    offset = jnp.where(
        where < STACK,
        inner - remainder(where, 8.0),
        remainder(remainder(outer, 48.0), 12.0) - inner,
    )
    gap = counting(size(HID, CHANNELS), row) - 10.0 * counting(size(HID, CHANNELS), col)
    lift = (gap >= 0.0) & (gap < 10.0)
    half = jnp.bfloat16
    return picks.astype(jnp.float32).astype(half), offset, lift.astype(jnp.float32).astype(half)


def weights_kernel(
    far1, far2, far3, far4, z_in, fwd2, fwd1, back2, back1, z_out, blocks, taps1, taps2, bias1, bias2, sems
):
    copies = fetch([(far1, taps1), (far2, taps2), (far3, bias1), (far4, bias2)], sems)
    blocks[...] = jnp.zeros_like(blocks)
    z_out[...] = z_in[...]
    spread, offset, lift = band_tables(True)
    spread_t, offset_t, lift_t = band_tables(False)
    for copy in copies:
        copy.wait()
    for b in range(3):
        for a in range(3):
            for e in range(3):
                tap = a * 3 + e
                for o in range(COEFFS):
                    blocks[b, tap * 6 + o, :] = taps2[o * 9 + a * 3 + b, e, :]
                for m in range(3):
                    blocks[b, 54 + tap * 3 + m, :] = taps1[m * 9 + a * 3 + b, e, :]
    tall = [jnp.zeros((2 * STACK, HID), jnp.float32)] * 2
    flat = [jnp.zeros((HID, 2 * STACK), jnp.float32)] * 2
    for b in range(3):
        for half, block in enumerate(split(blocks[b])):
            rows = dot(spread, block).astype(jnp.bfloat16)
            tall[half] = jnp.where(offset == float(b), dot(rows, lift_t), tall[half])
            cols = dot(lift, block, NT).astype(jnp.bfloat16)
            flat[half] = jnp.where(offset_t == float(b), dot(cols, spread_t), flat[half])
    for half in range(2):
        rows, cols = slice(half * 144, half * 144 + 144), slice(half * HID, half * HID + HID)
        for a in range(3):
            first = PLACE[a] * HID
            part = tall[half][a * 144 : a * 144 + 144]
            fwd2[rows, first : first + HID] = part.astype(jnp.bfloat16)
            part = tall[half][STACK + a * 144 : STACK + a * 144 + 144]
            back1[rows, first : first + HID] = part.astype(jnp.bfloat16)
        back2[cols, :] = flat[half][:, :STACK].astype(jnp.bfloat16)
    gap = counting((LOG, COEFFS), 0) - 8.0 * counting((LOG, COEFFS), 1)
    pick = ((gap >= 0.0) & (gap < 8.0)).astype(jnp.float32).astype(jnp.bfloat16)
    second = counting((LOG, 16), 1) < 1.0
    one = split(jnp.broadcast_to(bias1[...], (STACK, CHANNELS)))
    first = counting((HID, STACK), 1) == 4.0 * 48.0 + UNIT
    two = split(jnp.broadcast_to(bias2[...], (16, COEFFS)))
    fwd2[:, 3 * HID :] = jnp.zeros((288, 16), jnp.bfloat16)
    back1[:, 3 * HID :] = jnp.zeros((288, 16), jnp.bfloat16)
    for half in range(2):
        value = jnp.where(first, dot(lift, one[half], NT), flat[half][:, STACK:])
        fwd1[half * HID : half * HID + HID, :] = value.astype(jnp.bfloat16)
        value = jnp.where(second, dot(pick, two[half], NT), 0.0)
        start = half * 144 + LOG
        fwd2[start : start + LOG, 3 * HID :] = value.astype(jnp.bfloat16)


def pack_kernel(field, cot, out, ext):
    ext[...] = jnp.zeros_like(ext)
    for m in range(3):
        ext[m, 8:72, :] = field[m, 0]
    for q in range(PLANES):
        for m in range(3):
            out[q, m * REACH : (m + 1) * REACH, :] = ext[m, 8 * q + 6 : 8 * q + 18, :]
            out[q, 40 + 8 * m : 48 + 8 * m, :] = cot[m, 0, 8 * q : 8 * q + 8, :]
        out[q, 36:37, :] = jnp.ones((1, DEPTH), jnp.float32)
        out[q, 37:40, :] = jnp.zeros((3, DEPTH), jnp.float32)


def rim_kernel(packed, other, out):
    out[...] = packed[...]
    for m in range(3):
        out[0, m * REACH : m * REACH + 2, :] = other[m, 0, 62:64, :]
        out[PLANES - 1, m * REACH + 10 : m * REACH + 12, :] = other[m, 0, 0:2, :]


def unit_row():
    row = lax.broadcasted_iota(jnp.int32, (16, FLAT), 0)
    return jnp.where(row == 0, 1.0, 0.0).astype(jnp.bfloat16)


def stack_planes(value, first, sign, high, low):
    parts = split(value)
    for i in range(value.shape[1] // DEPTH):
        for a in range(3):
            rows = slice(PLACE[a] * HID, PLACE[a] * HID + HID)
            to = plane(first + i + sign * (a - 1))
            high[rows, to] = parts[0][:, i * DEPTH : (i + 1) * DEPTH]
            low[rows, to] = parts[1][:, i * DEPTH : (i + 1) * DEPTH]


def finish_planes(high, low):
    high[3 * HID :, :] = unit_row()
    low[3 * HID :, :] = jnp.zeros((16, FLAT), jnp.bfloat16)


def stack_logits(whole, x, l_taps):
    for e in range(3):
        parts = split(turn(whole, e - 1))
        for a in range(3):
            for half in range(2):
                first = half * STACK + (a * 3 + e) * 48
                l_taps[first : first + 48, plane(x + a - 1)] = parts[half]


def stack_field(field, taps):
    for x in range(PLANES):
        whole = field[x, 0:48, :]
        for e in range(3):
            parts = split(turn(whole, 1 - e))
            for a in range(3):
                rows = slice((a * 3 + e) * 48, (a * 3 + e) * 48 + 48)
                taps[rows, plane(x - a + 1)] = parts[0]
                taps[STACK + rows.start : STACK + rows.stop, plane(x - a + 1)] = parts[1]


def network(field, fwd1, fwd2, hidden, weights, u_taps, h_hi, h_lo, work):
    stack_field(field, u_taps)
    finish_planes(h_hi, h_lo)
    for pair in range(4):
        cut = slice(pair * 256, pair * 256 + 256)
        value = jnp.tanh(dot_stacked(fwd1, (u_taps[0:STACK, cut], u_taps[STACK:, cut])))
        hidden[:, cut] = value
        stack_planes(value, 2 * pair, -1, h_hi, h_lo)
    for pair in range(4):
        cut = slice(pair * 256, pair * 256 + 256)
        work[:, cut] = dot_stacked(fwd2, (h_hi[:, cut], h_lo[:, cut]))
    for x in range(PLANES):
        total = work[LOG : 2 * LOG, plane(x)]
        total = total + turn(work[0:LOG, plane(x)], 1) + turn(work[2 * LOG : 3 * LOG, plane(x)], -1)
        weights[:, plane(x)] = jax.nn.sigmoid(total)


def around(field, x, direction, sign):
    if direction == 0:
        return [field[(x + sign) % PLANES, m * REACH + RIM : m * REACH + RIM + SLAB, :] for m in range(3)]
    if direction == 1:
        first = RIM + sign
        return [field[x, m * REACH + first : m * REACH + first + SLAB, :] for m in range(3)]
    return [turn(field[x, m * REACH + RIM : m * REACH + RIM + SLAB, :], -sign) for m in range(3)]


def advected(field, weights, x):
    center = around(field, x, 0, 0)
    total = [jnp.zeros((SLAB, DEPTH), jnp.float32)] * 3
    for d in range(3):
        ahead = around(field, x, d, 1)
        behind = around(field, x, d, -1)
        plus = 0.5 * (center[d] + ahead[d])
        minus = 0.5 * (behind[d] + center[d])
        rate_up = weights[2 * d * SLAB : (2 * d + 1) * SLAB, plane(x)]
        rate_low = weights[(2 * d + 1) * SLAB : (2 * d + 2) * SLAB, plane(x)]
        for m in range(3):
            upper = center[m] + rate_up * (ahead[m] - center[m])
            lower = center[m] + rate_low * (behind[m] - center[m])
            total[m] = total[m] + plus * upper - minus * lower
    return [center[m] - KAPPA * total[m] for m in range(3)]


def mixed(values, table):
    outs = []
    for row in table:
        total = None
        for weight, value in zip(row, values):
            term = value * float(weight)
            total = term if total is None else total + term
        outs.append(total)
    return outs


def lane_groups(size):
    return lax.broadcasted_iota(jnp.int32, (size, DEPTH), 1) // BAND


def scatter_modes(source, rows, out):
    groups = lane_groups(rows)
    for p in range(4):
        for g in range(4):
            total = None
            for f in range(2):
                for t in range(2):
                    slot = 2 * f + t
                    value = turn(source(f, 2 * p + t), BAND * (slot - g))
                    total = value if total is None else jnp.where(groups == slot, value, total)
            if len(out.shape) == 3:
                out[p * 4 + g] = total
            else:
                for i in range(out.shape[1]):
                    out[p * 4 + g, i] = total[2 * i : 2 * i + 2]


def gather_modes(recv, f, k, first, rows):
    groups = lane_groups(rows)
    slot = 2 * f + k % 2
    total = None
    for g in range(4):
        value = turn(recv[(k // 2) * 4 + g, first : first + rows, :], BAND * (g - slot))
        total = value if total is None else jnp.where(groups == g, value, total)
    return total


def first_kernel_body(
    mode_x, recv, fwd1, fwd2, to_z, out, hidden, weights, u_taps, h_hi, h_lo, work, modes
):
    network(recv, fwd1, fwd2, hidden, weights, u_taps, h_hi, h_lo, work)
    table = (to_z[0], to_z[1])
    moved_field = [jnp.concatenate(advected(recv, weights, x), axis=0) for x in range(PLANES)]
    for f in range(2):
        planes = moved_field if f == 0 else [recv[x, 40:64, :] for x in range(PLANES)]
        for k, value in enumerate(mixed(planes, mode_x)):
            modes[f, k] = value
    for f in range(2):
        flat = modes[f].reshape(PLANES * 24, DEPTH)
        modes[f] = dot_stacked(stacked(flat), table).reshape(PLANES, 24, DEPTH)
    scatter_modes(lambda f, k: modes[f, k], 24, out)


def leray(parts):
    device = lax.axis_index("px") * 2 + lax.axis_index("py")
    pair = device // 4
    group = device % 4
    lane = lax.broadcasted_iota(jnp.int32, (ROWS, DEPTH), 1)
    row = lax.broadcasted_iota(jnp.int32, (ROWS, DEPTH), 0)
    odd_x = (lane // BAND) % 2
    odd_z = (lane // 16) % 2
    number_z = 16 * group + lane % 16
    top_x = (odd_x == 1) & (pair == 0)
    top_y = row == ROWS // 2
    top_z = (odd_z == 1) & (number_z == 0)
    number_y = row % (ROWS // 2)
    real = lambda value: value.astype(jnp.float32)
    rate_x = real(jnp.where(odd_x == 1, -pair, pair))
    rate_y = real(jnp.where(row < ROWS // 2, number_y, -number_y))
    rate_z = real(jnp.where(odd_z == 1, -number_z, number_z))
    high_x = real(jnp.where(top_x, PLANES // 2, 0))
    high_y = real(jnp.where(top_y, ROWS // 2, 0))
    high_z = real(jnp.where(top_z, DEPTH // 2, 0))
    size = rate_x * rate_x + rate_y * rate_y + rate_z * rate_z
    size = size + high_x * high_x + high_y * high_y + high_z * high_z
    inverse = 1.0 / jnp.maximum(size, 1.0)

    def slope_x(value):
        return rate_x * jnp.where(odd_x == 1, turn(value, BAND), turn(value, -BAND))

    def slope_y(value):
        return rate_y * jnp.concatenate([value[ROWS // 2 :], value[: ROWS // 2]], axis=0)

    def slope_z(value):
        return rate_z * jnp.where(odd_z == 1, turn(value, 16), turn(value, -16))

    spread = (slope_x(parts[0]) + slope_y(parts[1]) + slope_z(parts[2])) * inverse
    high = (high_x * parts[0] + high_y * parts[1] + high_z * parts[2]) * inverse
    return (
        parts[0] + slope_x(spread) - high_x * high,
        parts[1] + slope_y(spread) - high_y * high,
        parts[2] + slope_z(spread) - high_z * high,
    )


def beside(parts):
    return jnp.concatenate(parts, axis=1)


def part(value, m):
    return value[:, m * DEPTH : (m + 1) * DEPTH]


def two_halves(first, second):
    low = lax.broadcasted_iota(jnp.int32, first.shape, 1) < DEPTH // 2
    return jnp.where(low, first, turn(second, DEPTH // 2))


def both_kernel(recv, table_in, table_out, out):
    data = beside([recv[:, 8 * m : 8 * m + 8, :].reshape(ROWS, DEPTH) for m in range(3)])
    modes = dot_stacked(table_in, split(data))
    fixed = beside(leray([part(modes, m) for m in range(3)]))
    back = dot_stacked(table_out, split(fixed))
    for m in range(3):
        whole = part(back, m)
        out[:, 8 * m : 8 * m + 8, :] = whole[:ROWS].reshape(16, SLAB, DEPTH)
        rim = two_halves(whole[ROWS : ROWS + 32], whole[ROWS + 32 :])
        for device in range(16):
            out[device, 24 + 2 * m : 26 + 2 * m, :] = rim[2 * device : 2 * device + 2]
    out[:, 30:32, :] = jnp.zeros((16, 2, DEPTH), jnp.float32)


def one_kernel(recv, table_in, table_out, out, data):
    for device in range(16):
        for m in range(3):
            for i in range(2):
                first = 4 * device + 2 * i
                data[m, first : first + 2, :] = recv[device, 2 * m + i]
            data[m, 64 + 2 * device : 66 + 2 * device, :] = recv[device, 6 + m]
    modes = dot_stacked(table_in, split(beside([data[m] for m in range(3)])))
    low, high = modes[:ROWS], modes[ROWS:]
    fixed = beside(leray([part(low, m) + turn(part(high, m), DEPTH // 2) for m in range(3)]))
    back = dot_stacked(table_out, split(fixed))
    for m in range(3):
        whole = two_halves(part(back, m)[:64], part(back, m)[64:])
        for device in range(16):
            out[device, m] = whole[4 * device : 4 * device + 4]


def pullback(field, grad, hidden, weights, back2, back1, l_taps, p_hi, p_lo, work, slope):
    slope[...] = jnp.zeros_like(slope)
    row = lax.broadcasted_iota(jnp.int32, (SLAB, DEPTH), 0)
    stay = [None] * PLANES
    pushed = {}
    for x in range(PLANES):
        center = around(field, x, 0, 0)
        source = [-KAPPA * grad[x, m * SLAB : (m + 1) * SLAB, :] for m in range(3)]
        own = [grad[x, m * SLAB : (m + 1) * SLAB, :] for m in range(3)]
        logits = []
        for d in range(3):
            ahead = around(field, x, d, 1)
            behind = around(field, x, d, -1)
            plus = 0.5 * (center[d] + ahead[d])
            minus = 0.5 * (behind[d] + center[d])
            rate_up = weights[2 * d * SLAB : (2 * d + 1) * SLAB, plane(x)]
            rate_low = weights[(2 * d + 1) * SLAB : (2 * d + 2) * SLAB, plane(x)]
            grad_up = grad_low = grad_plus = grad_minus = None
            to_ahead, to_behind = [], []
            add = lambda total, term: term if total is None else total + term
            for m in range(3):
                gap_up = ahead[m] - center[m]
                gap_low = behind[m] - center[m]
                grad_plus = add(grad_plus, source[m] * (center[m] + rate_up * gap_up))
                grad_minus = add(grad_minus, -source[m] * (center[m] + rate_low * gap_low))
                grad_up = add(grad_up, source[m] * gap_up)
                grad_low = add(grad_low, -source[m] * gap_low)
                push_up = source[m] * plus
                push_low = -source[m] * minus
                to_ahead.append(push_up * rate_up)
                to_behind.append(push_low * rate_low)
                own[m] = own[m] + (push_up - to_ahead[m]) + (push_low - to_behind[m])
            own[d] = own[d] + 0.5 * (grad_plus + grad_minus)
            to_ahead[d] = to_ahead[d] + 0.5 * grad_plus
            to_behind[d] = to_behind[d] + 0.5 * grad_minus
            logits.append(grad_up * plus * rate_up * (1.0 - rate_up))
            logits.append(grad_low * minus * rate_low * (1.0 - rate_low))
            for m in range(3):
                if d == 0:
                    pushed[x, m, 1], pushed[x, m, -1] = to_ahead[m], to_behind[m]
                elif d == 1:
                    first = m * REACH + RIM
                    down = pltpu.roll(to_ahead[m], 1, 0)
                    up = pltpu.roll(to_behind[m], SLAB - 1, 0)
                    own[m] = own[m] + jnp.where(row > 0, down, 0.0) + jnp.where(row < SLAB - 1, up, 0.0)
                    slope[x, first + SLAB : first + SLAB + 1, :] = down[0:1]
                    slope[x, first - 1 : first, :] = up[SLAB - 1 :]
                else:
                    own[m] = own[m] + turn(to_ahead[m], 1) + turn(to_behind[m], -1)
        stay[x] = own
        whole = jnp.concatenate(logits, axis=0)
        stack_logits(whole, x, l_taps)
    for x in range(PLANES):
        for m in range(3):
            value = stay[x][m] + pushed[(x - 1) % PLANES, m, 1] + pushed[(x + 1) % PLANES, m, -1]
            slope[x, m * REACH + RIM : m * REACH + RIM + SLAB, :] = value
    for pair in range(4):
        cut = slice(pair * 256, pair * 256 + 256)
        value = dot_stacked(back2, (l_taps[0:STACK, cut], l_taps[STACK:, cut]))
        value = value * (1.0 - hidden[:, cut] * hidden[:, cut])
        stack_planes(value, 2 * pair, 1, p_hi, p_lo)
    finish_planes(p_hi, p_lo)
    for pair in range(4):
        cut = slice(pair * 256, pair * 256 + 256)
        work[:, cut] = dot_stacked(back1, (p_hi[:, cut], p_lo[:, cut]))
    for x in range(PLANES):
        total = slope[x, 0:40, :] + work[48:88, plane(x)]
        slope[x, 0:40, :] = total + turn(work[0:40, plane(x)], -1) + turn(work[96:136, plane(x)], 1)


def kernel_sums(u_taps, h_hi, h_lo, l_taps, p_hi, p_lo, sums):
    for first, taps, high, low in ((0, l_taps, h_hi, h_lo), (144, u_taps, p_hi, p_lo)):
        left = jnp.concatenate([taps[144:288, :], taps[STACK + 144 : STACK + 288, :]], axis=0)
        main = dot(left, high[...], NT)
        sums[first : first + 144, :] = main[:144] + (main[144:] + dot(left[:144], low[...], NT))


def second_kernel_body(
    mode_x, recv, fwd1, fwd2, back2, back1, to_z, from_z,
    out, sums,
    field, hidden, grad, modes, rows6, weights, work, slope,
    u_taps, h_hi, h_lo, l_taps, p_hi, p_lo,
):
    back_z = (from_z[0], from_z[1])
    for k in range(PLANES):
        modes[k, 0:32, :] = gather_modes(recv, 0, k, 0, 32)
        modes[k, 32:40, :] = gather_modes(recv, 1, k, 24, 8)
    flat = dot_stacked(stacked(modes[...].reshape(PLANES * 40, DEPTH)), back_z)
    modes[...] = flat.reshape(PLANES, 40, DEPTH)
    for x, value in enumerate(mixed([modes[k] for k in range(PLANES)], mode_x.T)):
        for m in range(3):
            first = m * REACH
            field[x, first : first + RIM, :] = value[24 + 2 * m : 26 + 2 * m]
            field[x, first + RIM : first + RIM + SLAB, :] = value[8 * m : 8 * m + 8]
            field[x, first + RIM + SLAB : first + REACH, :] = value[32 + 2 * m : 34 + 2 * m]
        field[x, 36:37, :] = jnp.ones((1, DEPTH), jnp.float32)
        field[x, 37:48, :] = jnp.zeros((11, DEPTH), jnp.float32)
    for k in range(PLANES):
        grad[k] = gather_modes(recv, 1, k, 0, 24)
    flat = dot_stacked(stacked(grad[...].reshape(PLANES * 24, DEPTH)), back_z)
    flat = flat.reshape(PLANES, 24, DEPTH)
    for x, value in enumerate(mixed([flat[k] for k in range(PLANES)], mode_x.T)):
        grad[x] = value
    network(field, fwd1, fwd2, hidden, weights, u_taps, h_hi, h_lo, work)
    pullback(
        field, grad, hidden, weights, back2, back1, l_taps, p_hi, p_lo, work, slope
    )
    kernel_sums(u_taps, h_hi, h_lo, l_taps, p_hi, p_lo, sums)
    for k, value in enumerate(mixed([slope[x, 0:40, :] for x in range(PLANES)], mode_x)):
        modes[k] = value
    flat = dot_stacked(stacked(modes[...].reshape(PLANES * 40, DEPTH)), (to_z[0], to_z[1]))
    modes[...] = flat.reshape(PLANES, 40, DEPTH)
    for h in range(2):
        for k in range(PLANES):
            for m in range(3):
                first = m * REACH + RIM + 4 * h
                rows6[h, k, 4 * m : 4 * m + 4, :] = modes[k, first : first + 4, :]
                first = m * REACH + (RIM + SLAB) * h
                rows6[h, k, 12 + 2 * m : 14 + 2 * m, :] = modes[k, first : first + 2, :]
            rows6[h, k, 18:24, :] = jnp.zeros((6, DEPTH), jnp.float32)
    scatter_modes(lambda h, k: rows6[h, k], 24, out)


def third_kernel_body(
    mode_x, recv, field, hidden, weights, u_taps, h_hi, h_lo, back2, back1, from_z, old_sums,
    spread_t, mask, lift,
    out,
    flat, grad, modes, l_taps, p_hi, p_lo, work, slope, sums, pieces,
):
    back_z = (from_z[0], from_z[1])
    flat[...] = jnp.zeros_like(flat)
    for device in range(16):
        for m in range(3):
            flat[device, 4 * m : 4 * m + 4, :] = recv[device, m]
    for h in range(2):
        for k in range(PLANES):
            modes[k] = gather_modes(flat, h, k, 0, 16)
        moved_back = dot_stacked(stacked(modes[...].reshape(PLANES * 16, DEPTH)), back_z)
        modes[...] = moved_back.reshape(PLANES, 16, DEPTH)
        for x, value in enumerate(mixed([modes[k] for k in range(PLANES)], mode_x.T)):
            for m in range(3):
                grad[x, m * SLAB + 4 * h : m * SLAB + 4 * h + 4, :] = value[m * 4 : m * 4 + 4, :]
    pullback(field, grad, hidden, weights, back2, back1, l_taps, p_hi, p_lo, work, slope)
    kernel_sums(u_taps, h_hi, h_lo, l_taps, p_hi, p_lo, sums)
    sums[...] += old_sums[...]
    for x in range(PLANES):
        out[x, 0:36, :] = slope[x, 0:36, :]
    pack_grads(sums, spread_t, mask, lift, pieces)
    for x in range(PLANES):
        out[x, 36:72, :] = pieces[0:36, :]


def pack_grads(sums, spread_t, mask, lift, pieces):
    whole = split(sums[...])
    empty = jnp.zeros((32, 512 - DEEP), jnp.float32)
    rows = []
    for b in range(3):
        rows.append(dot(spread_t[...], whole[0] * mask[b]) + dot(spread_t[...], whole[1] * mask[b]))
        rows.append(empty)
    placed = dot(stacked(beside(rows)), lift[...])
    placed = placed[:32] + placed[32:]
    pieces[0:28, :] = placed[0:28, 0:128]
    total = placed[0:8, 128:]
    for i in range(1, 4):
        total = total + turn(placed[8 * i : 8 * i + 8, 128:], 16 * i)
    pieces[28:36, :] = total


def fold_kernel(recv, main, edge, ext):
    ext[...] = jnp.zeros_like(ext)
    total = None
    for q in range(PLANES):
        for m in range(3):
            ext[m, 8 * q + 6 : 8 * q + 18, :] += recv[q, m * REACH : (m + 1) * REACH, :]
        block = recv[q, 36:72, :]
        total = block if total is None else total + block
    for m in range(3):
        main[m, 0] = ext[m, 8:72, :]
        edge[m * 8 : m * 8 + 2, :] = ext[m, 72:74, :]
        edge[m * 8 + 2 : m * 8 + 4, :] = ext[m, 6:8, :]
        edge[m * 8 + 4 : m * 8 + 8, :] = jnp.zeros((4, DEPTH), jnp.float32)
    edge[24:60, :] = total
    edge[60:64, :] = jnp.zeros((4, DEPTH), jnp.float32)


def last_kernel(main, edge, other, out, first, end1, second, end2, turned):
    for m in range(3):
        out[m, 0] = main[m, 0]
        out[m, 0, 0:2, :] += other[m * 8 : m * 8 + 2, :]
        out[m, 0, 62:64, :] += other[m * 8 + 2 : m * 8 + 4, :]
    grads = edge[24:64, :] + other[24:64, :]
    for slot in range(8):
        turned[slot] = turn(grads, -16 * slot)
    for b in range(3):
        for a in range(3):
            for e in range(3):
                for i in range(9):
                    row = e * 6 + i if i < 6 else 18 + e * 3 + i - 6
                    slot = 3 * b + a
                    slot, inner = (slot, row) if slot < 8 else (row // 8, 28 + row % 8)
                    line = turned[slot, inner, 0:16]
                    if i < 6:
                        second[i * 9 + a * 3 + b, e, :] = line
                    else:
                        first[(i - 6) * 9 + a * 3 + b, e, :] = line
    end1[...] = turned[1, 27:28, 0:16]
    for o in range(COEFFS):
        slot, inner = (4, 34 + o) if o < 2 else (5, 26 + o)
        end2[0:1, o : o + 1] = turned[slot, inner : inner + 1, 0:1]


def slab_device(velocity, cotangent, first_kernel, first_bias, second_kernel, second_bias):
    c = constants()
    mode_x = c["mode_x"]
    half = jnp.bfloat16
    f32 = lambda *dims: pltpu.VMEM(dims, jnp.float32)
    b16 = lambda *dims: pltpu.VMEM(dims, half)
    swap = [(0, 1), (1, 0)]

    other = lax.ppermute(velocity, "py", swap)
    packed = call(
        pack_kernel, shape(PLANES, 64, DEPTH), (velocity, cotangent), [f32(3, 80, DEPTH)], room=4
    )
    packed = call(rim_kernel, shape(PLANES, 64, DEPTH), (packed, other), room=4)
    recv = lax.all_to_all(packed, "px", 0, 0)

    fwd2, fwd1, back2, back1, to_z = call(
        weights_kernel,
        [
            shape(288, DEEP, kind=half),
            shape(2 * HID, STACK, kind=half),
            shape(2 * HID, STACK, kind=half),
            shape(288, DEEP, kind=half),
            shape(2, DEPTH, DEPTH, kind=half),
        ],
        (
            jnp.transpose(first_kernel, (1, 2, 3, 4, 0)).reshape(27, 3, CHANNELS),
            jnp.transpose(second_kernel, (0, 2, 3, 4, 1)).reshape(54, 3, CHANNELS),
            first_bias.reshape(1, CHANNELS),
            second_bias.reshape(1, COEFFS),
            c["to_z"],
        ),
        [
            f32(3, 96, CHANNELS),
            f32(27, 3, CHANNELS),
            f32(54, 3, CHANNELS),
            f32(1, CHANNELS),
            f32(1, COEFFS),
            pltpu.SemaphoreType.DMA((4,)),
        ],
        away=(0, 1, 2, 3),
    )

    near = lambda rows: [b16(rows, FLAT), b16(rows, FLAT)]
    stacks = near(2 * STACK)[:1] + near(DEEP) + near(2 * STACK)[:1] + near(DEEP)
    sent, hidden, weights, *kept = call(
        functools.partial(first_kernel_body, mode_x),
        [
            shape(16, 24, DEPTH),
            shape(HID, FLAT),
            shape(LOG, FLAT),
            shape(2 * STACK, FLAT, kind=half),
            shape(DEEP, FLAT, kind=half),
            shape(DEEP, FLAT, kind=half),
        ],
        (recv, fwd1, fwd2, to_z),
        [f32(144, FLAT), f32(2, PLANES, 24, DEPTH)],
    )
    both = ("px", "py")
    moved_modes = lax.all_to_all(sent, both, 0, 0)
    moved_modes = call(both_kernel, shape(16, 32, DEPTH), (moved_modes, c["both_in"], c["both_out"]))
    moved_modes = lax.all_to_all(moved_modes, both, 0, 0)

    sent, sums = call(
        functools.partial(second_kernel_body, mode_x),
        [shape(16, 9, 2, DEPTH), shape(288, DEEP)],
        (moved_modes, fwd1, fwd2, back2, back1, to_z, c["from_z"]),
        [
            f32(PLANES, 48, DEPTH),
            f32(HID, FLAT),
            f32(PLANES, 24, DEPTH),
            f32(PLANES, 40, DEPTH),
            f32(2, PLANES, 24, DEPTH),
            f32(LOG, FLAT),
            f32(144, FLAT),
            f32(PLANES, 48, DEPTH),
        ]
        + stacks,
    )
    moved_modes = lax.all_to_all(sent, both, 0, 0)
    moved_modes = call(
        one_kernel,
        shape(16, 3, 4, DEPTH),
        (moved_modes, c["one_in"], c["one_out"]),
        [f32(3, 96, DEPTH)],
    )
    moved_modes = lax.all_to_all(moved_modes, both, 0, 0)

    sent = call(
        functools.partial(third_kernel_body, mode_x),
        shape(PLANES, 72, DEPTH),
        (
            moved_modes, recv, hidden, weights, *kept, back2, back1, c["from_z"], sums,
            c["spread_t"], c["mask"], c["lift"],
        ),
        [f32(16, 16, DEPTH), f32(PLANES, 24, DEPTH), f32(PLANES, 16, DEPTH)]
        + stacks[3:]
        + [
            f32(144, FLAT),
            f32(PLANES, 48, DEPTH),
            f32(288, DEEP),
            f32(36, DEPTH),
        ],
    )
    recv = lax.all_to_all(sent, "px", 0, 0)
    main, edge = call(
        fold_kernel, [shape(3, 1, 64, DEPTH), shape(64, DEPTH)], (recv,), [f32(3, 80, DEPTH)]
    )
    other = lax.ppermute(edge, "py", swap)
    grad_velocity, first, end1, second, end2 = call(
        last_kernel,
        [
            shape(3, 1, 64, DEPTH),
            shape(27, 3, CHANNELS),
            shape(1, CHANNELS),
            shape(54, 3, CHANNELS),
            shape(1, COEFFS),
        ],
        (main, edge, other),
        [f32(8, 40, DEPTH)],
    )
    return (
        grad_velocity,
        jnp.transpose(first.reshape(3, 3, 3, 3, CHANNELS), (4, 0, 1, 2, 3)),
        end1.reshape(CHANNELS),
        jnp.transpose(second.reshape(COEFFS, 3, 3, 3, CHANNELS), (0, 4, 1, 2, 3)),
        end2.reshape(COEFFS),
    )


def fits_slabs(mesh):
    return mesh.shape["px"] == PLANES and mesh.shape["py"] == 2


def solution(mesh):
    return jax.shard_map(
        slab_device if fits_slabs(mesh) else on_device,
        mesh=mesh,
        in_specs=(
            P(None, ("groups", "px"), "py", None),
            P(None, ("groups", "px"), "py", None),
            P(),
            P(),
            P(),
            P(),
        ),
        out_specs=(
            P(None, ("groups", "px"), "py", None),
            P("groups", None, None, None, None),
            P("groups"),
            P("groups", None, None, None, None),
            P("groups"),
        ),
        check_vma=False,
    )
```

```python
import functools
import math

import jax
import jax.numpy as jnp
import numpy as np
from jax import lax
from jax.experimental import pallas as pl
from jax.experimental.pallas import tpu as pltpu
from jax.sharding import PartitionSpec as P

ITERS = 2


KAPPA = 0.25


def padded_2(value, sides, width):
    for axis, dim in sides:
        size, length = (lax.axis_size(axis), value.shape[dim])
        up = [(i, (i + 1) % size) for i in range(size)]
        down = [(j, i) for i, j in up]
        last = lax.slice_in_dim(value, length - width, length, axis=dim)
        initial = lax.slice_in_dim(value, 0, width, axis=dim)
        before = lax.ppermute(last, axis, up)
        after = lax.ppermute(initial, axis, down)
        value = jnp.concatenate([before, value, after], axis=dim)
    return value


def extend(field):
    rimmed = padded_2(field, (("px", 1), ("py", 2)), 1)
    return jnp.concatenate([rimmed[..., -1:], rimmed, rimmed[..., :1]], axis=3)


def across_columns(spectrum):
    return lax.all_to_all(spectrum, "px", split_axis=2, concat_axis=4, tiled=True)


def across_pairs(spectrum):
    return lax.all_to_all(spectrum, "py", split_axis=3, concat_axis=4, tiled=True)


def summed(grads):
    return lax.psum((grads[0], grads[1], grads[2], grads[3]), ("px", "py"))


def all_taps():
    return [
        (shift_x, shift_y, shift_z)
        for shift_x in range(3)
        for shift_y in range(3)
        for shift_z in range(3)
    ]


def gather_conv(padded, kernel):
    size_x = padded.shape[1] - 2
    size_y = padded.shape[2] - 2
    size_z = padded.shape[3] - 2
    stacked = jnp.concatenate(
        [
            padded[:, sx_one : sx_one + size_x, sy_one : sy_one + size_y, sz_one : sz_one + size_z]
            for sx_one, sy_one, sz_one in all_taps()
        ],
        axis=0,
    )
    matrix = jnp.transpose(kernel, (0, 2, 3, 4, 1)).reshape(kernel.shape[0], -1)
    result = jnp.einsum("ok,kxyz->oxyz", matrix, stacked, precision=lax.Precision.HIGHEST)
    return (result, stacked)


def scatter_conv(padded, kernel):
    outputs = kernel.shape[0]
    inputs = kernel.shape[1]
    size_x = padded.shape[1] - 2
    size_y = padded.shape[2] - 2
    size_z = padded.shape[3] - 2
    total = jnp.zeros((outputs, size_x, size_y, size_z), jnp.float32)
    for shift_x in range(3):
        matrix = jnp.transpose(kernel[:, :, shift_x], (0, 2, 3, 1)).reshape(outputs * 9, inputs)
        layer = jnp.einsum(
            "km,mxyz->kxyz",
            matrix,
            padded[:, shift_x : shift_x + size_x],
            precision=lax.Precision.HIGHEST,
        )
        layer = layer.reshape(outputs, 3, 3, size_x, size_y + 2, size_z + 2)
        for shift_y in range(3):
            for shift_z in range(3):
                total = (
                    total
                    + layer[
                        :,
                        shift_y,
                        shift_z,
                        :,
                        shift_y : shift_y + size_y,
                        shift_z : shift_z + size_z,
                    ]
                )
    return total


def flipped(kernel):
    return jnp.transpose(kernel[:, :, ::-1, ::-1, ::-1], (1, 0, 2, 3, 4))


def moved(padded, axis_dim, offset_cells):
    index = [slice(None), slice(1, -1), slice(1, -1), slice(1, -1)]
    index[axis_dim] = slice(1 + offset_cells, padded.shape[axis_dim] - 1 + offset_cells)
    return padded[tuple(index)]


def advect(padded, weights):
    center = moved(padded, 1, 0)
    total = jnp.zeros_like(center)
    for direction in range(3):
        ahead = moved(padded, direction + 1, 1)
        behind = moved(padded, direction + 1, -1)
        vplus = 0.5 * (center[direction] + ahead[direction])
        vminus = 0.5 * (behind[direction] + center[direction])
        upper = center + weights[2 * direction] * (ahead - center)
        lower = center + weights[2 * direction + 1] * (behind - center)
        total = total + vplus * upper - vminus * lower
    return total


def advect_back(padded, weights_pad, source_pad):
    center = moved(padded, 1, 0)
    source = moved(source_pad, 1, 0)
    weights = moved(weights_pad, 1, 0)
    grad_field = jnp.zeros_like(center)
    fluxes = []
    parts = []
    for direction in range(3):
        ahead = moved(padded, direction + 1, 1)
        behind = moved(padded, direction + 1, -1)
        vplus = 0.5 * (center[direction] + ahead[direction])
        vminus = 0.5 * (behind[direction] + center[direction])
        rate_up = weights[2 * direction]
        rate_low = weights[2 * direction + 1]
        rate_before = moved(weights_pad[2 * direction : 2 * direction + 1], direction + 1, -1)[0]
        rate_after = moved(weights_pad[2 * direction + 1 : 2 * direction + 2], direction + 1, 1)[0]
        source_before = moved(source_pad, direction + 1, -1)
        source_after = moved(source_pad, direction + 1, 1)
        upper = center + rate_up * (ahead - center)
        lower = center + rate_low * (behind - center)
        upper_before = behind + rate_before * (center - behind)
        lower_after = ahead + rate_after * (center - ahead)
        grad_field = grad_field + source * (vplus * (1.0 - rate_up) - vminus * (1.0 - rate_low))
        grad_field = (
            grad_field + vminus * rate_before * source_before - vplus * rate_after * source_after
        )
        fluxes.append(
            0.5
            * (
                jnp.sum(source * upper, 0)
                - jnp.sum(source * lower, 0)
                + jnp.sum(source_before * upper_before, 0)
                - jnp.sum(source_after * lower_after, 0)
            )
        )
        parts.append(jnp.sum(source * vplus * (ahead - center), 0))
        parts.append(-jnp.sum(source * vminus * (behind - center), 0))
    return (grad_field + jnp.stack(fluxes), jnp.stack(parts))


def tables(count):
    index = jnp.arange(count, dtype=jnp.int32)
    phase = index[:, None] * index[None, :] % count
    angle = phase.astype(jnp.float32) * (2.0 * math.pi / count)
    return (jnp.cos(angle), jnp.sin(angle))


def mix(form, data, table):
    return jnp.einsum(form, data, table, precision=lax.Precision.HIGHEST)


def waves(start, count, total):
    index = start + jnp.arange(count, dtype=jnp.int32)
    return jnp.where(index < total // 2, index, index - total).astype(jnp.float32)


def project(field):
    depth = field.shape[3]
    cos_z, sin_z = tables(depth)
    real_z = mix("cxyz,zk->cxky", field, cos_z)
    imag_z = -mix("cxyz,zk->cxky", field, sin_z)
    spectrum = across_pairs(jnp.stack([real_z, imag_z]))
    span_y = spectrum.shape[4]
    cos_y, sin_y = tables(span_y)
    real_y = mix("cxky,yq->cqkx", spectrum[0], cos_y) + mix("cxky,yq->cqkx", spectrum[1], sin_y)
    imag_y = mix("cxky,yq->cqkx", spectrum[1], cos_y) - mix("cxky,yq->cqkx", spectrum[0], sin_y)
    spectrum = across_columns(jnp.stack([real_y, imag_y]))
    span_x = spectrum.shape[4]
    cos_x, sin_x = tables(span_x)
    real_x = mix("cqkx,xp->cqkp", spectrum[0], cos_x) + mix("cqkx,xp->cqkp", spectrum[1], sin_x)
    imag_x = mix("cqkx,xp->cqkp", spectrum[1], cos_x) - mix("cqkx,xp->cqkp", spectrum[0], sin_x)
    rows_y = spectrum.shape[2]
    rows_z = spectrum.shape[3]
    wave_y = waves(lax.axis_index("px") * rows_y, rows_y, span_y)[:, None, None]
    wave_z = waves(lax.axis_index("py") * rows_z, rows_z, depth)[None, :, None]
    wave_x = waves(0, span_x, span_x)[None, None, :]
    size = jnp.maximum(wave_x * wave_x + wave_y * wave_y + wave_z * wave_z, 1.0)
    vectors = jnp.stack(jnp.broadcast_arrays(wave_x, wave_y, wave_z))
    real_x = real_x - vectors * (
        (wave_x * real_x[0] + wave_y * real_x[1] + wave_z * real_x[2]) / size
    )
    imag_x = imag_x - vectors * (
        (wave_x * imag_x[0] + wave_y * imag_x[1] + wave_z * imag_x[2]) / size
    )
    back_real = (mix("cqkp,px->cxkq", real_x, cos_x) - mix("cqkp,px->cxkq", imag_x, sin_x)) / span_x
    back_imag = (mix("cqkp,px->cxkq", imag_x, cos_x) + mix("cqkp,px->cxkq", real_x, sin_x)) / span_x
    spectrum = across_columns(jnp.stack([back_real, back_imag]))
    rows_real = (
        mix("cxkq,qy->cxyk", spectrum[0], cos_y) - mix("cxkq,qy->cxyk", spectrum[1], sin_y)
    ) / span_y
    rows_imag = (
        mix("cxkq,qy->cxyk", spectrum[1], cos_y) + mix("cxkq,qy->cxyk", spectrum[0], sin_y)
    ) / span_y
    spectrum = across_pairs(jnp.stack([rows_real, rows_imag]))
    return (
        mix("cxyk,kz->cxyz", spectrum[0], cos_z) - mix("cxyk,kz->cxyz", spectrum[1], sin_z)
    ) / depth


def forward_state(field, first_kernel, first_bias, second_kernel, second_bias):
    padded = extend(field)
    first_out, field_taps = gather_conv(padded, first_kernel)
    hidden = jnp.tanh(first_out + first_bias[:, None, None, None])
    weights = jax.nn.sigmoid(
        scatter_conv(extend(hidden), second_kernel) + second_bias[:, None, None, None]
    )
    return (padded, hidden, weights, field_taps)


def backward_step(state, upstream, first_kernel, second_kernel):
    padded, hidden, weights, field_taps = state
    moved_grad = project(upstream)
    source = -KAPPA * moved_grad
    stacked = extend(jnp.concatenate([source, weights], axis=0))
    grad_field, grad_weights = advect_back(padded, stacked[3:], stacked[:3])
    grad_field = grad_field + moved_grad
    grad_logits = grad_weights * weights * (1.0 - weights)
    logits_pad = extend(grad_logits)
    grad_hidden, logit_taps = gather_conv(logits_pad, flipped(second_kernel))
    product = jnp.einsum("kxyz,mxyz->km", logit_taps, hidden, precision=lax.Precision.HIGHEST)
    product = product.reshape(3, 3, 3, second_kernel.shape[0], second_kernel.shape[1])
    grad_second = jnp.transpose(product[::-1, ::-1, ::-1], (3, 4, 0, 1, 2))
    grad_second_bias = jnp.sum(grad_logits, axis=(1, 2, 3))
    grad_pre = grad_hidden * (1.0 - hidden * hidden)
    pre_pad = extend(grad_pre)
    grad_field = grad_field + scatter_conv(pre_pad, flipped(first_kernel))
    first_product = jnp.einsum(
        "oxyz,kxyz->ok", grad_pre, field_taps, precision=lax.Precision.HIGHEST
    )
    first_product = first_product.reshape(first_kernel.shape[0], 3, 3, 3, first_kernel.shape[1])
    grad_first = jnp.transpose(first_product, (0, 4, 1, 2, 3))
    grad_first_bias = jnp.sum(grad_pre, axis=(1, 2, 3))
    return (grad_field, (grad_first, grad_first_bias, grad_second, grad_second_bias))


def on_device(velocity, cotangent, first_kernel, first_bias, second_kernel, second_bias):
    field = velocity
    fields = [velocity]
    saved = []
    for section in range(ITERS):
        state = forward_state(field, first_kernel, first_bias, second_kernel, second_bias)
        saved.append(state)
        field = project(field - KAPPA * advect(state[0], state[2]))
        fields.append(field)
    upstream = cotangent
    totals = None
    for section in reversed(range(ITERS)):
        state = saved[section]
        upstream, grads = backward_step(state, upstream, first_kernel, second_kernel)
        grads = summed(grads)
        if totals is None:
            totals = grads
        else:
            totals = tuple((older + newer for older, newer in zip(totals, grads)))
    return (upstream, totals[0], totals[1], totals[2], totals[3])


SLAB = 8
RIM = 2
REACH = SLAB + 2 * RIM
WIDE = SLAB + 2
PLANES = 8
DEPTH = 128
ROWS = 128
CHANNELS = 16
COEFFS = 6
BAND = 32
HID = CHANNELS * WIDE
LOG = COEFFS * SLAB
STACK = 9 * 48
UNIT = 36
BROAD = HID + 16
DEEP = 3 * HID + 16
PLACE = (0, 2, 1)
FLAT = PLANES * DEPTH
NN = ((1,), (0,))
NT = ((1,), (1,))


def real_basis(count):
    half = count // 2
    angle = 2.0 * np.pi * np.arange(count) / count
    rows = [np.full(count, 1.0 / np.sqrt(count))]
    rows += [np.sqrt(2.0 / count) * np.cos(k * angle) for k in range(1, half)]
    rows += [np.cos(half * angle) / np.sqrt(count)]
    rows += [np.sqrt(2.0 / count) * np.sin(k * angle) for k in range(1, half)]
    return np.stack(rows)


def wide_table(table):
    high, low = halves(table)
    return np.concatenate([high, low, high], axis=1)


def tall_table(table):
    high, low = halves(table)
    return np.concatenate([high, high, low])


def halves(table):
    high = table.astype(np.float32).astype(jnp.bfloat16)
    low = (table - high.astype(np.float64)).astype(np.float32).astype(jnp.bfloat16)
    return high, low


def slab_of(device):
    return (device % 2) * PLANES + device // 2


@functools.cache
def constants():
    basis_z = real_basis(DEPTH)
    order = []
    for group in range(4):
        order += [16 * group + i for i in range(16)] + [64 + 16 * group + i for i in range(16)]
    mode_z = basis_z[order]
    basis_y = real_basis(ROWS)

    def rows(offset, count):
        at = [SLAB * slab_of(j) + offset + i for j in range(16) for i in range(count)]
        return basis_y[:, np.array(at) % ROWS]

    own, half_one, half_two = rows(0, SLAB), rows(0, 4), rows(4, 4)
    before, after = rows(-RIM, RIM), rows(SLAB, RIM)
    both_in = own
    both_out = np.concatenate([own, before, after], axis=1).T
    one_in = np.concatenate(
        [np.concatenate([half_one, before], axis=1), np.concatenate([half_two, after], axis=1)]
    )
    one_out = np.concatenate([half_one, half_two], axis=1).T

    spread = np.zeros((288, 32))
    mask = np.zeros((3, 288, DEEP))
    lanes = np.arange(CHANNELS) * WIDE
    for e in range(3):
        for o in range(COEFFS):
            for q in range(SLAB):
                row = e * 48 + o * SLAB + q
                spread[row, e * COEFFS + o] = 1.0
                for b in range(3):
                    for a in range(3):
                        mask[b, row, a * HID + lanes + q + b] = 1.0
        for m in range(3):
            for r in range(REACH):
                row = 144 + e * 48 + m * REACH + r
                spread[row, 18 + e * 3 + m] = 1.0
                for b in range(3):
                    for a in range(3):
                        if 0 <= r - b < WIDE:
                            mask[b, row, a * HID + lanes + r - b] = 1.0
    spread[144 + 48 + UNIT, 27] = 1.0
    mask[0, 144 + 48 + UNIT, PLACE[1] * HID : (PLACE[1] + 1) * HID] = 1.0
    mask[0, 48:96, 3 * HID] = 1.0
    lift = np.zeros((3, 512, 256))
    for b in range(3):
        for a in range(3):
            lift[b, PLACE[a] * HID + np.arange(HID), 16 * (3 * b + a) + np.arange(HID) // WIDE] = 1.0
    lift[0, 3 * HID, 128 + 64] = 1.0
    lift = lift.reshape(3 * 512, 256)
    half = jnp.bfloat16
    return dict(
        to_z=tall_table(mode_z.T),
        from_z=tall_table(mode_z),
        both_in=wide_table(both_in),
        both_out=wide_table(both_out),
        one_in=wide_table(one_in),
        one_out=wide_table(one_out),
        spread_t=np.ascontiguousarray(spread.T).astype(half),
        mask=mask.astype(half),
        lift=lift.astype(half),
    )


def dot(left, right, dims=NN):
    return lax.dot_general(left, right, (dims, ((), ())), preferred_element_type=jnp.float32)


def split(value):
    high = value.astype(jnp.bfloat16)
    return high, (value - high.astype(jnp.float32)).astype(jnp.bfloat16)


def dot_stacked(left, right, dims=NN):
    rows = left.shape[0] // 2
    main = dot(left[...], right[0], dims)
    return main[:rows] + (main[rows:] + dot(left[0:rows, :], right[1], dims))


def dot_wide(left, right):
    return dot(left[...], jnp.concatenate([right[0], right[0], right[1]], axis=0))


def widened(value):
    high, low = split(value)
    return jnp.concatenate([high, low, high], axis=1)


def stacked(value):
    return jnp.concatenate(split(value), axis=0)


def turn(value, shift):
    shift = shift % value.shape[-1]
    return value if shift == 0 else pltpu.roll(value, shift, value.ndim - 1)


def plane(x):
    x = x % PLANES
    return slice(x * DEPTH, (x + 1) * DEPTH)


def call(kernel, outs, args, scratch=(), room=16, away=()):
    single = not isinstance(outs, (list, tuple))
    vmem = pl.BlockSpec(memory_space=pltpu.VMEM)
    cost = pl.CostEstimate(flops=1, bytes_accessed=1, transcendentals=0) if away else None
    return pl.pallas_call(
        kernel,
        out_shape=outs,
        in_specs=[
            pl.BlockSpec(memory_space=pltpu.HBM) if i in away else vmem for i in range(len(args))
        ],
        out_specs=vmem if single else [vmem] * len(outs),
        scratch_shapes=list(scratch),
        cost_estimate=cost,
        compiler_params=pltpu.CompilerParams(vmem_limit_bytes=room * 2**20),
    )(*args)


def fetch(pairs, sems):
    copies = [pltpu.make_async_copy(src, dst, sems.at[i]) for i, (src, dst) in enumerate(pairs)]
    for copy in copies:
        copy.start()
    return copies


def shape(*dims, kind=jnp.float32):
    return jax.ShapeDtypeStruct(dims, kind)


def counting(size, dim):
    return lax.broadcasted_iota(jnp.int32, size, dim).astype(jnp.float32)


def remainder(value, count):
    return value - count * jnp.floor((value + 0.5) / count)


def band_tables(tall):
    row, col = (0, 1) if tall else (1, 0)
    size = lambda rows, cols: (rows, cols) if tall else (cols, rows)
    where = counting(size(2 * STACK, 96), row)
    to = counting(size(2 * STACK, 96), col)
    first = where - 8.0 * to
    third = to - 54.0
    second = where - STACK - (16.0 * third - 4.0 * remainder(third, 3.0))
    picks = ((to < 54.0) & (first >= 0.0) & (first < 8.0)) | (
        (to >= 54.0) & (to < 81.0) & (second >= 0.0) & (second < 12.0)
    )
    where = counting(size(2 * STACK, HID), row)
    inner = remainder(counting(size(2 * STACK, HID), col), 10.0)
    outer = where - STACK
    offset = jnp.where(
        where < STACK,
        inner - remainder(where, 8.0),
        remainder(remainder(outer, 48.0), 12.0) - inner,
    )
    gap = counting(size(HID, CHANNELS), row) - 10.0 * counting(size(HID, CHANNELS), col)
    lift = (gap >= 0.0) & (gap < 10.0)
    half = jnp.bfloat16
    return picks.astype(jnp.float32).astype(half), offset, lift.astype(jnp.float32).astype(half)


def weights_kernel(
    far1, far2, far3, far4, z_in, fwd2, fwd1, back2, back1, z_out, blocks, taps1, taps2, bias1, bias2, sems
):
    copies = fetch([(far1, taps1), (far2, taps2), (far3, bias1), (far4, bias2)], sems)
    blocks[...] = jnp.zeros_like(blocks)
    z_out[...] = z_in[...]
    spread, offset, lift = band_tables(True)
    spread_t, offset_t, lift_t = band_tables(False)
    for copy in copies:
        copy.wait()
    for b in range(3):
        for a in range(3):
            for e in range(3):
                tap = a * 3 + e
                for o in range(COEFFS):
                    blocks[b, tap * 6 + o, :] = taps2[o * 9 + a * 3 + b, e, :]
                for m in range(3):
                    blocks[b, 54 + tap * 3 + m, :] = taps1[m * 9 + a * 3 + b, e, :]
    tall = [jnp.zeros((2 * STACK, HID), jnp.float32)] * 2
    flat = [jnp.zeros((HID, 2 * STACK), jnp.float32)] * 2
    for b in range(3):
        for half, block in enumerate(split(blocks[b])):
            rows = dot(spread, block).astype(jnp.bfloat16)
            tall[half] = jnp.where(offset == float(b), dot(rows, lift_t), tall[half])
            cols = dot(lift, block, NT).astype(jnp.bfloat16)
            flat[half] = jnp.where(offset_t == float(b), dot(cols, spread_t), flat[half])
    for half in range(2):
        rows, cols = slice(half * 144, half * 144 + 144), slice(half * HID, half * HID + HID)
        for a in range(3):
            first = PLACE[a] * HID
            part = tall[half][a * 144 : a * 144 + 144]
            fwd2[rows, first : first + HID] = part.astype(jnp.bfloat16)
            part = tall[half][STACK + a * 144 : STACK + a * 144 + 144]
            back1[rows, first : first + HID] = part.astype(jnp.bfloat16)
        back2[cols, :] = flat[half][:, :STACK].astype(jnp.bfloat16)
    gap = counting((LOG, COEFFS), 0) - 8.0 * counting((LOG, COEFFS), 1)
    pick = ((gap >= 0.0) & (gap < 8.0)).astype(jnp.float32).astype(jnp.bfloat16)
    second = counting((LOG, 16), 1) < 1.0
    one = split(jnp.broadcast_to(bias1[...], (STACK, CHANNELS)))
    first = counting((HID, STACK), 1) == 4.0 * 48.0 + UNIT
    two = split(jnp.broadcast_to(bias2[...], (16, COEFFS)))
    fwd2[:, 3 * HID :] = jnp.zeros((288, 16), jnp.bfloat16)
    back1[:, 3 * HID :] = jnp.zeros((288, 16), jnp.bfloat16)
    for half in range(2):
        value = jnp.where(first, dot(lift, one[half], NT), flat[half][:, STACK:])
        fwd1[half * HID : half * HID + HID, :] = value.astype(jnp.bfloat16)
        value = jnp.where(second, dot(pick, two[half], NT), 0.0)
        start = half * 144 + LOG
        fwd2[start : start + LOG, 3 * HID :] = value.astype(jnp.bfloat16)


def pack_kernel(field, cot, out, ext):
    ext[...] = jnp.zeros_like(ext)
    for m in range(3):
        ext[m, 8:72, :] = field[m, 0]
    for q in range(PLANES):
        for m in range(3):
            out[q, m * REACH : (m + 1) * REACH, :] = ext[m, 8 * q + 6 : 8 * q + 18, :]
            out[q, 40 + 8 * m : 48 + 8 * m, :] = cot[m, 0, 8 * q : 8 * q + 8, :]
        out[q, 36:37, :] = jnp.ones((1, DEPTH), jnp.float32)
        out[q, 37:40, :] = jnp.zeros((3, DEPTH), jnp.float32)


def rim_kernel(packed, other, out):
    out[...] = packed[...]
    for m in range(3):
        out[0, m * REACH : m * REACH + 2, :] = other[m, 0, 62:64, :]
        out[PLANES - 1, m * REACH + 10 : m * REACH + 12, :] = other[m, 0, 0:2, :]


def unit_row():
    row = lax.broadcasted_iota(jnp.int32, (16, FLAT), 0)
    return jnp.where(row == 0, 1.0, 0.0).astype(jnp.bfloat16)


def stack_planes(value, cut, high, low):
    parts = split(value)
    high[0:HID, cut] = parts[0]
    low[0:HID, cut] = parts[1]


def finish_planes(high, low):
    high[HID:, :] = unit_row()
    low[HID:, :] = jnp.zeros((16, FLAT), jnp.bfloat16)


def shifted(taps, first_row, rows, first, count, shift):
    return beside(
        [taps[first_row : first_row + rows, plane(first + i + shift)] for i in range(count)]
    )


def nine(taps, half, first, count, sign):
    return jnp.concatenate(
        [shifted(taps, 144 * half, 144, first, count, sign * (a - 1)) for a in range(3)], axis=0
    )


def three(taps, first, count, sign):
    return jnp.concatenate(
        [shifted(taps, 0, HID, first, count, sign * shift) for shift in (-1, 1, 0)]
        + [shifted(taps, HID, 16, first, count, 0)],
        axis=0,
    )


def stack_logits(whole, x, taps):
    for e in range(3):
        for half, part_of in enumerate(split(turn(whole, e - 1))):
            taps[144 * half + 48 * e : 144 * half + 48 * e + 48, plane(x)] = part_of


def stack_field(field, taps):
    for x in range(PLANES):
        whole = field[x, 0:48, :]
        for e in range(3):
            for half, part_of in enumerate(split(turn(whole, 1 - e))):
                taps[144 * half + 48 * e : 144 * half + 48 * e + 48, plane(x)] = part_of


def network(field, fwd1, fwd2, hidden, weights, u_taps, h_hi, h_lo, work):
    stack_field(field, u_taps)
    finish_planes(h_hi, h_lo)
    for pair in range(4):
        cut = slice(pair * 256, pair * 256 + 256)
        taps = (nine(u_taps, 0, 2 * pair, 2, 1), nine(u_taps, 1, 2 * pair, 2, 1))
        value = jnp.tanh(dot_stacked(fwd1, taps))
        hidden[:, cut] = value
        stack_planes(value, cut, h_hi, h_lo)
    for pair in range(4):
        cut = slice(pair * 256, pair * 256 + 256)
        work[:, cut] = dot_stacked(fwd2, (three(h_hi, 2 * pair, 2, 1), three(h_lo, 2 * pair, 2, 1)))
    for x in range(PLANES):
        total = work[LOG : 2 * LOG, plane(x)]
        total = total + turn(work[0:LOG, plane(x)], 1) + turn(work[2 * LOG : 3 * LOG, plane(x)], -1)
        weights[:, plane(x)] = jax.nn.sigmoid(total)


def around(field, x, direction, sign):
    if direction == 0:
        return [field[(x + sign) % PLANES, m * REACH + RIM : m * REACH + RIM + SLAB, :] for m in range(3)]
    if direction == 1:
        first = RIM + sign
        return [field[x, m * REACH + first : m * REACH + first + SLAB, :] for m in range(3)]
    return [turn(field[x, m * REACH + RIM : m * REACH + RIM + SLAB, :], -sign) for m in range(3)]


def advected(field, weights, x):
    center = around(field, x, 0, 0)
    total = [jnp.zeros((SLAB, DEPTH), jnp.float32)] * 3
    for d in range(3):
        ahead = around(field, x, d, 1)
        behind = around(field, x, d, -1)
        plus = 0.5 * (center[d] + ahead[d])
        minus = 0.5 * (behind[d] + center[d])
        rate_up = weights[2 * d * SLAB : (2 * d + 1) * SLAB, plane(x)]
        rate_low = weights[(2 * d + 1) * SLAB : (2 * d + 2) * SLAB, plane(x)]
        for m in range(3):
            upper = center[m] + rate_up * (ahead[m] - center[m])
            lower = center[m] + rate_low * (behind[m] - center[m])
            total[m] = total[m] + plus * upper - minus * lower
    return [center[m] - KAPPA * total[m] for m in range(3)]


ROOT = math.sqrt(0.5)


def to_modes(x):
    s = [x[i] + x[i + 4] for i in range(4)]
    d = [x[i] - x[i + 4] for i in range(4)]
    even, odd = s[0] + s[2], s[1] + s[3]
    up, down = ROOT * (d[1] + d[3]), ROOT * (d[1] - d[3])
    scale = 0.5 * ROOT
    return [
        scale * (even + odd),
        scale * (even - odd),
        0.5 * (d[0] + down),
        0.5 * (up + d[2]),
        0.5 * (s[0] - s[2]),
        0.5 * (s[1] - s[3]),
        0.5 * (d[0] - down),
        0.5 * (up - d[2]),
    ]


def from_modes(v):
    even, odd = 0.5 * ROOT * (v[0] + v[1]), 0.5 * ROOT * (v[0] - v[1])
    cos, sin = 0.5 * v[4], 0.5 * v[5]
    e = [even + cos, odd + sin, even - cos, odd - sin]
    across, along = 0.5 * ROOT * (v[2] - v[6]), 0.5 * ROOT * (v[3] + v[7])
    o = [0.5 * (v[2] + v[6]), along + across, 0.5 * (v[3] - v[7]), along - across]
    return [e[i] + o[i] for i in range(4)] + [e[i] - o[i] for i in range(4)]


def lane_groups(size):
    return lax.broadcasted_iota(jnp.int32, (size, DEPTH), 1) // BAND


def scatter_modes(source, rows, out):
    groups = lane_groups(rows)
    for p in range(4):
        for g in range(4):
            total = None
            for f in range(2):
                for t in range(2):
                    slot = 2 * f + t
                    value = turn(source(f, 2 * p + t), BAND * (slot - g))
                    total = value if total is None else jnp.where(groups == slot, value, total)
            if len(out.shape) == 3:
                out[p * 4 + g] = total
            else:
                for i in range(out.shape[1]):
                    out[p * 4 + g, i] = total[2 * i : 2 * i + 2]


def gather_modes(recv, f, k, first, rows):
    groups = lane_groups(rows)
    slot = 2 * f + k % 2
    total = None
    for g in range(4):
        value = turn(recv[(k // 2) * 4 + g, first : first + rows, :], BAND * (g - slot))
        total = value if total is None else jnp.where(groups == g, value, total)
    return total


def first_kernel_body(
    recv, fwd1, fwd2, to_z, out, hidden, weights, u_taps, h_hi, h_lo, work, modes
):
    network(recv, fwd1, fwd2, hidden, weights, u_taps, h_hi, h_lo, work)
    table = to_z[...]
    moved_field = [jnp.concatenate(advected(recv, weights, x), axis=0) for x in range(PLANES)]
    for f in range(2):
        planes = moved_field if f == 0 else [recv[x, 40:64, :] for x in range(PLANES)]
        for k, value in enumerate(to_modes(planes)):
            modes[f, k] = value
    for f in range(2):
        flat = modes[f].reshape(PLANES * 24, DEPTH)
        modes[f] = dot(widened(flat), table).reshape(PLANES, 24, DEPTH)
    scatter_modes(lambda f, k: modes[f, k], 24, out)


def leray(parts):
    device = lax.axis_index("px") * 2 + lax.axis_index("py")
    pair = device // 4
    group = device % 4
    lane = lax.broadcasted_iota(jnp.int32, (ROWS, DEPTH), 1)
    row = lax.broadcasted_iota(jnp.int32, (ROWS, DEPTH), 0)
    odd_x = (lane // BAND) % 2
    odd_z = (lane // 16) % 2
    number_z = 16 * group + lane % 16
    top_x = (odd_x == 1) & (pair == 0)
    top_y = row == ROWS // 2
    top_z = (odd_z == 1) & (number_z == 0)
    number_y = row % (ROWS // 2)
    real = lambda value: value.astype(jnp.float32)
    rate_x = real(jnp.where(odd_x == 1, -pair, pair))
    rate_y = real(jnp.where(row < ROWS // 2, number_y, -number_y))
    rate_z = real(jnp.where(odd_z == 1, -number_z, number_z))
    high_x = real(jnp.where(top_x, PLANES // 2, 0))
    high_y = real(jnp.where(top_y, ROWS // 2, 0))
    high_z = real(jnp.where(top_z, DEPTH // 2, 0))
    size = rate_x * rate_x + rate_y * rate_y + rate_z * rate_z
    size = size + high_x * high_x + high_y * high_y + high_z * high_z
    inverse = 1.0 / jnp.maximum(size, 1.0)

    def slope_x(value):
        return rate_x * jnp.where(odd_x == 1, turn(value, BAND), turn(value, -BAND))

    def slope_y(value):
        return rate_y * jnp.concatenate([value[ROWS // 2 :], value[: ROWS // 2]], axis=0)

    def slope_z(value):
        return rate_z * jnp.where(odd_z == 1, turn(value, 16), turn(value, -16))

    spread = (slope_x(parts[0]) + slope_y(parts[1]) + slope_z(parts[2])) * inverse
    high = (high_x * parts[0] + high_y * parts[1] + high_z * parts[2]) * inverse
    return (
        parts[0] + slope_x(spread) - high_x * high,
        parts[1] + slope_y(spread) - high_y * high,
        parts[2] + slope_z(spread) - high_z * high,
    )


def beside(parts):
    return jnp.concatenate(parts, axis=1)


def part(value, m):
    return value[:, m * DEPTH : (m + 1) * DEPTH]


def two_halves(first, second):
    low = lax.broadcasted_iota(jnp.int32, first.shape, 1) < DEPTH // 2
    return jnp.where(low, first, turn(second, DEPTH // 2))


def both_kernel(recv, table_in, table_out, out):
    data = beside([recv[:, 8 * m : 8 * m + 8, :].reshape(ROWS, DEPTH) for m in range(3)])
    modes = dot_wide(table_in, split(data))
    fixed = beside(leray([part(modes, m) for m in range(3)]))
    back = dot_wide(table_out, split(fixed))
    for m in range(3):
        whole = part(back, m)
        out[:, 8 * m : 8 * m + 8, :] = whole[:ROWS].reshape(16, SLAB, DEPTH)
        rim = two_halves(whole[ROWS : ROWS + 32], whole[ROWS + 32 :])
        for device in range(16):
            out[device, 24 + 2 * m : 26 + 2 * m, :] = rim[2 * device : 2 * device + 2]
    out[:, 30:32, :] = jnp.zeros((16, 2, DEPTH), jnp.float32)


def one_kernel(recv, table_in, table_out, out, data):
    for device in range(16):
        for m in range(3):
            for i in range(2):
                first = 4 * device + 2 * i
                data[m, first : first + 2, :] = recv[device, 2 * m + i]
            data[m, 64 + 2 * device : 66 + 2 * device, :] = recv[device, 6 + m]
    modes = dot_wide(table_in, split(beside([data[m] for m in range(3)])))
    low, high = modes[:ROWS], modes[ROWS:]
    fixed = beside(leray([part(low, m) + turn(part(high, m), DEPTH // 2) for m in range(3)]))
    back = dot_wide(table_out, split(fixed))
    for m in range(3):
        whole = two_halves(part(back, m)[:64], part(back, m)[64:])
        for device in range(16):
            out[device, m] = whole[4 * device : 4 * device + 4]


def pullback(field, grad, hidden, weights, back2, back1, l_taps, p_hi, p_lo, work, slope, middle, late):
    slope[...] = jnp.zeros_like(slope)
    row = lax.broadcasted_iota(jnp.int32, (SLAB, DEPTH), 0)
    stay = [None] * PLANES
    pushed = {}
    for x in range(PLANES):
        center = around(field, x, 0, 0)
        source = [-KAPPA * grad[x, m * SLAB : (m + 1) * SLAB, :] for m in range(3)]
        own = [grad[x, m * SLAB : (m + 1) * SLAB, :] for m in range(3)]
        logits = []
        for d in range(3):
            ahead = around(field, x, d, 1)
            behind = around(field, x, d, -1)
            plus = 0.5 * (center[d] + ahead[d])
            minus = 0.5 * (behind[d] + center[d])
            rate_up = weights[2 * d * SLAB : (2 * d + 1) * SLAB, plane(x)]
            rate_low = weights[(2 * d + 1) * SLAB : (2 * d + 2) * SLAB, plane(x)]
            grad_up = grad_low = grad_plus = grad_minus = None
            to_ahead, to_behind = [], []
            add = lambda total, term: term if total is None else total + term
            for m in range(3):
                gap_up = ahead[m] - center[m]
                gap_low = behind[m] - center[m]
                grad_plus = add(grad_plus, source[m] * (center[m] + rate_up * gap_up))
                grad_minus = add(grad_minus, -source[m] * (center[m] + rate_low * gap_low))
                grad_up = add(grad_up, source[m] * gap_up)
                grad_low = add(grad_low, -source[m] * gap_low)
                push_up = source[m] * plus
                push_low = -source[m] * minus
                to_ahead.append(push_up * rate_up)
                to_behind.append(push_low * rate_low)
                own[m] = own[m] + (push_up - to_ahead[m]) + (push_low - to_behind[m])
            own[d] = own[d] + 0.5 * (grad_plus + grad_minus)
            to_ahead[d] = to_ahead[d] + 0.5 * grad_plus
            to_behind[d] = to_behind[d] + 0.5 * grad_minus
            logits.append(grad_up * plus * rate_up * (1.0 - rate_up))
            logits.append(grad_low * minus * rate_low * (1.0 - rate_low))
            for m in range(3):
                if d == 0:
                    pushed[x, m, 1], pushed[x, m, -1] = to_ahead[m], to_behind[m]
                elif d == 1:
                    first = m * REACH + RIM
                    down = pltpu.roll(to_ahead[m], 1, 0)
                    up = pltpu.roll(to_behind[m], SLAB - 1, 0)
                    own[m] = own[m] + jnp.where(row > 0, down, 0.0) + jnp.where(row < SLAB - 1, up, 0.0)
                    slope[x, first + SLAB : first + SLAB + 1, :] = down[0:1]
                    slope[x, first - 1 : first, :] = up[SLAB - 1 :]
                else:
                    own[m] = own[m] + turn(to_ahead[m], 1) + turn(to_behind[m], -1)
        stay[x] = own
        whole = jnp.concatenate(logits, axis=0)
        stack_logits(whole, x, l_taps)
    for x in range(PLANES):
        for m in range(3):
            value = stay[x][m] + pushed[(x - 1) % PLANES, m, 1] + pushed[(x + 1) % PLANES, m, -1]
            slope[x, m * REACH + RIM : m * REACH + RIM + SLAB, :] = value
    for pair in range(4):
        cut = slice(pair * 256, pair * 256 + 256)
        taps = (nine(l_taps, 0, 2 * pair, 2, -1), nine(l_taps, 1, 2 * pair, 2, -1))
        value = dot_stacked(back2, taps)
        value = value * (1.0 - hidden[:, cut] * hidden[:, cut])
        stack_planes(value, cut, p_hi, p_lo)
    finish_planes(p_hi, p_lo)
    middle()
    for pair in range(4):
        cut = slice(pair * 256, pair * 256 + 256)
        work[:, cut] = dot_stacked(back1, (three(p_hi, 2 * pair, 2, -1), three(p_lo, 2 * pair, 2, -1)))
    late()
    for x in range(PLANES):
        total = slope[x, 0:40, :] + work[48:88, plane(x)]
        slope[x, 0:40, :] = total + turn(work[0:40, plane(x)], -1) + turn(work[96:136, plane(x)], 1)


def kernel_sums(taps, high, low, sign):
    return dot_stacked(taps, (three(high, 0, PLANES, sign), three(low, 0, PLANES, sign)), NT)


def second_kernel_body(
    recv, fwd1, fwd2, back2, back1, to_z, from_z,
    out, sums,
    field, hidden, grad, modes, rows6, weights, work, slope,
    u_taps, h_hi, h_lo, l_taps, p_hi, p_lo,
):
    back_z = from_z[...]
    for k in range(PLANES):
        modes[k, 0:32, :] = gather_modes(recv, 0, k, 0, 32)
        modes[k, 32:40, :] = gather_modes(recv, 1, k, 24, 8)
    flat = dot(widened(modes[...].reshape(PLANES * 40, DEPTH)), back_z)
    modes[...] = flat.reshape(PLANES, 40, DEPTH)
    for x, value in enumerate(from_modes([modes[k] for k in range(PLANES)])):
        for m in range(3):
            first = m * REACH
            field[x, first : first + RIM, :] = value[24 + 2 * m : 26 + 2 * m]
            field[x, first + RIM : first + RIM + SLAB, :] = value[8 * m : 8 * m + 8]
            field[x, first + RIM + SLAB : first + REACH, :] = value[32 + 2 * m : 34 + 2 * m]
        field[x, 36:37, :] = jnp.ones((1, DEPTH), jnp.float32)
        field[x, 37:48, :] = jnp.zeros((11, DEPTH), jnp.float32)
    for k in range(PLANES):
        grad[k] = gather_modes(recv, 1, k, 0, 24)
    flat = dot(widened(grad[...].reshape(PLANES * 24, DEPTH)), back_z)
    flat = flat.reshape(PLANES, 24, DEPTH)
    for x, value in enumerate(from_modes([flat[k] for k in range(PLANES)])):
        grad[x] = value
    network(field, fwd1, fwd2, hidden, weights, u_taps, h_hi, h_lo, work)

    def middle():
        sums[0:144, :] = kernel_sums(l_taps, h_hi, h_lo, 1)

    def late():
        sums[144:, :] = kernel_sums(u_taps, p_hi, p_lo, -1)

    pullback(
        field, grad, hidden, weights, back2, back1, l_taps, p_hi, p_lo, work, slope, middle, late
    )
    for k, value in enumerate(to_modes([slope[x, 0:40, :] for x in range(PLANES)])):
        modes[k] = value
    flat = dot(widened(modes[...].reshape(PLANES * 40, DEPTH)), to_z[...])
    modes[...] = flat.reshape(PLANES, 40, DEPTH)
    for h in range(2):
        for k in range(PLANES):
            for m in range(3):
                first = m * REACH + RIM + 4 * h
                rows6[h, k, 4 * m : 4 * m + 4, :] = modes[k, first : first + 4, :]
                first = m * REACH + (RIM + SLAB) * h
                rows6[h, k, 12 + 2 * m : 14 + 2 * m, :] = modes[k, first : first + 2, :]
            rows6[h, k, 18:24, :] = jnp.zeros((6, DEPTH), jnp.float32)
    scatter_modes(lambda h, k: rows6[h, k], 24, out)


def third_kernel_body(
    recv, field, hidden, weights, u_taps, h_hi, h_lo, back2, back1, from_z, old_sums,
    spread_t, mask, lift,
    out,
    flat, grad, modes, l_taps, p_hi, p_lo, work, slope, sums, pieces,
):
    back_z = from_z[...]
    flat[...] = jnp.zeros_like(flat)
    for device in range(16):
        for m in range(3):
            flat[device, 4 * m : 4 * m + 4, :] = recv[device, m]
    for h in range(2):
        for k in range(PLANES):
            modes[k] = gather_modes(flat, h, k, 0, 16)
        moved_back = dot(widened(modes[...].reshape(PLANES * 16, DEPTH)), back_z)
        modes[...] = moved_back.reshape(PLANES, 16, DEPTH)
        for x, value in enumerate(from_modes([modes[k] for k in range(PLANES)])):
            for m in range(3):
                grad[x, m * SLAB + 4 * h : m * SLAB + 4 * h + 4, :] = value[m * 4 : m * 4 + 4, :]

    def middle():
        sums[0:144, :] = old_sums[0:144, :] + kernel_sums(l_taps, h_hi, h_lo, 1)
        sums[144:, :] = old_sums[144:, :] + kernel_sums(u_taps, p_hi, p_lo, -1)

    def late():
        pack_grads(sums, spread_t, mask, lift, pieces)

    pullback(
        field, grad, hidden, weights, back2, back1, l_taps, p_hi, p_lo, work, slope, middle, late
    )
    for x in range(PLANES):
        out[x, 0:36, :] = slope[x, 0:36, :]
    for x in range(PLANES):
        out[x, 36:72, :] = pieces[0:36, :]


def pack_grads(sums, spread_t, mask, lift, pieces):
    whole = split(sums[...])
    empty = jnp.zeros((32, 512 - DEEP), jnp.float32)
    rows = []
    for b in range(3):
        rows.append(dot(spread_t[...], whole[0] * mask[b]) + dot(spread_t[...], whole[1] * mask[b]))
        rows.append(empty)
    placed = dot(stacked(beside(rows)), lift[...])
    placed = placed[:32] + placed[32:]
    pieces[0:28, :] = placed[0:28, 0:128]
    total = placed[0:8, 128:]
    for i in range(1, 4):
        total = total + turn(placed[8 * i : 8 * i + 8, 128:], 16 * i)
    pieces[28:36, :] = total


def fold_kernel(recv, main, edge, ext):
    ext[...] = jnp.zeros_like(ext)
    total = None
    for q in range(PLANES):
        for m in range(3):
            ext[m, 8 * q + 6 : 8 * q + 18, :] += recv[q, m * REACH : (m + 1) * REACH, :]
        block = recv[q, 36:72, :]
        total = block if total is None else total + block
    for m in range(3):
        main[m, 0] = ext[m, 8:72, :]
        edge[m * 8 : m * 8 + 2, :] = ext[m, 72:74, :]
        edge[m * 8 + 2 : m * 8 + 4, :] = ext[m, 6:8, :]
        edge[m * 8 + 4 : m * 8 + 8, :] = jnp.zeros((4, DEPTH), jnp.float32)
    edge[24:60, :] = total
    edge[60:64, :] = jnp.zeros((4, DEPTH), jnp.float32)


def last_kernel(main, edge, other, out, first, end1, second, end2, turned):
    for m in range(3):
        out[m, 0] = main[m, 0]
        out[m, 0, 0:2, :] += other[m * 8 : m * 8 + 2, :]
        out[m, 0, 62:64, :] += other[m * 8 + 2 : m * 8 + 4, :]
    grads = edge[24:64, :] + other[24:64, :]
    for slot in range(8):
        turned[slot] = turn(grads, -16 * slot)
    for b in range(3):
        for a in range(3):
            for e in range(3):
                for i in range(9):
                    row = e * 6 + i if i < 6 else 18 + e * 3 + i - 6
                    slot = 3 * b + a
                    slot, inner = (slot, row) if slot < 8 else (row // 8, 28 + row % 8)
                    line = turned[slot, inner, 0:16]
                    if i < 6:
                        second[i * 9 + a * 3 + b, e, :] = line
                    else:
                        first[(i - 6) * 9 + a * 3 + b, e, :] = line
    end1[...] = turned[1, 27:28, 0:16]
    for o in range(COEFFS):
        slot, inner = (4, 34 + o) if o < 2 else (5, 26 + o)
        end2[0:1, o : o + 1] = turned[slot, inner : inner + 1, 0:1]


def slab_device(velocity, cotangent, first_kernel, first_bias, second_kernel, second_bias):
    c = constants()
    half = jnp.bfloat16
    f32 = lambda *dims: pltpu.VMEM(dims, jnp.float32)
    b16 = lambda *dims: pltpu.VMEM(dims, half)
    swap = [(0, 1), (1, 0)]

    other = lax.ppermute(velocity, "py", swap)
    packed = call(
        pack_kernel, shape(PLANES, 64, DEPTH), (velocity, cotangent), [f32(3, 80, DEPTH)], room=4
    )
    packed = call(rim_kernel, shape(PLANES, 64, DEPTH), (packed, other), room=4)
    recv = lax.all_to_all(packed, "px", 0, 0)

    fwd2, fwd1, back2, back1, to_z = call(
        weights_kernel,
        [
            shape(288, DEEP, kind=half),
            shape(2 * HID, STACK, kind=half),
            shape(2 * HID, STACK, kind=half),
            shape(288, DEEP, kind=half),
            shape(3 * DEPTH, DEPTH, kind=half),
        ],
        (
            jnp.transpose(first_kernel, (1, 2, 3, 4, 0)).reshape(27, 3, CHANNELS),
            jnp.transpose(second_kernel, (0, 2, 3, 4, 1)).reshape(54, 3, CHANNELS),
            first_bias.reshape(1, CHANNELS),
            second_bias.reshape(1, COEFFS),
            c["to_z"],
        ),
        [
            f32(3, 96, CHANNELS),
            f32(27, 3, CHANNELS),
            f32(54, 3, CHANNELS),
            f32(1, CHANNELS),
            f32(1, COEFFS),
            pltpu.SemaphoreType.DMA((4,)),
        ],
        away=(0, 1, 2, 3),
    )

    near = lambda rows: [b16(rows, FLAT), b16(rows, FLAT)]
    stacks = near(288)[:1] + near(BROAD) + near(288)[:1] + near(BROAD)
    sent, hidden, weights, *kept = call(
        first_kernel_body,
        [
            shape(16, 24, DEPTH),
            shape(HID, FLAT),
            shape(LOG, FLAT),
            shape(288, FLAT, kind=half),
            shape(BROAD, FLAT, kind=half),
            shape(BROAD, FLAT, kind=half),
        ],
        (recv, fwd1, fwd2, to_z),
        [f32(144, FLAT), f32(2, PLANES, 24, DEPTH)],
    )
    both = ("px", "py")
    moved_modes = lax.all_to_all(sent, both, 0, 0)
    moved_modes = call(both_kernel, shape(16, 32, DEPTH), (moved_modes, c["both_in"], c["both_out"]))
    moved_modes = lax.all_to_all(moved_modes, both, 0, 0)

    sent, sums = call(
        second_kernel_body,
        [shape(16, 9, 2, DEPTH), shape(288, DEEP)],
        (moved_modes, fwd1, fwd2, back2, back1, to_z, c["from_z"]),
        [
            f32(PLANES, 48, DEPTH),
            f32(HID, FLAT),
            f32(PLANES, 24, DEPTH),
            f32(PLANES, 40, DEPTH),
            f32(2, PLANES, 24, DEPTH),
            f32(LOG, FLAT),
            f32(144, FLAT),
            f32(PLANES, 48, DEPTH),
        ]
        + stacks,
    )
    moved_modes = lax.all_to_all(sent, both, 0, 0)
    moved_modes = call(
        one_kernel,
        shape(16, 3, 4, DEPTH),
        (moved_modes, c["one_in"], c["one_out"]),
        [f32(3, 96, DEPTH)],
    )
    moved_modes = lax.all_to_all(moved_modes, both, 0, 0)

    sent = call(
        third_kernel_body,
        shape(PLANES, 72, DEPTH),
        (
            moved_modes, recv, hidden, weights, *kept, back2, back1, c["from_z"], sums,
            c["spread_t"], c["mask"], c["lift"],
        ),
        [f32(16, 16, DEPTH), f32(PLANES, 24, DEPTH), f32(PLANES, 16, DEPTH)]
        + stacks[3:]
        + [
            f32(144, FLAT),
            f32(PLANES, 48, DEPTH),
            f32(288, DEEP),
            f32(36, DEPTH),
        ],
    )
    recv = lax.all_to_all(sent, "px", 0, 0)
    main, edge = call(
        fold_kernel, [shape(3, 1, 64, DEPTH), shape(64, DEPTH)], (recv,), [f32(3, 80, DEPTH)]
    )
    other = lax.ppermute(edge, "py", swap)
    grad_velocity, first, end1, second, end2 = call(
        last_kernel,
        [
            shape(3, 1, 64, DEPTH),
            shape(27, 3, CHANNELS),
            shape(1, CHANNELS),
            shape(54, 3, CHANNELS),
            shape(1, COEFFS),
        ],
        (main, edge, other),
        [f32(8, 40, DEPTH)],
    )
    return (
        grad_velocity,
        jnp.transpose(first.reshape(3, 3, 3, 3, CHANNELS), (4, 0, 1, 2, 3)),
        end1.reshape(CHANNELS),
        jnp.transpose(second.reshape(COEFFS, 3, 3, 3, CHANNELS), (0, 4, 1, 2, 3)),
        end2.reshape(COEFFS),
    )


def fits_slabs(mesh):
    return mesh.shape["px"] == PLANES and mesh.shape["py"] == 2


def solution(mesh):
    return jax.shard_map(
        slab_device if fits_slabs(mesh) else on_device,
        mesh=mesh,
        in_specs=(
            P(None, ("groups", "px"), "py", None),
            P(None, ("groups", "px"), "py", None),
            P(),
            P(),
            P(),
            P(),
        ),
        out_specs=(
            P(None, ("groups", "px"), "py", None),
            P("groups", None, None, None, None),
            P("groups"),
            P("groups", None, None, None, None),
            P("groups"),
        ),
        check_vma=False,
    )
```

```python
import functools
import math

import jax
import jax.numpy as jnp
import numpy as np
from jax import lax
from jax.experimental import pallas as pl
from jax.experimental.pallas import tpu as pltpu
from jax.sharding import PartitionSpec as P

ITERS = 2


KAPPA = 0.25


def padded_2(value, sides, width):
    for axis, dim in sides:
        size, length = (lax.axis_size(axis), value.shape[dim])
        up = [(i, (i + 1) % size) for i in range(size)]
        down = [(j, i) for i, j in up]
        last = lax.slice_in_dim(value, length - width, length, axis=dim)
        initial = lax.slice_in_dim(value, 0, width, axis=dim)
        before = lax.ppermute(last, axis, up)
        after = lax.ppermute(initial, axis, down)
        value = jnp.concatenate([before, value, after], axis=dim)
    return value


def extend(field):
    rimmed = padded_2(field, (("px", 1), ("py", 2)), 1)
    return jnp.concatenate([rimmed[..., -1:], rimmed, rimmed[..., :1]], axis=3)


def across_columns(spectrum):
    return lax.all_to_all(spectrum, "px", split_axis=2, concat_axis=4, tiled=True)


def across_pairs(spectrum):
    return lax.all_to_all(spectrum, "py", split_axis=3, concat_axis=4, tiled=True)


def summed(grads):
    return lax.psum((grads[0], grads[1], grads[2], grads[3]), ("px", "py"))


def all_taps():
    return [
        (shift_x, shift_y, shift_z)
        for shift_x in range(3)
        for shift_y in range(3)
        for shift_z in range(3)
    ]


def gather_conv(padded, kernel):
    size_x = padded.shape[1] - 2
    size_y = padded.shape[2] - 2
    size_z = padded.shape[3] - 2
    stacked = jnp.concatenate(
        [
            padded[:, sx_one : sx_one + size_x, sy_one : sy_one + size_y, sz_one : sz_one + size_z]
            for sx_one, sy_one, sz_one in all_taps()
        ],
        axis=0,
    )
    matrix = jnp.transpose(kernel, (0, 2, 3, 4, 1)).reshape(kernel.shape[0], -1)
    result = jnp.einsum("ok,kxyz->oxyz", matrix, stacked, precision=lax.Precision.HIGHEST)
    return (result, stacked)


def scatter_conv(padded, kernel):
    outputs = kernel.shape[0]
    inputs = kernel.shape[1]
    size_x = padded.shape[1] - 2
    size_y = padded.shape[2] - 2
    size_z = padded.shape[3] - 2
    total = jnp.zeros((outputs, size_x, size_y, size_z), jnp.float32)
    for shift_x in range(3):
        matrix = jnp.transpose(kernel[:, :, shift_x], (0, 2, 3, 1)).reshape(outputs * 9, inputs)
        layer = jnp.einsum(
            "km,mxyz->kxyz",
            matrix,
            padded[:, shift_x : shift_x + size_x],
            precision=lax.Precision.HIGHEST,
        )
        layer = layer.reshape(outputs, 3, 3, size_x, size_y + 2, size_z + 2)
        for shift_y in range(3):
            for shift_z in range(3):
                total = (
                    total
                    + layer[
                        :,
                        shift_y,
                        shift_z,
                        :,
                        shift_y : shift_y + size_y,
                        shift_z : shift_z + size_z,
                    ]
                )
    return total


def flipped(kernel):
    return jnp.transpose(kernel[:, :, ::-1, ::-1, ::-1], (1, 0, 2, 3, 4))


def moved(padded, axis_dim, offset_cells):
    index = [slice(None), slice(1, -1), slice(1, -1), slice(1, -1)]
    index[axis_dim] = slice(1 + offset_cells, padded.shape[axis_dim] - 1 + offset_cells)
    return padded[tuple(index)]


def advect(padded, weights):
    center = moved(padded, 1, 0)
    total = jnp.zeros_like(center)
    for direction in range(3):
        ahead = moved(padded, direction + 1, 1)
        behind = moved(padded, direction + 1, -1)
        vplus = 0.5 * (center[direction] + ahead[direction])
        vminus = 0.5 * (behind[direction] + center[direction])
        upper = center + weights[2 * direction] * (ahead - center)
        lower = center + weights[2 * direction + 1] * (behind - center)
        total = total + vplus * upper - vminus * lower
    return total


def advect_back(padded, weights_pad, source_pad):
    center = moved(padded, 1, 0)
    source = moved(source_pad, 1, 0)
    weights = moved(weights_pad, 1, 0)
    grad_field = jnp.zeros_like(center)
    fluxes = []
    parts = []
    for direction in range(3):
        ahead = moved(padded, direction + 1, 1)
        behind = moved(padded, direction + 1, -1)
        vplus = 0.5 * (center[direction] + ahead[direction])
        vminus = 0.5 * (behind[direction] + center[direction])
        rate_up = weights[2 * direction]
        rate_low = weights[2 * direction + 1]
        rate_before = moved(weights_pad[2 * direction : 2 * direction + 1], direction + 1, -1)[0]
        rate_after = moved(weights_pad[2 * direction + 1 : 2 * direction + 2], direction + 1, 1)[0]
        source_before = moved(source_pad, direction + 1, -1)
        source_after = moved(source_pad, direction + 1, 1)
        upper = center + rate_up * (ahead - center)
        lower = center + rate_low * (behind - center)
        upper_before = behind + rate_before * (center - behind)
        lower_after = ahead + rate_after * (center - ahead)
        grad_field = grad_field + source * (vplus * (1.0 - rate_up) - vminus * (1.0 - rate_low))
        grad_field = (
            grad_field + vminus * rate_before * source_before - vplus * rate_after * source_after
        )
        fluxes.append(
            0.5
            * (
                jnp.sum(source * upper, 0)
                - jnp.sum(source * lower, 0)
                + jnp.sum(source_before * upper_before, 0)
                - jnp.sum(source_after * lower_after, 0)
            )
        )
        parts.append(jnp.sum(source * vplus * (ahead - center), 0))
        parts.append(-jnp.sum(source * vminus * (behind - center), 0))
    return (grad_field + jnp.stack(fluxes), jnp.stack(parts))


def tables(count):
    index = jnp.arange(count, dtype=jnp.int32)
    phase = index[:, None] * index[None, :] % count
    angle = phase.astype(jnp.float32) * (2.0 * math.pi / count)
    return (jnp.cos(angle), jnp.sin(angle))


def mix(form, data, table):
    return jnp.einsum(form, data, table, precision=lax.Precision.HIGHEST)


def waves(start, count, total):
    index = start + jnp.arange(count, dtype=jnp.int32)
    return jnp.where(index < total // 2, index, index - total).astype(jnp.float32)


def project(field):
    depth = field.shape[3]
    cos_z, sin_z = tables(depth)
    real_z = mix("cxyz,zk->cxky", field, cos_z)
    imag_z = -mix("cxyz,zk->cxky", field, sin_z)
    spectrum = across_pairs(jnp.stack([real_z, imag_z]))
    span_y = spectrum.shape[4]
    cos_y, sin_y = tables(span_y)
    real_y = mix("cxky,yq->cqkx", spectrum[0], cos_y) + mix("cxky,yq->cqkx", spectrum[1], sin_y)
    imag_y = mix("cxky,yq->cqkx", spectrum[1], cos_y) - mix("cxky,yq->cqkx", spectrum[0], sin_y)
    spectrum = across_columns(jnp.stack([real_y, imag_y]))
    span_x = spectrum.shape[4]
    cos_x, sin_x = tables(span_x)
    real_x = mix("cqkx,xp->cqkp", spectrum[0], cos_x) + mix("cqkx,xp->cqkp", spectrum[1], sin_x)
    imag_x = mix("cqkx,xp->cqkp", spectrum[1], cos_x) - mix("cqkx,xp->cqkp", spectrum[0], sin_x)
    rows_y = spectrum.shape[2]
    rows_z = spectrum.shape[3]
    wave_y = waves(lax.axis_index("px") * rows_y, rows_y, span_y)[:, None, None]
    wave_z = waves(lax.axis_index("py") * rows_z, rows_z, depth)[None, :, None]
    wave_x = waves(0, span_x, span_x)[None, None, :]
    size = jnp.maximum(wave_x * wave_x + wave_y * wave_y + wave_z * wave_z, 1.0)
    vectors = jnp.stack(jnp.broadcast_arrays(wave_x, wave_y, wave_z))
    real_x = real_x - vectors * (
        (wave_x * real_x[0] + wave_y * real_x[1] + wave_z * real_x[2]) / size
    )
    imag_x = imag_x - vectors * (
        (wave_x * imag_x[0] + wave_y * imag_x[1] + wave_z * imag_x[2]) / size
    )
    back_real = (mix("cqkp,px->cxkq", real_x, cos_x) - mix("cqkp,px->cxkq", imag_x, sin_x)) / span_x
    back_imag = (mix("cqkp,px->cxkq", imag_x, cos_x) + mix("cqkp,px->cxkq", real_x, sin_x)) / span_x
    spectrum = across_columns(jnp.stack([back_real, back_imag]))
    rows_real = (
        mix("cxkq,qy->cxyk", spectrum[0], cos_y) - mix("cxkq,qy->cxyk", spectrum[1], sin_y)
    ) / span_y
    rows_imag = (
        mix("cxkq,qy->cxyk", spectrum[1], cos_y) + mix("cxkq,qy->cxyk", spectrum[0], sin_y)
    ) / span_y
    spectrum = across_pairs(jnp.stack([rows_real, rows_imag]))
    return (
        mix("cxyk,kz->cxyz", spectrum[0], cos_z) - mix("cxyk,kz->cxyz", spectrum[1], sin_z)
    ) / depth


def forward_state(field, first_kernel, first_bias, second_kernel, second_bias):
    padded = extend(field)
    first_out, field_taps = gather_conv(padded, first_kernel)
    hidden = jnp.tanh(first_out + first_bias[:, None, None, None])
    weights = jax.nn.sigmoid(
        scatter_conv(extend(hidden), second_kernel) + second_bias[:, None, None, None]
    )
    return (padded, hidden, weights, field_taps)


def backward_step(state, upstream, first_kernel, second_kernel):
    padded, hidden, weights, field_taps = state
    moved_grad = project(upstream)
    source = -KAPPA * moved_grad
    stacked = extend(jnp.concatenate([source, weights], axis=0))
    grad_field, grad_weights = advect_back(padded, stacked[3:], stacked[:3])
    grad_field = grad_field + moved_grad
    grad_logits = grad_weights * weights * (1.0 - weights)
    logits_pad = extend(grad_logits)
    grad_hidden, logit_taps = gather_conv(logits_pad, flipped(second_kernel))
    product = jnp.einsum("kxyz,mxyz->km", logit_taps, hidden, precision=lax.Precision.HIGHEST)
    product = product.reshape(3, 3, 3, second_kernel.shape[0], second_kernel.shape[1])
    grad_second = jnp.transpose(product[::-1, ::-1, ::-1], (3, 4, 0, 1, 2))
    grad_second_bias = jnp.sum(grad_logits, axis=(1, 2, 3))
    grad_pre = grad_hidden * (1.0 - hidden * hidden)
    pre_pad = extend(grad_pre)
    grad_field = grad_field + scatter_conv(pre_pad, flipped(first_kernel))
    first_product = jnp.einsum(
        "oxyz,kxyz->ok", grad_pre, field_taps, precision=lax.Precision.HIGHEST
    )
    first_product = first_product.reshape(first_kernel.shape[0], 3, 3, 3, first_kernel.shape[1])
    grad_first = jnp.transpose(first_product, (0, 4, 1, 2, 3))
    grad_first_bias = jnp.sum(grad_pre, axis=(1, 2, 3))
    return (grad_field, (grad_first, grad_first_bias, grad_second, grad_second_bias))


def on_device(velocity, cotangent, first_kernel, first_bias, second_kernel, second_bias):
    field = velocity
    fields = [velocity]
    saved = []
    for section in range(ITERS):
        state = forward_state(field, first_kernel, first_bias, second_kernel, second_bias)
        saved.append(state)
        field = project(field - KAPPA * advect(state[0], state[2]))
        fields.append(field)
    upstream = cotangent
    totals = None
    for section in reversed(range(ITERS)):
        state = saved[section]
        upstream, grads = backward_step(state, upstream, first_kernel, second_kernel)
        grads = summed(grads)
        if totals is None:
            totals = grads
        else:
            totals = tuple((older + newer for older, newer in zip(totals, grads)))
    return (upstream, totals[0], totals[1], totals[2], totals[3])


SLAB = 8
RIM = 2
REACH = SLAB + 2 * RIM
WIDE = SLAB + 2
PLANES = 8
DEPTH = 128
ROWS = 128
CHANNELS = 16
COEFFS = 6
BAND = 32
HID = CHANNELS * WIDE
LOG = COEFFS * SLAB
STACK = 9 * 48
UNIT = 36
BROAD = HID + 16
DEEP = 3 * HID + 16
PLACE = (0, 2, 1)
FLAT = PLANES * DEPTH
NN = ((1,), (0,))
NT = ((1,), (1,))


def real_basis(count):
    half = count // 2
    angle = 2.0 * np.pi * np.arange(count) / count
    rows = [np.full(count, 1.0 / np.sqrt(count))]
    rows += [np.sqrt(2.0 / count) * np.cos(k * angle) for k in range(1, half)]
    rows += [np.cos(half * angle) / np.sqrt(count)]
    rows += [np.sqrt(2.0 / count) * np.sin(k * angle) for k in range(1, half)]
    return np.stack(rows)


def wide_table(table):
    high, low = halves(table)
    return np.concatenate([high, low, high], axis=1)


def tall_table(table):
    high, low = halves(table)
    return np.concatenate([high, high, low])


def halves(table):
    high = table.astype(np.float32).astype(jnp.bfloat16)
    low = (table - high.astype(np.float64)).astype(np.float32).astype(jnp.bfloat16)
    return high, low


def slab_of(device):
    return (device % 2) * PLANES + device // 2


@functools.cache
def constants():
    basis_z = real_basis(DEPTH)
    order = []
    for group in range(4):
        order += [16 * group + i for i in range(16)] + [64 + 16 * group + i for i in range(16)]
    mode_z = basis_z[order]
    basis_y = real_basis(ROWS)

    def rows(offset, count):
        at = [SLAB * slab_of(j) + offset + i for j in range(16) for i in range(count)]
        return basis_y[:, np.array(at) % ROWS]

    own, half_one, half_two = rows(0, SLAB), rows(0, 4), rows(4, 4)
    before, after = rows(-RIM, RIM), rows(SLAB, RIM)
    both_in = own
    both_out = np.concatenate([own, before, after], axis=1).T
    one_in = np.concatenate(
        [np.concatenate([half_one, before], axis=1), np.concatenate([half_two, after], axis=1)]
    )
    one_out = np.concatenate([half_one, half_two], axis=1).T

    spread = np.zeros((288, 32))
    mask = np.zeros((3, 288, DEEP))
    lanes = np.arange(CHANNELS) * WIDE
    for e in range(3):
        for o in range(COEFFS):
            for q in range(SLAB):
                row = e * 48 + o * SLAB + q
                spread[row, e * COEFFS + o] = 1.0
                for b in range(3):
                    for a in range(3):
                        mask[b, row, a * HID + lanes + q + b] = 1.0
        for m in range(3):
            for r in range(REACH):
                row = 144 + e * 48 + m * REACH + r
                spread[row, 18 + e * 3 + m] = 1.0
                for b in range(3):
                    for a in range(3):
                        if 0 <= r - b < WIDE:
                            mask[b, row, a * HID + lanes + r - b] = 1.0
    spread[144 + 48 + UNIT, 27] = 1.0
    mask[0, 144 + 48 + UNIT, PLACE[1] * HID : (PLACE[1] + 1) * HID] = 1.0
    mask[0, 48:96, 3 * HID] = 1.0
    lift = np.zeros((3, 512, 256))
    for b in range(3):
        for a in range(3):
            lift[b, PLACE[a] * HID + np.arange(HID), 16 * (3 * b + a) + np.arange(HID) // WIDE] = 1.0
    lift[0, 3 * HID, 128 + 64] = 1.0
    lift = lift.reshape(3 * 512, 256)
    half = jnp.bfloat16
    return dict(
        to_z=tall_table(mode_z.T),
        from_z=tall_table(mode_z),
        both_in=wide_table(both_in),
        both_out=wide_table(both_out),
        one_in=wide_table(one_in),
        one_out=wide_table(one_out),
        spread_t=np.concatenate([spread.T, spread.T], axis=1).astype(half),
        mask=mask.astype(half),
        lift=lift.astype(half),
    )


def dot(left, right, dims=NN):
    return lax.dot_general(left, right, (dims, ((), ())), preferred_element_type=jnp.float32)


def split(value):
    high = value.astype(jnp.bfloat16)
    return high, (value - high.astype(jnp.float32)).astype(jnp.bfloat16)


def dot_stacked(left, right, dims=NN):
    rows = left.shape[0] // 2
    main = dot(left[...], right[0], dims)
    return main[:rows] + (main[rows:] + dot(left[0:rows, :], right[1], dims))


def dot_wide(left, right):
    return dot(left[...], jnp.concatenate([right[0], right[0], right[1]], axis=0))


def widened(value):
    high, low = split(value)
    return jnp.concatenate([high, low, high], axis=1)


def stacked(value):
    return jnp.concatenate(split(value), axis=0)


def turn(value, shift):
    shift = shift % value.shape[-1]
    return value if shift == 0 else pltpu.roll(value, shift, value.ndim - 1)


def plane(x):
    x = x % PLANES
    return slice(x * DEPTH, (x + 1) * DEPTH)


def call(kernel, outs, args, scratch=(), room=16, away=()):
    single = not isinstance(outs, (list, tuple))
    vmem = pl.BlockSpec(memory_space=pltpu.VMEM)
    cost = pl.CostEstimate(flops=1, bytes_accessed=1, transcendentals=0) if away else None
    return pl.pallas_call(
        kernel,
        out_shape=outs,
        in_specs=[
            pl.BlockSpec(memory_space=pltpu.HBM) if i in away else vmem for i in range(len(args))
        ],
        out_specs=vmem if single else [vmem] * len(outs),
        scratch_shapes=list(scratch),
        cost_estimate=cost,
        compiler_params=pltpu.CompilerParams(vmem_limit_bytes=room * 2**20),
    )(*args)


def fetch(pairs, sems):
    copies = [pltpu.make_async_copy(src, dst, sems.at[i]) for i, (src, dst) in enumerate(pairs)]
    for copy in copies:
        copy.start()
    return copies


def shape(*dims, kind=jnp.float32):
    return jax.ShapeDtypeStruct(dims, kind)


def counting(size, dim):
    return lax.broadcasted_iota(jnp.int32, size, dim).astype(jnp.float32)


def remainder(value, count):
    return value - count * jnp.floor((value + 0.5) / count)


def band_tables(tall):
    row, col = (0, 1) if tall else (1, 0)
    size = lambda rows, cols: (rows, cols) if tall else (cols, rows)
    where = counting(size(2 * STACK, 96), row)
    to = counting(size(2 * STACK, 96), col)
    first = where - 8.0 * to
    third = to - 54.0
    second = where - STACK - (16.0 * third - 4.0 * remainder(third, 3.0))
    picks = ((to < 54.0) & (first >= 0.0) & (first < 8.0)) | (
        (to >= 54.0) & (to < 81.0) & (second >= 0.0) & (second < 12.0)
    )
    where = counting(size(2 * STACK, HID), row)
    inner = remainder(counting(size(2 * STACK, HID), col), 10.0)
    outer = where - STACK
    offset = jnp.where(
        where < STACK,
        inner - remainder(where, 8.0),
        remainder(remainder(outer, 48.0), 12.0) - inner,
    )
    gap = counting(size(HID, CHANNELS), row) - 10.0 * counting(size(HID, CHANNELS), col)
    lift = (gap >= 0.0) & (gap < 10.0)
    half = jnp.bfloat16
    return picks.astype(jnp.float32).astype(half), offset, lift.astype(jnp.float32).astype(half)


def weights_kernel(
    far1, far2, far3, far4, z_in, fwd2, fwd1, back2, back1, z_out, blocks, taps1, taps2, bias1, bias2, sems
):
    copies = fetch([(far1, taps1), (far2, taps2), (far3, bias1), (far4, bias2)], sems)
    blocks[...] = jnp.zeros_like(blocks)
    z_out[...] = z_in[...]
    spread, offset, lift = band_tables(True)
    spread_t, offset_t, lift_t = band_tables(False)
    for copy in copies:
        copy.wait()
    for b in range(3):
        for a in range(3):
            for e in range(3):
                tap = a * 3 + e
                for o in range(COEFFS):
                    blocks[b, tap * 6 + o, :] = taps2[o * 9 + a * 3 + b, e, :]
                for m in range(3):
                    blocks[b, 54 + tap * 3 + m, :] = taps1[m * 9 + a * 3 + b, e, :]
    tall = [jnp.zeros((2 * STACK, HID), jnp.float32)] * 2
    flat = [jnp.zeros((HID, 2 * STACK), jnp.float32)] * 2
    for b in range(3):
        for half, block in enumerate(split(blocks[b])):
            rows = dot(spread, block).astype(jnp.bfloat16)
            tall[half] = jnp.where(offset == float(b), dot(rows, lift_t), tall[half])
            cols = dot(lift, block, NT).astype(jnp.bfloat16)
            flat[half] = jnp.where(offset_t == float(b), dot(cols, spread_t), flat[half])
    for half in range(2):
        rows, cols = slice(half * 144, half * 144 + 144), slice(half * HID, half * HID + HID)
        for a in range(3):
            first = PLACE[a] * HID
            part = tall[half][a * 144 : a * 144 + 144]
            fwd2[rows, first : first + HID] = part.astype(jnp.bfloat16)
            part = tall[half][STACK + a * 144 : STACK + a * 144 + 144]
            back1[rows, first : first + HID] = part.astype(jnp.bfloat16)
        back2[cols, :] = flat[half][:, :STACK].astype(jnp.bfloat16)
    gap = counting((LOG, COEFFS), 0) - 8.0 * counting((LOG, COEFFS), 1)
    pick = ((gap >= 0.0) & (gap < 8.0)).astype(jnp.float32).astype(jnp.bfloat16)
    second = counting((LOG, 16), 1) < 1.0
    one = split(jnp.broadcast_to(bias1[...], (STACK, CHANNELS)))
    first = counting((HID, STACK), 1) == 4.0 * 48.0 + UNIT
    two = split(jnp.broadcast_to(bias2[...], (16, COEFFS)))
    fwd2[:, 3 * HID :] = jnp.zeros((288, 16), jnp.bfloat16)
    back1[:, 3 * HID :] = jnp.zeros((288, 16), jnp.bfloat16)
    for half in range(2):
        value = jnp.where(first, dot(lift, one[half], NT), flat[half][:, STACK:])
        fwd1[half * HID : half * HID + HID, :] = value.astype(jnp.bfloat16)
        value = jnp.where(second, dot(pick, two[half], NT), 0.0)
        start = half * 144 + LOG
        fwd2[start : start + LOG, 3 * HID :] = value.astype(jnp.bfloat16)


def pack_kernel(fields, out, ext):
    ext[...] = jnp.zeros_like(ext)
    for m in range(3):
        ext[m, 8:72, :] = fields[m, 0]
    for q in range(PLANES):
        for m in range(3):
            out[q, m * REACH : (m + 1) * REACH, :] = ext[m, 8 * q + 6 : 8 * q + 18, :]
            out[q, 40 + 8 * m : 48 + 8 * m, :] = fields[3 + m, 0, 8 * q : 8 * q + 8, :]
        out[q, 36:37, :] = jnp.ones((1, DEPTH), jnp.float32)
        out[q, 37:40, :] = jnp.zeros((3, DEPTH), jnp.float32)


def rim_kernel(packed, other, out):
    out[...] = packed[...]
    for m in range(3):
        out[0, m * REACH : m * REACH + 2, :] = other[m, 0, 62:64, :]
        out[PLANES - 1, m * REACH + 10 : m * REACH + 12, :] = other[m, 0, 0:2, :]


def unit_row():
    row = lax.broadcasted_iota(jnp.int32, (16, FLAT), 0)
    return jnp.where(row == 0, 1.0, 0.0).astype(jnp.bfloat16)


def stack_planes(value, cut, high, low):
    parts = split(value)
    high[0:HID, cut] = parts[0]
    low[0:HID, cut] = parts[1]


def finish_planes(high, low):
    high[HID:, :] = unit_row()
    low[HID:, :] = jnp.zeros((16, FLAT), jnp.bfloat16)


def shifted(taps, first_row, rows, first, count, shift):
    return beside(
        [taps[first_row : first_row + rows, plane(first + i + shift)] for i in range(count)]
    )


def nine(taps, half, first, count, sign):
    return jnp.concatenate(
        [shifted(taps, 144 * half, 144, first, count, sign * (a - 1)) for a in range(3)], axis=0
    )


def three(taps, first, count, sign):
    return jnp.concatenate(
        [shifted(taps, 0, HID, first, count, sign * shift) for shift in (-1, 1, 0)]
        + [shifted(taps, HID, 16, first, count, 0)],
        axis=0,
    )


def stack_logits(whole, x, taps):
    for e in range(3):
        for half, part_of in enumerate(split(turn(whole, e - 1))):
            taps[144 * half + 48 * e : 144 * half + 48 * e + 48, plane(x)] = part_of


def stack_field(field, taps):
    for x in range(PLANES):
        whole = field[x, 0:48, :]
        for e in range(3):
            for half, part_of in enumerate(split(turn(whole, 1 - e))):
                taps[144 * half + 48 * e : 144 * half + 48 * e + 48, plane(x)] = part_of


def network(field, fwd1, fwd2, hidden, weights, u_taps, h_hi, h_lo, work):
    stack_field(field, u_taps)
    finish_planes(h_hi, h_lo)
    for pair in range(4):
        cut = slice(pair * 256, pair * 256 + 256)
        taps = (nine(u_taps, 0, 2 * pair, 2, 1), nine(u_taps, 1, 2 * pair, 2, 1))
        value = jnp.tanh(dot_stacked(fwd1, taps))
        hidden[:, cut] = value
        stack_planes(value, cut, h_hi, h_lo)
    for pair in range(4):
        cut = slice(pair * 256, pair * 256 + 256)
        work[:, cut] = dot_stacked(fwd2, (three(h_hi, 2 * pair, 2, 1), three(h_lo, 2 * pair, 2, 1)))
    for x in range(PLANES):
        total = work[LOG : 2 * LOG, plane(x)]
        total = total + turn(work[0:LOG, plane(x)], 1) + turn(work[2 * LOG : 3 * LOG, plane(x)], -1)
        weights[:, plane(x)] = jax.nn.sigmoid(total)


def around(field, x, direction, sign):
    if direction == 0:
        return [field[(x + sign) % PLANES, m * REACH + RIM : m * REACH + RIM + SLAB, :] for m in range(3)]
    if direction == 1:
        first = RIM + sign
        return [field[x, m * REACH + first : m * REACH + first + SLAB, :] for m in range(3)]
    return [turn(field[x, m * REACH + RIM : m * REACH + RIM + SLAB, :], -sign) for m in range(3)]


def advected(field, weights, x):
    center = around(field, x, 0, 0)
    total = [jnp.zeros((SLAB, DEPTH), jnp.float32)] * 3
    for d in range(3):
        ahead = around(field, x, d, 1)
        behind = around(field, x, d, -1)
        plus = 0.5 * (center[d] + ahead[d])
        minus = 0.5 * (behind[d] + center[d])
        rate_up = weights[2 * d * SLAB : (2 * d + 1) * SLAB, plane(x)]
        rate_low = weights[(2 * d + 1) * SLAB : (2 * d + 2) * SLAB, plane(x)]
        for m in range(3):
            upper = center[m] + rate_up * (ahead[m] - center[m])
            lower = center[m] + rate_low * (behind[m] - center[m])
            total[m] = total[m] + plus * upper - minus * lower
    return [center[m] - KAPPA * total[m] for m in range(3)]


ROOT = math.sqrt(0.5)


def to_modes(x):
    s = [x[i] + x[i + 4] for i in range(4)]
    d = [x[i] - x[i + 4] for i in range(4)]
    even, odd = s[0] + s[2], s[1] + s[3]
    up, down = ROOT * (d[1] + d[3]), ROOT * (d[1] - d[3])
    scale = 0.5 * ROOT
    return [
        scale * (even + odd),
        scale * (even - odd),
        0.5 * (d[0] + down),
        0.5 * (up + d[2]),
        0.5 * (s[0] - s[2]),
        0.5 * (s[1] - s[3]),
        0.5 * (d[0] - down),
        0.5 * (up - d[2]),
    ]


def from_modes(v):
    even, odd = 0.5 * ROOT * (v[0] + v[1]), 0.5 * ROOT * (v[0] - v[1])
    cos, sin = 0.5 * v[4], 0.5 * v[5]
    e = [even + cos, odd + sin, even - cos, odd - sin]
    across, along = 0.5 * ROOT * (v[2] - v[6]), 0.5 * ROOT * (v[3] + v[7])
    o = [0.5 * (v[2] + v[6]), along + across, 0.5 * (v[3] - v[7]), along - across]
    return [e[i] + o[i] for i in range(4)] + [e[i] - o[i] for i in range(4)]


def lane_groups(size):
    return lax.broadcasted_iota(jnp.int32, (size, DEPTH), 1) // BAND


def scatter_modes(source, rows, out):
    groups = lane_groups(rows)
    for p in range(4):
        for g in range(4):
            total = None
            for f in range(2):
                for t in range(2):
                    slot = 2 * f + t
                    value = turn(source(f, 2 * p + t), BAND * (slot - g))
                    total = value if total is None else jnp.where(groups == slot, value, total)
            if len(out.shape) == 3:
                out[p * 4 + g] = total
            else:
                for i in range(out.shape[1]):
                    out[p * 4 + g, i] = total[2 * i : 2 * i + 2]


def gather_modes(recv, f, k, first, rows):
    groups = lane_groups(rows)
    slot = 2 * f + k % 2
    total = None
    for g in range(4):
        value = turn(recv[(k // 2) * 4 + g, first : first + rows, :], BAND * (g - slot))
        total = value if total is None else jnp.where(groups == g, value, total)
    return total


def first_kernel_body(
    recv, fwd1, fwd2, to_z, out, hidden, weights, u_taps, h_hi, h_lo, work, modes
):
    network(recv, fwd1, fwd2, hidden, weights, u_taps, h_hi, h_lo, work)
    table = to_z[...]
    moved_field = [jnp.concatenate(advected(recv, weights, x), axis=0) for x in range(PLANES)]
    for f in range(2):
        planes = moved_field if f == 0 else [recv[x, 40:64, :] for x in range(PLANES)]
        for k, value in enumerate(to_modes(planes)):
            modes[f, k] = value
    for f in range(2):
        flat = modes[f].reshape(PLANES * 24, DEPTH)
        modes[f] = dot(widened(flat), table).reshape(PLANES, 24, DEPTH)
    scatter_modes(lambda f, k: modes[f, k], 24, out)


def leray(parts):
    device = lax.axis_index("px") * 2 + lax.axis_index("py")
    pair = device // 4
    group = device % 4
    lane = lax.broadcasted_iota(jnp.int32, (ROWS, DEPTH), 1)
    row = lax.broadcasted_iota(jnp.int32, (ROWS, DEPTH), 0)
    odd_x = (lane // BAND) % 2
    odd_z = (lane // 16) % 2
    number_z = 16 * group + lane % 16
    top_x = (odd_x == 1) & (pair == 0)
    top_y = row == ROWS // 2
    top_z = (odd_z == 1) & (number_z == 0)
    number_y = row % (ROWS // 2)
    real = lambda value: value.astype(jnp.float32)
    rate_x = real(jnp.where(odd_x == 1, -pair, pair))
    rate_y = real(jnp.where(row < ROWS // 2, number_y, -number_y))
    rate_z = real(jnp.where(odd_z == 1, -number_z, number_z))
    high_x = real(jnp.where(top_x, PLANES // 2, 0))
    high_y = real(jnp.where(top_y, ROWS // 2, 0))
    high_z = real(jnp.where(top_z, DEPTH // 2, 0))
    size = rate_x * rate_x + rate_y * rate_y + rate_z * rate_z
    size = size + high_x * high_x + high_y * high_y + high_z * high_z
    inverse = 1.0 / jnp.maximum(size, 1.0)

    def slope_x(value):
        return rate_x * jnp.where(odd_x == 1, turn(value, BAND), turn(value, -BAND))

    def slope_y(value):
        return rate_y * jnp.concatenate([value[ROWS // 2 :], value[: ROWS // 2]], axis=0)

    def slope_z(value):
        return rate_z * jnp.where(odd_z == 1, turn(value, 16), turn(value, -16))

    spread = (slope_x(parts[0]) + slope_y(parts[1]) + slope_z(parts[2])) * inverse
    high = (high_x * parts[0] + high_y * parts[1] + high_z * parts[2]) * inverse
    return (
        parts[0] + slope_x(spread) - high_x * high,
        parts[1] + slope_y(spread) - high_y * high,
        parts[2] + slope_z(spread) - high_z * high,
    )


def beside(parts):
    return jnp.concatenate(parts, axis=1)


def part(value, m):
    return value[:, m * DEPTH : (m + 1) * DEPTH]


def two_halves(first, second):
    low = lax.broadcasted_iota(jnp.int32, first.shape, 1) < DEPTH // 2
    return jnp.where(low, first, turn(second, DEPTH // 2))


def both_kernel(recv, table_in, table_out, out):
    data = beside([recv[:, 8 * m : 8 * m + 8, :].reshape(ROWS, DEPTH) for m in range(3)])
    modes = dot_wide(table_in, split(data))
    fixed = beside(leray([part(modes, m) for m in range(3)]))
    back = dot_wide(table_out, split(fixed))
    for m in range(3):
        whole = part(back, m)
        out[:, 8 * m : 8 * m + 8, :] = whole[:ROWS].reshape(16, SLAB, DEPTH)
        rim = two_halves(whole[ROWS : ROWS + 32], whole[ROWS + 32 :])
        for device in range(16):
            out[device, 24 + 2 * m : 26 + 2 * m, :] = rim[2 * device : 2 * device + 2]
    out[:, 30:32, :] = jnp.zeros((16, 2, DEPTH), jnp.float32)


def one_kernel(recv, table_in, table_out, out, data):
    for device in range(16):
        for m in range(3):
            for i in range(2):
                first = 4 * device + 2 * i
                data[m, first : first + 2, :] = recv[device, 2 * m + i]
            data[m, 64 + 2 * device : 66 + 2 * device, :] = recv[device, 6 + m]
    modes = dot_wide(table_in, split(beside([data[m] for m in range(3)])))
    low, high = modes[:ROWS], modes[ROWS:]
    fixed = beside(leray([part(low, m) + turn(part(high, m), DEPTH // 2) for m in range(3)]))
    back = dot_wide(table_out, split(fixed))
    for m in range(3):
        whole = two_halves(part(back, m)[:64], part(back, m)[64:])
        for device in range(16):
            out[device, m] = whole[4 * device : 4 * device + 4]


def pullback(field, grad, hidden, weights, back2, back1, l_taps, p_hi, p_lo, work, slope, middle, late):
    slope[...] = jnp.zeros_like(slope)
    row = lax.broadcasted_iota(jnp.int32, (SLAB, DEPTH), 0)
    stay = [None] * PLANES
    pushed = {}
    for x in range(PLANES):
        center = around(field, x, 0, 0)
        source = [-KAPPA * grad[x, m * SLAB : (m + 1) * SLAB, :] for m in range(3)]
        own = [grad[x, m * SLAB : (m + 1) * SLAB, :] for m in range(3)]
        logits = []
        for d in range(3):
            ahead = around(field, x, d, 1)
            behind = around(field, x, d, -1)
            plus = 0.5 * (center[d] + ahead[d])
            minus = 0.5 * (behind[d] + center[d])
            rate_up = weights[2 * d * SLAB : (2 * d + 1) * SLAB, plane(x)]
            rate_low = weights[(2 * d + 1) * SLAB : (2 * d + 2) * SLAB, plane(x)]
            grad_up = grad_low = grad_plus = grad_minus = None
            to_ahead, to_behind = [], []
            add = lambda total, term: term if total is None else total + term
            for m in range(3):
                gap_up = ahead[m] - center[m]
                gap_low = behind[m] - center[m]
                grad_plus = add(grad_plus, source[m] * (center[m] + rate_up * gap_up))
                grad_minus = add(grad_minus, -source[m] * (center[m] + rate_low * gap_low))
                grad_up = add(grad_up, source[m] * gap_up)
                grad_low = add(grad_low, -source[m] * gap_low)
                push_up = source[m] * plus
                push_low = -source[m] * minus
                to_ahead.append(push_up * rate_up)
                to_behind.append(push_low * rate_low)
                own[m] = own[m] + (push_up - to_ahead[m]) + (push_low - to_behind[m])
            own[d] = own[d] + 0.5 * (grad_plus + grad_minus)
            to_ahead[d] = to_ahead[d] + 0.5 * grad_plus
            to_behind[d] = to_behind[d] + 0.5 * grad_minus
            logits.append(grad_up * plus * rate_up * (1.0 - rate_up))
            logits.append(grad_low * minus * rate_low * (1.0 - rate_low))
            for m in range(3):
                if d == 0:
                    pushed[x, m, 1], pushed[x, m, -1] = to_ahead[m], to_behind[m]
                elif d == 1:
                    first = m * REACH + RIM
                    down = pltpu.roll(to_ahead[m], 1, 0)
                    up = pltpu.roll(to_behind[m], SLAB - 1, 0)
                    own[m] = own[m] + jnp.where(row > 0, down, 0.0) + jnp.where(row < SLAB - 1, up, 0.0)
                    slope[x, first + SLAB : first + SLAB + 1, :] = down[0:1]
                    slope[x, first - 1 : first, :] = up[SLAB - 1 :]
                else:
                    own[m] = own[m] + turn(to_ahead[m], 1) + turn(to_behind[m], -1)
        stay[x] = own
        whole = jnp.concatenate(logits, axis=0)
        stack_logits(whole, x, l_taps)
    for x in range(PLANES):
        for m in range(3):
            value = stay[x][m] + pushed[(x - 1) % PLANES, m, 1] + pushed[(x + 1) % PLANES, m, -1]
            slope[x, m * REACH + RIM : m * REACH + RIM + SLAB, :] = value
    for pair in range(4):
        cut = slice(pair * 256, pair * 256 + 256)
        taps = (nine(l_taps, 0, 2 * pair, 2, -1), nine(l_taps, 1, 2 * pair, 2, -1))
        value = dot_stacked(back2, taps)
        value = value * (1.0 - hidden[:, cut] * hidden[:, cut])
        stack_planes(value, cut, p_hi, p_lo)
    finish_planes(p_hi, p_lo)
    middle()
    for pair in range(4):
        cut = slice(pair * 256, pair * 256 + 256)
        work[:, cut] = dot_stacked(back1, (three(p_hi, 2 * pair, 2, -1), three(p_lo, 2 * pair, 2, -1)))
    late()
    for x in range(PLANES):
        total = slope[x, 0:40, :] + work[48:88, plane(x)]
        slope[x, 0:40, :] = total + turn(work[0:40, plane(x)], -1) + turn(work[96:136, plane(x)], 1)


def kernel_sums(taps, high, low, sign):
    return dot_stacked(taps, (three(high, 0, PLANES, sign), three(low, 0, PLANES, sign)), NT)


def second_kernel_body(
    recv, fwd1, fwd2, back2, back1, to_z, from_z,
    out, sums,
    field, hidden, grad, modes, rows6, weights, work, slope,
    u_taps, h_hi, h_lo, l_taps, p_hi, p_lo,
):
    back_z = from_z[...]
    for k in range(PLANES):
        modes[k, 0:32, :] = gather_modes(recv, 0, k, 0, 32)
        modes[k, 32:40, :] = gather_modes(recv, 1, k, 24, 8)
    flat = dot(widened(modes[...].reshape(PLANES * 40, DEPTH)), back_z)
    modes[...] = flat.reshape(PLANES, 40, DEPTH)
    for x, value in enumerate(from_modes([modes[k] for k in range(PLANES)])):
        for m in range(3):
            first = m * REACH
            field[x, first : first + RIM, :] = value[24 + 2 * m : 26 + 2 * m]
            field[x, first + RIM : first + RIM + SLAB, :] = value[8 * m : 8 * m + 8]
            field[x, first + RIM + SLAB : first + REACH, :] = value[32 + 2 * m : 34 + 2 * m]
        field[x, 36:37, :] = jnp.ones((1, DEPTH), jnp.float32)
        field[x, 37:48, :] = jnp.zeros((11, DEPTH), jnp.float32)
    for k in range(PLANES):
        grad[k] = gather_modes(recv, 1, k, 0, 24)
    flat = dot(widened(grad[...].reshape(PLANES * 24, DEPTH)), back_z)
    flat = flat.reshape(PLANES, 24, DEPTH)
    for x, value in enumerate(from_modes([flat[k] for k in range(PLANES)])):
        grad[x] = value
    network(field, fwd1, fwd2, hidden, weights, u_taps, h_hi, h_lo, work)

    def middle():
        sums[0:144, :] = kernel_sums(l_taps, h_hi, h_lo, 1)

    def late():
        sums[144:, :] = kernel_sums(u_taps, p_hi, p_lo, -1)

    pullback(
        field, grad, hidden, weights, back2, back1, l_taps, p_hi, p_lo, work, slope, middle, late
    )
    for k, value in enumerate(to_modes([slope[x, 0:40, :] for x in range(PLANES)])):
        modes[k] = value
    flat = dot(widened(modes[...].reshape(PLANES * 40, DEPTH)), to_z[...])
    modes[...] = flat.reshape(PLANES, 40, DEPTH)
    for h in range(2):
        for k in range(PLANES):
            for m in range(3):
                first = m * REACH + RIM + 4 * h
                rows6[h, k, 4 * m : 4 * m + 4, :] = modes[k, first : first + 4, :]
                first = m * REACH + (RIM + SLAB) * h
                rows6[h, k, 12 + 2 * m : 14 + 2 * m, :] = modes[k, first : first + 2, :]
            rows6[h, k, 18:24, :] = jnp.zeros((6, DEPTH), jnp.float32)
    scatter_modes(lambda h, k: rows6[h, k], 24, out)


def third_kernel_body(
    recv, field, hidden, weights, u_taps, h_hi, h_lo, back2, back1, from_z, old_sums,
    spread_t, mask, lift,
    out,
    flat, grad, modes, l_taps, p_hi, p_lo, work, slope, sums, pieces,
):
    back_z = from_z[...]
    flat[...] = jnp.zeros_like(flat)
    for device in range(16):
        for m in range(3):
            flat[device, 4 * m : 4 * m + 4, :] = recv[device, m]
    for h in range(2):
        for k in range(PLANES):
            modes[k] = gather_modes(flat, h, k, 0, 16)
        moved_back = dot(widened(modes[...].reshape(PLANES * 16, DEPTH)), back_z)
        modes[...] = moved_back.reshape(PLANES, 16, DEPTH)
        for x, value in enumerate(from_modes([modes[k] for k in range(PLANES)])):
            for m in range(3):
                grad[x, m * SLAB + 4 * h : m * SLAB + 4 * h + 4, :] = value[m * 4 : m * 4 + 4, :]

    def middle():
        sums[0:144, :] = old_sums[0:144, :] + kernel_sums(l_taps, h_hi, h_lo, 1)
        sums[144:, :] = old_sums[144:, :] + kernel_sums(u_taps, p_hi, p_lo, -1)

    def late():
        pack_grads(sums, spread_t, mask, lift, pieces)

    pullback(
        field, grad, hidden, weights, back2, back1, l_taps, p_hi, p_lo, work, slope, middle, late
    )
    for x in range(PLANES):
        out[x, 0:36, :] = slope[x, 0:36, :]
    for x in range(PLANES):
        out[x, 36:72, :] = pieces[0:36, :]


def pack_grads(sums, spread_t, mask, lift, pieces):
    whole = split(sums[...])
    empty = jnp.zeros((32, 512 - DEEP), jnp.float32)
    rows = []
    for b in range(3):
        both = jnp.concatenate([whole[0] * mask[b], whole[1] * mask[b]], axis=0)
        rows.append(dot(spread_t[...], both))
        rows.append(empty)
    placed = dot(stacked(beside(rows)), lift[...])
    placed = placed[:32] + placed[32:]
    pieces[0:28, :] = placed[0:28, 0:128]
    total = placed[0:8, 128:]
    for i in range(1, 4):
        total = total + turn(placed[8 * i : 8 * i + 8, 128:], 16 * i)
    pieces[28:36, :] = total


def fold_kernel(recv, main, edge, ext):
    ext[...] = jnp.zeros_like(ext)
    total = None
    for q in range(PLANES):
        for m in range(3):
            ext[m, 8 * q + 6 : 8 * q + 18, :] += recv[q, m * REACH : (m + 1) * REACH, :]
        block = recv[q, 36:72, :]
        total = block if total is None else total + block
    for m in range(3):
        main[m, 0] = ext[m, 8:72, :]
        edge[m * 8 : m * 8 + 2, :] = ext[m, 72:74, :]
        edge[m * 8 + 2 : m * 8 + 4, :] = ext[m, 6:8, :]
        edge[m * 8 + 4 : m * 8 + 8, :] = jnp.zeros((4, DEPTH), jnp.float32)
    edge[24:60, :] = total
    edge[60:64, :] = jnp.zeros((4, DEPTH), jnp.float32)


def last_kernel(main, edge, other, out, first, end1, second, end2, turned):
    for m in range(3):
        out[m, 0] = main[m, 0]
        out[m, 0, 0:2, :] += other[m * 8 : m * 8 + 2, :]
        out[m, 0, 62:64, :] += other[m * 8 + 2 : m * 8 + 4, :]
    grads = edge[24:64, :] + other[24:64, :]
    for slot in range(8):
        turned[slot] = turn(grads, -16 * slot)
    for b in range(3):
        for a in range(3):
            for e in range(3):
                for i in range(9):
                    row = e * 6 + i if i < 6 else 18 + e * 3 + i - 6
                    slot = 3 * b + a
                    slot, inner = (slot, row) if slot < 8 else (row // 8, 28 + row % 8)
                    line = turned[slot, inner, 0:16]
                    if i < 6:
                        second[i * 9 + a * 3 + b, e, :] = line
                    else:
                        first[(i - 6) * 9 + a * 3 + b, e, :] = line
    end1[...] = turned[1, 27:28, 0:16]
    for o in range(COEFFS):
        slot, inner = (4, 34 + o) if o < 2 else (5, 26 + o)
        end2[0:1, o : o + 1] = turned[slot, inner : inner + 1, 0:1]


def slab_device(velocity, cotangent, first_kernel, first_bias, second_kernel, second_bias):
    c = constants()
    half = jnp.bfloat16
    f32 = lambda *dims: pltpu.VMEM(dims, jnp.float32)
    b16 = lambda *dims: pltpu.VMEM(dims, half)
    swap = [(0, 1), (1, 0)]

    other = lax.ppermute(velocity, "py", swap)
    fields = jnp.concatenate([velocity, cotangent], axis=0)
    packed = call(
        pack_kernel, shape(PLANES, 64, DEPTH), (fields,), [f32(3, 80, DEPTH)], room=4
    )
    packed = call(rim_kernel, shape(PLANES, 64, DEPTH), (packed, other), room=4)
    recv = lax.all_to_all(packed, "px", 0, 0)

    fwd2, fwd1, back2, back1, to_z = call(
        weights_kernel,
        [
            shape(288, DEEP, kind=half),
            shape(2 * HID, STACK, kind=half),
            shape(2 * HID, STACK, kind=half),
            shape(288, DEEP, kind=half),
            shape(3 * DEPTH, DEPTH, kind=half),
        ],
        (
            jnp.transpose(first_kernel, (1, 2, 3, 4, 0)).reshape(27, 3, CHANNELS),
            jnp.transpose(second_kernel, (0, 2, 3, 4, 1)).reshape(54, 3, CHANNELS),
            first_bias.reshape(1, CHANNELS),
            second_bias.reshape(1, COEFFS),
            c["to_z"],
        ),
        [
            f32(3, 96, CHANNELS),
            f32(27, 3, CHANNELS),
            f32(54, 3, CHANNELS),
            f32(1, CHANNELS),
            f32(1, COEFFS),
            pltpu.SemaphoreType.DMA((4,)),
        ],
        away=(0, 1, 2, 3),
    )

    near = lambda rows: [b16(rows, FLAT), b16(rows, FLAT)]
    stacks = near(288)[:1] + near(BROAD) + near(288)[:1] + near(BROAD)
    sent, hidden, weights, *kept = call(
        first_kernel_body,
        [
            shape(16, 24, DEPTH),
            shape(HID, FLAT),
            shape(LOG, FLAT),
            shape(288, FLAT, kind=half),
            shape(BROAD, FLAT, kind=half),
            shape(BROAD, FLAT, kind=half),
        ],
        (recv, fwd1, fwd2, to_z),
        [f32(144, FLAT), f32(2, PLANES, 24, DEPTH)],
    )
    both = ("px", "py")
    moved_modes = lax.all_to_all(sent, both, 0, 0)
    moved_modes = call(both_kernel, shape(16, 32, DEPTH), (moved_modes, c["both_in"], c["both_out"]))
    moved_modes = lax.all_to_all(moved_modes, both, 0, 0)

    sent, sums = call(
        second_kernel_body,
        [shape(16, 9, 2, DEPTH), shape(288, DEEP)],
        (moved_modes, fwd1, fwd2, back2, back1, to_z, c["from_z"]),
        [
            f32(PLANES, 48, DEPTH),
            f32(HID, FLAT),
            f32(PLANES, 24, DEPTH),
            f32(PLANES, 40, DEPTH),
            f32(2, PLANES, 24, DEPTH),
            f32(LOG, FLAT),
            f32(144, FLAT),
            f32(PLANES, 48, DEPTH),
        ]
        + stacks,
    )
    moved_modes = lax.all_to_all(sent, both, 0, 0)
    moved_modes = call(
        one_kernel,
        shape(16, 3, 4, DEPTH),
        (moved_modes, c["one_in"], c["one_out"]),
        [f32(3, 96, DEPTH)],
    )
    moved_modes = lax.all_to_all(moved_modes, both, 0, 0)

    sent = call(
        third_kernel_body,
        shape(PLANES, 72, DEPTH),
        (
            moved_modes, recv, hidden, weights, *kept, back2, back1, c["from_z"], sums,
            c["spread_t"], c["mask"], c["lift"],
        ),
        [f32(16, 16, DEPTH), f32(PLANES, 24, DEPTH), f32(PLANES, 16, DEPTH)]
        + stacks[3:]
        + [
            f32(144, FLAT),
            f32(PLANES, 48, DEPTH),
            f32(288, DEEP),
            f32(36, DEPTH),
        ],
    )
    recv = lax.all_to_all(sent, "px", 0, 0)
    main, edge = call(
        fold_kernel, [shape(3, 1, 64, DEPTH), shape(64, DEPTH)], (recv,), [f32(3, 80, DEPTH)]
    )
    other = lax.ppermute(edge, "py", swap)
    grad_velocity, first, end1, second, end2 = call(
        last_kernel,
        [
            shape(3, 1, 64, DEPTH),
            shape(27, 3, CHANNELS),
            shape(1, CHANNELS),
            shape(54, 3, CHANNELS),
            shape(1, COEFFS),
        ],
        (main, edge, other),
        [f32(8, 40, DEPTH)],
    )
    return (
        grad_velocity,
        jnp.transpose(first.reshape(3, 3, 3, 3, CHANNELS), (4, 0, 1, 2, 3)),
        end1.reshape(CHANNELS),
        jnp.transpose(second.reshape(COEFFS, 3, 3, 3, CHANNELS), (0, 4, 1, 2, 3)),
        end2.reshape(COEFFS),
    )


def fits_slabs(mesh):
    return mesh.shape["px"] == PLANES and mesh.shape["py"] == 2


def solution(mesh):
    return jax.shard_map(
        slab_device if fits_slabs(mesh) else on_device,
        mesh=mesh,
        in_specs=(
            P(None, ("groups", "px"), "py", None),
            P(None, ("groups", "px"), "py", None),
            P(),
            P(),
            P(),
            P(),
        ),
        out_specs=(
            P(None, ("groups", "px"), "py", None),
            P("groups", None, None, None, None),
            P("groups"),
            P("groups", None, None, None, None),
            P("groups"),
        ),
        check_vma=False,
    )
```

```python
import functools
import math

import jax
import jax.numpy as jnp
import numpy as np
from jax import lax
from jax.experimental import pallas as pl
from jax.experimental.pallas import tpu as pltpu
from jax.sharding import PartitionSpec as P

ITERS = 2


KAPPA = 0.25


def padded_2(value, sides, width):
    for axis, dim in sides:
        size, length = (lax.axis_size(axis), value.shape[dim])
        up = [(i, (i + 1) % size) for i in range(size)]
        down = [(j, i) for i, j in up]
        last = lax.slice_in_dim(value, length - width, length, axis=dim)
        initial = lax.slice_in_dim(value, 0, width, axis=dim)
        before = lax.ppermute(last, axis, up)
        after = lax.ppermute(initial, axis, down)
        value = jnp.concatenate([before, value, after], axis=dim)
    return value


def extend(field):
    rimmed = padded_2(field, (("px", 1), ("py", 2)), 1)
    return jnp.concatenate([rimmed[..., -1:], rimmed, rimmed[..., :1]], axis=3)


def across_columns(spectrum):
    return lax.all_to_all(spectrum, "px", split_axis=2, concat_axis=4, tiled=True)


def across_pairs(spectrum):
    return lax.all_to_all(spectrum, "py", split_axis=3, concat_axis=4, tiled=True)


def summed(grads):
    return lax.psum((grads[0], grads[1], grads[2], grads[3]), ("px", "py"))


def all_taps():
    return [
        (shift_x, shift_y, shift_z)
        for shift_x in range(3)
        for shift_y in range(3)
        for shift_z in range(3)
    ]


def gather_conv(padded, kernel):
    size_x = padded.shape[1] - 2
    size_y = padded.shape[2] - 2
    size_z = padded.shape[3] - 2
    stacked = jnp.concatenate(
        [
            padded[:, sx_one : sx_one + size_x, sy_one : sy_one + size_y, sz_one : sz_one + size_z]
            for sx_one, sy_one, sz_one in all_taps()
        ],
        axis=0,
    )
    matrix = jnp.transpose(kernel, (0, 2, 3, 4, 1)).reshape(kernel.shape[0], -1)
    result = jnp.einsum("ok,kxyz->oxyz", matrix, stacked, precision=lax.Precision.HIGHEST)
    return (result, stacked)


def scatter_conv(padded, kernel):
    outputs = kernel.shape[0]
    inputs = kernel.shape[1]
    size_x = padded.shape[1] - 2
    size_y = padded.shape[2] - 2
    size_z = padded.shape[3] - 2
    total = jnp.zeros((outputs, size_x, size_y, size_z), jnp.float32)
    for shift_x in range(3):
        matrix = jnp.transpose(kernel[:, :, shift_x], (0, 2, 3, 1)).reshape(outputs * 9, inputs)
        layer = jnp.einsum(
            "km,mxyz->kxyz",
            matrix,
            padded[:, shift_x : shift_x + size_x],
            precision=lax.Precision.HIGHEST,
        )
        layer = layer.reshape(outputs, 3, 3, size_x, size_y + 2, size_z + 2)
        for shift_y in range(3):
            for shift_z in range(3):
                total = (
                    total
                    + layer[
                        :,
                        shift_y,
                        shift_z,
                        :,
                        shift_y : shift_y + size_y,
                        shift_z : shift_z + size_z,
                    ]
                )
    return total


def flipped(kernel):
    return jnp.transpose(kernel[:, :, ::-1, ::-1, ::-1], (1, 0, 2, 3, 4))


def moved(padded, axis_dim, offset_cells):
    index = [slice(None), slice(1, -1), slice(1, -1), slice(1, -1)]
    index[axis_dim] = slice(1 + offset_cells, padded.shape[axis_dim] - 1 + offset_cells)
    return padded[tuple(index)]


def advect(padded, weights):
    center = moved(padded, 1, 0)
    total = jnp.zeros_like(center)
    for direction in range(3):
        ahead = moved(padded, direction + 1, 1)
        behind = moved(padded, direction + 1, -1)
        vplus = 0.5 * (center[direction] + ahead[direction])
        vminus = 0.5 * (behind[direction] + center[direction])
        upper = center + weights[2 * direction] * (ahead - center)
        lower = center + weights[2 * direction + 1] * (behind - center)
        total = total + vplus * upper - vminus * lower
    return total


def advect_back(padded, weights_pad, source_pad):
    center = moved(padded, 1, 0)
    source = moved(source_pad, 1, 0)
    weights = moved(weights_pad, 1, 0)
    grad_field = jnp.zeros_like(center)
    fluxes = []
    parts = []
    for direction in range(3):
        ahead = moved(padded, direction + 1, 1)
        behind = moved(padded, direction + 1, -1)
        vplus = 0.5 * (center[direction] + ahead[direction])
        vminus = 0.5 * (behind[direction] + center[direction])
        rate_up = weights[2 * direction]
        rate_low = weights[2 * direction + 1]
        rate_before = moved(weights_pad[2 * direction : 2 * direction + 1], direction + 1, -1)[0]
        rate_after = moved(weights_pad[2 * direction + 1 : 2 * direction + 2], direction + 1, 1)[0]
        source_before = moved(source_pad, direction + 1, -1)
        source_after = moved(source_pad, direction + 1, 1)
        upper = center + rate_up * (ahead - center)
        lower = center + rate_low * (behind - center)
        upper_before = behind + rate_before * (center - behind)
        lower_after = ahead + rate_after * (center - ahead)
        grad_field = grad_field + source * (vplus * (1.0 - rate_up) - vminus * (1.0 - rate_low))
        grad_field = (
            grad_field + vminus * rate_before * source_before - vplus * rate_after * source_after
        )
        fluxes.append(
            0.5
            * (
                jnp.sum(source * upper, 0)
                - jnp.sum(source * lower, 0)
                + jnp.sum(source_before * upper_before, 0)
                - jnp.sum(source_after * lower_after, 0)
            )
        )
        parts.append(jnp.sum(source * vplus * (ahead - center), 0))
        parts.append(-jnp.sum(source * vminus * (behind - center), 0))
    return (grad_field + jnp.stack(fluxes), jnp.stack(parts))


def tables(count):
    index = jnp.arange(count, dtype=jnp.int32)
    phase = index[:, None] * index[None, :] % count
    angle = phase.astype(jnp.float32) * (2.0 * math.pi / count)
    return (jnp.cos(angle), jnp.sin(angle))


def mix(form, data, table):
    return jnp.einsum(form, data, table, precision=lax.Precision.HIGHEST)


def waves(start, count, total):
    index = start + jnp.arange(count, dtype=jnp.int32)
    return jnp.where(index < total // 2, index, index - total).astype(jnp.float32)


def project(field):
    depth = field.shape[3]
    cos_z, sin_z = tables(depth)
    real_z = mix("cxyz,zk->cxky", field, cos_z)
    imag_z = -mix("cxyz,zk->cxky", field, sin_z)
    spectrum = across_pairs(jnp.stack([real_z, imag_z]))
    span_y = spectrum.shape[4]
    cos_y, sin_y = tables(span_y)
    real_y = mix("cxky,yq->cqkx", spectrum[0], cos_y) + mix("cxky,yq->cqkx", spectrum[1], sin_y)
    imag_y = mix("cxky,yq->cqkx", spectrum[1], cos_y) - mix("cxky,yq->cqkx", spectrum[0], sin_y)
    spectrum = across_columns(jnp.stack([real_y, imag_y]))
    span_x = spectrum.shape[4]
    cos_x, sin_x = tables(span_x)
    real_x = mix("cqkx,xp->cqkp", spectrum[0], cos_x) + mix("cqkx,xp->cqkp", spectrum[1], sin_x)
    imag_x = mix("cqkx,xp->cqkp", spectrum[1], cos_x) - mix("cqkx,xp->cqkp", spectrum[0], sin_x)
    rows_y = spectrum.shape[2]
    rows_z = spectrum.shape[3]
    wave_y = waves(lax.axis_index("px") * rows_y, rows_y, span_y)[:, None, None]
    wave_z = waves(lax.axis_index("py") * rows_z, rows_z, depth)[None, :, None]
    wave_x = waves(0, span_x, span_x)[None, None, :]
    size = jnp.maximum(wave_x * wave_x + wave_y * wave_y + wave_z * wave_z, 1.0)
    vectors = jnp.stack(jnp.broadcast_arrays(wave_x, wave_y, wave_z))
    real_x = real_x - vectors * (
        (wave_x * real_x[0] + wave_y * real_x[1] + wave_z * real_x[2]) / size
    )
    imag_x = imag_x - vectors * (
        (wave_x * imag_x[0] + wave_y * imag_x[1] + wave_z * imag_x[2]) / size
    )
    back_real = (mix("cqkp,px->cxkq", real_x, cos_x) - mix("cqkp,px->cxkq", imag_x, sin_x)) / span_x
    back_imag = (mix("cqkp,px->cxkq", imag_x, cos_x) + mix("cqkp,px->cxkq", real_x, sin_x)) / span_x
    spectrum = across_columns(jnp.stack([back_real, back_imag]))
    rows_real = (
        mix("cxkq,qy->cxyk", spectrum[0], cos_y) - mix("cxkq,qy->cxyk", spectrum[1], sin_y)
    ) / span_y
    rows_imag = (
        mix("cxkq,qy->cxyk", spectrum[1], cos_y) + mix("cxkq,qy->cxyk", spectrum[0], sin_y)
    ) / span_y
    spectrum = across_pairs(jnp.stack([rows_real, rows_imag]))
    return (
        mix("cxyk,kz->cxyz", spectrum[0], cos_z) - mix("cxyk,kz->cxyz", spectrum[1], sin_z)
    ) / depth


def forward_state(field, first_kernel, first_bias, second_kernel, second_bias):
    padded = extend(field)
    first_out, field_taps = gather_conv(padded, first_kernel)
    hidden = jnp.tanh(first_out + first_bias[:, None, None, None])
    weights = jax.nn.sigmoid(
        scatter_conv(extend(hidden), second_kernel) + second_bias[:, None, None, None]
    )
    return (padded, hidden, weights, field_taps)


def backward_step(state, upstream, first_kernel, second_kernel):
    padded, hidden, weights, field_taps = state
    moved_grad = project(upstream)
    source = -KAPPA * moved_grad
    stacked = extend(jnp.concatenate([source, weights], axis=0))
    grad_field, grad_weights = advect_back(padded, stacked[3:], stacked[:3])
    grad_field = grad_field + moved_grad
    grad_logits = grad_weights * weights * (1.0 - weights)
    logits_pad = extend(grad_logits)
    grad_hidden, logit_taps = gather_conv(logits_pad, flipped(second_kernel))
    product = jnp.einsum("kxyz,mxyz->km", logit_taps, hidden, precision=lax.Precision.HIGHEST)
    product = product.reshape(3, 3, 3, second_kernel.shape[0], second_kernel.shape[1])
    grad_second = jnp.transpose(product[::-1, ::-1, ::-1], (3, 4, 0, 1, 2))
    grad_second_bias = jnp.sum(grad_logits, axis=(1, 2, 3))
    grad_pre = grad_hidden * (1.0 - hidden * hidden)
    pre_pad = extend(grad_pre)
    grad_field = grad_field + scatter_conv(pre_pad, flipped(first_kernel))
    first_product = jnp.einsum(
        "oxyz,kxyz->ok", grad_pre, field_taps, precision=lax.Precision.HIGHEST
    )
    first_product = first_product.reshape(first_kernel.shape[0], 3, 3, 3, first_kernel.shape[1])
    grad_first = jnp.transpose(first_product, (0, 4, 1, 2, 3))
    grad_first_bias = jnp.sum(grad_pre, axis=(1, 2, 3))
    return (grad_field, (grad_first, grad_first_bias, grad_second, grad_second_bias))


def on_device(velocity, cotangent, first_kernel, first_bias, second_kernel, second_bias):
    field = velocity
    fields = [velocity]
    saved = []
    for section in range(ITERS):
        state = forward_state(field, first_kernel, first_bias, second_kernel, second_bias)
        saved.append(state)
        field = project(field - KAPPA * advect(state[0], state[2]))
        fields.append(field)
    upstream = cotangent
    totals = None
    for section in reversed(range(ITERS)):
        state = saved[section]
        upstream, grads = backward_step(state, upstream, first_kernel, second_kernel)
        grads = summed(grads)
        if totals is None:
            totals = grads
        else:
            totals = tuple((older + newer for older, newer in zip(totals, grads)))
    return (upstream, totals[0], totals[1], totals[2], totals[3])


SLAB = 8
RIM = 2
REACH = SLAB + 2 * RIM
WIDE = SLAB + 2
PLANES = 8
DEPTH = 128
ROWS = 128
CHANNELS = 16
COEFFS = 6
BAND = 32
HID = CHANNELS * WIDE
LOG = COEFFS * SLAB
STACK = 9 * 48
UNIT = 36
BROAD = HID + 16
DEEP = 3 * HID + 16
PLACE = (0, 2, 1)
FLAT = PLANES * DEPTH
NN = ((1,), (0,))
NT = ((1,), (1,))


def real_basis(count):
    half = count // 2
    angle = 2.0 * np.pi * np.arange(count) / count
    rows = [np.full(count, 1.0 / np.sqrt(count))]
    rows += [np.sqrt(2.0 / count) * np.cos(k * angle) for k in range(1, half)]
    rows += [np.cos(half * angle) / np.sqrt(count)]
    rows += [np.sqrt(2.0 / count) * np.sin(k * angle) for k in range(1, half)]
    return np.stack(rows)


def wide_table(table):
    high, low = halves(table)
    return np.concatenate([high, low, high], axis=1)


def tall_table(table):
    high, low = halves(table)
    return np.concatenate([high, high, low])


def halves(table):
    high = table.astype(np.float32).astype(jnp.bfloat16)
    low = (table - high.astype(np.float64)).astype(np.float32).astype(jnp.bfloat16)
    return high, low


def slab_of(device):
    return (device % 2) * PLANES + device // 2


@functools.cache
def constants():
    basis_z = real_basis(DEPTH)
    order = []
    for group in range(4):
        order += [16 * group + i for i in range(16)] + [64 + 16 * group + i for i in range(16)]
    mode_z = basis_z[order]
    basis_y = real_basis(ROWS)

    def rows(offset, count):
        at = [SLAB * slab_of(j) + offset + i for j in range(16) for i in range(count)]
        return basis_y[:, np.array(at) % ROWS]

    own, half_one, half_two = rows(0, SLAB), rows(0, 4), rows(4, 4)
    before, after = rows(-RIM, RIM), rows(SLAB, RIM)
    both_in = own
    both_out = np.concatenate([own, before, after], axis=1).T
    one_in = np.concatenate(
        [np.concatenate([half_one, before], axis=1), np.concatenate([half_two, after], axis=1)]
    )
    one_out = np.concatenate([half_one, half_two], axis=1).T

    spread = np.zeros((288, 32))
    mask = np.zeros((3, 288, DEEP))
    lanes = np.arange(CHANNELS) * WIDE
    for e in range(3):
        for o in range(COEFFS):
            for q in range(SLAB):
                row = e * 48 + o * SLAB + q
                spread[row, e * COEFFS + o] = 1.0
                for b in range(3):
                    for a in range(3):
                        mask[b, row, a * HID + lanes + q + b] = 1.0
        for m in range(3):
            for r in range(REACH):
                row = 144 + e * 48 + m * REACH + r
                spread[row, 18 + e * 3 + m] = 1.0
                for b in range(3):
                    for a in range(3):
                        if 0 <= r - b < WIDE:
                            mask[b, row, a * HID + lanes + r - b] = 1.0
    spread[144 + 48 + UNIT, 27] = 1.0
    mask[0, 144 + 48 + UNIT, PLACE[1] * HID : (PLACE[1] + 1) * HID] = 1.0
    mask[0, 48:96, 3 * HID] = 1.0
    lift = np.zeros((3, 512, 256))
    for b in range(3):
        for a in range(3):
            lift[b, PLACE[a] * HID + np.arange(HID), 16 * (3 * b + a) + np.arange(HID) // WIDE] = 1.0
    lift[0, 3 * HID, 128 + 96] = 1.0
    lift = lift.reshape(3 * 512, 256)
    half = jnp.bfloat16
    return dict(
        to_z=tall_table(mode_z.T),
        from_z=tall_table(mode_z),
        both_in=wide_table(both_in),
        both_out=wide_table(both_out),
        one_in=wide_table(one_in),
        one_out=wide_table(one_out),
        spread_t=np.concatenate([spread.T, spread.T], axis=1).astype(half),
        mask=mask.astype(half),
        lift=lift.astype(half),
    )


def dot(left, right, dims=NN):
    return lax.dot_general(left, right, (dims, ((), ())), preferred_element_type=jnp.float32)


def split(value):
    high = value.astype(jnp.bfloat16)
    return high, (value - high.astype(jnp.float32)).astype(jnp.bfloat16)


def dot_stacked(left, right, dims=NN):
    rows = left.shape[0] // 2
    main = dot(left[...], right[0], dims)
    return main[:rows] + (main[rows:] + dot(left[0:rows, :], right[1], dims))


def dot_wide(left, right):
    return dot(left[...], jnp.concatenate([right[0], right[0], right[1]], axis=0))


def widened(value):
    high, low = split(value)
    return jnp.concatenate([high, low, high], axis=1)


def stacked(value):
    return jnp.concatenate(split(value), axis=0)


def turn(value, shift):
    shift = shift % value.shape[-1]
    return value if shift == 0 else pltpu.roll(value, shift, value.ndim - 1)


def plane(x):
    x = x % PLANES
    return slice(x * DEPTH, (x + 1) * DEPTH)


def call(kernel, outs, args, scratch=(), room=16, away=()):
    single = not isinstance(outs, (list, tuple))
    vmem = pl.BlockSpec(memory_space=pltpu.VMEM)
    cost = pl.CostEstimate(flops=1, bytes_accessed=1, transcendentals=0) if away else None
    return pl.pallas_call(
        kernel,
        out_shape=outs,
        in_specs=[
            pl.BlockSpec(memory_space=pltpu.HBM) if i in away else vmem for i in range(len(args))
        ],
        out_specs=vmem if single else [vmem] * len(outs),
        scratch_shapes=list(scratch),
        cost_estimate=cost,
        compiler_params=pltpu.CompilerParams(vmem_limit_bytes=room * 2**20),
    )(*args)


def fetch(pairs, sems):
    copies = [pltpu.make_async_copy(src, dst, sems.at[i]) for i, (src, dst) in enumerate(pairs)]
    for copy in copies:
        copy.start()
    return copies


def shape(*dims, kind=jnp.float32):
    return jax.ShapeDtypeStruct(dims, kind)


def counting(size, dim):
    return lax.broadcasted_iota(jnp.int32, size, dim).astype(jnp.float32)


def remainder(value, count):
    return value - count * jnp.floor((value + 0.5) / count)


def band_tables(tall):
    row, col = (0, 1) if tall else (1, 0)
    size = lambda rows, cols: (rows, cols) if tall else (cols, rows)
    where = counting(size(2 * STACK, 96), row)
    to = counting(size(2 * STACK, 96), col)
    first = where - 8.0 * to
    third = to - 54.0
    second = where - STACK - (16.0 * third - 4.0 * remainder(third, 3.0))
    picks = ((to < 54.0) & (first >= 0.0) & (first < 8.0)) | (
        (to >= 54.0) & (to < 81.0) & (second >= 0.0) & (second < 12.0)
    )
    where = counting(size(2 * STACK, HID), row)
    inner = remainder(counting(size(2 * STACK, HID), col), 10.0)
    outer = where - STACK
    offset = jnp.where(
        where < STACK,
        inner - remainder(where, 8.0),
        remainder(remainder(outer, 48.0), 12.0) - inner,
    )
    gap = counting(size(HID, CHANNELS), row) - 10.0 * counting(size(HID, CHANNELS), col)
    lift = (gap >= 0.0) & (gap < 10.0)
    half = jnp.bfloat16
    return picks.astype(jnp.float32).astype(half), offset, lift.astype(jnp.float32).astype(half)


def weights_kernel(
    far1, far2, far3, far4, z_in, fwd2, fwd1, back2, back1, z_out, blocks, taps1, taps2, bias1, bias2, sems
):
    copies = fetch([(far1, taps1), (far2, taps2), (far3, bias1), (far4, bias2)], sems)
    blocks[...] = jnp.zeros_like(blocks)
    z_out[...] = z_in[...]
    spread, offset, lift = band_tables(True)
    spread_t, offset_t, lift_t = band_tables(False)
    for copy in copies:
        copy.wait()
    for b in range(3):
        for a in range(3):
            for e in range(3):
                tap = a * 3 + e
                for o in range(COEFFS):
                    blocks[b, tap * 6 + o, :] = taps2[o * 9 + a * 3 + b, e, :]
                for m in range(3):
                    blocks[b, 54 + tap * 3 + m, :] = taps1[m * 9 + a * 3 + b, e, :]
    tall = [jnp.zeros((2 * STACK, HID), jnp.float32)] * 2
    flat = [jnp.zeros((HID, 2 * STACK), jnp.float32)] * 2
    for b in range(3):
        for half, block in enumerate(split(blocks[b])):
            rows = dot(spread, block).astype(jnp.bfloat16)
            tall[half] = jnp.where(offset == float(b), dot(rows, lift_t), tall[half])
            cols = dot(lift, block, NT).astype(jnp.bfloat16)
            flat[half] = jnp.where(offset_t == float(b), dot(cols, spread_t), flat[half])
    for half in range(2):
        rows, cols = slice(half * 144, half * 144 + 144), slice(half * HID, half * HID + HID)
        for a in range(3):
            first = PLACE[a] * HID
            part = tall[half][a * 144 : a * 144 + 144]
            fwd2[rows, first : first + HID] = part.astype(jnp.bfloat16)
            part = tall[half][STACK + a * 144 : STACK + a * 144 + 144]
            back1[rows, first : first + HID] = part.astype(jnp.bfloat16)
        back2[cols, :] = flat[half][:, :STACK].astype(jnp.bfloat16)
    gap = counting((LOG, COEFFS), 0) - 8.0 * counting((LOG, COEFFS), 1)
    pick = ((gap >= 0.0) & (gap < 8.0)).astype(jnp.float32).astype(jnp.bfloat16)
    second = counting((LOG, 16), 1) < 1.0
    one = split(jnp.broadcast_to(bias1[...], (STACK, CHANNELS)))
    first = counting((HID, STACK), 1) == 4.0 * 48.0 + UNIT
    two = split(jnp.broadcast_to(bias2[...], (16, COEFFS)))
    fwd2[:, 3 * HID :] = jnp.zeros((288, 16), jnp.bfloat16)
    back1[:, 3 * HID :] = jnp.zeros((288, 16), jnp.bfloat16)
    for half in range(2):
        value = jnp.where(first, dot(lift, one[half], NT), flat[half][:, STACK:])
        fwd1[half * HID : half * HID + HID, :] = value.astype(jnp.bfloat16)
        value = jnp.where(second, dot(pick, two[half], NT), 0.0)
        start = half * 144 + LOG
        fwd2[start : start + LOG, 3 * HID :] = value.astype(jnp.bfloat16)


def pack_kernel(fields, out, ext):
    ext[...] = jnp.zeros_like(ext)
    for m in range(3):
        ext[m, 8:72, :] = fields[m, 0]
    for q in range(PLANES):
        for m in range(3):
            out[q, m * REACH : (m + 1) * REACH, :] = ext[m, 8 * q + 6 : 8 * q + 18, :]
            out[q, 36 + 8 * m : 44 + 8 * m, :] = fields[3 + m, 0, 8 * q : 8 * q + 8, :]
        out[q, 60:64, :] = jnp.zeros((4, DEPTH), jnp.float32)


def rim_kernel(packed, other, out):
    for q in range(PLANES):
        for i in range(15):
            out[q, i] = packed[q, 4 * i : 4 * i + 4, :]
    for m in range(3):
        out[0, 3 * m, 0:2, :] = other[m, 0, 62:64, :]
        out[PLANES - 1, 3 * m + 2, 2:4, :] = other[m, 0, 0:2, :]


def unit_row():
    row = lax.broadcasted_iota(jnp.int32, (16, FLAT), 0)
    return jnp.where(row == 0, 1.0, 0.0).astype(jnp.bfloat16)


def stack_planes(value, cut, high, low):
    parts = split(value)
    high[0:HID, cut] = parts[0]
    low[0:HID, cut] = parts[1]


def finish_planes(high, low):
    high[HID:, :] = unit_row()
    low[HID:, :] = jnp.zeros((16, FLAT), jnp.bfloat16)


def shifted(taps, first_row, rows, first, count, shift):
    return beside(
        [taps[first_row : first_row + rows, plane(first + i + shift)] for i in range(count)]
    )


def nine(taps, half, first, count, sign):
    return jnp.concatenate(
        [shifted(taps, 144 * half, 144, first, count, sign * (a - 1)) for a in range(3)], axis=0
    )


def three(taps, first, count, sign):
    return jnp.concatenate(
        [shifted(taps, 0, HID, first, count, sign * shift) for shift in (-1, 1, 0)]
        + [shifted(taps, HID, 16, first, count, 0)],
        axis=0,
    )


def stack_logits(whole, x, taps):
    for e in range(3):
        for half, part_of in enumerate(split(turn(whole, e - 1))):
            taps[144 * half + 48 * e : 144 * half + 48 * e + 48, plane(x)] = part_of


def stack_field(field, taps):
    for x in range(PLANES):
        whole = field[x, 0:48, :]
        for e in range(3):
            for half, part_of in enumerate(split(turn(whole, 1 - e))):
                taps[144 * half + 48 * e : 144 * half + 48 * e + 48, plane(x)] = part_of


def network(field, fwd1, fwd2, hidden, weights, u_taps, h_hi, h_lo, work):
    stack_field(field, u_taps)
    finish_planes(h_hi, h_lo)
    for pair in range(4):
        cut = slice(pair * 256, pair * 256 + 256)
        taps = (nine(u_taps, 0, 2 * pair, 2, 1), nine(u_taps, 1, 2 * pair, 2, 1))
        value = jnp.tanh(dot_stacked(fwd1, taps))
        hidden[:, cut] = value
        stack_planes(value, cut, h_hi, h_lo)
    for pair in range(4):
        cut = slice(pair * 256, pair * 256 + 256)
        work[:, cut] = dot_stacked(fwd2, (three(h_hi, 2 * pair, 2, 1), three(h_lo, 2 * pair, 2, 1)))
    for x in range(PLANES):
        total = work[LOG : 2 * LOG, plane(x)]
        total = total + turn(work[0:LOG, plane(x)], 1) + turn(work[2 * LOG : 3 * LOG, plane(x)], -1)
        weights[:, plane(x)] = jax.nn.sigmoid(total)


def own_rows(field):
    return [
        [field[x, m * REACH + RIM : m * REACH + RIM + SLAB, :] for m in range(3)] for x in range(PLANES)
    ]


def around(field, own, x, direction, sign):
    if direction == 0:
        return own[(x + sign) % PLANES]
    if direction == 1:
        first = RIM + sign
        return [field[x, m * REACH + first : m * REACH + first + SLAB, :] for m in range(3)]
    return [turn(value, -sign) for value in own[x]]


def advected(field, cells, weights, x):
    center = cells[x]
    total = [jnp.zeros((SLAB, DEPTH), jnp.float32)] * 3
    for d in range(3):
        ahead = around(field, cells, x, d, 1)
        behind = around(field, cells, x, d, -1)
        plus = 0.5 * (center[d] + ahead[d])
        minus = 0.5 * (behind[d] + center[d])
        rate_up = weights[2 * d * SLAB : (2 * d + 1) * SLAB, plane(x)]
        rate_low = weights[(2 * d + 1) * SLAB : (2 * d + 2) * SLAB, plane(x)]
        for m in range(3):
            upper = center[m] + rate_up * (ahead[m] - center[m])
            lower = center[m] + rate_low * (behind[m] - center[m])
            total[m] = total[m] + plus * upper - minus * lower
    return [center[m] - KAPPA * total[m] for m in range(3)]


ROOT = math.sqrt(0.5)


def to_modes(x):
    s = [x[i] + x[i + 4] for i in range(4)]
    d = [x[i] - x[i + 4] for i in range(4)]
    even, odd = s[0] + s[2], s[1] + s[3]
    up, down = ROOT * (d[1] + d[3]), ROOT * (d[1] - d[3])
    scale = 0.5 * ROOT
    return [
        scale * (even + odd),
        scale * (even - odd),
        0.5 * (d[0] + down),
        0.5 * (up + d[2]),
        0.5 * (s[0] - s[2]),
        0.5 * (s[1] - s[3]),
        0.5 * (d[0] - down),
        0.5 * (up - d[2]),
    ]


def from_modes(v):
    even, odd = 0.5 * ROOT * (v[0] + v[1]), 0.5 * ROOT * (v[0] - v[1])
    cos, sin = 0.5 * v[4], 0.5 * v[5]
    e = [even + cos, odd + sin, even - cos, odd - sin]
    across, along = 0.5 * ROOT * (v[2] - v[6]), 0.5 * ROOT * (v[3] + v[7])
    o = [0.5 * (v[2] + v[6]), along + across, 0.5 * (v[3] - v[7]), along - across]
    return [e[i] + o[i] for i in range(4)] + [e[i] - o[i] for i in range(4)]


def lane_groups(size):
    return lax.broadcasted_iota(jnp.int32, (size, DEPTH), 1) // BAND


def scatter_modes(source, rows, out):
    groups = lane_groups(rows)
    for p in range(4):
        for g in range(4):
            total = None
            for f in range(2):
                for t in range(2):
                    slot = 2 * f + t
                    value = turn(source(f, 2 * p + t), BAND * (slot - g))
                    total = value if total is None else jnp.where(groups == slot, value, total)
            if len(out.shape) == 3:
                out[p * 4 + g] = total
            else:
                for i in range(out.shape[1]):
                    out[p * 4 + g, i] = total[2 * i : 2 * i + 2]


def gather_modes(recv, f, k, first, rows):
    groups = lane_groups(rows)
    slot = 2 * f + k % 2
    total = None
    for g in range(4):
        value = turn(recv[(k // 2) * 4 + g, first : first + rows, :], BAND * (g - slot))
        total = value if total is None else jnp.where(groups == g, value, total)
    return total


def first_kernel_body(
    recv, fwd1, fwd2, to_z, out, field, hidden, weights, u_taps, h_hi, h_lo, work, modes, cot
):
    for x in range(PLANES):
        for i in range(9):
            field[x, 4 * i : 4 * i + 4, :] = recv[x, i]
        field[x, 36:37, :] = jnp.ones((1, DEPTH), jnp.float32)
        field[x, 37:48, :] = jnp.zeros((11, DEPTH), jnp.float32)
        for i in range(6):
            cot[x, 4 * i : 4 * i + 4, :] = recv[x, 9 + i]
    network(field, fwd1, fwd2, hidden, weights, u_taps, h_hi, h_lo, work)
    table = to_z[...]
    cells = own_rows(field)
    moved_field = [jnp.concatenate(advected(field, cells, weights, x), axis=0) for x in range(PLANES)]
    for f in range(2):
        planes = moved_field if f == 0 else [cot[x] for x in range(PLANES)]
        for k, value in enumerate(to_modes(planes)):
            modes[f, k] = value
    for f in range(2):
        flat = modes[f].reshape(PLANES * 24, DEPTH)
        modes[f] = dot(widened(flat), table).reshape(PLANES, 24, DEPTH)
    scatter_modes(lambda f, k: modes[f, k], 24, out)


def leray(parts):
    device = lax.axis_index("px") * 2 + lax.axis_index("py")
    pair = device // 4
    group = device % 4
    lane = lax.broadcasted_iota(jnp.int32, (ROWS, DEPTH), 1)
    row = lax.broadcasted_iota(jnp.int32, (ROWS, DEPTH), 0)
    odd_x = (lane // BAND) % 2
    odd_z = (lane // 16) % 2
    number_z = 16 * group + lane % 16
    top_x = (odd_x == 1) & (pair == 0)
    top_y = row == ROWS // 2
    top_z = (odd_z == 1) & (number_z == 0)
    number_y = row % (ROWS // 2)
    real = lambda value: value.astype(jnp.float32)
    rate_x = real(jnp.where(odd_x == 1, -pair, pair))
    rate_y = real(jnp.where(row < ROWS // 2, number_y, -number_y))
    rate_z = real(jnp.where(odd_z == 1, -number_z, number_z))
    high_x = real(jnp.where(top_x, PLANES // 2, 0))
    high_y = real(jnp.where(top_y, ROWS // 2, 0))
    high_z = real(jnp.where(top_z, DEPTH // 2, 0))
    size = rate_x * rate_x + rate_y * rate_y + rate_z * rate_z
    size = size + high_x * high_x + high_y * high_y + high_z * high_z
    inverse = 1.0 / jnp.maximum(size, 1.0)

    def slope_x(value):
        return rate_x * jnp.where(odd_x == 1, turn(value, BAND), turn(value, -BAND))

    def slope_y(value):
        return rate_y * jnp.concatenate([value[ROWS // 2 :], value[: ROWS // 2]], axis=0)

    def slope_z(value):
        return rate_z * jnp.where(odd_z == 1, turn(value, 16), turn(value, -16))

    spread = (slope_x(parts[0]) + slope_y(parts[1]) + slope_z(parts[2])) * inverse
    high = (high_x * parts[0] + high_y * parts[1] + high_z * parts[2]) * inverse
    return (
        parts[0] + slope_x(spread) - high_x * high,
        parts[1] + slope_y(spread) - high_y * high,
        parts[2] + slope_z(spread) - high_z * high,
    )


def beside(parts):
    return jnp.concatenate(parts, axis=1)


def part(value, m):
    return value[:, m * DEPTH : (m + 1) * DEPTH]


def two_halves(first, second):
    low = lax.broadcasted_iota(jnp.int32, first.shape, 1) < DEPTH // 2
    return jnp.where(low, first, turn(second, DEPTH // 2))


def both_kernel(recv, table_in, table_out, out):
    data = beside([recv[:, 8 * m : 8 * m + 8, :].reshape(ROWS, DEPTH) for m in range(3)])
    modes = dot_wide(table_in, split(data))
    fixed = beside(leray([part(modes, m) for m in range(3)]))
    back = dot_wide(table_out, split(fixed))
    for m in range(3):
        whole = part(back, m)
        out[:, 8 * m : 8 * m + 8, :] = whole[:ROWS].reshape(16, SLAB, DEPTH)
        rim = two_halves(whole[ROWS : ROWS + 32], whole[ROWS + 32 :])
        for device in range(16):
            out[device, 24 + 2 * m : 26 + 2 * m, :] = rim[2 * device : 2 * device + 2]
    out[:, 30:32, :] = jnp.zeros((16, 2, DEPTH), jnp.float32)


def one_kernel(recv, table_in, table_out, out, data):
    for device in range(16):
        for m in range(3):
            for i in range(2):
                first = 4 * device + 2 * i
                data[m, first : first + 2, :] = recv[device, 2 * m + i]
            data[m, 64 + 2 * device : 66 + 2 * device, :] = recv[device, 6 + m]
    modes = dot_wide(table_in, split(beside([data[m] for m in range(3)])))
    low, high = modes[:ROWS], modes[ROWS:]
    fixed = beside(leray([part(low, m) + turn(part(high, m), DEPTH // 2) for m in range(3)]))
    back = dot_wide(table_out, split(fixed))
    for m in range(3):
        whole = two_halves(part(back, m)[:64], part(back, m)[64:])
        for device in range(16):
            out[device, m] = whole[4 * device : 4 * device + 4]


def pullback(field, grad, hidden, weights, back2, back1, l_taps, p_hi, p_lo, work, slope, middle, late):
    slope[...] = jnp.zeros_like(slope)
    row = lax.broadcasted_iota(jnp.int32, (SLAB, DEPTH), 0)
    stay = [None] * PLANES
    cells = own_rows(field)
    pushed = {}
    for x in range(PLANES):
        center = cells[x]
        source = [-KAPPA * grad[x, m * SLAB : (m + 1) * SLAB, :] for m in range(3)]
        own = [grad[x, m * SLAB : (m + 1) * SLAB, :] for m in range(3)]
        logits = []
        for d in range(3):
            ahead = around(field, cells, x, d, 1)
            behind = around(field, cells, x, d, -1)
            plus = 0.5 * (center[d] + ahead[d])
            minus = 0.5 * (behind[d] + center[d])
            rate_up = weights[2 * d * SLAB : (2 * d + 1) * SLAB, plane(x)]
            rate_low = weights[(2 * d + 1) * SLAB : (2 * d + 2) * SLAB, plane(x)]
            grad_up = grad_low = grad_plus = grad_minus = None
            to_ahead, to_behind = [], []
            add = lambda total, term: term if total is None else total + term
            for m in range(3):
                gap_up = ahead[m] - center[m]
                gap_low = behind[m] - center[m]
                grad_plus = add(grad_plus, source[m] * (center[m] + rate_up * gap_up))
                grad_minus = add(grad_minus, -source[m] * (center[m] + rate_low * gap_low))
                grad_up = add(grad_up, source[m] * gap_up)
                grad_low = add(grad_low, -source[m] * gap_low)
                push_up = source[m] * plus
                push_low = -source[m] * minus
                to_ahead.append(push_up * rate_up)
                to_behind.append(push_low * rate_low)
                own[m] = own[m] + (push_up - to_ahead[m]) + (push_low - to_behind[m])
            own[d] = own[d] + 0.5 * (grad_plus + grad_minus)
            to_ahead[d] = to_ahead[d] + 0.5 * grad_plus
            to_behind[d] = to_behind[d] + 0.5 * grad_minus
            logits.append(grad_up * plus * rate_up * (1.0 - rate_up))
            logits.append(grad_low * minus * rate_low * (1.0 - rate_low))
            for m in range(3):
                if d == 0:
                    pushed[x, m, 1], pushed[x, m, -1] = to_ahead[m], to_behind[m]
                elif d == 1:
                    first = m * REACH + RIM
                    down = pltpu.roll(to_ahead[m], 1, 0)
                    up = pltpu.roll(to_behind[m], SLAB - 1, 0)
                    own[m] = own[m] + jnp.where(row > 0, down, 0.0) + jnp.where(row < SLAB - 1, up, 0.0)
                    slope[x, first + SLAB : first + SLAB + 1, :] = down[0:1]
                    slope[x, first - 1 : first, :] = up[SLAB - 1 :]
                else:
                    own[m] = own[m] + turn(to_ahead[m], 1) + turn(to_behind[m], -1)
        stay[x] = own
        whole = jnp.concatenate(logits, axis=0)
        stack_logits(whole, x, l_taps)
    for x in range(PLANES):
        for m in range(3):
            value = stay[x][m] + pushed[(x - 1) % PLANES, m, 1] + pushed[(x + 1) % PLANES, m, -1]
            slope[x, m * REACH + RIM : m * REACH + RIM + SLAB, :] = value
    for pair in range(4):
        cut = slice(pair * 256, pair * 256 + 256)
        taps = (nine(l_taps, 0, 2 * pair, 2, -1), nine(l_taps, 1, 2 * pair, 2, -1))
        value = dot_stacked(back2, taps)
        value = value * (1.0 - hidden[:, cut] * hidden[:, cut])
        stack_planes(value, cut, p_hi, p_lo)
    finish_planes(p_hi, p_lo)
    middle()
    for pair in range(4):
        cut = slice(pair * 256, pair * 256 + 256)
        work[:, cut] = dot_stacked(back1, (three(p_hi, 2 * pair, 2, -1), three(p_lo, 2 * pair, 2, -1)))
    late()
    for x in range(PLANES):
        total = slope[x, 0:40, :] + work[48:88, plane(x)]
        slope[x, 0:40, :] = total + turn(work[0:40, plane(x)], -1) + turn(work[96:136, plane(x)], 1)


def kernel_sums(taps, high, low, sign):
    return dot_stacked(taps, (three(high, 0, PLANES, sign), three(low, 0, PLANES, sign)), NT)


def second_kernel_body(
    recv, fwd1, fwd2, back2, back1, to_z, from_z,
    out, sums,
    field, hidden, grad, modes, rows6, weights, work, slope,
    u_taps, h_hi, h_lo, l_taps, p_hi, p_lo,
):
    back_z = from_z[...]
    for k in range(PLANES):
        modes[k, 0:32, :] = gather_modes(recv, 0, k, 0, 32)
        modes[k, 32:40, :] = gather_modes(recv, 1, k, 24, 8)
    flat = dot(widened(modes[...].reshape(PLANES * 40, DEPTH)), back_z)
    modes[...] = flat.reshape(PLANES, 40, DEPTH)
    for x, value in enumerate(from_modes([modes[k] for k in range(PLANES)])):
        for m in range(3):
            first = m * REACH
            field[x, first : first + RIM, :] = value[24 + 2 * m : 26 + 2 * m]
            field[x, first + RIM : first + RIM + SLAB, :] = value[8 * m : 8 * m + 8]
            field[x, first + RIM + SLAB : first + REACH, :] = value[32 + 2 * m : 34 + 2 * m]
        field[x, 36:37, :] = jnp.ones((1, DEPTH), jnp.float32)
        field[x, 37:48, :] = jnp.zeros((11, DEPTH), jnp.float32)
    for k in range(PLANES):
        grad[k] = gather_modes(recv, 1, k, 0, 24)
    flat = dot(widened(grad[...].reshape(PLANES * 24, DEPTH)), back_z)
    flat = flat.reshape(PLANES, 24, DEPTH)
    for x, value in enumerate(from_modes([flat[k] for k in range(PLANES)])):
        grad[x] = value
    network(field, fwd1, fwd2, hidden, weights, u_taps, h_hi, h_lo, work)

    def middle():
        sums[0:144, :] = kernel_sums(l_taps, h_hi, h_lo, 1)

    def late():
        sums[144:, :] = kernel_sums(u_taps, p_hi, p_lo, -1)

    pullback(
        field, grad, hidden, weights, back2, back1, l_taps, p_hi, p_lo, work, slope, middle, late
    )
    for k, value in enumerate(to_modes([slope[x, 0:40, :] for x in range(PLANES)])):
        modes[k] = value
    flat = dot(widened(modes[...].reshape(PLANES * 40, DEPTH)), to_z[...])
    modes[...] = flat.reshape(PLANES, 40, DEPTH)
    for h in range(2):
        for k in range(PLANES):
            for m in range(3):
                first = m * REACH + RIM + 4 * h
                rows6[h, k, 4 * m : 4 * m + 4, :] = modes[k, first : first + 4, :]
                first = m * REACH + (RIM + SLAB) * h
                rows6[h, k, 12 + 2 * m : 14 + 2 * m, :] = modes[k, first : first + 2, :]
            rows6[h, k, 18:24, :] = jnp.zeros((6, DEPTH), jnp.float32)
    scatter_modes(lambda h, k: rows6[h, k], 24, out)


def third_kernel_body(
    recv, field, hidden, weights, u_taps, h_hi, h_lo, back2, back1, from_z, old_sums,
    spread_t, mask, lift,
    out,
    flat, grad, modes, l_taps, p_hi, p_lo, work, slope, sums, pieces,
):
    back_z = from_z[...]
    flat[...] = jnp.zeros_like(flat)
    for device in range(16):
        for m in range(3):
            flat[device, 4 * m : 4 * m + 4, :] = recv[device, m]
    for h in range(2):
        for k in range(PLANES):
            modes[k] = gather_modes(flat, h, k, 0, 16)
        moved_back = dot(widened(modes[...].reshape(PLANES * 16, DEPTH)), back_z)
        modes[...] = moved_back.reshape(PLANES, 16, DEPTH)
        for x, value in enumerate(from_modes([modes[k] for k in range(PLANES)])):
            for m in range(3):
                grad[x, m * SLAB + 4 * h : m * SLAB + 4 * h + 4, :] = value[m * 4 : m * 4 + 4, :]

    def middle():
        sums[0:144, :] = old_sums[0:144, :] + kernel_sums(l_taps, h_hi, h_lo, 1)
        sums[144:, :] = old_sums[144:, :] + kernel_sums(u_taps, p_hi, p_lo, -1)

    def late():
        pack_grads(sums, spread_t, mask, lift, pieces)

    pullback(
        field, grad, hidden, weights, back2, back1, l_taps, p_hi, p_lo, work, slope, middle, late
    )
    for x in range(PLANES):
        for i in range(9):
            out[x, i] = slope[x, 4 * i : 4 * i + 4, :]
    for x in range(PLANES):
        for i in range(8):
            out[x, 9 + i] = pieces[4 * i : 4 * i + 4, :]


def pack_grads(sums, spread_t, mask, lift, pieces):
    whole = split(sums[...])
    empty = jnp.zeros((32, 512 - DEEP), jnp.float32)
    rows = []
    for b in range(3):
        both = jnp.concatenate([whole[0] * mask[b], whole[1] * mask[b]], axis=0)
        rows.append(dot(spread_t[...], both))
        rows.append(empty)
    placed = dot(stacked(beside(rows)), lift[...])
    placed = placed[:32] + placed[32:]
    pieces[0:28, :] = placed[0:28, 0:128]
    rest = placed[:, 128:]
    lane = lax.broadcasted_iota(jnp.int32, rest.shape, 1)
    low, high = jnp.where(lane < 64, rest, 0.0), jnp.where(lane < 64, 0.0, rest)
    total = turn(high[4:8], 16) + turn(high[8:12], 17)
    for i in range(7):
        total = total + turn(low[4 * i : 4 * i + 4], 16 * i)
    pieces[28:32, :] = total


def fold_kernel(recv, main, edge, ext):
    ext[...] = jnp.zeros_like(ext)
    total = None
    for q in range(PLANES):
        for m in range(3):
            for i in range(3):
                first = 8 * q + 6 + 4 * i
                ext[m, first : first + 4, :] += recv[q, 3 * m + i]
        block = recv[q, 9:17]
        total = block if total is None else total + block
    for m in range(3):
        main[m, 0] = ext[m, 8:72, :]
        edge[m * 8 : m * 8 + 2, :] = ext[m, 72:74, :]
        edge[m * 8 + 2 : m * 8 + 4, :] = ext[m, 6:8, :]
        edge[m * 8 + 4 : m * 8 + 8, :] = jnp.zeros((4, DEPTH), jnp.float32)
    for i in range(8):
        edge[24 + 4 * i : 28 + 4 * i, :] = total[i]


def last_kernel(main, edge, other, out, first, end1, second, end2, turned):
    for m in range(3):
        out[m, 0] = main[m, 0]
        out[m, 0, 0:2, :] += other[m * 8 : m * 8 + 2, :]
        out[m, 0, 62:64, :] += other[m * 8 + 2 : m * 8 + 4, :]
    grads = edge[24:56, :] + other[24:56, :]
    for slot in range(8):
        turned[slot] = turn(grads, -16 * slot)
    for b in range(3):
        for a in range(3):
            for e in range(3):
                for i in range(9):
                    row = e * 6 + i if i < 6 else 18 + e * 3 + i - 6
                    slot = 3 * b + a
                    slot, inner = (slot, row) if slot < 8 else (row // 4, 28 + row % 4)
                    line = turned[slot, inner, 0:16]
                    if i < 6:
                        second[i * 9 + a * 3 + b, e, :] = line
                    else:
                        first[(i - 6) * 9 + a * 3 + b, e, :] = line
    end1[...] = turned[1, 27:28, 0:16]
    for o in range(COEFFS):
        inner, place = 28 + (6 + o) % 4, (6 + o) // 4 - 1
        end2[0:1, o : o + 1] = turned[7, inner : inner + 1, place : place + 1]


def slab_device(velocity, cotangent, first_kernel, first_bias, second_kernel, second_bias):
    c = constants()
    half = jnp.bfloat16
    f32 = lambda *dims: pltpu.VMEM(dims, jnp.float32)
    b16 = lambda *dims: pltpu.VMEM(dims, half)
    swap = [(0, 1), (1, 0)]

    other = lax.ppermute(velocity, "py", swap)
    fields = jnp.concatenate([velocity, cotangent], axis=0)
    packed = call(
        pack_kernel, shape(PLANES, 64, DEPTH), (fields,), [f32(3, 80, DEPTH)], room=4
    )
    packed = call(rim_kernel, shape(PLANES, 15, 4, DEPTH), (packed, other), room=4)
    recv = lax.all_to_all(packed, "px", 0, 0)

    fwd2, fwd1, back2, back1, to_z = call(
        weights_kernel,
        [
            shape(288, DEEP, kind=half),
            shape(2 * HID, STACK, kind=half),
            shape(2 * HID, STACK, kind=half),
            shape(288, DEEP, kind=half),
            shape(3 * DEPTH, DEPTH, kind=half),
        ],
        (
            jnp.transpose(first_kernel, (1, 2, 3, 4, 0)).reshape(27, 3, CHANNELS),
            jnp.transpose(second_kernel, (0, 2, 3, 4, 1)).reshape(54, 3, CHANNELS),
            first_bias.reshape(1, CHANNELS),
            second_bias.reshape(1, COEFFS),
            c["to_z"],
        ),
        [
            f32(3, 96, CHANNELS),
            f32(27, 3, CHANNELS),
            f32(54, 3, CHANNELS),
            f32(1, CHANNELS),
            f32(1, COEFFS),
            pltpu.SemaphoreType.DMA((4,)),
        ],
        away=(0, 1, 2, 3),
    )

    near = lambda rows: [b16(rows, FLAT), b16(rows, FLAT)]
    stacks = near(288)[:1] + near(BROAD) + near(288)[:1] + near(BROAD)
    sent, field, hidden, weights, *kept = call(
        first_kernel_body,
        [
            shape(16, 24, DEPTH),
            shape(PLANES, 48, DEPTH),
            shape(HID, FLAT),
            shape(LOG, FLAT),
            shape(288, FLAT, kind=half),
            shape(BROAD, FLAT, kind=half),
            shape(BROAD, FLAT, kind=half),
        ],
        (recv, fwd1, fwd2, to_z),
        [f32(144, FLAT), f32(2, PLANES, 24, DEPTH), f32(PLANES, 24, DEPTH)],
    )
    both = ("px", "py")
    moved_modes = lax.all_to_all(sent, both, 0, 0)
    moved_modes = call(both_kernel, shape(16, 32, DEPTH), (moved_modes, c["both_in"], c["both_out"]))
    moved_modes = lax.all_to_all(moved_modes, both, 0, 0)

    sent, sums = call(
        second_kernel_body,
        [shape(16, 9, 2, DEPTH), shape(288, DEEP)],
        (moved_modes, fwd1, fwd2, back2, back1, to_z, c["from_z"]),
        [
            f32(PLANES, 48, DEPTH),
            f32(HID, FLAT),
            f32(PLANES, 24, DEPTH),
            f32(PLANES, 40, DEPTH),
            f32(2, PLANES, 24, DEPTH),
            f32(LOG, FLAT),
            f32(144, FLAT),
            f32(PLANES, 48, DEPTH),
        ]
        + stacks,
    )
    moved_modes = lax.all_to_all(sent, both, 0, 0)
    moved_modes = call(
        one_kernel,
        shape(16, 3, 4, DEPTH),
        (moved_modes, c["one_in"], c["one_out"]),
        [f32(3, 96, DEPTH)],
    )
    moved_modes = lax.all_to_all(moved_modes, both, 0, 0)

    sent = call(
        third_kernel_body,
        shape(PLANES, 17, 4, DEPTH),
        (
            moved_modes, field, hidden, weights, *kept, back2, back1, c["from_z"], sums,
            c["spread_t"], c["mask"], c["lift"],
        ),
        [f32(16, 16, DEPTH), f32(PLANES, 24, DEPTH), f32(PLANES, 16, DEPTH)]
        + stacks[3:]
        + [
            f32(144, FLAT),
            f32(PLANES, 48, DEPTH),
            f32(288, DEEP),
            f32(32, DEPTH),
        ],
    )
    recv = lax.all_to_all(sent, "px", 0, 0)
    main, edge = call(
        fold_kernel, [shape(3, 1, 64, DEPTH), shape(56, DEPTH)], (recv,), [f32(3, 80, DEPTH)]
    )
    other = lax.ppermute(edge, "py", swap)
    grad_velocity, first, end1, second, end2 = call(
        last_kernel,
        [
            shape(3, 1, 64, DEPTH),
            shape(27, 3, CHANNELS),
            shape(1, CHANNELS),
            shape(54, 3, CHANNELS),
            shape(1, COEFFS),
        ],
        (main, edge, other),
        [f32(8, 32, DEPTH)],
    )
    return (
        grad_velocity,
        jnp.transpose(first.reshape(3, 3, 3, 3, CHANNELS), (4, 0, 1, 2, 3)),
        end1.reshape(CHANNELS),
        jnp.transpose(second.reshape(COEFFS, 3, 3, 3, CHANNELS), (0, 4, 1, 2, 3)),
        end2.reshape(COEFFS),
    )


def fits_slabs(mesh):
    return mesh.shape["px"] == PLANES and mesh.shape["py"] == 2


def solution(mesh):
    return jax.shard_map(
        slab_device if fits_slabs(mesh) else on_device,
        mesh=mesh,
        in_specs=(
            P(None, ("groups", "px"), "py", None),
            P(None, ("groups", "px"), "py", None),
            P(),
            P(),
            P(),
            P(),
        ),
        out_specs=(
            P(None, ("groups", "px"), "py", None),
            P("groups", None, None, None, None),
            P("groups"),
            P("groups", None, None, None, None),
            P("groups"),
        ),
        check_vma=False,
    )
```

```python
import functools
import math

import jax
import jax.numpy as jnp
import numpy as np
from jax import lax
from jax.experimental import pallas as pl
from jax.experimental.pallas import tpu as pltpu
from jax.sharding import PartitionSpec as P

ITERS = 2


KAPPA = 0.25


def padded_2(value, sides, width):
    for axis, dim in sides:
        size, length = (lax.axis_size(axis), value.shape[dim])
        up = [(i, (i + 1) % size) for i in range(size)]
        down = [(j, i) for i, j in up]
        last = lax.slice_in_dim(value, length - width, length, axis=dim)
        initial = lax.slice_in_dim(value, 0, width, axis=dim)
        before = lax.ppermute(last, axis, up)
        after = lax.ppermute(initial, axis, down)
        value = jnp.concatenate([before, value, after], axis=dim)
    return value


def extend(field):
    rimmed = padded_2(field, (("px", 1), ("py", 2)), 1)
    return jnp.concatenate([rimmed[..., -1:], rimmed, rimmed[..., :1]], axis=3)


def across_columns(spectrum):
    return lax.all_to_all(spectrum, "px", split_axis=2, concat_axis=4, tiled=True)


def across_pairs(spectrum):
    return lax.all_to_all(spectrum, "py", split_axis=3, concat_axis=4, tiled=True)


def summed(grads):
    return lax.psum((grads[0], grads[1], grads[2], grads[3]), ("px", "py"))


def all_taps():
    return [
        (shift_x, shift_y, shift_z)
        for shift_x in range(3)
        for shift_y in range(3)
        for shift_z in range(3)
    ]


def gather_conv(padded, kernel):
    size_x = padded.shape[1] - 2
    size_y = padded.shape[2] - 2
    size_z = padded.shape[3] - 2
    stacked = jnp.concatenate(
        [
            padded[:, sx_one : sx_one + size_x, sy_one : sy_one + size_y, sz_one : sz_one + size_z]
            for sx_one, sy_one, sz_one in all_taps()
        ],
        axis=0,
    )
    matrix = jnp.transpose(kernel, (0, 2, 3, 4, 1)).reshape(kernel.shape[0], -1)
    result = jnp.einsum("ok,kxyz->oxyz", matrix, stacked, precision=lax.Precision.HIGHEST)
    return (result, stacked)


def scatter_conv(padded, kernel):
    outputs = kernel.shape[0]
    inputs = kernel.shape[1]
    size_x = padded.shape[1] - 2
    size_y = padded.shape[2] - 2
    size_z = padded.shape[3] - 2
    total = jnp.zeros((outputs, size_x, size_y, size_z), jnp.float32)
    for shift_x in range(3):
        matrix = jnp.transpose(kernel[:, :, shift_x], (0, 2, 3, 1)).reshape(outputs * 9, inputs)
        layer = jnp.einsum(
            "km,mxyz->kxyz",
            matrix,
            padded[:, shift_x : shift_x + size_x],
            precision=lax.Precision.HIGHEST,
        )
        layer = layer.reshape(outputs, 3, 3, size_x, size_y + 2, size_z + 2)
        for shift_y in range(3):
            for shift_z in range(3):
                total = (
                    total
                    + layer[
                        :,
                        shift_y,
                        shift_z,
                        :,
                        shift_y : shift_y + size_y,
                        shift_z : shift_z + size_z,
                    ]
                )
    return total


def flipped(kernel):
    return jnp.transpose(kernel[:, :, ::-1, ::-1, ::-1], (1, 0, 2, 3, 4))


def moved(padded, axis_dim, offset_cells):
    index = [slice(None), slice(1, -1), slice(1, -1), slice(1, -1)]
    index[axis_dim] = slice(1 + offset_cells, padded.shape[axis_dim] - 1 + offset_cells)
    return padded[tuple(index)]


def advect(padded, weights):
    center = moved(padded, 1, 0)
    total = jnp.zeros_like(center)
    for direction in range(3):
        ahead = moved(padded, direction + 1, 1)
        behind = moved(padded, direction + 1, -1)
        vplus = 0.5 * (center[direction] + ahead[direction])
        vminus = 0.5 * (behind[direction] + center[direction])
        upper = center + weights[2 * direction] * (ahead - center)
        lower = center + weights[2 * direction + 1] * (behind - center)
        total = total + vplus * upper - vminus * lower
    return total


def advect_back(padded, weights_pad, source_pad):
    center = moved(padded, 1, 0)
    source = moved(source_pad, 1, 0)
    weights = moved(weights_pad, 1, 0)
    grad_field = jnp.zeros_like(center)
    fluxes = []
    parts = []
    for direction in range(3):
        ahead = moved(padded, direction + 1, 1)
        behind = moved(padded, direction + 1, -1)
        vplus = 0.5 * (center[direction] + ahead[direction])
        vminus = 0.5 * (behind[direction] + center[direction])
        rate_up = weights[2 * direction]
        rate_low = weights[2 * direction + 1]
        rate_before = moved(weights_pad[2 * direction : 2 * direction + 1], direction + 1, -1)[0]
        rate_after = moved(weights_pad[2 * direction + 1 : 2 * direction + 2], direction + 1, 1)[0]
        source_before = moved(source_pad, direction + 1, -1)
        source_after = moved(source_pad, direction + 1, 1)
        upper = center + rate_up * (ahead - center)
        lower = center + rate_low * (behind - center)
        upper_before = behind + rate_before * (center - behind)
        lower_after = ahead + rate_after * (center - ahead)
        grad_field = grad_field + source * (vplus * (1.0 - rate_up) - vminus * (1.0 - rate_low))
        grad_field = (
            grad_field + vminus * rate_before * source_before - vplus * rate_after * source_after
        )
        fluxes.append(
            0.5
            * (
                jnp.sum(source * upper, 0)
                - jnp.sum(source * lower, 0)
                + jnp.sum(source_before * upper_before, 0)
                - jnp.sum(source_after * lower_after, 0)
            )
        )
        parts.append(jnp.sum(source * vplus * (ahead - center), 0))
        parts.append(-jnp.sum(source * vminus * (behind - center), 0))
    return (grad_field + jnp.stack(fluxes), jnp.stack(parts))


def tables(count):
    index = jnp.arange(count, dtype=jnp.int32)
    phase = index[:, None] * index[None, :] % count
    angle = phase.astype(jnp.float32) * (2.0 * math.pi / count)
    return (jnp.cos(angle), jnp.sin(angle))


def mix(form, data, table):
    return jnp.einsum(form, data, table, precision=lax.Precision.HIGHEST)


def waves(start, count, total):
    index = start + jnp.arange(count, dtype=jnp.int32)
    return jnp.where(index < total // 2, index, index - total).astype(jnp.float32)


def project(field):
    depth = field.shape[3]
    cos_z, sin_z = tables(depth)
    real_z = mix("cxyz,zk->cxky", field, cos_z)
    imag_z = -mix("cxyz,zk->cxky", field, sin_z)
    spectrum = across_pairs(jnp.stack([real_z, imag_z]))
    span_y = spectrum.shape[4]
    cos_y, sin_y = tables(span_y)
    real_y = mix("cxky,yq->cqkx", spectrum[0], cos_y) + mix("cxky,yq->cqkx", spectrum[1], sin_y)
    imag_y = mix("cxky,yq->cqkx", spectrum[1], cos_y) - mix("cxky,yq->cqkx", spectrum[0], sin_y)
    spectrum = across_columns(jnp.stack([real_y, imag_y]))
    span_x = spectrum.shape[4]
    cos_x, sin_x = tables(span_x)
    real_x = mix("cqkx,xp->cqkp", spectrum[0], cos_x) + mix("cqkx,xp->cqkp", spectrum[1], sin_x)
    imag_x = mix("cqkx,xp->cqkp", spectrum[1], cos_x) - mix("cqkx,xp->cqkp", spectrum[0], sin_x)
    rows_y = spectrum.shape[2]
    rows_z = spectrum.shape[3]
    wave_y = waves(lax.axis_index("px") * rows_y, rows_y, span_y)[:, None, None]
    wave_z = waves(lax.axis_index("py") * rows_z, rows_z, depth)[None, :, None]
    wave_x = waves(0, span_x, span_x)[None, None, :]
    size = jnp.maximum(wave_x * wave_x + wave_y * wave_y + wave_z * wave_z, 1.0)
    vectors = jnp.stack(jnp.broadcast_arrays(wave_x, wave_y, wave_z))
    real_x = real_x - vectors * (
        (wave_x * real_x[0] + wave_y * real_x[1] + wave_z * real_x[2]) / size
    )
    imag_x = imag_x - vectors * (
        (wave_x * imag_x[0] + wave_y * imag_x[1] + wave_z * imag_x[2]) / size
    )
    back_real = (mix("cqkp,px->cxkq", real_x, cos_x) - mix("cqkp,px->cxkq", imag_x, sin_x)) / span_x
    back_imag = (mix("cqkp,px->cxkq", imag_x, cos_x) + mix("cqkp,px->cxkq", real_x, sin_x)) / span_x
    spectrum = across_columns(jnp.stack([back_real, back_imag]))
    rows_real = (
        mix("cxkq,qy->cxyk", spectrum[0], cos_y) - mix("cxkq,qy->cxyk", spectrum[1], sin_y)
    ) / span_y
    rows_imag = (
        mix("cxkq,qy->cxyk", spectrum[1], cos_y) + mix("cxkq,qy->cxyk", spectrum[0], sin_y)
    ) / span_y
    spectrum = across_pairs(jnp.stack([rows_real, rows_imag]))
    return (
        mix("cxyk,kz->cxyz", spectrum[0], cos_z) - mix("cxyk,kz->cxyz", spectrum[1], sin_z)
    ) / depth


def forward_state(field, first_kernel, first_bias, second_kernel, second_bias):
    padded = extend(field)
    first_out, field_taps = gather_conv(padded, first_kernel)
    hidden = jnp.tanh(first_out + first_bias[:, None, None, None])
    weights = jax.nn.sigmoid(
        scatter_conv(extend(hidden), second_kernel) + second_bias[:, None, None, None]
    )
    return (padded, hidden, weights, field_taps)


def backward_step(state, upstream, first_kernel, second_kernel):
    padded, hidden, weights, field_taps = state
    moved_grad = project(upstream)
    source = -KAPPA * moved_grad
    stacked = extend(jnp.concatenate([source, weights], axis=0))
    grad_field, grad_weights = advect_back(padded, stacked[3:], stacked[:3])
    grad_field = grad_field + moved_grad
    grad_logits = grad_weights * weights * (1.0 - weights)
    logits_pad = extend(grad_logits)
    grad_hidden, logit_taps = gather_conv(logits_pad, flipped(second_kernel))
    product = jnp.einsum("kxyz,mxyz->km", logit_taps, hidden, precision=lax.Precision.HIGHEST)
    product = product.reshape(3, 3, 3, second_kernel.shape[0], second_kernel.shape[1])
    grad_second = jnp.transpose(product[::-1, ::-1, ::-1], (3, 4, 0, 1, 2))
    grad_second_bias = jnp.sum(grad_logits, axis=(1, 2, 3))
    grad_pre = grad_hidden * (1.0 - hidden * hidden)
    pre_pad = extend(grad_pre)
    grad_field = grad_field + scatter_conv(pre_pad, flipped(first_kernel))
    first_product = jnp.einsum(
        "oxyz,kxyz->ok", grad_pre, field_taps, precision=lax.Precision.HIGHEST
    )
    first_product = first_product.reshape(first_kernel.shape[0], 3, 3, 3, first_kernel.shape[1])
    grad_first = jnp.transpose(first_product, (0, 4, 1, 2, 3))
    grad_first_bias = jnp.sum(grad_pre, axis=(1, 2, 3))
    return (grad_field, (grad_first, grad_first_bias, grad_second, grad_second_bias))


def on_device(velocity, cotangent, first_kernel, first_bias, second_kernel, second_bias):
    field = velocity
    fields = [velocity]
    saved = []
    for section in range(ITERS):
        state = forward_state(field, first_kernel, first_bias, second_kernel, second_bias)
        saved.append(state)
        field = project(field - KAPPA * advect(state[0], state[2]))
        fields.append(field)
    upstream = cotangent
    totals = None
    for section in reversed(range(ITERS)):
        state = saved[section]
        upstream, grads = backward_step(state, upstream, first_kernel, second_kernel)
        grads = summed(grads)
        if totals is None:
            totals = grads
        else:
            totals = tuple((older + newer for older, newer in zip(totals, grads)))
    return (upstream, totals[0], totals[1], totals[2], totals[3])


SLAB = 8
RIM = 2
REACH = SLAB + 2 * RIM
WIDE = SLAB + 2
PLANES = 8
DEPTH = 128
ROWS = 128
CHANNELS = 16
COEFFS = 6
BAND = 32
HID = CHANNELS * WIDE
LOG = COEFFS * SLAB
STACK = 9 * 48
UNIT = 36
BROAD = HID + 16
DEEP = 3 * HID + 16
PLACE = (0, 2, 1)
FLAT = PLANES * DEPTH
NN = ((1,), (0,))
NT = ((1,), (1,))


def real_basis(count):
    half = count // 2
    angle = 2.0 * np.pi * np.arange(count) / count
    rows = [np.full(count, 1.0 / np.sqrt(count))]
    rows += [np.sqrt(2.0 / count) * np.cos(k * angle) for k in range(1, half)]
    rows += [np.cos(half * angle) / np.sqrt(count)]
    rows += [np.sqrt(2.0 / count) * np.sin(k * angle) for k in range(1, half)]
    return np.stack(rows)


def wide_table(table):
    high, low = halves(table)
    return np.concatenate([high, low, high], axis=1)


def tall_table(table):
    high, low = halves(table)
    return np.concatenate([high, high, low])


def halves(table):
    high = table.astype(np.float32).astype(jnp.bfloat16)
    low = (table - high.astype(np.float64)).astype(np.float32).astype(jnp.bfloat16)
    return high, low


def slab_of(device):
    return (device % 2) * PLANES + device // 2


@functools.cache
def constants():
    basis_z = real_basis(DEPTH)
    order = []
    for group in range(4):
        order += [16 * group + i for i in range(16)] + [64 + 16 * group + i for i in range(16)]
    mode_z = basis_z[order]
    basis_y = real_basis(ROWS)

    def rows(offset, count):
        at = [SLAB * slab_of(j) + offset + i for j in range(16) for i in range(count)]
        return basis_y[:, np.array(at) % ROWS]

    own, half_one, half_two = rows(0, SLAB), rows(0, 4), rows(4, 4)
    before, after = rows(-RIM, RIM), rows(SLAB, RIM)
    both_in = own
    both_out = np.concatenate([own, before, after], axis=1).T
    one_in = np.concatenate(
        [np.concatenate([half_one, before], axis=1), np.concatenate([half_two, after], axis=1)]
    )
    one_out = np.concatenate([half_one, half_two], axis=1).T

    spread = np.zeros((288, 32))
    mask = np.zeros((3, 288, DEEP))
    lanes = np.arange(CHANNELS) * WIDE
    for e in range(3):
        for o in range(COEFFS):
            for q in range(SLAB):
                row = e * 48 + o * SLAB + q
                spread[row, e * COEFFS + o] = 1.0
                for b in range(3):
                    for a in range(3):
                        mask[b, row, a * HID + lanes + q + b] = 1.0
        for m in range(3):
            for r in range(REACH):
                row = 144 + e * 48 + m * REACH + r
                spread[row, 18 + e * 3 + m] = 1.0
                for b in range(3):
                    for a in range(3):
                        if 0 <= r - b < WIDE:
                            mask[b, row, a * HID + lanes + r - b] = 1.0
    spread[144 + 48 + UNIT, 27] = 1.0
    mask[0, 144 + 48 + UNIT, PLACE[1] * HID : (PLACE[1] + 1) * HID] = 1.0
    mask[0, 48:96, 3 * HID] = 1.0
    lift = np.zeros((3, 512, 256))
    for b in range(3):
        for a in range(3):
            lift[b, PLACE[a] * HID + np.arange(HID), 16 * (3 * b + a) + np.arange(HID) // WIDE] = 1.0
    lift[0, 3 * HID, 128 + 96] = 1.0
    lift = lift.reshape(3 * 512, 256)
    half = jnp.bfloat16
    return dict(
        to_z=tall_table(mode_z.T),
        from_z=tall_table(mode_z),
        both_in=wide_table(both_in),
        both_out=wide_table(both_out),
        one_in=wide_table(one_in),
        one_out=wide_table(one_out),
        spread_t=np.concatenate([spread.T, spread.T], axis=1).astype(half),
        mask=mask.astype(half),
        lift=lift.astype(half),
    )


def dot(left, right, dims=NN):
    return lax.dot_general(left, right, (dims, ((), ())), preferred_element_type=jnp.float32)


def split(value):
    high = value.astype(jnp.bfloat16)
    return high, (value - high.astype(jnp.float32)).astype(jnp.bfloat16)


def dot_stacked(left, right, dims=NN):
    rows = left.shape[0] // 2
    main = dot(left[...], right[0], dims)
    return main[:rows] + (main[rows:] + dot(left[0:rows, :], right[1], dims))


def dot_wide(left, right):
    return dot(left[...], jnp.concatenate([right[0], right[0], right[1]], axis=0))


def widened(value):
    high, low = split(value)
    return jnp.concatenate([high, low, high], axis=1)


def stacked(value):
    return jnp.concatenate(split(value), axis=0)


def turn(value, shift):
    shift = shift % value.shape[-1]
    return value if shift == 0 else pltpu.roll(value, shift, value.ndim - 1)


def plane(x):
    x = x % PLANES
    return slice(x * DEPTH, (x + 1) * DEPTH)


def call(kernel, outs, args, scratch=(), room=16, away=()):
    single = not isinstance(outs, (list, tuple))
    vmem = pl.BlockSpec(memory_space=pltpu.VMEM)
    cost = pl.CostEstimate(flops=1, bytes_accessed=1, transcendentals=0) if away else None
    return pl.pallas_call(
        kernel,
        out_shape=outs,
        in_specs=[
            pl.BlockSpec(memory_space=pltpu.HBM) if i in away else vmem for i in range(len(args))
        ],
        out_specs=vmem if single else [vmem] * len(outs),
        scratch_shapes=list(scratch),
        cost_estimate=cost,
        compiler_params=pltpu.CompilerParams(vmem_limit_bytes=room * 2**20),
    )(*args)


def fetch(pairs, sems):
    copies = [pltpu.make_async_copy(src, dst, sems.at[i]) for i, (src, dst) in enumerate(pairs)]
    for copy in copies:
        copy.start()
    return copies


def shape(*dims, kind=jnp.float32):
    return jax.ShapeDtypeStruct(dims, kind)


def counting(size, dim):
    return lax.broadcasted_iota(jnp.int32, size, dim).astype(jnp.float32)


def remainder(value, count):
    return value - count * jnp.floor((value + 0.5) / count)


def band_tables(tall):
    row, col = (0, 1) if tall else (1, 0)
    size = lambda rows, cols: (rows, cols) if tall else (cols, rows)
    where = counting(size(2 * STACK, 96), row)
    to = counting(size(2 * STACK, 96), col)
    first = where - 8.0 * to
    third = to - 54.0
    second = where - STACK - (16.0 * third - 4.0 * remainder(third, 3.0))
    picks = ((to < 54.0) & (first >= 0.0) & (first < 8.0)) | (
        (to >= 54.0) & (to < 81.0) & (second >= 0.0) & (second < 12.0)
    )
    where = counting(size(2 * STACK, HID), row)
    inner = remainder(counting(size(2 * STACK, HID), col), 10.0)
    outer = where - STACK
    offset = jnp.where(
        where < STACK,
        inner - remainder(where, 8.0),
        remainder(remainder(outer, 48.0), 12.0) - inner,
    )
    gap = counting(size(HID, CHANNELS), row) - 10.0 * counting(size(HID, CHANNELS), col)
    lift = (gap >= 0.0) & (gap < 10.0)
    half = jnp.bfloat16
    return picks.astype(jnp.float32).astype(half), offset, lift.astype(jnp.float32).astype(half)


def weights_kernel(
    far1, far2, far3, far4, z_in, fwd2, fwd1, back2, back1, z_out, blocks, taps1, taps2, bias1, bias2, sems
):
    copies = fetch([(far1, taps1), (far2, taps2), (far3, bias1), (far4, bias2)], sems)
    blocks[...] = jnp.zeros_like(blocks)
    z_out[...] = z_in[...]
    spread, offset, lift = band_tables(True)
    spread_t, offset_t, lift_t = band_tables(False)
    for copy in copies:
        copy.wait()
    for b in range(3):
        for a in range(3):
            for e in range(3):
                tap = a * 3 + e
                for o in range(COEFFS):
                    blocks[b, tap * 6 + o, :] = taps2[o * 9 + a * 3 + b, e, :]
                for m in range(3):
                    blocks[b, 54 + tap * 3 + m, :] = taps1[m * 9 + a * 3 + b, e, :]
    tall = [jnp.zeros((2 * STACK, HID), jnp.float32)] * 2
    flat = [jnp.zeros((HID, 2 * STACK), jnp.float32)] * 2
    for b in range(3):
        for half, block in enumerate(split(blocks[b])):
            rows = dot(spread, block).astype(jnp.bfloat16)
            tall[half] = jnp.where(offset == float(b), dot(rows, lift_t), tall[half])
            cols = dot(lift, block, NT).astype(jnp.bfloat16)
            flat[half] = jnp.where(offset_t == float(b), dot(cols, spread_t), flat[half])
    for half in range(2):
        rows, cols = slice(half * 144, half * 144 + 144), slice(half * HID, half * HID + HID)
        for a in range(3):
            first = PLACE[a] * HID
            part = tall[half][a * 144 : a * 144 + 144]
            fwd2[rows, first : first + HID] = part.astype(jnp.bfloat16)
            part = tall[half][STACK + a * 144 : STACK + a * 144 + 144]
            back1[rows, first : first + HID] = part.astype(jnp.bfloat16)
        back2[cols, :] = flat[half][:, :STACK].astype(jnp.bfloat16)
    gap = counting((LOG, COEFFS), 0) - 8.0 * counting((LOG, COEFFS), 1)
    pick = ((gap >= 0.0) & (gap < 8.0)).astype(jnp.float32).astype(jnp.bfloat16)
    second = counting((LOG, 16), 1) < 1.0
    one = split(jnp.broadcast_to(bias1[...], (STACK, CHANNELS)))
    first = counting((HID, STACK), 1) == 4.0 * 48.0 + UNIT
    two = split(jnp.broadcast_to(bias2[...], (16, COEFFS)))
    fwd2[:, 3 * HID :] = jnp.zeros((288, 16), jnp.bfloat16)
    back1[:, 3 * HID :] = jnp.zeros((288, 16), jnp.bfloat16)
    for half in range(2):
        value = jnp.where(first, dot(lift, one[half], NT), flat[half][:, STACK:])
        fwd1[half * HID : half * HID + HID, :] = value.astype(jnp.bfloat16)
        value = jnp.where(second, dot(pick, two[half], NT), 0.0)
        start = half * 144 + LOG
        fwd2[start : start + LOG, 3 * HID :] = value.astype(jnp.bfloat16)


def pack_kernel(fields, out, ext):
    ext[...] = jnp.zeros_like(ext)
    for m in range(3):
        ext[m, 8:72, :] = fields[m, 0]
    for q in range(PLANES):
        for m in range(3):
            out[q, m * REACH : (m + 1) * REACH, :] = ext[m, 8 * q + 6 : 8 * q + 18, :]
            out[q, 36 + 8 * m : 44 + 8 * m, :] = fields[3 + m, 0, 8 * q : 8 * q + 8, :]
        out[q, 60:64, :] = jnp.zeros((4, DEPTH), jnp.float32)


def rim_kernel(packed, other, out):
    for q in range(PLANES):
        for i in range(15):
            out[q, i] = packed[q, 4 * i : 4 * i + 4, :]
    for m in range(3):
        out[0, 3 * m, 0:2, :] = other[m, 0, 62:64, :]
        out[PLANES - 1, 3 * m + 2, 2:4, :] = other[m, 0, 0:2, :]


def unit_row():
    row = lax.broadcasted_iota(jnp.int32, (16, FLAT), 0)
    return jnp.where(row == 0, 1.0, 0.0).astype(jnp.bfloat16)


def stack_planes(value, cut, high, low):
    parts = split(value)
    high[0:HID, cut] = parts[0]
    low[0:HID, cut] = parts[1]


def finish_planes(high, low):
    high[HID:, :] = unit_row()
    low[HID:, :] = jnp.zeros((16, FLAT), jnp.bfloat16)


def shifted(taps, first_row, rows, first, count, shift):
    return beside(
        [taps[first_row : first_row + rows, plane(first + i + shift)] for i in range(count)]
    )


def nine(taps, half, first, count, sign):
    return jnp.concatenate(
        [shifted(taps, 144 * half, 144, first, count, sign * (a - 1)) for a in range(3)], axis=0
    )


def three(taps, first, count, sign):
    return jnp.concatenate(
        [shifted(taps, 0, HID, first, count, sign * shift) for shift in (-1, 1, 0)]
        + [shifted(taps, HID, 16, first, count, 0)],
        axis=0,
    )


def stack_logits(whole, x, taps):
    for e in range(3):
        for half, part_of in enumerate(split(turn(whole, e - 1))):
            taps[144 * half + 48 * e : 144 * half + 48 * e + 48, plane(x)] = part_of


def stack_field(field, taps):
    for x in range(PLANES):
        whole = field[x, 0:48, :]
        for e in range(3):
            for half, part_of in enumerate(split(turn(whole, 1 - e))):
                taps[144 * half + 48 * e : 144 * half + 48 * e + 48, plane(x)] = part_of


def network(field, fwd1, fwd2, hidden, weights, u_taps, h_hi, h_lo, work):
    stack_field(field, u_taps)
    finish_planes(h_hi, h_lo)
    for pair in range(4):
        cut = slice(pair * 256, pair * 256 + 256)
        taps = (nine(u_taps, 0, 2 * pair, 2, 1), nine(u_taps, 1, 2 * pair, 2, 1))
        value = jnp.tanh(dot_stacked(fwd1, taps))
        hidden[:, cut] = value
        stack_planes(value, cut, h_hi, h_lo)
    for pair in range(4):
        cut = slice(pair * 256, pair * 256 + 256)
        work[:, cut] = dot_stacked(fwd2, (three(h_hi, 2 * pair, 2, 1), three(h_lo, 2 * pair, 2, 1)))
    for x in range(PLANES):
        total = work[LOG : 2 * LOG, plane(x)]
        total = total + turn(work[0:LOG, plane(x)], 1) + turn(work[2 * LOG : 3 * LOG, plane(x)], -1)
        weights[:, plane(x)] = jax.nn.sigmoid(total)


def own_rows(field):
    return [
        [field[x, m * REACH + RIM : m * REACH + RIM + SLAB, :] for m in range(3)] for x in range(PLANES)
    ]


def around(field, own, x, direction, sign):
    if direction == 0:
        return own[(x + sign) % PLANES]
    if direction == 1:
        first = RIM + sign
        return [field[x, m * REACH + first : m * REACH + first + SLAB, :] for m in range(3)]
    return [turn(value, -sign) for value in own[x]]


def advected(field, cells, weights, x):
    center = cells[x]
    total = [jnp.zeros((SLAB, DEPTH), jnp.float32)] * 3
    for d in range(3):
        ahead = around(field, cells, x, d, 1)
        behind = around(field, cells, x, d, -1)
        plus = 0.5 * (center[d] + ahead[d])
        minus = 0.5 * (behind[d] + center[d])
        rate_up = weights[2 * d * SLAB : (2 * d + 1) * SLAB, plane(x)]
        rate_low = weights[(2 * d + 1) * SLAB : (2 * d + 2) * SLAB, plane(x)]
        for m in range(3):
            upper = center[m] + rate_up * (ahead[m] - center[m])
            lower = center[m] + rate_low * (behind[m] - center[m])
            total[m] = total[m] + plus * upper - minus * lower
    return [center[m] - KAPPA * total[m] for m in range(3)]


ROOT = math.sqrt(0.5)


def to_modes(x):
    s = [x[i] + x[i + 4] for i in range(4)]
    d = [x[i] - x[i + 4] for i in range(4)]
    even, odd = s[0] + s[2], s[1] + s[3]
    up, down = ROOT * (d[1] + d[3]), ROOT * (d[1] - d[3])
    scale = 0.5 * ROOT
    return [
        scale * (even + odd),
        scale * (even - odd),
        0.5 * (d[0] + down),
        0.5 * (up + d[2]),
        0.5 * (s[0] - s[2]),
        0.5 * (s[1] - s[3]),
        0.5 * (d[0] - down),
        0.5 * (up - d[2]),
    ]


def from_modes(v):
    even, odd = 0.5 * ROOT * (v[0] + v[1]), 0.5 * ROOT * (v[0] - v[1])
    cos, sin = 0.5 * v[4], 0.5 * v[5]
    e = [even + cos, odd + sin, even - cos, odd - sin]
    across, along = 0.5 * ROOT * (v[2] - v[6]), 0.5 * ROOT * (v[3] + v[7])
    o = [0.5 * (v[2] + v[6]), along + across, 0.5 * (v[3] - v[7]), along - across]
    return [e[i] + o[i] for i in range(4)] + [e[i] - o[i] for i in range(4)]


def lane_groups(size):
    return lax.broadcasted_iota(jnp.int32, (size, DEPTH), 1) // BAND


def scatter_modes(source, rows, out):
    groups = lane_groups(rows)
    for p in range(4):
        for g in range(4):
            total = None
            for f in range(2):
                for t in range(2):
                    slot = 2 * f + t
                    value = turn(source(f, 2 * p + t), BAND * (slot - g))
                    total = value if total is None else jnp.where(groups == slot, value, total)
            if len(out.shape) == 3:
                out[p * 4 + g] = total
            else:
                for i in range(out.shape[1]):
                    out[p * 4 + g, i] = total[2 * i : 2 * i + 2]


def gather_modes(recv, f, k, first, rows):
    groups = lane_groups(rows)
    slot = 2 * f + k % 2
    total = None
    for g in range(4):
        value = turn(recv[(k // 2) * 4 + g, first : first + rows, :], BAND * (g - slot))
        total = value if total is None else jnp.where(groups == g, value, total)
    return total


def first_kernel_body(
    recv, fwd1, fwd2, to_z, out, field, hidden, weights, u_taps, h_hi, h_lo, work, modes, cot
):
    for x in range(PLANES):
        for i in range(9):
            field[x, 4 * i : 4 * i + 4, :] = recv[x, i]
        field[x, 36:37, :] = jnp.ones((1, DEPTH), jnp.float32)
        field[x, 37:48, :] = jnp.zeros((11, DEPTH), jnp.float32)
        for i in range(6):
            cot[x, 4 * i : 4 * i + 4, :] = recv[x, 9 + i]
    network(field, fwd1, fwd2, hidden, weights, u_taps, h_hi, h_lo, work)
    table = to_z[...]
    cells = own_rows(field)
    moved_field = [jnp.concatenate(advected(field, cells, weights, x), axis=0) for x in range(PLANES)]
    for f in range(2):
        planes = moved_field if f == 0 else [cot[x] for x in range(PLANES)]
        for k, value in enumerate(to_modes(planes)):
            modes[f, k] = value
    for f in range(2):
        flat = modes[f].reshape(PLANES * 24, DEPTH)
        modes[f] = dot(widened(flat), table).reshape(PLANES, 24, DEPTH)
    scatter_modes(lambda f, k: modes[f, k], 24, out)


def leray(parts):
    device = lax.axis_index("px") * 2 + lax.axis_index("py")
    pair = device // 4
    group = device % 4
    lane = lax.broadcasted_iota(jnp.int32, (ROWS, DEPTH), 1)
    row = lax.broadcasted_iota(jnp.int32, (ROWS, DEPTH), 0)
    odd_x = (lane // BAND) % 2
    odd_z = (lane // 16) % 2
    number_z = 16 * group + lane % 16
    top_x = (odd_x == 1) & (pair == 0)
    top_y = row == ROWS // 2
    top_z = (odd_z == 1) & (number_z == 0)
    number_y = row % (ROWS // 2)
    real = lambda value: value.astype(jnp.float32)
    rate_x = real(jnp.where(odd_x == 1, -pair, pair))
    rate_y = real(jnp.where(row < ROWS // 2, number_y, -number_y))
    rate_z = real(jnp.where(odd_z == 1, -number_z, number_z))
    high_x = real(jnp.where(top_x, PLANES // 2, 0))
    high_y = real(jnp.where(top_y, ROWS // 2, 0))
    high_z = real(jnp.where(top_z, DEPTH // 2, 0))
    size = rate_x * rate_x + rate_y * rate_y + rate_z * rate_z
    size = size + high_x * high_x + high_y * high_y + high_z * high_z
    inverse = 1.0 / jnp.maximum(size, 1.0)

    def slope_x(value):
        return rate_x * jnp.where(odd_x == 1, turn(value, BAND), turn(value, -BAND))

    def slope_y(value):
        return rate_y * jnp.concatenate([value[ROWS // 2 :], value[: ROWS // 2]], axis=0)

    def slope_z(value):
        return rate_z * jnp.where(odd_z == 1, turn(value, 16), turn(value, -16))

    spread = (slope_x(parts[0]) + slope_y(parts[1]) + slope_z(parts[2])) * inverse
    high = (high_x * parts[0] + high_y * parts[1] + high_z * parts[2]) * inverse
    return (
        parts[0] + slope_x(spread) - high_x * high,
        parts[1] + slope_y(spread) - high_y * high,
        parts[2] + slope_z(spread) - high_z * high,
    )


def beside(parts):
    return jnp.concatenate(parts, axis=1)


def part(value, m):
    return value[:, m * DEPTH : (m + 1) * DEPTH]


def two_halves(first, second):
    low = lax.broadcasted_iota(jnp.int32, first.shape, 1) < DEPTH // 2
    return jnp.where(low, first, turn(second, DEPTH // 2))


def both_kernel(recv, table_in, table_out, out):
    data = beside([recv[:, 8 * m : 8 * m + 8, :].reshape(ROWS, DEPTH) for m in range(3)])
    modes = dot_wide(table_in, split(data))
    fixed = beside(leray([part(modes, m) for m in range(3)]))
    back = dot_wide(table_out, split(fixed))
    for m in range(3):
        whole = part(back, m)
        out[:, 8 * m : 8 * m + 8, :] = whole[:ROWS].reshape(16, SLAB, DEPTH)
        rim = two_halves(whole[ROWS : ROWS + 32], whole[ROWS + 32 :])
        for device in range(16):
            out[device, 24 + 2 * m : 26 + 2 * m, :] = rim[2 * device : 2 * device + 2]
    out[:, 30:32, :] = jnp.zeros((16, 2, DEPTH), jnp.float32)


def one_kernel(recv, table_in, table_out, out, data):
    for device in range(16):
        for m in range(3):
            for i in range(2):
                first = 4 * device + 2 * i
                data[m, first : first + 2, :] = recv[device, 2 * m + i]
            data[m, 64 + 2 * device : 66 + 2 * device, :] = recv[device, 6 + m]
    modes = dot_wide(table_in, split(beside([data[m] for m in range(3)])))
    low, high = modes[:ROWS], modes[ROWS:]
    fixed = beside(leray([part(low, m) + turn(part(high, m), DEPTH // 2) for m in range(3)]))
    back = dot_wide(table_out, split(fixed))
    for m in range(3):
        whole = two_halves(part(back, m)[:64], part(back, m)[64:])
        for device in range(16):
            out[device, m] = whole[4 * device : 4 * device + 4]


def pullback(field, grad, hidden, weights, back2, back1, l_taps, p_hi, p_lo, work, slope, middle, late):
    slope[...] = jnp.zeros_like(slope)
    row = lax.broadcasted_iota(jnp.int32, (SLAB, DEPTH), 0)
    stay = [None] * PLANES
    cells = own_rows(field)
    pushed = {}
    for x in range(PLANES):
        center = cells[x]
        source = [-KAPPA * grad[x, m * SLAB : (m + 1) * SLAB, :] for m in range(3)]
        own = [grad[x, m * SLAB : (m + 1) * SLAB, :] for m in range(3)]
        logits = []
        for d in range(3):
            ahead = around(field, cells, x, d, 1)
            behind = around(field, cells, x, d, -1)
            plus = 0.5 * (center[d] + ahead[d])
            minus = 0.5 * (behind[d] + center[d])
            rate_up = weights[2 * d * SLAB : (2 * d + 1) * SLAB, plane(x)]
            rate_low = weights[(2 * d + 1) * SLAB : (2 * d + 2) * SLAB, plane(x)]
            grad_up = grad_low = grad_plus = grad_minus = None
            to_ahead, to_behind = [], []
            add = lambda total, term: term if total is None else total + term
            for m in range(3):
                gap_up = ahead[m] - center[m]
                gap_low = behind[m] - center[m]
                grad_plus = add(grad_plus, source[m] * (center[m] + rate_up * gap_up))
                grad_minus = add(grad_minus, -source[m] * (center[m] + rate_low * gap_low))
                grad_up = add(grad_up, source[m] * gap_up)
                grad_low = add(grad_low, -source[m] * gap_low)
                push_up = source[m] * plus
                push_low = -source[m] * minus
                to_ahead.append(push_up * rate_up)
                to_behind.append(push_low * rate_low)
                own[m] = own[m] + (push_up - to_ahead[m]) + (push_low - to_behind[m])
            own[d] = own[d] + 0.5 * (grad_plus + grad_minus)
            to_ahead[d] = to_ahead[d] + 0.5 * grad_plus
            to_behind[d] = to_behind[d] + 0.5 * grad_minus
            logits.append(grad_up * plus * rate_up * (1.0 - rate_up))
            logits.append(grad_low * minus * rate_low * (1.0 - rate_low))
            for m in range(3):
                if d == 0:
                    pushed[x, m, 1], pushed[x, m, -1] = to_ahead[m], to_behind[m]
                elif d == 1:
                    first = m * REACH + RIM
                    down = pltpu.roll(to_ahead[m], 1, 0)
                    up = pltpu.roll(to_behind[m], SLAB - 1, 0)
                    own[m] = own[m] + jnp.where(row > 0, down, 0.0) + jnp.where(row < SLAB - 1, up, 0.0)
                    slope[x, first + SLAB : first + SLAB + 1, :] = down[0:1]
                    slope[x, first - 1 : first, :] = up[SLAB - 1 :]
                else:
                    own[m] = own[m] + turn(to_ahead[m], 1) + turn(to_behind[m], -1)
        stay[x] = own
        whole = jnp.concatenate(logits, axis=0)
        stack_logits(whole, x, l_taps)
    for x in range(PLANES):
        for m in range(3):
            value = stay[x][m] + pushed[(x - 1) % PLANES, m, 1] + pushed[(x + 1) % PLANES, m, -1]
            slope[x, m * REACH + RIM : m * REACH + RIM + SLAB, :] = value
    for pair in range(4):
        cut = slice(pair * 256, pair * 256 + 256)
        taps = (nine(l_taps, 0, 2 * pair, 2, -1), nine(l_taps, 1, 2 * pair, 2, -1))
        value = dot_stacked(back2, taps)
        value = value * (1.0 - hidden[:, cut] * hidden[:, cut])
        stack_planes(value, cut, p_hi, p_lo)
    finish_planes(p_hi, p_lo)
    middle()
    for pair in range(4):
        cut = slice(pair * 256, pair * 256 + 256)
        work[:, cut] = dot_stacked(back1, (three(p_hi, 2 * pair, 2, -1), three(p_lo, 2 * pair, 2, -1)))
    late()
    for x in range(PLANES):
        total = slope[x, 0:40, :] + work[48:88, plane(x)]
        slope[x, 0:40, :] = total + turn(work[0:40, plane(x)], -1) + turn(work[96:136, plane(x)], 1)


def kernel_sums(taps, high, low, sign):
    return dot_stacked(taps, (three(high, 0, PLANES, sign), three(low, 0, PLANES, sign)), NT)


def second_kernel_body(
    recv, fwd1, fwd2, back2, back1, to_z, from_z,
    out, sums,
    field, hidden, grad, modes, rows6, weights, work, slope,
    u_taps, h_hi, h_lo, l_taps, p_hi, p_lo,
):
    back_z = from_z[...]
    for k in range(PLANES):
        modes[k, 0:32, :] = gather_modes(recv, 0, k, 0, 32)
        modes[k, 32:40, :] = gather_modes(recv, 1, k, 24, 8)
    flat = dot(widened(modes[...].reshape(PLANES * 40, DEPTH)), back_z)
    modes[...] = flat.reshape(PLANES, 40, DEPTH)
    for x, value in enumerate(from_modes([modes[k] for k in range(PLANES)])):
        for m in range(3):
            first = m * REACH
            field[x, first : first + RIM, :] = value[24 + 2 * m : 26 + 2 * m]
            field[x, first + RIM : first + RIM + SLAB, :] = value[8 * m : 8 * m + 8]
            field[x, first + RIM + SLAB : first + REACH, :] = value[32 + 2 * m : 34 + 2 * m]
        field[x, 36:37, :] = jnp.ones((1, DEPTH), jnp.float32)
        field[x, 37:48, :] = jnp.zeros((11, DEPTH), jnp.float32)
    network(field, fwd1, fwd2, hidden, weights, u_taps, h_hi, h_lo, work)
    for k in range(PLANES):
        grad[k] = gather_modes(recv, 1, k, 0, 24)
    flat = dot(widened(grad[...].reshape(PLANES * 24, DEPTH)), back_z)
    flat = flat.reshape(PLANES, 24, DEPTH)
    for x, value in enumerate(from_modes([flat[k] for k in range(PLANES)])):
        grad[x] = value

    def middle():
        sums[0:144, :] = kernel_sums(l_taps, h_hi, h_lo, 1)

    def late():
        sums[144:, :] = kernel_sums(u_taps, p_hi, p_lo, -1)

    pullback(
        field, grad, hidden, weights, back2, back1, l_taps, p_hi, p_lo, work, slope, middle, late
    )
    for k, value in enumerate(to_modes([slope[x, 0:40, :] for x in range(PLANES)])):
        modes[k] = value
    flat = dot(widened(modes[...].reshape(PLANES * 40, DEPTH)), to_z[...])
    modes[...] = flat.reshape(PLANES, 40, DEPTH)
    for h in range(2):
        for k in range(PLANES):
            for m in range(3):
                first = m * REACH + RIM + 4 * h
                rows6[h, k, 4 * m : 4 * m + 4, :] = modes[k, first : first + 4, :]
                first = m * REACH + (RIM + SLAB) * h
                rows6[h, k, 12 + 2 * m : 14 + 2 * m, :] = modes[k, first : first + 2, :]
            rows6[h, k, 18:24, :] = jnp.zeros((6, DEPTH), jnp.float32)
    scatter_modes(lambda h, k: rows6[h, k], 24, out)


def third_kernel_body(
    recv, field, hidden, weights, u_taps, h_hi, h_lo, back2, back1, from_z, old_sums,
    spread_t, mask, lift,
    out,
    flat, grad, modes, l_taps, p_hi, p_lo, work, slope, sums, pieces,
):
    back_z = from_z[...]
    flat[...] = jnp.zeros_like(flat)
    for device in range(16):
        for m in range(3):
            flat[device, 4 * m : 4 * m + 4, :] = recv[device, m]
    for h in range(2):
        for k in range(PLANES):
            modes[k] = gather_modes(flat, h, k, 0, 16)
        moved_back = dot(widened(modes[...].reshape(PLANES * 16, DEPTH)), back_z)
        modes[...] = moved_back.reshape(PLANES, 16, DEPTH)
        for x, value in enumerate(from_modes([modes[k] for k in range(PLANES)])):
            for m in range(3):
                grad[x, m * SLAB + 4 * h : m * SLAB + 4 * h + 4, :] = value[m * 4 : m * 4 + 4, :]

    def middle():
        sums[0:144, :] = old_sums[0:144, :] + kernel_sums(l_taps, h_hi, h_lo, 1)
        sums[144:, :] = old_sums[144:, :] + kernel_sums(u_taps, p_hi, p_lo, -1)

    def late():
        pack_grads(sums, spread_t, mask, lift, pieces)

    pullback(
        field, grad, hidden, weights, back2, back1, l_taps, p_hi, p_lo, work, slope, middle, late
    )
    for x in range(PLANES):
        for i in range(9):
            out[x, i] = slope[x, 4 * i : 4 * i + 4, :]
    for x in range(PLANES):
        for i in range(8):
            out[x, 9 + i] = pieces[4 * i : 4 * i + 4, :]


def pack_grads(sums, spread_t, mask, lift, pieces):
    whole = split(sums[...])
    empty = jnp.zeros((32, 512 - DEEP), jnp.float32)
    rows = []
    for b in range(3):
        both = jnp.concatenate([whole[0] * mask[b], whole[1] * mask[b]], axis=0)
        rows.append(dot(spread_t[...], both))
        rows.append(empty)
    placed = dot(stacked(beside(rows)), lift[...])
    placed = placed[:32] + placed[32:]
    pieces[0:28, :] = placed[0:28, 0:128]
    rest = placed[:, 128:]
    lane = lax.broadcasted_iota(jnp.int32, rest.shape, 1)
    low, high = jnp.where(lane < 64, rest, 0.0), jnp.where(lane < 64, 0.0, rest)
    total = turn(high[4:8], 16) + turn(high[8:12], 17)
    for i in range(7):
        total = total + turn(low[4 * i : 4 * i + 4], 16 * i)
    pieces[28:32, :] = total


def fold_kernel(recv, main, edge, ext):
    ext[...] = jnp.zeros_like(ext)
    total = None
    for q in range(PLANES):
        for m in range(3):
            for i in range(3):
                first = 8 * q + 6 + 4 * i
                ext[m, first : first + 4, :] += recv[q, 3 * m + i]
        block = recv[q, 9:17]
        total = block if total is None else total + block
    for m in range(3):
        main[m, 0] = ext[m, 8:72, :]
        edge[m * 8 : m * 8 + 2, :] = ext[m, 72:74, :]
        edge[m * 8 + 2 : m * 8 + 4, :] = ext[m, 6:8, :]
        edge[m * 8 + 4 : m * 8 + 8, :] = jnp.zeros((4, DEPTH), jnp.float32)
    for i in range(8):
        edge[24 + 4 * i : 28 + 4 * i, :] = total[i]


def last_kernel(main, edge, other, out, first, end1, second, end2, turned):
    for m in range(3):
        out[m, 0] = main[m, 0]
        out[m, 0, 0:2, :] += other[m * 8 : m * 8 + 2, :]
        out[m, 0, 62:64, :] += other[m * 8 + 2 : m * 8 + 4, :]
    grads = edge[24:56, :] + other[24:56, :]
    for slot in range(8):
        turned[slot] = turn(grads, -16 * slot)
    for b in range(3):
        for a in range(3):
            for e in range(3):
                for i in range(9):
                    row = e * 6 + i if i < 6 else 18 + e * 3 + i - 6
                    slot = 3 * b + a
                    slot, inner = (slot, row) if slot < 8 else (row // 4, 28 + row % 4)
                    line = turned[slot, inner, 0:16]
                    if i < 6:
                        second[i * 9 + a * 3 + b, e, :] = line
                    else:
                        first[(i - 6) * 9 + a * 3 + b, e, :] = line
    end1[...] = turned[1, 27:28, 0:16]
    for o in range(COEFFS):
        inner, place = 28 + (6 + o) % 4, (6 + o) // 4 - 1
        end2[0:1, o : o + 1] = turned[7, inner : inner + 1, place : place + 1]


def slab_device(velocity, cotangent, first_kernel, first_bias, second_kernel, second_bias):
    c = constants()
    half = jnp.bfloat16
    f32 = lambda *dims: pltpu.VMEM(dims, jnp.float32)
    b16 = lambda *dims: pltpu.VMEM(dims, half)
    swap = [(0, 1), (1, 0)]

    other = lax.ppermute(velocity, "py", swap)
    fields = jnp.concatenate([velocity, cotangent], axis=0)
    packed = call(
        pack_kernel, shape(PLANES, 64, DEPTH), (fields,), [f32(3, 80, DEPTH)], room=4
    )
    packed = call(rim_kernel, shape(PLANES, 15, 4, DEPTH), (packed, other), room=4)
    recv = lax.all_to_all(packed, "px", 0, 0)

    fwd2, fwd1, back2, back1, to_z = call(
        weights_kernel,
        [
            shape(288, DEEP, kind=half),
            shape(2 * HID, STACK, kind=half),
            shape(2 * HID, STACK, kind=half),
            shape(288, DEEP, kind=half),
            shape(3 * DEPTH, DEPTH, kind=half),
        ],
        (
            jnp.transpose(first_kernel, (1, 2, 3, 4, 0)).reshape(27, 3, CHANNELS),
            jnp.transpose(second_kernel, (0, 2, 3, 4, 1)).reshape(54, 3, CHANNELS),
            first_bias.reshape(1, CHANNELS),
            second_bias.reshape(1, COEFFS),
            c["to_z"],
        ),
        [
            f32(3, 96, CHANNELS),
            f32(27, 3, CHANNELS),
            f32(54, 3, CHANNELS),
            f32(1, CHANNELS),
            f32(1, COEFFS),
            pltpu.SemaphoreType.DMA((4,)),
        ],
        away=(0, 1, 2, 3),
    )

    near = lambda rows: [b16(rows, FLAT), b16(rows, FLAT)]
    stacks = near(288)[:1] + near(BROAD) + near(288)[:1] + near(BROAD)
    sent, field, hidden, weights, *kept = call(
        first_kernel_body,
        [
            shape(16, 24, DEPTH),
            shape(PLANES, 48, DEPTH),
            shape(HID, FLAT),
            shape(LOG, FLAT),
            shape(288, FLAT, kind=half),
            shape(BROAD, FLAT, kind=half),
            shape(BROAD, FLAT, kind=half),
        ],
        (recv, fwd1, fwd2, to_z),
        [f32(144, FLAT), f32(2, PLANES, 24, DEPTH), f32(PLANES, 24, DEPTH)],
    )
    both = ("px", "py")
    moved_modes = lax.all_to_all(sent, both, 0, 0)
    moved_modes = call(both_kernel, shape(16, 32, DEPTH), (moved_modes, c["both_in"], c["both_out"]))
    moved_modes = lax.all_to_all(moved_modes, both, 0, 0)

    sent, sums = call(
        second_kernel_body,
        [shape(16, 9, 2, DEPTH), shape(288, DEEP)],
        (moved_modes, fwd1, fwd2, back2, back1, to_z, c["from_z"]),
        [
            f32(PLANES, 48, DEPTH),
            f32(HID, FLAT),
            f32(PLANES, 24, DEPTH),
            f32(PLANES, 40, DEPTH),
            f32(2, PLANES, 24, DEPTH),
            f32(LOG, FLAT),
            f32(144, FLAT),
            f32(PLANES, 48, DEPTH),
        ]
        + stacks,
    )
    moved_modes = lax.all_to_all(sent, both, 0, 0)
    moved_modes = call(
        one_kernel,
        shape(16, 3, 4, DEPTH),
        (moved_modes, c["one_in"], c["one_out"]),
        [f32(3, 96, DEPTH)],
    )
    moved_modes = lax.all_to_all(moved_modes, both, 0, 0)

    sent = call(
        third_kernel_body,
        shape(PLANES, 17, 4, DEPTH),
        (
            moved_modes, field, hidden, weights, *kept, back2, back1, c["from_z"], sums,
            c["spread_t"], c["mask"], c["lift"],
        ),
        [f32(16, 16, DEPTH), f32(PLANES, 24, DEPTH), f32(PLANES, 16, DEPTH)]
        + stacks[3:]
        + [
            f32(144, FLAT),
            f32(PLANES, 48, DEPTH),
            f32(288, DEEP),
            f32(32, DEPTH),
        ],
    )
    recv = lax.all_to_all(sent, "px", 0, 0)
    main, edge = call(
        fold_kernel, [shape(3, 1, 64, DEPTH), shape(56, DEPTH)], (recv,), [f32(3, 80, DEPTH)]
    )
    other = lax.ppermute(edge, "py", swap)
    grad_velocity, first, end1, second, end2 = call(
        last_kernel,
        [
            shape(3, 1, 64, DEPTH),
            shape(27, 3, CHANNELS),
            shape(1, CHANNELS),
            shape(54, 3, CHANNELS),
            shape(1, COEFFS),
        ],
        (main, edge, other),
        [f32(8, 32, DEPTH)],
    )
    return (
        grad_velocity,
        jnp.transpose(first.reshape(3, 3, 3, 3, CHANNELS), (4, 0, 1, 2, 3)),
        end1.reshape(CHANNELS),
        jnp.transpose(second.reshape(COEFFS, 3, 3, 3, CHANNELS), (0, 4, 1, 2, 3)),
        end2.reshape(COEFFS),
    )


def fits_slabs(mesh):
    return mesh.shape["px"] == PLANES and mesh.shape["py"] == 2


def solution(mesh):
    return jax.shard_map(
        slab_device if fits_slabs(mesh) else on_device,
        mesh=mesh,
        in_specs=(
            P(None, ("groups", "px"), "py", None),
            P(None, ("groups", "px"), "py", None),
            P(),
            P(),
            P(),
            P(),
        ),
        out_specs=(
            P(None, ("groups", "px"), "py", None),
            P("groups", None, None, None, None),
            P("groups"),
            P("groups", None, None, None, None),
            P("groups"),
        ),
        check_vma=False,
    )
```
